32 devices in a mesh: dp: 8 (over z, y), ctx: 4 (over x, core).
Axes of the slice: x: 2, y: 2, z: 4, core: 2. Of those that a mesh axis runs over, the one named last changes fastest.
Arguments:
- tokens: bfloat16 [8, 1376, 1024], P('dp', 'ctx'), may hold values from -6 to 6
- counts: int32 [8, 4], P('dp', 'ctx'), may hold values from 301 to 344, as said below
- w_qkv: bfloat16 [1024, 3072], P(('dp', 'ctx')), may hold values from -0.1875 to 0.1875
- w_proj: bfloat16 [1024, 1024], P(None, ('dp', 'ctx')), may hold values from -2.5 to 2.5
- w_fc1: bfloat16 [1024, 4096], P(('dp', 'ctx')), may hold values from -0.1875 to 0.1875
- fc1_bias: bfloat16 [4096], P(('dp', 'ctx')), may hold values from -3 to 3
- w_fc2: bfloat16 [4096, 1024], P(None, ('dp', 'ctx')), may hold values from -0.09375 to 0.09375
- vectors: bfloat16 [10, 1024], P(None, ('dp', 'ctx')), as said below
- cotangent: bfloat16 [8, 1376, 1024], P('dp', 'ctx'), may hold values from -6 to 6
Outputs:
- output: bfloat16 [8, 1376, 1024], P('dp', 'ctx')
- input_grad: bfloat16 [8, 1376, 1024], P('dp', 'ctx')
- grad_qkv: float32 [1024, 3072], P(('dp', 'ctx'))
- grad_proj: float32 [1024, 1024], P(None, ('dp', 'ctx'))
- grad_fc1: float32 [1024, 4096], P(('dp', 'ctx'))
- grad_fc1_bias: float32 [4096], P(('dp', 'ctx'))
- grad_fc2: float32 [4096, 1024], P(None, ('dp', 'ctx'))
- grad_vectors: float32 [10, 1024], P(None, ('dp', 'ctx'))
The draws below stay inside these ranges and needn't reach their ends.
Inputs may be any that keep to these rules, and one draw needn't show every extreme that they name: `counts`: in every image one device holds 344 live tokens and another 344 - 344 // 8. `vectors`: rows 0, 5, 6 and 9 are positive.
All inputs are finite; a program needn't handle non-finite values.
Results may differ from the reference program's by a relative error of at most 0.017.
Values may be sent and summed in bfloat16 or wider, within the bound.
No kernel may reach another device: no remote copies, remote signals or barrier semaphores. Data moves between devices by JAX's collectives and lax.ppermute only.
A program may use at most 192 MiB of HBM per device.

```python
import jax
import jax.numpy as jnp
from jax import lax

D = 1024
FF = 4096
HD = 64
CAP = 344
IMAGES = 8
SLOTS = 1376


def draw_counts(key, part):
    key = jax.random.fold_in(key, 11)
    columns = SLOTS // CAP
    top_key, offset_key, fill_key = jax.random.split(key, 3)
    filled = jax.random.randint(fill_key, (IMAGES, columns), CAP - CAP // 8, CAP + 1)
    top_column = jax.random.randint(top_key, (IMAGES, 1), 0, columns)
    offset = jax.random.randint(offset_key, (IMAGES, 1), 1, columns)
    bottom_column = (top_column + offset) % columns
    placed = lax.broadcasted_iota(jnp.int32, (IMAGES, columns), 1)
    filled = jnp.where(placed == bottom_column, CAP - CAP // 8, filled)
    return jnp.where(placed == top_column, CAP, filled).astype(jnp.int32)


def draw_vectors(key, part):
    key = jax.random.fold_in(key, 23)
    positive_key, signed_key = jax.random.split(key, 2)
    positive = jnp.exp(jax.random.uniform(positive_key, (4, D), jnp.float32, -0.69, 0.69))
    factors = jnp.array([0.5, 0.5, 0.05, 0.5, 0.5, 0.5], jnp.float32)[:, None]
    signed = jax.random.normal(signed_key, (6, D), jnp.float32) * factors
    stacked = jnp.stack([positive[0], signed[0], signed[1], signed[2], signed[3], positive[1], positive[2], signed[4], signed[5], positive[3]])
    return stacked.astype(jnp.bfloat16)


def strengthened(entries, key, source, target, shards_of, factor):
    owner, partner = [(jnp.arange(entries.shape[axis_at]) // (entries.shape[axis_at] // shards_of)).reshape([-1 if axis == axis_at else 1 for axis in range(entries.ndim)]) for axis_at in (source, target)]
    chosen = jax.random.permutation(key, shards_of)[partner]
    strong = (owner == chosen) | (owner == (partner + shards_of // 2) % shards_of)
    return jnp.where(strong, factor * entries, entries)


def block_levels(key, dims, pieces, least, high):
    def one(dim, shards_of):
        draws = jax.random.uniform(jax.random.fold_in(jax.random.fold_in(key, 6), dim), (shards_of,), jnp.float32, least / len(pieces), high / len(pieces))
        return jnp.repeat(jnp.exp(draws), dims[dim] // shards_of).reshape((-1,) + (1,) * (len(dims) - dim - 1))

    factor_of = one(*pieces[0])
    for cut in pieces[1:]:
        factor_of = factor_of * one(*cut)
    return factor_of


def normal_values(key, shape, scale, reach, shards=(), kind=jnp.bfloat16):
    entries = jax.random.normal(key, shape, jnp.float32) * scale
    if len(shards) > 0:
        entries = block_levels(key, shape, shards, -0.22, 0.18) * entries
    return jnp.clip(entries, min=-reach, max=reach).astype(kind)


def noise_with(stream_key, shape, deviation, most, cuts, heavy, dtype=jnp.bfloat16):
    values = deviation * jax.random.normal(stream_key, shape, jnp.float32)
    if cuts:
        values = values * block_levels(stream_key, shape, cuts, -0.22, 0.18)
    return jnp.clip(strengthened(values, jax.random.fold_in(stream_key, 3), *heavy), -most, most).astype(dtype)


def setup_inputs(seed: int = 0) -> dict:
    splits = jax.random.split(jax.random.key(seed), 10)
    tokens = noise_with(splits[0], (IMAGES, SLOTS, D), 1.0, 6.0, ((0, 8), (1, 4)), (0, 2, 8, 2.0))
    counts = draw_counts(jax.random.fold_in(splits[9], 71), 0)
    w_qkv = normal_values(splits[2], (D, 3 * D), D ** -0.5, 0.1875, ((0, 32),))
    w_proj = normal_values(splits[3], (D, D), (max(1, D * 8 // SLOTS)) ** -0.5, 2.5, ((1, 32),))
    w_fc1 = normal_values(splits[4], (D, FF), D ** -0.5, 0.1875, ((0, 32),))
    fc1_bias = normal_values(splits[5], (FF,), 0.5, 3.0, ((0, 32),))
    w_fc2 = normal_values(splits[6], (FF, D), FF ** -0.5, 0.09375, ((1, 32),))
    vectors = draw_vectors(jax.random.fold_in(splits[9], 71), 0)
    cotangent = noise_with(splits[8], (IMAGES, SLOTS, D), 1.0, 6.0, ((0, 8), (1, 4)), (0, 2, 8, 2.0))
    return {"tokens": tokens, "counts": counts, "w_qkv": w_qkv, "w_proj": w_proj, "w_fc1": w_fc1, "fc1_bias": fc1_bias, "w_fc2": w_fc2, "vectors": vectors, "cotangent": cotangent}


@jax.custom_vjp
def low(v):
    return lax.optimization_barrier(v.astype(jnp.bfloat16)).astype(jnp.float32)

@jax.custom_vjp
def low_back(v):
    return v

def low_keep(v):
    return (low(v), None)

def low_pass(kept, grad):
    return (grad,)

def back_keep(v):
    return (v, None)

def back_low(kept, grad):
    return (low(grad),)
low.defvjp(low_keep, low_pass)
low_back.defvjp(back_keep, back_low)
EPSILON = 1e-06
MASKED_SCORE = -1e+30
HIGHEST = lax.Precision.HIGHEST

def normalize(inputs, gain, shift):
    center = lax.optimization_barrier(jnp.mean(inputs, axis=-1, keepdims=True))
    centered = inputs - center
    spread = lax.optimization_barrier(jnp.mean(centered * centered, axis=-1, keepdims=True))
    return centered * lax.rsqrt(spread + EPSILON) * gain + shift

def matmul(left, right):
    return jnp.dot(left, right, precision=HIGHEST)

def image_block(params, image, live):
    w_qkv, w_proj, w_fc1, fc1_bias, w_fc2, vectors = params
    width = image.shape[1]
    head_count = width // HD
    slot_count = image.shape[0]
    normed1 = low(normalize(image, vectors[0], vectors[1]))
    qkv_bias = jnp.concatenate([vectors[2], jnp.zeros_like(vectors[2]), vectors[3]])
    projected = low(low_back(matmul(normed1, w_qkv) + qkv_bias))

    def heads_first(block):
        return block.reshape(slot_count, head_count, HD).transpose(1, 0, 2)
    queries = heads_first(projected[:, :width])
    key_rows = heads_first(projected[:, width:2 * width])
    value_rows = heads_first(projected[:, 2 * width:])
    raw_score = low_back(jnp.einsum('hqd,hkd->hqk', queries, key_rows, precision=HIGHEST))
    scores = jnp.where(live[None, None, :], raw_score * HD ** (-0.5), MASKED_SCORE)
    row_top = lax.optimization_barrier(jnp.max(scores, axis=-1, keepdims=True))
    exponent = jnp.exp(scores - row_top)
    row_total = lax.optimization_barrier(jnp.sum(exponent, axis=-1, keepdims=True))
    attended = jnp.einsum('hqk,hkd->hqd', low(exponent), value_rows, precision=HIGHEST) / row_total
    attended = low(low_back(attended.transpose(1, 0, 2).reshape(slot_count, width)))
    branch_one = low_back(matmul(attended, w_proj) + vectors[4])
    middle = image + vectors[5] * branch_one
    normed2 = low(normalize(middle, vectors[6], vectors[7]))
    hidden_pre = low_back(matmul(normed2, w_fc1) + fc1_bias)
    activated = low(jax.nn.gelu(hidden_pre, approximate=False))
    branch_two = low_back(matmul(activated, w_fc2) + vectors[8])
    return middle + vectors[9] * branch_two

def forward(inputs, params, live):

    def one_image(pair):
        return image_block(params, pair[0], pair[1])
    return lax.map(jax.checkpoint(one_image), (inputs, live))

def reference(tokens, counts, w_qkv, w_proj, w_fc1, fc1_bias, w_fc2, vectors, cotangent):
    slot_index = lax.broadcasted_iota(jnp.int32, (1, SLOTS), 1)
    within = slot_index % CAP
    live = within < jnp.repeat(counts, CAP, axis=1)
    params = tuple((weight.astype(jnp.float32) for weight in (w_qkv, w_proj, w_fc1, fc1_bias, w_fc2, vectors)))
    inputs = tokens.astype(jnp.float32)

    def whole(values_in, *weights):
        return forward(values_in, weights, live)
    result, pullback = jax.vjp(whole, inputs, *params)
    start_grad = cotangent.astype(jnp.float32) * live[:, :, None].astype(jnp.float32)
    grads = pullback(start_grad)
    return (result.astype(jnp.bfloat16), grads[0].astype(jnp.bfloat16), grads[1], grads[2], grads[3], grads[4], grads[5], grads[6])
```

```python
import jax
import jax.numpy as jnp
from jax import lax
from jax.experimental import pallas as pl
from jax.experimental.pallas import tpu as pltpu
from jax.sharding import PartitionSpec as P

HD = 64
PAIR = 2 * HD
EXTRA = 128
EPSILON = 1e-06
MASKED_SCORE = -1e30
SQRT_HALF = 0.7071067811865476
INV_ROOT_TWO_PI = 0.3989422804014327
BF = jnp.bfloat16
F32 = jnp.float32


def dot(left, right, left_dim, right_dim):
    return lax.dot_general(
        left, right, (((left_dim,), (right_dim,)), ((), ())), preferred_element_type=F32
    )


def unit_rows(inputs):
    centered = inputs - jnp.mean(inputs, axis=-1, keepdims=True)
    spread = jnp.mean(centered * centered, axis=-1, keepdims=True)
    inverse = lax.rsqrt(spread + EPSILON)
    return (centered * inverse, inverse)


def norm_back(grad_in, unit, inverse, gain):
    scaled = grad_in * gain
    inner = (
        scaled
        - jnp.mean(scaled, axis=-1, keepdims=True)
        - unit * jnp.mean(scaled * unit, axis=-1, keepdims=True)
    )
    return inner * inverse


def query_chunks(length):
    step = 512
    return [(start, min(step, length - start)) for start in range(0, length, step)]


def attend_kernel(qkv_ref, bias_ref, out_ref, lse_ref):
    length = qkv_ref.shape[0]
    key_bias = bias_ref[...]
    for head in range(2):
        keys = qkv_ref[:, PAIR + head * HD : PAIR + (head + 1) * HD]
        values = qkv_ref[:, 2 * PAIR + head * HD : 2 * PAIR + (head + 1) * HD]
        for start, size in query_chunks(length):
            queries = qkv_ref[start : start + size, head * HD : (head + 1) * HD]
            queries = queries * jnp.asarray(HD**-0.5, BF)
            scores = dot(keys, queries, 1, 1) + key_bias
            top = jnp.max(scores, axis=0, keepdims=True)
            expo = jnp.exp(scores - top)
            total = jnp.sum(expo, axis=0, keepdims=True)
            mixed = dot(values, expo.astype(BF), 0, 0) / total
            out_ref[start : start + size, head * HD : (head + 1) * HD] = mixed.T
            lse_ref[0, head : head + 1, start : start + size] = top + jnp.log(total)


def attend(qkv, key_bias):
    length, width = qkv.shape
    pairs = width // (3 * PAIR)
    return pl.pallas_call(
        attend_kernel,
        grid=(pairs,),
        in_specs=[
            pl.BlockSpec((length, 3 * PAIR), lambda p: (0, p)),
            pl.BlockSpec((length, 1), lambda p: (0, 0)),
        ],
        out_specs=[
            pl.BlockSpec((length, PAIR), lambda p: (0, p)),
            pl.BlockSpec((1, 2, length), lambda p: (p, 0, 0)),
        ],
        out_shape=[
            jax.ShapeDtypeStruct((length, pairs * PAIR), F32),
            jax.ShapeDtypeStruct((pairs, 2, length), F32),
        ],
        compiler_params=pltpu.CompilerParams(vmem_limit_bytes=48 * 1024 * 1024),
        cost_estimate=pl.CostEstimate(
            flops=pairs * 2 * 4 * length * length * 256,
            bytes_accessed=length * width * 4,
            transcendentals=pairs * 2 * length * length,
        ),
        name="attend",
    )(qkv, key_bias)


def attend_back_kernel(qkv_ref, bias_ref, att_ref, grad_ref, lse_ref, out_ref):
    length = qkv_ref.shape[0]
    factor = HD**-0.5
    key_bias = bias_ref[...]
    for head in range(2):
        low, high = head * HD, (head + 1) * HD
        keys = qkv_ref[:, PAIR + low : PAIR + high]
        values = qkv_ref[:, 2 * PAIR + low : 2 * PAIR + high]
        key_grad = jnp.zeros((length, HD), F32)
        value_grad = jnp.zeros((length, HD), F32)
        for start, size in query_chunks(length):
            rows = slice(start, start + size)
            queries = qkv_ref[rows, low:high] * jnp.asarray(factor, BF)
            grads = grad_ref[rows, low:high]
            product = grads.astype(F32) * att_ref[rows, low:high]
            delta = jnp.sum(product.T, axis=0, keepdims=True)
            scores = dot(keys, queries, 1, 1) + key_bias
            probs = jnp.exp(scores - lse_ref[0, head : head + 1, rows])
            value_grad += dot(probs.astype(BF), grads, 1, 0)
            raw = (probs * (dot(values, grads, 1, 1) - delta)).astype(BF)
            key_grad += dot(raw, queries, 1, 0)
            query_grad = dot(keys, raw, 0, 0).T * factor
            out_ref[rows, low:high] = query_grad.astype(BF)
        out_ref[:, PAIR + low : PAIR + high] = key_grad.astype(BF)
        out_ref[:, 2 * PAIR + low : 2 * PAIR + high] = value_grad.astype(BF)


def attend_back(qkv, key_bias, attended, grads, lse):
    length, width = qkv.shape
    pairs = width // (3 * PAIR)
    return pl.pallas_call(
        attend_back_kernel,
        grid=(pairs,),
        in_specs=[
            pl.BlockSpec((length, 3 * PAIR), lambda p: (0, p)),
            pl.BlockSpec((length, 1), lambda p: (0, 0)),
            pl.BlockSpec((length, PAIR), lambda p: (0, p)),
            pl.BlockSpec((length, PAIR), lambda p: (0, p)),
            pl.BlockSpec((1, 2, length), lambda p: (p, 0, 0)),
        ],
        out_specs=pl.BlockSpec((length, 3 * PAIR), lambda p: (0, p)),
        out_shape=jax.ShapeDtypeStruct((length, width), BF),
        compiler_params=pltpu.CompilerParams(vmem_limit_bytes=48 * 1024 * 1024),
        cost_estimate=pl.CostEstimate(
            flops=pairs * 2 * 10 * length * length * 256,
            bytes_accessed=length * width * 6,
            transcendentals=pairs * 2 * length * length,
        ),
        name="attend_back",
    )(qkv, key_bias, attended, grads, lse)


def local(tokens, counts, w_qkv, w_proj, w_fc1, fc1_bias, w_fc2, vectors, cotangent):
    _, capacity, width = tokens.shape
    hidden = w_fc1.shape[1]
    rows = w_qkv.shape[0]
    group = lax.axis_size("ctx")
    place = lax.axis_index("ctx")
    head_width = width // group
    pairs = head_width // PAIR
    hidden_part = hidden // group
    bias_cols = hidden // width
    vector_count = vectors.shape[0]

    def swap(value, bit):
        return lax.ppermute(value, "ctx", [(i, i ^ bit) for i in range(group)])

    def gather(own):
        pieces = {0: own}
        bit = group // 2
        while bit >= 1:
            order = sorted(pieces)
            other = swap(jnp.concatenate([pieces[j] for j in order], axis=0), bit)
            size = own.shape[0]
            for spot, j in enumerate(order):
                pieces[j ^ bit] = other[spot * size : (spot + 1) * size]
            bit //= 2
        return jnp.concatenate([pieces[j] for j in range(group)], axis=0)

    def scatter(parts):
        pieces = {j: parts[j * capacity : (j + 1) * capacity] for j in range(group)}
        bit = 1
        while bit < group:
            sent = sorted(j for j in pieces if j & bit)
            low = jnp.concatenate([pieces[j] for j in sent], axis=0).astype(BF)
            other = swap(low, bit).astype(F32)
            for spot, j in enumerate(sent):
                piece = other[spot * capacity : (spot + 1) * capacity]
                pieces[j ^ bit] = pieces[j ^ bit] + piece
                del pieces[j]
            bit *= 2
        return pieces[0]

    def exchange(blocks):
        relative = [lax.dynamic_index_in_dim(blocks, place, 0, False)]
        for bit in range(1, group):
            sent = lax.dynamic_index_in_dim(blocks, place ^ bit, 0, False)
            relative.append(swap(sent, bit))
        stacked = jnp.stack(relative)
        ordered = [lax.dynamic_index_in_dim(stacked, place ^ s, 0, False) for s in range(group)]
        return (jnp.stack(ordered), relative)

    part_qkv = (
        w_qkv.reshape(rows, 3, group, pairs, PAIR)
        .transpose(2, 0, 3, 1, 4)
        .reshape(group, rows, 3 * head_width)
    )
    part_proj = w_proj.reshape(group, head_width, rows).transpose(0, 2, 1)
    count = counts[0, 0]
    extra = jnp.concatenate(
        [
            vectors.T,
            fc1_bias.reshape(rows, bias_cols),
            jnp.broadcast_to((count // 128).astype(BF), (rows, 1)),
            jnp.broadcast_to((count % 128).astype(BF), (rows, 1)),
        ],
        axis=1,
    )
    extra = jnp.pad(extra, ((0, 0), (0, EXTRA - extra.shape[1])))
    part_extra = jnp.broadcast_to(extra[None], (group, rows, EXTRA))
    part_fc1 = w_fc1.reshape(rows, group, hidden_part).transpose(1, 0, 2)
    part_fc2 = w_fc2.reshape(group, hidden_part, rows).transpose(0, 2, 1)
    first, first_relative = exchange(jnp.concatenate([part_qkv, part_proj, part_extra], axis=2))
    second, _ = exchange(jnp.concatenate([part_fc1, part_fc2], axis=2))
    first_all = lax.all_gather(first.reshape(group * rows, -1), "dp", axis=0, tiled=True)
    second_all = lax.all_gather(second.reshape(group * rows, -1), "dp", axis=0, tiled=True)
    weight_qkv = first_all[:, : 3 * head_width]
    weight_proj = first_all[:, 3 * head_width : 4 * head_width]
    gathered_extra = first_all[:, 4 * head_width :].astype(F32)
    vector_rows = gathered_extra[:, :vector_count].T
    bias_all = gathered_extra[:, vector_count : vector_count + bias_cols].reshape(hidden)
    bias_fc1 = lax.dynamic_slice_in_dim(bias_all, place * hidden_part, hidden_part)
    weight_fc1 = second_all[:, :hidden_part]
    weight_fc2 = second_all[:, hidden_part:]

    def own_part(row):
        return lax.dynamic_slice_in_dim(row, place * head_width, head_width)

    count_column = 4 * head_width + vector_count + bias_cols
    live_rows = []
    for block in first_relative:
        piece = block[0, count_column : count_column + 2].astype(F32)
        bound = piece[0] * 128.0 + piece[1]
        slot = lax.broadcasted_iota(jnp.int32, (capacity, 1), 0).astype(F32)
        live_rows.append(slot < bound)
    live = jnp.concatenate(live_rows, axis=0)
    key_bias = jnp.where(live, 0.0, MASKED_SCORE).astype(F32)

    tokens_all = gather(tokens[0])
    cotangent_all = gather(cotangent[0])

    inputs = tokens[0].astype(F32)
    unit1_all, _ = unit_rows(tokens_all.astype(F32))
    normed1 = (unit1_all * vector_rows[0] + vector_rows[1]).astype(BF)
    bias_q = own_part(vector_rows[2]).reshape(pairs, 1, PAIR)
    bias_v = own_part(vector_rows[3]).reshape(pairs, 1, PAIR)
    qkv_bias = jnp.concatenate([bias_q, jnp.zeros_like(bias_q), bias_v], axis=1).reshape(-1)
    qkv = (dot(normed1, weight_qkv, 1, 0) + qkv_bias).astype(BF)
    attended, lse = attend(qkv, key_bias)
    attended_low = attended.astype(BF)
    branch1 = scatter(dot(attended_low, weight_proj, 1, 1)) + vector_rows[4]
    middle = inputs + vector_rows[5] * branch1
    unit2, inverse2 = unit_rows(middle)
    normed2 = gather((unit2 * vector_rows[6] + vector_rows[7]).astype(BF))
    hidden_pre = dot(normed2, weight_fc1, 1, 0) + bias_fc1
    gauss_cdf = 0.5 * (1.0 + lax.erf(hidden_pre * SQRT_HALF))
    activated = (hidden_pre * gauss_cdf).astype(BF)
    slope = gauss_cdf + hidden_pre * jnp.exp(-0.5 * hidden_pre * hidden_pre) * INV_ROOT_TWO_PI
    branch2 = scatter(dot(activated, weight_fc2, 1, 1)) + vector_rows[8]
    output = (middle + vector_rows[9] * branch2).astype(BF)

    out_grad_all = jnp.where(live, cotangent_all.astype(F32), 0.0)
    out_grad = jnp.where(live_rows[0], cotangent[0].astype(F32), 0.0)
    grad_scale2 = jnp.sum(out_grad * branch2, axis=0)
    mlp_grad = (out_grad_all * vector_rows[9]).astype(BF)
    own_mlp_grad = (out_grad * vector_rows[9]).astype(BF)
    grad_fbias = jnp.sum(own_mlp_grad.astype(F32), axis=0)
    grad_wfc2 = dot(mlp_grad, activated, 0, 0).astype(BF)
    pre_grad = (dot(mlp_grad, weight_fc2, 1, 0) * slope).astype(BF)
    grad_bfc1 = jnp.sum(pre_grad.astype(F32), axis=0)
    grad_wfc1 = dot(normed2, pre_grad, 0, 0).astype(BF)
    owned_mlp = lax.psum_scatter(
        jnp.concatenate([grad_wfc1, grad_wfc2], axis=1), "dp", scatter_dimension=0, tiled=True
    )
    norm2_grad = scatter(dot(pre_grad, weight_fc1, 1, 1))
    grad_gain2 = jnp.sum(norm2_grad * unit2, axis=0)
    grad_shift2 = jnp.sum(norm2_grad, axis=0)
    middle_grad = out_grad + norm_back(norm2_grad, unit2, inverse2, vector_rows[6])
    grad_scale1 = jnp.sum(middle_grad * branch1, axis=0)
    own_branch_grad = (middle_grad * vector_rows[5]).astype(BF)
    grad_pbias = jnp.sum(own_branch_grad.astype(F32), axis=0)
    branch_grad = gather(own_branch_grad)
    attended_grad = dot(branch_grad, weight_proj, 1, 0).astype(BF)
    grad_wproj = dot(branch_grad, attended_low, 0, 0).astype(BF)
    qkv_grad = attend_back(qkv, key_bias, attended, attended_grad, lse)
    qkv_sums = jnp.sum(qkv_grad.astype(F32), axis=0).reshape(pairs, 3, PAIR)
    grad_wqkv = dot(normed1, qkv_grad, 0, 0).astype(BF)
    norm1_part = dot(qkv_grad, weight_qkv, 1, 1)
    grad_gain1 = jnp.sum(norm1_part * unit1_all, axis=0)
    grad_shift1 = jnp.sum(norm1_part, axis=0)

    def placed(part, length):
        return lax.dynamic_update_slice_in_dim(
            jnp.zeros((length,), F32), part.reshape(-1), place * part.size, 0
        )

    grad_rows = jnp.stack(
        [
            grad_gain1,
            grad_shift1,
            placed(qkv_sums[:, 0], width),
            placed(qkv_sums[:, 2], width),
            grad_pbias,
            grad_scale1,
            grad_gain2,
            grad_shift2,
            grad_fbias,
            grad_scale2,
        ]
    )
    grad_extra = jnp.concatenate(
        [grad_rows.T, placed(grad_bfc1, hidden).reshape(width, bias_cols)], axis=1
    )
    grad_extra = jnp.pad(grad_extra, ((0, 0), (0, EXTRA - grad_extra.shape[1]))).astype(BF)
    owned_attn = lax.psum_scatter(
        jnp.concatenate([grad_wqkv, grad_wproj, grad_extra], axis=1),
        "dp",
        scatter_dimension=0,
        tiled=True,
    )
    norm1_grad = scatter(norm1_part)
    unit1, inverse1 = unit_rows(inputs)
    input_grad = (middle_grad + norm_back(norm1_grad, unit1, inverse1, vector_rows[0])).astype(BF)

    final_mlp, _ = exchange(owned_mlp.reshape(group, rows, -1))
    final_attn, _ = exchange(owned_attn.reshape(group, rows, -1))
    final_mlp = final_mlp.astype(F32)
    final_attn = final_attn.astype(F32)
    out_fc1 = final_mlp[:, :, :hidden_part].transpose(1, 0, 2).reshape(rows, hidden)
    out_fc2 = final_mlp[:, :, hidden_part:].transpose(0, 2, 1).reshape(hidden, rows)
    out_qkv = (
        final_attn[:, :, : 3 * head_width]
        .reshape(group, rows, pairs, 3, PAIR)
        .transpose(1, 3, 0, 2, 4)
        .reshape(rows, 3 * width)
    )
    out_proj = (
        final_attn[:, :, 3 * head_width : 4 * head_width].transpose(0, 2, 1).reshape(width, rows)
    )
    out_extra = jnp.sum(final_attn[:, :, 4 * head_width :], axis=0)
    out_vectors = out_extra[:, :vector_count].T
    out_bias = out_extra[:, vector_count : vector_count + bias_cols].reshape(-1)
    return (
        output[None],
        input_grad[None],
        out_qkv,
        out_proj,
        out_fc1,
        out_bias,
        out_fc2,
        out_vectors,
    )


def solution(mesh):
    both = ("dp", "ctx")
    in_specs = (
        P("dp", "ctx", None),
        P("dp", "ctx"),
        P(both, None),
        P(None, both),
        P(both, None),
        P(both),
        P(None, both),
        P(None, both),
        P("dp", "ctx", None),
    )
    out_specs = (
        P("dp", "ctx", None),
        P("dp", "ctx", None),
        P(both, None),
        P(None, both),
        P(both, None),
        P(both),
        P(None, both),
        P(None, both),
    )
    return jax.shard_map(local, mesh=mesh, in_specs=in_specs, out_specs=out_specs, check_vma=False)
```

```python
import jax
import jax.numpy as jnp
from jax import lax
from jax.experimental import pallas as pl
from jax.experimental.pallas import tpu as pltpu
from jax.sharding import PartitionSpec as P

HD = 64
PAIR = 2 * HD
EXTRA = 128
EPSILON = 1e-06
MASKED_SCORE = -1e30
SQRT_HALF = 0.7071067811865476
INV_ROOT_TWO_PI = 0.3989422804014327
BF = jnp.bfloat16
F32 = jnp.float32
PARAMS = pltpu.CompilerParams(vmem_limit_bytes=48 * 1024 * 1024)
VMEM = pl.BlockSpec(memory_space=pltpu.VMEM)
SMEM = pl.BlockSpec(memory_space=pltpu.SMEM)


def shaped(shape, dtype):
    return jax.ShapeDtypeStruct(shape, dtype)


def dot(left, right, left_dim, right_dim):
    return lax.dot_general(
        left, right, (((left_dim,), (right_dim,)), ((), ())), preferred_element_type=F32
    )


def lanes(start, size):
    return pl.ds(pl.multiple_of(start, 128), size)


def unit_rows(inputs):
    centered = inputs - jnp.mean(inputs, axis=-1, keepdims=True)
    spread = jnp.mean(centered * centered, axis=-1, keepdims=True)
    inverse = lax.rsqrt(spread + EPSILON)
    return (centered * inverse, inverse)


def norm_back(grad_in, unit, inverse, gain):
    scaled = grad_in * gain
    inner = (
        scaled
        - jnp.mean(scaled, axis=-1, keepdims=True)
        - unit * jnp.mean(scaled * unit, axis=-1, keepdims=True)
    )
    return inner * inverse


def cut_kernel(ids_ref, count_ref, qkv_ref, proj_ref, fc1_ref, fc2_ref, vec_ref, bias_ref, *rest):
    outs, extra_ref = rest[:-1], rest[-1]
    group = len(outs) // 2
    place = ids_ref[0]
    width = proj_ref.shape[1]
    part = width // group
    hidden_part = fc1_ref.shape[1] // group
    vector_count, bias_cols = vec_ref.shape[0], bias_ref.shape[0]
    column = vector_count + bias_cols
    lane = lax.broadcasted_iota(jnp.int32, extra_ref.shape, 1)
    count = count_ref[0, 0]
    high = (count >> 7).astype(F32)
    low = (count & 127).astype(F32)
    extra_ref[...] = jnp.where(lane == column, high, jnp.where(lane == column + 1, low, 0.0))
    extra_ref[:, :vector_count] = vec_ref[...].astype(F32).T
    extra_ref[:, vector_count:column] = bias_ref[...].astype(F32).T
    extra = extra_ref[...].astype(BF)
    for k in range(group):
        target = place ^ k
        first, second = outs[k], outs[group + k]
        for third in range(3):
            for pair in range(part // PAIR):
                spot = (pair * 3 + third) * PAIR
                first[:, spot : spot + PAIR] = qkv_ref[
                    :, lanes(third * width + target * part + pair * PAIR, PAIR)
                ]
        first[:, 3 * part : 4 * part] = proj_ref[:, lanes(target * part, part)]
        first[:, 4 * part :] = extra
        second[:, :hidden_part] = fc1_ref[:, lanes(target * hidden_part, hidden_part)]
        second[:, hidden_part:] = fc2_ref[:, lanes(target * hidden_part, hidden_part)]


def cut(ids, counts, w_qkv, w_proj_t, w_fc1, w_fc2_t, vectors, bias, group):
    rows, width = w_proj_t.shape
    part, hidden_part = width // group, w_fc1.shape[1] // group
    return pl.pallas_call(
        cut_kernel,
        in_specs=[SMEM, SMEM] + [VMEM] * 6,
        out_specs=[VMEM] * (2 * group),
        out_shape=[shaped((rows, 4 * part + EXTRA), BF)] * group
        + [shaped((rows, 2 * hidden_part), BF)] * group,
        scratch_shapes=[pltpu.VMEM((rows, EXTRA), F32)],
        compiler_params=PARAMS,
        name="cut",
    )(ids, counts, w_qkv, w_proj_t, w_fc1, w_fc2_t, vectors, bias)


def project_kernel(ordered, group, ids_ref, tokens_ref, *rest):
    pieces, (qkv_w, proj_w, rows_ref, normed_ref, out_ref, mean_ref, inv_ref) = rest[:-9], rest[-9:-2]
    extra_ref, bias_ref = rest[-2:]
    place, row = ids_ref[0], ids_ref[1]
    width = tokens_ref.shape[1]
    part = proj_w.shape[1]
    size = pieces[0].shape[0]

    def lay(block, start, count):
        where = pl.ds(start, count)
        qkv_w[where, :] = block[:, : 3 * part]
        proj_w[where, :] = block[:, 3 * part : 4 * part]
        extra_ref[where, :] = block[:, 4 * part :].astype(F32)

    if ordered:
        lay(pieces[0], 0, size)
    else:
        sub = size // group
        for m, piece in enumerate(pieces):
            for j in range(group):
                start = (row ^ m) * size + (place ^ j) * sub
                lay(piece.at[j * sub : (j + 1) * sub], pl.multiple_of(start, sub), sub)
    turned = extra_ref[...].T
    rows_ref[...] = turned[: rows_ref.shape[0]]
    bias_ref[...] = jnp.zeros(bias_ref.shape, F32)
    for pair in range(part // PAIR):
        for third, line in ((0, 2), (2, 3)):
            spot = (pair * 3 + third) * PAIR
            bias_ref[0:1, spot : spot + PAIR] = rows_ref[
                line : line + 1, lanes(place * part + pair * PAIR, PAIR)
            ]
    gain, shift, bias = rows_ref[0:1, :], rows_ref[1:2, :], bias_ref[0:1, :]
    half = tokens_ref.shape[0] // 2
    for start in (0, half):
        span = slice(start, start + half)
        inputs = tokens_ref[span, :].astype(F32)
        mean = jnp.mean(inputs, axis=-1, keepdims=True)
        centered = inputs - mean
        inverse = lax.rsqrt(jnp.mean(centered * centered, axis=-1, keepdims=True) + EPSILON)
        normed = (centered * inverse * gain + shift).astype(BF)
        normed_ref[span, :] = normed
        mean_ref[span, :] = mean
        inv_ref[span, :] = inverse
        out_ref[span, :] = (dot(normed, qkv_w[...], 1, 0) + bias).astype(BF)


def project(ids, tokens_all, pieces, group, ordered):
    length, width = tokens_all.shape
    part = width // group
    return pl.pallas_call(
        lambda *refs: project_kernel(ordered, group, *refs),
        in_specs=[SMEM] + [VMEM] * (1 + len(pieces)),
        out_specs=[VMEM] * 7,
        out_shape=[
            shaped((width, 3 * part), BF),
            shaped((width, part), BF),
            shaped((16, width), F32),
            shaped((length, width), BF),
            shaped((length, 3 * part), BF),
            shaped((length, 1), F32),
            shaped((length, 1), F32),
        ],
        scratch_shapes=[pltpu.VMEM((width, EXTRA), F32), pltpu.VMEM((8, 3 * part), F32)],
        compiler_params=PARAMS,
        cost_estimate=pl.CostEstimate(
            flops=6 * length * width * part, bytes_accessed=12_000_000, transcendentals=0
        ),
        name="project",
    )(ids, tokens_all, *pieces)


def query_chunks(length):
    step = 512
    return [(start, min(step, length - start)) for start in range(0, length, step)]


def attend_kernel(qkv_ref, bias_ref, proj_ref, out_ref, low_ref, lse_ref, branch_ref, acc_ref):
    length = qkv_ref.shape[0]
    key_bias = bias_ref[...]
    for head in range(2):
        keys = qkv_ref[:, PAIR + head * HD : PAIR + (head + 1) * HD]
        values = qkv_ref[:, 2 * PAIR + head * HD : 2 * PAIR + (head + 1) * HD]
        for start, size in query_chunks(length):
            queries = qkv_ref[start : start + size, head * HD : (head + 1) * HD]
            queries = queries * jnp.asarray(HD**-0.5, BF)
            scores = dot(keys, queries, 1, 1) + key_bias
            top = jnp.max(scores, axis=0, keepdims=True)
            expo = jnp.exp(scores - top)
            total = jnp.sum(expo, axis=0, keepdims=True)
            mixed = (dot(values, expo.astype(BF), 0, 0) / total).T
            out_ref[start : start + size, head * HD : (head + 1) * HD] = mixed
            low_ref[start : start + size, head * HD : (head + 1) * HD] = mixed.astype(BF)
            lse_ref[0, head : head + 1, start : start + size] = top + jnp.log(total)
    pair = pl.program_id(0)
    product = dot(low_ref[...], proj_ref[...], 1, 1)

    @pl.when(pair == 0)
    def _():
        acc_ref[...] = product

    @pl.when(pair > 0)
    def _():
        acc_ref[...] += product

    @pl.when(pair == pl.num_programs(0) - 1)
    def _():
        branch_ref[...] = acc_ref[...].astype(BF)


def attend(qkv, key_bias, weight_proj):
    length, columns = qkv.shape
    pairs = columns // (3 * PAIR)
    width = weight_proj.shape[0]
    return pl.pallas_call(
        attend_kernel,
        grid=(pairs,),
        in_specs=[
            pl.BlockSpec((length, 3 * PAIR), lambda p: (0, p)),
            pl.BlockSpec((length, 1), lambda p: (0, 0)),
            pl.BlockSpec((width, PAIR), lambda p: (0, p)),
        ],
        out_specs=[
            pl.BlockSpec((length, PAIR), lambda p: (0, p)),
            pl.BlockSpec((length, PAIR), lambda p: (0, p)),
            pl.BlockSpec((1, 2, length), lambda p: (p, 0, 0)),
            pl.BlockSpec((length, width), lambda p: (0, 0)),
        ],
        out_shape=[
            shaped((length, pairs * PAIR), F32),
            shaped((length, pairs * PAIR), BF),
            shaped((pairs, 2, length), F32),
            shaped((length, width), BF),
        ],
        scratch_shapes=[pltpu.VMEM((length, width), F32)],
        compiler_params=PARAMS,
        cost_estimate=pl.CostEstimate(
            flops=pairs * 2 * 4 * length * length * 256,
            bytes_accessed=length * columns * 4,
            transcendentals=pairs * 2 * length * length,
        ),
        name="attend",
    )(qkv, key_bias, weight_proj)


def attend_back_kernel(
    qkv_ref, bias_ref, att_ref, near_ref, far_ref, proj_ref, lse_ref, out_ref, sums_ref, grad_ref
):
    length = qkv_ref.shape[0]
    half = near_ref.shape[0]
    factor = HD**-0.5
    key_bias = bias_ref[...]
    grad_ref[:half, :] = dot(near_ref[...], proj_ref[...], 1, 0).astype(BF)
    grad_ref[half:, :] = dot(far_ref[...], proj_ref[...], 1, 0).astype(BF)
    for head in range(2):
        low, high = head * HD, (head + 1) * HD
        keys = qkv_ref[:, PAIR + low : PAIR + high]
        values = qkv_ref[:, 2 * PAIR + low : 2 * PAIR + high]
        key_grad = jnp.zeros((length, HD), F32)
        value_grad = jnp.zeros((length, HD), F32)
        for start, size in query_chunks(length):
            rows = slice(start, start + size)
            queries = qkv_ref[rows, low:high] * jnp.asarray(factor, BF)
            grads = grad_ref[rows, low:high]
            product = grads.astype(F32) * att_ref[rows, low:high]
            delta = jnp.sum(product.T, axis=0, keepdims=True)
            scores = dot(keys, queries, 1, 1) + key_bias
            probs = jnp.exp(scores - lse_ref[0, head : head + 1, rows])
            value_grad += dot(probs.astype(BF), grads, 1, 0)
            raw = (probs * (dot(values, grads, 1, 1) - delta)).astype(BF)
            key_grad += dot(raw, queries, 1, 0)
            query_grad = dot(keys, raw, 0, 0).T * factor
            out_ref[rows, low:high] = query_grad.astype(BF)
        out_ref[:, PAIR + low : PAIR + high] = key_grad.astype(BF)
        out_ref[:, 2 * PAIR + low : 2 * PAIR + high] = value_grad.astype(BF)
    sums_ref[0] = jnp.sum(out_ref[...].astype(F32), axis=0, keepdims=True)


def attend_back(qkv, key_bias, attended, near, far, weight_proj, lse):
    length, columns = qkv.shape
    pairs = columns // (3 * PAIR)
    half, width = near.shape
    return pl.pallas_call(
        attend_back_kernel,
        grid=(pairs,),
        in_specs=[
            pl.BlockSpec((length, 3 * PAIR), lambda p: (0, p)),
            pl.BlockSpec((length, 1), lambda p: (0, 0)),
            pl.BlockSpec((length, PAIR), lambda p: (0, p)),
            pl.BlockSpec((half, width), lambda p: (0, 0)),
            pl.BlockSpec((half, width), lambda p: (0, 0)),
            pl.BlockSpec((width, PAIR), lambda p: (0, p)),
            pl.BlockSpec((1, 2, length), lambda p: (p, 0, 0)),
        ],
        out_specs=[
            pl.BlockSpec((length, 3 * PAIR), lambda p: (0, p)),
            pl.BlockSpec((1, 1, 3 * PAIR), lambda p: (p, 0, 0)),
        ],
        out_shape=[shaped((length, columns), BF), shaped((pairs, 1, 3 * PAIR), F32)],
        scratch_shapes=[pltpu.VMEM((length, PAIR), BF)],
        compiler_params=PARAMS,
        cost_estimate=pl.CostEstimate(
            flops=pairs * 2 * 10 * length * length * 256,
            bytes_accessed=length * columns * 6,
            transcendentals=pairs * 2 * length * length,
        ),
        name="attend_back",
    )(qkv, key_bias, attended, near, far, weight_proj, lse)


def mlp_kernel(
    normed_ref, grad_ref, fc1_ref, fc2_ref, bias_ref,
    act_ref, pre_ref, back_ref, branch_ref, sums_ref, back_acc, branch_acc,
):
    step = pl.program_id(0)
    pre = dot(normed_ref[...], fc1_ref[...], 1, 0) + bias_ref[...]
    cdf = 0.5 * (1.0 + lax.erf(pre * SQRT_HALF))
    act = (pre * cdf).astype(BF)
    slope = cdf + pre * jnp.exp(-0.5 * pre * pre) * INV_ROOT_TWO_PI
    pre_grad = (dot(grad_ref[...], fc2_ref[...], 1, 0) * slope).astype(BF)
    act_ref[...] = act
    pre_ref[...] = pre_grad
    sums_ref[...] = jnp.sum(pre_grad.astype(F32), axis=0, keepdims=True)
    back = dot(pre_grad, fc1_ref[...], 1, 1)
    branch = dot(act, fc2_ref[...], 1, 1)

    @pl.when(step == 0)
    def _():
        back_acc[...] = back
        branch_acc[...] = branch

    @pl.when(step > 0)
    def _():
        back_acc[...] += back
        branch_acc[...] += branch

    @pl.when(step == pl.num_programs(0) - 1)
    def _():
        back_ref[...] = back_acc[...].astype(BF)
        branch_ref[...] = branch_acc[...].astype(BF)


def mlp(normed, grads, weights, bias):
    length, width = normed.shape
    hidden = weights.shape[1] // 2
    step = 256
    steps = hidden // step
    whole = pl.BlockSpec((length, width), lambda i: (0, 0))
    cols = pl.BlockSpec((length, step), lambda i: (0, i))
    return pl.pallas_call(
        mlp_kernel,
        grid=(steps,),
        in_specs=[
            whole,
            whole,
            pl.BlockSpec((width, step), lambda i: (0, i)),
            pl.BlockSpec((width, step), lambda i: (0, steps + i)),
            pl.BlockSpec((1, step), lambda i: (0, i)),
        ],
        out_specs=[cols, cols, whole, whole, pl.BlockSpec((1, step), lambda i: (0, i))],
        out_shape=[
            shaped((length, hidden), BF),
            shaped((length, hidden), BF),
            shaped((length, width), BF),
            shaped((length, width), BF),
            shaped((1, hidden), F32),
        ],
        scratch_shapes=[pltpu.VMEM((length, width), F32)] * 2,
        compiler_params=PARAMS,
        cost_estimate=pl.CostEstimate(
            flops=8 * length * width * hidden,
            bytes_accessed=12_000_000,
            transcendentals=2 * length * hidden,
        ),
        name="mlp",
    )(normed, grads, weights, weights, bias)


def mlp_weights_kernel(norm_a, norm_b, grad_a, grad_b, pre_a, pre_b, act_a, act_b, out_ref):
    hidden = pre_a.shape[1]
    first = dot(norm_a[...], pre_a[...], 0, 0) + dot(norm_b[...], pre_b[...], 0, 0)
    out_ref[:, :hidden] = first.astype(BF)
    second = dot(grad_a[...], act_a[...], 0, 0) + dot(grad_b[...], act_b[...], 0, 0)
    out_ref[:, hidden:] = second.astype(BF)


def mlp_weights(normed, grads, pres, acts):
    length, width = normed[0].shape
    hidden = pres[0].shape[1]
    step = 256
    cols = pl.BlockSpec((length, step), lambda i: (0, i))
    whole = pl.BlockSpec((length, hidden), lambda i: (0, 0))
    return pl.pallas_call(
        mlp_weights_kernel,
        grid=(width // step,),
        in_specs=[cols] * 4 + [whole] * 4,
        out_specs=pl.BlockSpec((step, 2 * hidden), lambda i: (i, 0)),
        out_shape=shaped((width, 2 * hidden), BF),
        compiler_params=PARAMS,
        cost_estimate=pl.CostEstimate(
            flops=8 * length * width * hidden, bytes_accessed=16_000_000, transcendentals=0
        ),
        name="mlp_weights",
    )(*normed, *grads, *pres, *acts)


def qkv_back_kernel(grad_ref, weight_ref, tokens_ref, mean_ref, inv_ref, out_ref, sums_ref):
    step = pl.program_id(0)
    part = dot(grad_ref[...], weight_ref[...], 1, 1)
    out_ref[...] = part.astype(BF)
    unit = (tokens_ref[...].astype(F32) - mean_ref[...]) * inv_ref[...]

    @pl.when(step == 0)
    def _():
        sums_ref[...] = jnp.zeros(sums_ref.shape, F32)

    sums_ref[0:1, :] += jnp.sum(part * unit, axis=0, keepdims=True)
    sums_ref[1:2, :] += jnp.sum(part, axis=0, keepdims=True)


def qkv_back(qkv_grad, weight, tokens_all, mean, inverse):
    length, width = tokens_all.shape
    columns = qkv_grad.shape[1]
    half = length // 2
    return pl.pallas_call(
        qkv_back_kernel,
        grid=(2,),
        in_specs=[
            pl.BlockSpec((half, columns), lambda i: (i, 0)),
            pl.BlockSpec((width, columns), lambda i: (0, 0)),
            pl.BlockSpec((half, width), lambda i: (i, 0)),
            pl.BlockSpec((half, 1), lambda i: (i, 0)),
            pl.BlockSpec((half, 1), lambda i: (i, 0)),
        ],
        out_specs=[
            pl.BlockSpec((half, width), lambda i: (i, 0)),
            pl.BlockSpec((8, width), lambda i: (0, 0)),
        ],
        out_shape=[shaped((length, width), BF), shaped((8, width), F32)],
        compiler_params=PARAMS,
        cost_estimate=pl.CostEstimate(
            flops=2 * length * width * columns, bytes_accessed=10_000_000, transcendentals=0
        ),
        name="qkv_back",
    )(qkv_grad, weight, tokens_all, mean, inverse)


def attn_weights_kernel(
    direct, ids_ref, normed_ref, grad_ref, near_ref, far_ref, att_ref, norm1_ref, sums_ref,
    bias_ref, *rest,
):
    vector_refs, outs = rest[:6], rest[6:-3]
    rows_ref, turned_ref, block_ref = rest[-3:]
    place, row = ids_ref[0], ids_ref[1]
    width = normed_ref.shape[1]
    part = att_ref.shape[1]
    half = near_ref.shape[0]
    rows_ref[...] = jnp.zeros(rows_ref.shape, F32)
    rows_ref[0:2, :] = norm1_ref[0:2, :]
    for pair in range(part // PAIR):
        where = lanes(place * part + pair * PAIR, PAIR)
        rows_ref[2:3, where] = sums_ref[pair, :, :PAIR]
        rows_ref[3:4, where] = sums_ref[pair, :, 2 * PAIR :]
    for line, ref in enumerate(vector_refs):
        rows_ref[4 + line : 5 + line, :] = ref[...]
    for line in range(bias_ref.shape[0]):
        rows_ref[10 + line : 11 + line, lanes(place * part, part)] = bias_ref[line : line + 1, :]
    turned_ref[...] = rows_ref[...].T
    step = block_ref.shape[0]
    for k in range(width // step):
        start = pl.multiple_of(((row >> 1) ^ k) * step, step) if direct else k * step
        cols = pl.ds(start, step)
        block_ref[:, : 3 * part] = dot(normed_ref[:, cols], grad_ref[...], 0, 0)
        block_ref[:, 3 * part : 4 * part] = dot(near_ref[:, cols], att_ref[:half, :], 0, 0) + dot(
            far_ref[:, cols], att_ref[half:, :], 0, 0
        )
        block_ref[:, 4 * part :] = turned_ref[cols, :]
        if direct:
            size = step // 2
            side = row & 1
            outs[2 * k][...] = block_ref[pl.ds(pl.multiple_of(side * size, size), size), :].astype(BF)
            outs[2 * k + 1][...] = block_ref[
                pl.ds(pl.multiple_of((1 - side) * size, size), size), :
            ].astype(BF)
        else:
            outs[0][k * step : (k + 1) * step, :] = block_ref[...].astype(BF)


def attn_weights(ids, normed1, qkv_grad, near, far, att_low, norm1_sums, sums, bias, rows, blocks):
    length, width = normed1.shape
    part = att_low.shape[1]
    columns = 4 * part + EXTRA
    direct = blocks > 0
    step = 2 * (width // blocks) if direct else 256
    out_shape = [shaped((width // blocks, columns), BF)] * blocks if direct else [
        shaped((width, columns), BF)
    ]
    return pl.pallas_call(
        lambda *refs: attn_weights_kernel(direct, *refs),
        in_specs=[SMEM] + [VMEM] * (8 + len(rows)),
        out_specs=[VMEM] * len(out_shape),
        out_shape=out_shape,
        scratch_shapes=[
            pltpu.VMEM((EXTRA, width), F32),
            pltpu.VMEM((width, EXTRA), F32),
            pltpu.VMEM((step, columns), F32),
        ],
        compiler_params=PARAMS,
        cost_estimate=pl.CostEstimate(
            flops=8 * length * width * part, bytes_accessed=14_000_000, transcendentals=0
        ),
        name="attn_weights",
    )(ids, normed1, qkv_grad, near, far, att_low, norm1_sums, sums, bias, *rows)


def total(ids, terms, group):
    size, columns = terms[0].shape
    rows = size // group

    def kernel(ids_ref, *refs):
        ins, outs, sum_ref = refs[: len(terms)], refs[len(terms) : -1], refs[-1]
        value = ins[0][...].astype(F32)
        for ref in ins[1:]:
            value = value + ref[...].astype(F32)
        sum_ref[...] = value
        for k, out in enumerate(outs):
            start = pl.multiple_of((ids_ref[0] ^ k) * rows, rows)
            out[...] = sum_ref[pl.ds(start, rows), :].astype(BF)

    return pl.pallas_call(
        kernel,
        in_specs=[SMEM] + [VMEM] * len(terms),
        out_specs=[VMEM] * group,
        out_shape=[shaped((rows, columns), BF)] * group,
        scratch_shapes=[pltpu.VMEM((size, columns), F32)],
        compiler_params=PARAMS,
        name="total",
    )(ids, *terms)


def place_attn_kernel(ids_ref, *refs):
    group = len(refs) - 3
    blocks, (qkv_ref, proj_ref, extra_ref) = refs[:group], refs[group:]
    width = proj_ref.shape[1]
    part = width // group
    extra = jnp.zeros(extra_ref.shape[::-1], F32)
    for k, block in enumerate(blocks):
        source = ids_ref[0] ^ k
        for third in range(3):
            for pair in range(part // PAIR):
                spot = (pair * 3 + third) * PAIR
                where = lanes(third * width + source * part + pair * PAIR, PAIR)
                qkv_ref[:, where] = block[:, spot : spot + PAIR].astype(F32)
        proj_ref[:, lanes(source * part, part)] = block[:, 3 * part : 4 * part].astype(F32)
        extra = extra + block[:, 4 * part :].astype(F32)
    extra_ref[...] = extra.T


def place_attn(ids, blocks, width):
    rows = blocks[0].shape[0]
    return pl.pallas_call(
        place_attn_kernel,
        in_specs=[SMEM] + [VMEM] * len(blocks),
        out_specs=[VMEM] * 3,
        out_shape=[
            shaped((rows, 3 * width), F32),
            shaped((rows, width), F32),
            shaped((EXTRA, rows), F32),
        ],
        compiler_params=PARAMS,
        name="place_attn",
    )(ids, *blocks)


def place_mlp_kernel(ids_ref, *refs):
    group = len(refs) - 2
    blocks, (fc1_ref, fc2_ref) = refs[:group], refs[group:]
    part = fc1_ref.shape[1] // group
    for k, block in enumerate(blocks):
        where = lanes((ids_ref[0] ^ k) * part, part)
        fc1_ref[:, where] = block[:, :part].astype(F32)
        fc2_ref[:, where] = block[:, part:].astype(F32)


def place_mlp(ids, blocks, hidden):
    rows = blocks[0].shape[0]
    return pl.pallas_call(
        place_mlp_kernel,
        in_specs=[SMEM] + [VMEM] * len(blocks),
        out_specs=[VMEM] * 2,
        out_shape=[shaped((rows, hidden), F32)] * 2,
        compiler_params=PARAMS,
        name="place_mlp",
    )(ids, *blocks)


def local(tokens, counts, w_qkv, w_proj, w_fc1, fc1_bias, w_fc2, vectors, cotangent):
    _, capacity, width = tokens.shape
    hidden = w_fc1.shape[1]
    rows = w_qkv.shape[0]
    group, replicas = lax.axis_size("ctx"), lax.axis_size("dp")
    place, replica = lax.axis_index("ctx"), lax.axis_index("dp")
    ids = jnp.stack([place, replica]).astype(jnp.int32)
    head_width = width // group
    hidden_part = hidden // group
    bias_cols = hidden // width
    vector_count = vectors.shape[0]
    direct = replicas <= 8

    def swap(value, bit, axis="ctx"):
        size = group if axis == "ctx" else replicas
        return lax.ppermute(value, axis, [(i, i ^ bit) for i in range(size)])

    def gather(own):
        pieces = [own]
        for j in range(1, group):
            bit = j & -j
            pieces.append(swap(pieces[j ^ bit], bit))
        return pieces

    def scatter(parts):
        pieces = dict(enumerate(parts))
        bit = 1
        while bit < group:
            for j in sorted((j for j in pieces if j & bit), reverse=True):
                other = swap(pieces[j].astype(BF), bit).astype(F32)
                pieces[j ^ bit] = pieces[j ^ bit].astype(F32) + other
                del pieces[j]
            bit *= 2
        return pieces[0].astype(F32)

    def split(whole):
        return [whole[j * capacity : (j + 1) * capacity] for j in range(whole.shape[0] // capacity)]

    def exchange(relative):
        return [relative[0]] + [swap(relative[k], k) for k in range(1, group)]

    def in_order(relative):
        stacked = jnp.stack(relative)
        return jnp.concatenate(
            [lax.dynamic_index_in_dim(stacked, place ^ s, 0, False) for s in range(group)], axis=0
        )

    cuts = cut(
        ids, counts, w_qkv, w_proj.T, w_fc1, w_fc2.T, vectors, fc1_bias.reshape(bias_cols, rows), group
    )
    first = exchange(cuts[:group])
    tokens_pieces = gather(tokens[0])
    second = exchange(cuts[group:])
    if direct:
        shards = {0: jnp.concatenate(first, axis=0)}
        for m in range(2, replicas, 2):
            shards[m] = swap(shards[0], m, "dp")
        for m in range(1, replicas, 2):
            shards[m] = swap(shards[m - 1], 1, "dp")
        first_pieces = [shards[m] for m in range(replicas)]
    else:
        first_pieces = [lax.all_gather(in_order(first), "dp", axis=0, tiled=True)]
    second_all = lax.all_gather(in_order(second), "dp", axis=0, tiled=True)

    count_column = 4 * head_width + vector_count + bias_cols
    live = []
    for block in first:
        piece = block[0, count_column : count_column + 2].astype(F32)
        bound = piece[0] * 128.0 + piece[1]
        slot = lax.broadcasted_iota(jnp.int32, (capacity, 1), 0).astype(F32)
        live.append(slot < bound)
    key_bias = jnp.where(jnp.concatenate(live, axis=0), 0.0, MASKED_SCORE).astype(F32)

    cotangent_pieces = gather(cotangent[0])
    tokens_all = jnp.concatenate(tokens_pieces, axis=0)
    weight_qkv, weight_proj, vector_rows, normed1, qkv, mean1, inverse1_all = project(
        ids, tokens_all, first_pieces, group, not direct
    )
    bias_part = lax.dynamic_slice_in_dim(
        vector_rows[vector_count : vector_count + bias_cols], place * head_width, head_width, axis=1
    )
    bias_fc1 = bias_part.reshape(bias_cols, head_width // rows, rows).transpose(1, 0, 2)
    bias_fc1 = bias_fc1.reshape(1, hidden_part)

    inputs = tokens[0].astype(F32)
    attended, attended_low, lse, branch1_part = attend(qkv, key_bias, weight_proj)
    branch1 = scatter(split(branch1_part)) + vector_rows[4]
    middle = inputs + vector_rows[5] * branch1
    unit2, inverse2 = unit_rows(middle)
    pieces = gather((unit2 * vector_rows[6] + vector_rows[7]).astype(BF))
    normed2 = [jnp.concatenate(pieces[: group // 2]), jnp.concatenate(pieces[group // 2 :])]

    out_grads = [
        jnp.where(keep, piece.astype(F32), 0.0) for keep, piece in zip(live, cotangent_pieces)
    ]
    out_grad = out_grads[0]
    mlp_grads = [(piece * vector_rows[9]).astype(BF) for piece in out_grads]
    grad_fbias = jnp.sum(mlp_grads[0].astype(F32), axis=0, keepdims=True)
    mlp_grad = [jnp.concatenate(mlp_grads[: group // 2]), jnp.concatenate(mlp_grads[group // 2 :])]
    near = mlp(normed2[0], mlp_grad[0], second_all, bias_fc1)
    far = mlp(normed2[1], mlp_grad[1], second_all, bias_fc1)
    acts, pres, backs, branches, bias_sums = zip(near, far)
    norm2_grad = scatter(split(backs[0]) + split(backs[1]))
    grad_mlp = mlp_weights(normed2, mlp_grad, pres, acts)
    owned_mlp = lax.psum_scatter(grad_mlp, "dp", scatter_dimension=0, tiled=True)
    branch2 = scatter(split(branches[0]) + split(branches[1])) + vector_rows[8]
    output = (middle + vector_rows[9] * branch2).astype(BF)
    grad_scale2 = jnp.sum(out_grad * branch2, axis=0, keepdims=True)
    grad_bfc1 = (bias_sums[0] + bias_sums[1]).reshape(head_width // rows, bias_cols, rows)
    grad_bfc1 = grad_bfc1.transpose(1, 0, 2).reshape(bias_cols, head_width)

    grad_gain2 = jnp.sum(norm2_grad * unit2, axis=0, keepdims=True)
    grad_shift2 = jnp.sum(norm2_grad, axis=0, keepdims=True)
    middle_grad = out_grad + norm_back(norm2_grad, unit2, inverse2, vector_rows[6])
    grad_scale1 = jnp.sum(middle_grad * branch1, axis=0, keepdims=True)
    own_branch_grad = (middle_grad * vector_rows[5]).astype(BF)
    grad_pbias = jnp.sum(own_branch_grad.astype(F32), axis=0, keepdims=True)
    pieces = gather(own_branch_grad)
    branch_grad = [jnp.concatenate(pieces[: group // 2]), jnp.concatenate(pieces[group // 2 :])]
    qkv_grad, qkv_sums = attend_back(
        qkv, key_bias, attended, branch_grad[0], branch_grad[1], weight_proj, lse
    )
    norm1_part, norm1_sums = qkv_back(qkv_grad, weight_qkv, tokens_all, mean1, inverse1_all)
    vector_grads = [grad_pbias, grad_scale1, grad_gain2, grad_shift2, grad_fbias, grad_scale2]
    parts = attn_weights(
        ids, normed1, qkv_grad, branch_grad[0], branch_grad[1], attended_low, norm1_sums, qkv_sums,
        grad_bfc1, vector_grads, replicas if direct else 0,
    )
    if direct:
        terms = []
        for k in range(replicas // 2):
            other = swap(parts[2 * k + 1], 1, "dp")
            if k == 0:
                terms += [parts[0], other]
            else:
                summed = (parts[2 * k].astype(F32) + other.astype(F32)).astype(BF)
                terms.append(swap(summed, 2 * k, "dp"))
        cuts_attn = total(ids, terms, group)
        cuts_mlp = total(ids, [owned_mlp], group)
    else:
        owned_attn = lax.psum_scatter(parts[0], "dp", scatter_dimension=0, tiled=True)

        def relative(owned):
            blocks = owned.reshape(group, rows, -1)
            return [lax.dynamic_index_in_dim(blocks, place ^ k, 0, False) for k in range(group)]

        cuts_attn, cuts_mlp = relative(owned_attn), relative(owned_mlp)
    norm1_grad = scatter(split(norm1_part))
    unit1 = (inputs - mean1[:capacity]) * inverse1_all[:capacity]
    input_grad = (
        middle_grad + norm_back(norm1_grad, unit1, inverse1_all[:capacity], vector_rows[0])
    ).astype(BF)

    out_fc1, out_fc2 = place_mlp(ids, exchange(cuts_mlp), hidden)
    out_qkv, out_proj, out_extra = place_attn(ids, exchange(cuts_attn), width)
    return (
        output[None],
        input_grad[None],
        out_qkv,
        out_proj.T,
        out_fc1,
        out_extra[vector_count : vector_count + bias_cols].reshape(-1),
        out_fc2.T,
        out_extra[:vector_count],
    )


def solution(mesh):
    both = ("dp", "ctx")
    in_specs = (
        P("dp", "ctx", None),
        P("dp", "ctx"),
        P(both, None),
        P(None, both),
        P(both, None),
        P(both),
        P(None, both),
        P(None, both),
        P("dp", "ctx", None),
    )
    out_specs = (
        P("dp", "ctx", None),
        P("dp", "ctx", None),
        P(both, None),
        P(None, both),
        P(both, None),
        P(both),
        P(None, both),
        P(None, both),
    )
    return jax.shard_map(local, mesh=mesh, in_specs=in_specs, out_specs=out_specs, check_vma=False)
```

```python
import jax
import jax.numpy as jnp
from jax import lax
from jax.experimental import pallas as pl
from jax.experimental.pallas import tpu as pltpu
from jax.sharding import PartitionSpec as P

HD = 64
PAIR = 2 * HD
EXTRA = 128
EPSILON = 1e-06
MASKED_SCORE = -1e30
SQRT_HALF = 0.7071067811865476
INV_ROOT_TWO_PI = 0.3989422804014327
BF = jnp.bfloat16
F32 = jnp.float32
PARAMS = pltpu.CompilerParams(vmem_limit_bytes=48 * 1024 * 1024)
VMEM = pl.BlockSpec(memory_space=pltpu.VMEM)
SMEM = pl.BlockSpec(memory_space=pltpu.SMEM)


def shaped(shape, dtype):
    return jax.ShapeDtypeStruct(shape, dtype)


def dot(left, right, left_dim, right_dim):
    return lax.dot_general(
        left, right, (((left_dim,), (right_dim,)), ((), ())), preferred_element_type=F32
    )


def lanes(start, size):
    return pl.ds(pl.multiple_of(start, 128), size)


def unit_rows(inputs):
    centered = inputs - jnp.mean(inputs, axis=-1, keepdims=True)
    spread = jnp.mean(centered * centered, axis=-1, keepdims=True)
    inverse = lax.rsqrt(spread + EPSILON)
    return (centered * inverse, inverse)


def norm_back(grad_in, unit, inverse, gain):
    scaled = grad_in * gain
    inner = (
        scaled
        - jnp.mean(scaled, axis=-1, keepdims=True)
        - unit * jnp.mean(scaled * unit, axis=-1, keepdims=True)
    )
    return inner * inverse


def cut_kernel(ids_ref, count_ref, qkv_ref, proj_ref, fc1_ref, fc2_ref, vec_ref, bias_ref, *rest):
    outs, extra_ref = rest[:-1], rest[-1]
    group = len(outs) // 2
    place = ids_ref[0]
    width = proj_ref.shape[1]
    part = width // group
    hidden_part = fc1_ref.shape[1] // group
    vector_count, bias_cols = vec_ref.shape[0], bias_ref.shape[0]
    column = vector_count + bias_cols
    lane = lax.broadcasted_iota(jnp.int32, extra_ref.shape, 1)
    count = count_ref[0, 0]
    high = (count >> 7).astype(F32)
    low = (count & 127).astype(F32)
    extra_ref[...] = jnp.where(lane == column, high, jnp.where(lane == column + 1, low, 0.0))
    extra_ref[:, :vector_count] = vec_ref[...].astype(F32).T
    extra_ref[:, vector_count:column] = bias_ref[...].astype(F32).T
    extra = extra_ref[...].astype(BF)
    for k in range(group):
        target = place ^ k
        first, second = outs[k], outs[group + k]
        for third in range(3):
            for pair in range(part // PAIR):
                spot = (pair * 3 + third) * PAIR
                first[:, spot : spot + PAIR] = qkv_ref[
                    :, lanes(third * width + target * part + pair * PAIR, PAIR)
                ]
        first[:, 3 * part : 4 * part] = proj_ref[:, lanes(target * part, part)]
        first[:, 4 * part :] = extra
        second[:, :hidden_part] = fc1_ref[:, lanes(target * hidden_part, hidden_part)]
        second[:, hidden_part:] = fc2_ref[:, lanes(target * hidden_part, hidden_part)]


def cut(ids, counts, w_qkv, w_proj_t, w_fc1, w_fc2_t, vectors, bias, group):
    rows, width = w_proj_t.shape
    part, hidden_part = width // group, w_fc1.shape[1] // group
    return pl.pallas_call(
        cut_kernel,
        in_specs=[SMEM, SMEM] + [VMEM] * 6,
        out_specs=[VMEM] * (2 * group),
        out_shape=[shaped((rows, 4 * part + EXTRA), BF)] * group
        + [shaped((rows, 2 * hidden_part), BF)] * group,
        scratch_shapes=[pltpu.VMEM((rows, EXTRA), F32)],
        compiler_params=pltpu.CompilerParams(vmem_limit_bytes=60 * 1024 * 1024),
        name="cut",
    )(ids, counts, w_qkv, w_proj_t, w_fc1, w_fc2_t, vectors, bias)


def project_kernel(ordered, group, ids_ref, tokens_ref, *rest):
    pieces, (qkv_w, proj_w, rows_ref, normed_ref, out_ref, mean_ref, inv_ref) = rest[:-9], rest[-9:-2]
    extra_ref, bias_ref = rest[-2:]
    place, row = ids_ref[0], ids_ref[1]
    width = tokens_ref.shape[1]
    part = proj_w.shape[1]
    size = pieces[0].shape[0]

    def lay(block, start, count):
        where = pl.ds(start, count)
        qkv_w[where, :] = block[:, : 3 * part]
        proj_w[where, :] = block[:, 3 * part : 4 * part]
        extra_ref[where, :] = block[:, 4 * part :].astype(F32)

    if ordered:
        lay(pieces[0], 0, size)
    else:
        sub = size // group
        for m, piece in enumerate(pieces):
            for j in range(group):
                start = (row ^ m) * size + (place ^ j) * sub
                lay(piece.at[j * sub : (j + 1) * sub], pl.multiple_of(start, sub), sub)
    turned = extra_ref[...].T
    rows_ref[...] = turned[: rows_ref.shape[0]]
    bias_ref[...] = jnp.zeros(bias_ref.shape, F32)
    for pair in range(part // PAIR):
        for third, line in ((0, 2), (2, 3)):
            spot = (pair * 3 + third) * PAIR
            bias_ref[0:1, spot : spot + PAIR] = rows_ref[
                line : line + 1, lanes(place * part + pair * PAIR, PAIR)
            ]
    gain, shift, bias = rows_ref[0:1, :], rows_ref[1:2, :], bias_ref[0:1, :]
    half = tokens_ref.shape[0] // 2
    for start in (0, half):
        span = slice(start, start + half)
        inputs = tokens_ref[span, :].astype(F32)
        mean = jnp.mean(inputs, axis=-1, keepdims=True)
        centered = inputs - mean
        inverse = lax.rsqrt(jnp.mean(centered * centered, axis=-1, keepdims=True) + EPSILON)
        normed = (centered * inverse * gain + shift).astype(BF)
        normed_ref[span, :] = normed
        mean_ref[span, :] = mean
        inv_ref[span, :] = inverse
        out_ref[span, :] = (dot(normed, qkv_w[...], 1, 0) + bias).astype(BF)


def project(ids, tokens_all, pieces, group, ordered):
    length, width = tokens_all.shape
    part = width // group
    return pl.pallas_call(
        lambda *refs: project_kernel(ordered, group, *refs),
        in_specs=[SMEM] + [VMEM] * (1 + len(pieces)),
        out_specs=[VMEM] * 7,
        out_shape=[
            shaped((width, 3 * part), BF),
            shaped((width, part), BF),
            shaped((16, width), F32),
            shaped((length, width), BF),
            shaped((length, 3 * part), BF),
            shaped((length, 1), F32),
            shaped((length, 1), F32),
        ],
        scratch_shapes=[pltpu.VMEM((width, EXTRA), F32), pltpu.VMEM((8, 3 * part), F32)],
        compiler_params=PARAMS,
        cost_estimate=pl.CostEstimate(
            flops=6 * length * width * part, bytes_accessed=12_000_000, transcendentals=0
        ),
        name="project",
    )(ids, tokens_all, *pieces)


def query_chunks(length):
    step = 512
    return [(start, min(step, length - start)) for start in range(0, length, step)]


def attend_kernel(qkv_ref, bias_ref, out_ref, low_ref, lse_ref):
    length = qkv_ref.shape[0]
    key_bias = bias_ref[...]
    for head in range(2):
        keys = qkv_ref[:, PAIR + head * HD : PAIR + (head + 1) * HD]
        values = qkv_ref[:, 2 * PAIR + head * HD : 2 * PAIR + (head + 1) * HD]
        for start, size in query_chunks(length):
            queries = qkv_ref[start : start + size, head * HD : (head + 1) * HD]
            queries = queries * jnp.asarray(HD**-0.5, BF)
            scores = dot(keys, queries, 1, 1) + key_bias
            top = jnp.max(scores, axis=0, keepdims=True)
            expo = jnp.exp(scores - top)
            total = jnp.sum(expo, axis=0, keepdims=True)
            mixed = (dot(values, expo.astype(BF), 0, 0) / total).T
            out_ref[start : start + size, head * HD : (head + 1) * HD] = mixed
            low_ref[start : start + size, head * HD : (head + 1) * HD] = mixed.astype(BF)
            lse_ref[0, head : head + 1, start : start + size] = top + jnp.log(total)


def attend(qkv, key_bias):
    length, columns = qkv.shape
    pairs = columns // (3 * PAIR)
    return pl.pallas_call(
        attend_kernel,
        grid=(pairs,),
        in_specs=[
            pl.BlockSpec((length, 3 * PAIR), lambda p: (0, p)),
            pl.BlockSpec((length, 1), lambda p: (0, 0)),
        ],
        out_specs=[
            pl.BlockSpec((length, PAIR), lambda p: (0, p)),
            pl.BlockSpec((length, PAIR), lambda p: (0, p)),
            pl.BlockSpec((1, 2, length), lambda p: (p, 0, 0)),
        ],
        out_shape=[
            shaped((length, pairs * PAIR), F32),
            shaped((length, pairs * PAIR), BF),
            shaped((pairs, 2, length), F32),
        ],
        compiler_params=PARAMS,
        cost_estimate=pl.CostEstimate(
            flops=pairs * 2 * 4 * length * length * 256,
            bytes_accessed=length * columns * 4,
            transcendentals=pairs * 2 * length * length,
        ),
        name="attend",
    )(qkv, key_bias)


def attend_back_kernel(qkv_ref, bias_ref, att_ref, lse_ref, *rest):
    pieces, (out_ref, sums_ref, grad_ref) = rest[:-3], rest[-3:]
    length = qkv_ref.shape[0]
    size = pieces[0].shape[0]
    factor = HD**-0.5
    key_bias = bias_ref[...]
    for j, piece in enumerate(pieces):
        grad_ref[j * size : (j + 1) * size, :] = piece[...].astype(F32)
    for head in range(2):
        low, high = head * HD, (head + 1) * HD
        keys = qkv_ref[:, PAIR + low : PAIR + high]
        values = qkv_ref[:, 2 * PAIR + low : 2 * PAIR + high]
        key_grad = jnp.zeros((length, HD), F32)
        value_grad = jnp.zeros((length, HD), F32)
        for start, size in query_chunks(length):
            rows = slice(start, start + size)
            queries = qkv_ref[rows, low:high] * jnp.asarray(factor, BF)
            product = grad_ref[rows, low:high] * att_ref[rows, low:high]
            grads = grad_ref[rows, low:high].astype(BF)
            delta = jnp.sum(product.T, axis=0, keepdims=True)
            scores = dot(keys, queries, 1, 1) + key_bias
            probs = jnp.exp(scores - lse_ref[0, head : head + 1, rows])
            value_grad += dot(probs.astype(BF), grads, 1, 0)
            raw = (probs * (dot(values, grads, 1, 1) - delta)).astype(BF)
            key_grad += dot(raw, queries, 1, 0)
            query_grad = dot(keys, raw, 0, 0).T * factor
            out_ref[rows, low:high] = query_grad.astype(BF)
        out_ref[:, PAIR + low : PAIR + high] = key_grad.astype(BF)
        out_ref[:, 2 * PAIR + low : 2 * PAIR + high] = value_grad.astype(BF)
    sums_ref[0] = jnp.sum(out_ref[...].astype(F32), axis=0, keepdims=True)


def attend_back(qkv, key_bias, attended, lse, pieces):
    length, columns = qkv.shape
    pairs = columns // (3 * PAIR)
    size = pieces[0].shape[0]
    return pl.pallas_call(
        attend_back_kernel,
        grid=(pairs,),
        in_specs=[
            pl.BlockSpec((length, 3 * PAIR), lambda p: (0, p)),
            pl.BlockSpec((length, 1), lambda p: (0, 0)),
            pl.BlockSpec((length, PAIR), lambda p: (0, p)),
            pl.BlockSpec((1, 2, length), lambda p: (p, 0, 0)),
        ]
        + [pl.BlockSpec((size, PAIR), lambda p: (0, p))] * len(pieces),
        out_specs=[
            pl.BlockSpec((length, 3 * PAIR), lambda p: (0, p)),
            pl.BlockSpec((1, 1, 3 * PAIR), lambda p: (p, 0, 0)),
        ],
        out_shape=[shaped((length, columns), BF), shaped((pairs, 1, 3 * PAIR), F32)],
        scratch_shapes=[pltpu.VMEM((length, PAIR), F32)],
        compiler_params=PARAMS,
        cost_estimate=pl.CostEstimate(
            flops=pairs * 2 * 10 * length * length * 256,
            bytes_accessed=length * columns * 6,
            transcendentals=pairs * 2 * length * length,
        ),
        name="attend_back",
    )(qkv, key_bias, attended, lse, *pieces)


def middle_kernel(group, rows_ref, tokens_ref, *rest):
    parts, weights, (branch_ref, middle_ref, normed_ref, unit_ref, inv_ref) = (
        rest[:group], rest[group : 2 * group], rest[2 * group :]
    )
    branch = dot(parts[0][...], weights[0][...], 1, 1)
    for part, weight in zip(parts[1:], weights[1:]):
        branch = branch + dot(part[...], weight[...], 1, 1)
    branch = branch + rows_ref[4:5, :]
    branch_ref[...] = branch
    middle = tokens_ref[...].astype(F32) + rows_ref[5:6, :] * branch
    middle_ref[...] = middle
    unit, inverse = unit_rows(middle)
    unit_ref[...] = unit
    inv_ref[...] = inverse
    normed_ref[...] = (unit * rows_ref[6:7, :] + rows_ref[7:8, :]).astype(BF)


def middle_step(rows, tokens, parts, weights):
    length, width = tokens.shape
    group = len(parts)
    full = shaped((length, width), F32)
    return pl.pallas_call(
        lambda *refs: middle_kernel(group, *refs),
        in_specs=[VMEM] * (2 + 2 * group),
        out_specs=[VMEM] * 5,
        out_shape=[full, full, shaped((length, width), BF), full, shaped((length, 1), F32)],
        compiler_params=PARAMS,
        cost_estimate=pl.CostEstimate(
            flops=2 * length * width * width, bytes_accessed=8_000_000, transcendentals=0
        ),
        name="middle",
    )(rows, tokens, *parts, *weights)


def turn_kernel(group, terms, rows_ref, live_ref, cot_ref, unit_ref, inv_ref, branch_ref, *rest):
    backs, weights, outs = rest[:terms], rest[terms : terms + group], rest[terms + group :]
    middle_ref, grad_ref, sums_ref = outs[:3]
    norm_grad = backs[0][...].astype(F32)
    for ref in backs[1:]:
        norm_grad = norm_grad + ref[...].astype(F32)
    unit = unit_ref[...]
    out_grad = cot_ref[...].astype(F32) * live_ref[...]
    middle = out_grad + norm_back(norm_grad, unit, inv_ref[...], rows_ref[6:7, :])
    middle_ref[...] = middle
    low = (middle * rows_ref[5:6, :]).astype(BF)
    grad_ref[...] = low
    sums_ref[...] = jnp.zeros(sums_ref.shape, F32)
    sums_ref[0:1, :] = jnp.sum(low.astype(F32), axis=0, keepdims=True)
    sums_ref[1:2, :] = jnp.sum(middle * branch_ref[...], axis=0, keepdims=True)
    sums_ref[2:3, :] = jnp.sum(norm_grad * unit, axis=0, keepdims=True)
    sums_ref[3:4, :] = jnp.sum(norm_grad, axis=0, keepdims=True)
    for out, weight in zip(outs[3:], weights):
        out[...] = dot(low, weight[...], 1, 0).astype(BF)


def turn(rows, live, cotangent, unit, inverse, branch, backs, weights):
    length, width = cotangent.shape
    part = weights[0].shape[1]
    group = len(weights)
    return pl.pallas_call(
        lambda *refs: turn_kernel(group, len(backs), *refs),
        in_specs=[VMEM] * (6 + len(backs) + group),
        out_specs=[VMEM] * (3 + group),
        out_shape=[shaped((length, width), F32), shaped((length, width), BF), shaped((8, width), F32)]
        + [shaped((length, part), BF)] * group,
        compiler_params=PARAMS,
        cost_estimate=pl.CostEstimate(
            flops=2 * length * width * width, bytes_accessed=10_000_000, transcendentals=0
        ),
        name="turn",
    )(rows, live, cotangent, unit, inverse, branch, *backs, *weights)


def proj_weights_kernel(grad_ref, *rest):
    half = len(rest) // 2
    for part, out in zip(rest[:half], rest[half:]):
        out[...] = dot(grad_ref[...], part[...], 0, 0).astype(BF)


def proj_weights(grads, parts):
    length, width = grads.shape
    part = parts[0].shape[1]
    return pl.pallas_call(
        proj_weights_kernel,
        in_specs=[VMEM] * (1 + len(parts)),
        out_specs=[VMEM] * len(parts),
        out_shape=[shaped((width, part), BF)] * len(parts),
        compiler_params=PARAMS,
        cost_estimate=pl.CostEstimate(
            flops=2 * length * width * width, bytes_accessed=4_000_000, transcendentals=0
        ),
        name="proj_weights",
    )(grads, *parts)


def mlp_kernel(
    normed_ref, grad_ref, fc1_ref, fc2_ref, bias_ref,
    act_ref, pre_ref, back0_ref, back1_ref, branch0_ref, branch1_ref, sums_ref, back_acc, branch_acc,
):
    step = pl.program_id(0)
    pre = dot(normed_ref[...], fc1_ref[...], 1, 0) + bias_ref[...]
    cdf = 0.5 * (1.0 + lax.erf(pre * SQRT_HALF))
    act = (pre * cdf).astype(BF)
    slope = cdf + pre * jnp.exp(-0.5 * pre * pre) * INV_ROOT_TWO_PI
    pre_grad = (dot(grad_ref[...], fc2_ref[...], 1, 0) * slope).astype(BF)
    act_ref[...] = act
    pre_ref[...] = pre_grad
    sums_ref[...] = jnp.sum(pre_grad.astype(F32), axis=0, keepdims=True)
    back = dot(pre_grad, fc1_ref[...], 1, 1)
    branch = dot(act, fc2_ref[...], 1, 1)

    @pl.when(step == 0)
    def _():
        back_acc[...] = back
        branch_acc[...] = branch

    @pl.when(step > 0)
    def _():
        back_acc[...] += back
        branch_acc[...] += branch

    @pl.when(step == pl.num_programs(0) - 1)
    def _():
        size = back0_ref.shape[0]
        back0_ref[...] = back_acc[:size, :].astype(BF)
        back1_ref[...] = back_acc[size:, :].astype(BF)
        branch0_ref[...] = branch_acc[:size, :].astype(BF)
        branch1_ref[...] = branch_acc[size:, :].astype(BF)


def mlp(normed, grads, weights, bias):
    length, width = normed.shape
    hidden = weights.shape[1] // 2
    step = 256
    steps = hidden // step
    whole = pl.BlockSpec((length, width), lambda i: (0, 0))
    piece = pl.BlockSpec((length // 2, width), lambda i: (0, 0))
    cols = pl.BlockSpec((length, step), lambda i: (0, i))
    return pl.pallas_call(
        mlp_kernel,
        grid=(steps,),
        in_specs=[
            whole,
            whole,
            pl.BlockSpec((width, step), lambda i: (0, i)),
            pl.BlockSpec((width, step), lambda i: (0, steps + i)),
            pl.BlockSpec((1, step), lambda i: (0, i)),
        ],
        out_specs=[cols, cols] + [piece] * 4 + [pl.BlockSpec((1, step), lambda i: (0, i))],
        out_shape=[
            shaped((length, hidden), BF),
            shaped((length, hidden), BF),
        ]
        + [shaped((length // 2, width), BF)] * 4
        + [shaped((1, hidden), F32)],
        scratch_shapes=[pltpu.VMEM((length, width), F32)] * 2,
        compiler_params=PARAMS,
        cost_estimate=pl.CostEstimate(
            flops=8 * length * width * hidden,
            bytes_accessed=12_000_000,
            transcendentals=2 * length * hidden,
        ),
        name="mlp",
    )(normed, grads, weights, weights, bias)


def mlp_weights_kernel(norm_a, norm_b, grad_a, grad_b, pre_a, pre_b, act_a, act_b, out_ref):
    hidden = pre_a.shape[1]
    first = dot(norm_a[...], pre_a[...], 0, 0) + dot(norm_b[...], pre_b[...], 0, 0)
    out_ref[:, :hidden] = first.astype(BF)
    second = dot(grad_a[...], act_a[...], 0, 0) + dot(grad_b[...], act_b[...], 0, 0)
    out_ref[:, hidden:] = second.astype(BF)


def mlp_weights(normed, grads, pres, acts):
    length, width = normed[0].shape
    hidden = pres[0].shape[1]
    step = 256
    cols = pl.BlockSpec((length, step), lambda i: (0, i))
    whole = pl.BlockSpec((length, hidden), lambda i: (0, 0))
    return pl.pallas_call(
        mlp_weights_kernel,
        grid=(width // step,),
        in_specs=[cols] * 4 + [whole] * 4,
        out_specs=pl.BlockSpec((step, 2 * hidden), lambda i: (i, 0)),
        out_shape=shaped((width, 2 * hidden), BF),
        compiler_params=PARAMS,
        cost_estimate=pl.CostEstimate(
            flops=8 * length * width * hidden, bytes_accessed=16_000_000, transcendentals=0
        ),
        name="mlp_weights",
    )(*normed, *grads, *pres, *acts)


def qkv_back_kernel(grad_ref, weight_ref, tokens_ref, mean_ref, inv_ref, out_ref, sums_ref):
    step = pl.program_id(0)
    part = dot(grad_ref[...], weight_ref[...], 1, 1)
    out_ref[...] = part.astype(BF)
    unit = (tokens_ref[...].astype(F32) - mean_ref[...]) * inv_ref[...]

    @pl.when(step == 0)
    def _():
        sums_ref[...] = jnp.zeros(sums_ref.shape, F32)

    sums_ref[0:1, :] += jnp.sum(part * unit, axis=0, keepdims=True)
    sums_ref[1:2, :] += jnp.sum(part, axis=0, keepdims=True)


def qkv_back(qkv_grad, weight, tokens_all, mean, inverse):
    length, width = tokens_all.shape
    columns = qkv_grad.shape[1]
    half = length // 2
    return pl.pallas_call(
        qkv_back_kernel,
        grid=(2,),
        in_specs=[
            pl.BlockSpec((half, columns), lambda i: (i, 0)),
            pl.BlockSpec((width, columns), lambda i: (0, 0)),
            pl.BlockSpec((half, width), lambda i: (i, 0)),
            pl.BlockSpec((half, 1), lambda i: (i, 0)),
            pl.BlockSpec((half, 1), lambda i: (i, 0)),
        ],
        out_specs=[
            pl.BlockSpec((half, width), lambda i: (i, 0)),
            pl.BlockSpec((8, width), lambda i: (0, 0)),
        ],
        out_shape=[shaped((length, width), BF), shaped((8, width), F32)],
        compiler_params=PARAMS,
        cost_estimate=pl.CostEstimate(
            flops=2 * length * width * columns, bytes_accessed=10_000_000, transcendentals=0
        ),
        name="qkv_back",
    )(qkv_grad, weight, tokens_all, mean, inverse)


def attn_weights_kernel(
    direct, terms, ids_ref, normed_ref, grad_ref, norm1_ref, sums_ref, turn_ref, fbias_ref,
    scale2_ref, bias_ref, *rest,
):
    projs, outs = rest[:terms], rest[terms:-3]
    rows_ref, turned_ref, block_ref = rest[-3:]
    place, row = ids_ref[0], ids_ref[1]
    width = normed_ref.shape[1]
    part = projs[0].shape[1]
    rows_ref[...] = jnp.zeros(rows_ref.shape, F32)
    rows_ref[0:2, :] = norm1_ref[0:2, :]
    for pair in range(part // PAIR):
        where = lanes(place * part + pair * PAIR, PAIR)
        rows_ref[2:3, where] = sums_ref[pair, :, :PAIR]
        rows_ref[3:4, where] = sums_ref[pair, :, 2 * PAIR :]
    rows_ref[4:8, :] = turn_ref[0:4, :]
    rows_ref[8:9, :] = fbias_ref[...]
    rows_ref[9:10, :] = scale2_ref[...]
    for line in range(bias_ref.shape[0]):
        rows_ref[10 + line : 11 + line, lanes(place * part, part)] = bias_ref[line : line + 1, :]
    turned_ref[...] = rows_ref[...].T
    step = block_ref.shape[0]
    for k in range(width // step):
        start = pl.multiple_of(((row >> 1) ^ k) * step, step) if direct else k * step
        cols = pl.ds(start, step)
        block_ref[:, : 3 * part] = dot(normed_ref[:, cols], grad_ref[...], 0, 0)
        proj = projs[0][cols, :].astype(F32)
        for ref in projs[1:]:
            proj = proj + ref[cols, :].astype(F32)
        block_ref[:, 3 * part : 4 * part] = proj
        block_ref[:, 4 * part :] = turned_ref[cols, :]
        if direct:
            size = step // 2
            side = row & 1
            outs[2 * k][...] = block_ref[pl.ds(pl.multiple_of(side * size, size), size), :].astype(BF)
            outs[2 * k + 1][...] = block_ref[
                pl.ds(pl.multiple_of((1 - side) * size, size), size), :
            ].astype(BF)
        else:
            outs[0][k * step : (k + 1) * step, :] = block_ref[...].astype(BF)


def attn_weights(ids, normed1, qkv_grad, sums, projs, blocks):
    length, width = normed1.shape
    part = projs[0].shape[1]
    columns = 4 * part + EXTRA
    direct = blocks > 0
    step = 2 * (width // blocks) if direct else 256
    out_shape = [shaped((width // blocks, columns), BF)] * blocks if direct else [
        shaped((width, columns), BF)
    ]
    return pl.pallas_call(
        lambda *refs: attn_weights_kernel(direct, len(projs), *refs),
        in_specs=[SMEM] + [VMEM] * (2 + len(sums) + len(projs)),
        out_specs=[VMEM] * len(out_shape),
        out_shape=out_shape,
        scratch_shapes=[
            pltpu.VMEM((EXTRA, width), F32),
            pltpu.VMEM((width, EXTRA), F32),
            pltpu.VMEM((step, columns), F32),
        ],
        compiler_params=PARAMS,
        cost_estimate=pl.CostEstimate(
            flops=6 * length * width * part, bytes_accessed=12_000_000, transcendentals=0
        ),
        name="attn_weights",
    )(ids, normed1, qkv_grad, *sums, *projs)


def total(ids, terms, group):
    size, columns = terms[0].shape
    rows = size // group

    def kernel(ids_ref, *refs):
        ins, outs, sum_ref = refs[: len(terms)], refs[len(terms) : -1], refs[-1]
        value = ins[0][...].astype(F32)
        for ref in ins[1:]:
            value = value + ref[...].astype(F32)
        sum_ref[...] = value
        for k, out in enumerate(outs):
            start = pl.multiple_of((ids_ref[0] ^ k) * rows, rows)
            out[...] = sum_ref[pl.ds(start, rows), :].astype(BF)

    return pl.pallas_call(
        kernel,
        in_specs=[SMEM] + [VMEM] * len(terms),
        out_specs=[VMEM] * group,
        out_shape=[shaped((rows, columns), BF)] * group,
        scratch_shapes=[pltpu.VMEM((size, columns), F32)],
        compiler_params=PARAMS,
        name="total",
    )(ids, *terms)


def place_attn_kernel(ids_ref, *refs):
    group = len(refs) - 3
    blocks, (qkv_ref, proj_ref, extra_ref) = refs[:group], refs[group:]
    width = proj_ref.shape[1]
    part = width // group
    extra = jnp.zeros(extra_ref.shape[::-1], F32)
    for k, block in enumerate(blocks):
        source = ids_ref[0] ^ k
        for third in range(3):
            for pair in range(part // PAIR):
                spot = (pair * 3 + third) * PAIR
                where = lanes(third * width + source * part + pair * PAIR, PAIR)
                qkv_ref[:, where] = block[:, spot : spot + PAIR].astype(F32)
        proj_ref[:, lanes(source * part, part)] = block[:, 3 * part : 4 * part].astype(F32)
        extra = extra + block[:, 4 * part :].astype(F32)
    extra_ref[...] = extra.T


def place_attn(ids, blocks, width):
    rows = blocks[0].shape[0]
    return pl.pallas_call(
        place_attn_kernel,
        in_specs=[SMEM] + [VMEM] * len(blocks),
        out_specs=[VMEM] * 3,
        out_shape=[
            shaped((rows, 3 * width), F32),
            shaped((rows, width), F32),
            shaped((EXTRA, rows), F32),
        ],
        compiler_params=PARAMS,
        name="place_attn",
    )(ids, *blocks)


def place_mlp_kernel(ids_ref, *refs):
    group = len(refs) - 2
    blocks, (fc1_ref, fc2_ref) = refs[:group], refs[group:]
    part = fc1_ref.shape[1] // group
    for k, block in enumerate(blocks):
        where = lanes((ids_ref[0] ^ k) * part, part)
        fc1_ref[:, where] = block[:, :part].astype(F32)
        fc2_ref[:, where] = block[:, part:].astype(F32)


def place_mlp(ids, blocks, hidden):
    rows = blocks[0].shape[0]
    return pl.pallas_call(
        place_mlp_kernel,
        in_specs=[SMEM] + [VMEM] * len(blocks),
        out_specs=[VMEM] * 2,
        out_shape=[shaped((rows, hidden), F32)] * 2,
        compiler_params=PARAMS,
        name="place_mlp",
    )(ids, *blocks)


def local(tokens, counts, w_qkv, w_proj, w_fc1, fc1_bias, w_fc2, vectors, cotangent):
    _, capacity, width = tokens.shape
    hidden = w_fc1.shape[1]
    rows = w_qkv.shape[0]
    group, replicas = lax.axis_size("ctx"), lax.axis_size("dp")
    place, replica = lax.axis_index("ctx"), lax.axis_index("dp")
    ids = jnp.stack([place, replica]).astype(jnp.int32)
    head_width = width // group
    hidden_part = hidden // group
    bias_cols = hidden // width
    vector_count = vectors.shape[0]
    direct = replicas <= 8

    def swap(value, bit, axis="ctx"):
        size = group if axis == "ctx" else replicas
        return lax.ppermute(value, axis, [(i, i ^ bit) for i in range(size)])

    def after(value, *before):
        return lax.optimization_barrier((value,) + before)[0]

    def gather(own, *before):
        pieces = [own]
        for j in range(1, group):
            bit = j & -j
            source = pieces[j ^ bit]
            pieces.append(swap(after(source, *before) if j ^ bit else source, bit))
        return pieces

    def scatter(parts, *before, mids=None):
        pieces = {j: [part] for j, part in enumerate(parts)}

        def added(terms):
            if len(terms) == 1:
                return terms[0]
            return sum(term.astype(F32) for term in terms).astype(BF)

        bit = 1
        while bit < group:
            for j in sorted((j for j in pieces if j & bit), reverse=True):
                value = added(pieces.pop(j))
                if bit > 1:
                    if mids is not None:
                        mids.append(value)
                    value = after(value, *before)
                pieces[j ^ bit].append(swap(value, bit))
            bit *= 2
        return pieces[0]

    def total_of(terms):
        return sum(term.astype(F32) for term in terms)

    def split(whole):
        return [whole[j * capacity : (j + 1) * capacity] for j in range(whole.shape[0] // capacity)]

    def exchange(relative):
        return [relative[0]] + [swap(relative[k], k) for k in range(1, group)]

    def in_order(relative):
        stacked = jnp.stack(relative)
        return jnp.concatenate(
            [lax.dynamic_index_in_dim(stacked, place ^ s, 0, False) for s in range(group)], axis=0
        )

    cuts = cut(
        ids, counts, w_qkv, w_proj.T, w_fc1, w_fc2.T, vectors, fc1_bias.reshape(bias_cols, rows), group
    )
    first = exchange(cuts[:group])
    if direct:
        shards = {0: jnp.concatenate(first, axis=0)}
        for m in range(replicas - 2, 0, -2):
            shards[m] = swap(shards[0], m, "dp")
        arrived = [shards[m] for m in range(2, replicas, 2)]
    else:
        first_pieces = [lax.all_gather(in_order(first), "dp", axis=0, tiled=True)]
        arrived = first_pieces
    tokens_pieces = gather(after(tokens[0], *first))
    if direct:
        for m in range(1, replicas, 2):
            shards[m] = swap(after(shards[m - 1], tokens_pieces[group // 2]), 1, "dp")
        first_pieces = [shards[m] for m in range(replicas)]
        arrived = [shards[1], shards[3]]
    second = exchange([after(block, *arrived) for block in cuts[group:]])
    second_shard = in_order(second)
    second_all = lax.all_gather(second_shard, "dp", axis=0, tiled=True)

    count_column = 4 * head_width + vector_count + bias_cols
    live = []
    for block in first:
        piece = block[0, count_column : count_column + 2].astype(F32)
        bound = piece[0] * 128.0 + piece[1]
        slot = lax.broadcasted_iota(jnp.int32, (capacity, 1), 0).astype(F32)
        live.append((slot < bound).astype(F32))
    key_bias = jnp.where(jnp.concatenate(live, axis=0) > 0.0, 0.0, MASKED_SCORE).astype(F32)

    tokens_all = after(jnp.concatenate(tokens_pieces, axis=0), second_shard)
    weight_qkv, weight_proj, vector_rows, normed1, qkv, mean1, inverse1_all = project(
        ids, tokens_all, first_pieces, group, not direct
    )
    bias_part = lax.dynamic_slice_in_dim(
        vector_rows[vector_count : vector_count + bias_cols], place * head_width, head_width, axis=1
    )
    bias_fc1 = bias_part.reshape(bias_cols, head_width // rows, rows).transpose(1, 0, 2)
    bias_fc1 = bias_fc1.reshape(1, hidden_part)

    cotangent_pieces = gather(after(cotangent[0], *second, *first_pieces), qkv)
    attended, attended_low, lse = attend(qkv, key_bias)
    projs = gather(weight_proj, attended_low)
    attended_own = exchange(split(attended_low))
    branch1, middle, normed2_own, unit2, inverse2 = middle_step(
        vector_rows, tokens[0], attended_own, projs
    )
    pieces = gather(normed2_own)
    normed2 = [jnp.concatenate(pieces[: group // 2]), jnp.concatenate(pieces[group // 2 :])]

    mlp_grads = [
        (piece.astype(F32) * keep * vector_rows[9]).astype(BF)
        for keep, piece in zip(live, cotangent_pieces)
    ]
    grad_fbias = jnp.sum(mlp_grads[0].astype(F32), axis=0, keepdims=True)
    mlp_grad = [jnp.concatenate(mlp_grads[: group // 2]), jnp.concatenate(mlp_grads[group // 2 :])]
    near = mlp(normed2[0], mlp_grad[0], second_all, bias_fc1)
    far = mlp(normed2[1], mlp_grad[1], second_all, after(bias_fc1, near[6]))
    norm2_terms = scatter([near[2], near[3], far[2], far[3]])
    grad_mlp = mlp_weights(normed2, mlp_grad, (near[1], far[1]), (near[0], far[0]))
    owned_mlp = lax.psum_scatter(grad_mlp, "dp", scatter_dimension=0, tiled=True)
    grad_bfc1 = (near[6] + far[6]).reshape(head_width // rows, bias_cols, rows)
    grad_bfc1 = grad_bfc1.transpose(1, 0, 2).reshape(bias_cols, head_width)

    middle_grad, branch_grad, turn_sums, *att_grads = turn(
        vector_rows, live[0], cotangent[0], unit2, inverse2, branch1, norm2_terms, projs
    )
    att_grads = exchange(att_grads)
    mids = []
    proj_terms = scatter(proj_weights(branch_grad, attended_own), mids=mids)
    branch2_terms = scatter([near[4], near[5], far[4], far[5]], *att_grads, mids=mids)
    qkv_grad, qkv_sums = attend_back(qkv, key_bias, attended, after(lse, *mids), att_grads)
    norm1_part, norm1_sums = qkv_back(qkv_grad, weight_qkv, tokens_all, mean1, inverse1_all)
    branch2 = total_of(branch2_terms) + vector_rows[8]
    output = (middle + vector_rows[9] * branch2).astype(BF)
    grad_scale2 = jnp.sum(
        cotangent[0].astype(F32) * live[0] * branch2, axis=0, keepdims=True
    )
    parts = attn_weights(
        ids, normed1, qkv_grad,
        [norm1_sums, qkv_sums, turn_sums, grad_fbias, grad_scale2, grad_bfc1],
        proj_terms, replicas if direct else 0,
    )
    if direct:
        terms, last = [], []
        for k in list(range(replicas // 2 - 1, -1, -1)):
            other = swap(after(parts[2 * k + 1], *last), 1, "dp")
            if k == 0:
                terms += [parts[0], other]
            else:
                summed = (parts[2 * k].astype(F32) + other.astype(F32)).astype(BF)
                terms.append(swap(summed, 2 * k, "dp"))
            last = [other]
        cuts_mlp = total(ids, [owned_mlp], group)
    else:
        owned_attn = lax.psum_scatter(parts[0], "dp", scatter_dimension=0, tiled=True)

        def relative(owned):
            blocks = owned.reshape(group, rows, -1)
            return [lax.dynamic_index_in_dim(blocks, place ^ k, 0, False) for k in range(group)]

        cuts_mlp = relative(owned_mlp)
    out_fc1, out_fc2 = place_mlp(ids, exchange(cuts_mlp), hidden)
    if direct:
        cuts_attn = total(after(ids, out_fc1), terms, group)
    else:
        cuts_attn = relative(owned_attn)
    norm1_grad = total_of(scatter(split(norm1_part)))
    inputs = tokens[0].astype(F32)
    inverse1 = inverse1_all[:capacity]
    unit1 = (inputs - mean1[:capacity]) * inverse1
    input_grad = (middle_grad + norm_back(norm1_grad, unit1, inverse1, vector_rows[0])).astype(BF)

    out_qkv, out_proj, out_extra = place_attn(ids, exchange(cuts_attn), width)
    return (
        output[None],
        input_grad[None],
        out_qkv,
        out_proj.T,
        out_fc1,
        out_extra[vector_count : vector_count + bias_cols].reshape(-1),
        out_fc2.T,
        out_extra[:vector_count],
    )


def solution(mesh):
    both = ("dp", "ctx")
    in_specs = (
        P("dp", "ctx", None),
        P("dp", "ctx"),
        P(both, None),
        P(None, both),
        P(both, None),
        P(both),
        P(None, both),
        P(None, both),
        P("dp", "ctx", None),
    )
    out_specs = (
        P("dp", "ctx", None),
        P("dp", "ctx", None),
        P(both, None),
        P(None, both),
        P(both, None),
        P(both),
        P(None, both),
        P(None, both),
    )
    return jax.shard_map(local, mesh=mesh, in_specs=in_specs, out_specs=out_specs, check_vma=False)
```

```python
import jax
import jax.numpy as jnp
from jax import lax
from jax.experimental import pallas as pl
from jax.experimental.pallas import tpu as pltpu
from jax.sharding import PartitionSpec as P

HD = 64
PAIR = 2 * HD
EXTRA = 128
EPSILON = 1e-06
MASKED_SCORE = -1e30
SQRT_HALF = 0.7071067811865476
INV_ROOT_TWO_PI = 0.3989422804014327
BF = jnp.bfloat16
F32 = jnp.float32
PARAMS = pltpu.CompilerParams(vmem_limit_bytes=60 * 1024 * 1024)
VMEM = pl.BlockSpec(memory_space=pltpu.VMEM)
SMEM = pl.BlockSpec(memory_space=pltpu.SMEM)


def shaped(shape, dtype):
    return jax.ShapeDtypeStruct(shape, dtype)


def dot(left, right, left_dim, right_dim):
    return lax.dot_general(
        left, right, (((left_dim,), (right_dim,)), ((), ())), preferred_element_type=F32
    )


def lanes(start, size):
    return pl.ds(pl.multiple_of(start, 128), size)


def unit_rows(inputs):
    centered = inputs - jnp.mean(inputs, axis=-1, keepdims=True)
    spread = jnp.mean(centered * centered, axis=-1, keepdims=True)
    inverse = lax.rsqrt(spread + EPSILON)
    return (centered * inverse, inverse)


def norm_back(grad_in, unit, inverse, gain):
    scaled = grad_in * gain
    inner = (
        scaled
        - jnp.mean(scaled, axis=-1, keepdims=True)
        - unit * jnp.mean(scaled * unit, axis=-1, keepdims=True)
    )
    return inner * inverse


def cut_kernel(ids_ref, count_ref, qkv_ref, proj_ref, fc1_ref, fc2_ref, vec_ref, bias_ref, *rest):
    outs, extra_ref = rest[:-1], rest[-1]
    group = len(outs) // 2
    place = ids_ref[0]
    width = proj_ref.shape[1]
    part = width // group
    hidden_part = fc1_ref.shape[1] // group
    vector_count, bias_cols = vec_ref.shape[0], bias_ref.shape[0]
    column = vector_count + bias_cols
    lane = lax.broadcasted_iota(jnp.int32, extra_ref.shape, 1)
    count = count_ref[0, 0]
    high = (count >> 7).astype(F32)
    low = (count & 127).astype(F32)
    extra_ref[...] = jnp.where(lane == column, high, jnp.where(lane == column + 1, low, 0.0))
    extra_ref[:, :vector_count] = vec_ref[...].astype(F32).T
    extra_ref[:, vector_count:column] = bias_ref[...].astype(F32).T
    extra = extra_ref[...].astype(BF)
    for k in range(group):
        target = place ^ k
        first, second = outs[k], outs[group + k]
        for third in range(3):
            for pair in range(part // PAIR):
                spot = (pair * 3 + third) * PAIR
                first[:, spot : spot + PAIR] = qkv_ref[
                    :, lanes(third * width + target * part + pair * PAIR, PAIR)
                ]
        first[:, 3 * part : 4 * part] = proj_ref[:, lanes(target * part, part)]
        first[:, 4 * part :] = extra
        second[:, :hidden_part] = fc1_ref[:, lanes(target * hidden_part, hidden_part)]
        second[:, hidden_part:] = fc2_ref[:, lanes(target * hidden_part, hidden_part)]


def cut(ids, counts, w_qkv, w_proj_t, w_fc1, w_fc2_t, vectors, bias, group):
    rows, width = w_proj_t.shape
    part, hidden_part = width // group, w_fc1.shape[1] // group
    return pl.pallas_call(
        cut_kernel,
        in_specs=[SMEM, SMEM] + [VMEM] * 6,
        out_specs=[VMEM] * (2 * group),
        out_shape=[shaped((rows, 4 * part + EXTRA), BF)] * group
        + [shaped((rows, 2 * hidden_part), BF)] * group,
        scratch_shapes=[pltpu.VMEM((rows, EXTRA), F32)],
        compiler_params=PARAMS,
        name="cut",
    )(ids, counts, w_qkv, w_proj_t, w_fc1, w_fc2_t, vectors, bias)


def project_kernel(ordered, group, ids_ref, *rest):
    tokens, pieces, outs = rest[:group], rest[group:-11], rest[-11:]
    qkv_w, proj_w, rows_ref, normed_ref, out_ref, mean_ref, inv_ref, fc1_ref = outs[:8]
    extra_ref, bias_ref, small_ref = outs[8:]
    place, row = ids_ref[0], ids_ref[1]
    capacity, width = tokens[0].shape
    part = proj_w.shape[1]
    size = pieces[0].shape[0]

    def lay(block, start, count):
        where = pl.ds(start, count)
        qkv_w[where, :] = block[:, : 3 * part]
        proj_w[where, :] = block[:, 3 * part : 4 * part]
        extra_ref[where, :] = block[:, 4 * part :].astype(F32)

    if ordered:
        lay(pieces[0], 0, size)
        shard = ordered
    else:
        sub = shard = size // group
        for m, piece in enumerate(pieces):
            for j in range(group):
                start = (row ^ m) * size + (place ^ j) * sub
                lay(piece.at[j * sub : (j + 1) * sub], pl.multiple_of(start, sub), sub)
    turned = extra_ref[...].T
    rows_ref[...] = turned[: rows_ref.shape[0]]
    bias_ref[...] = jnp.zeros(bias_ref.shape, F32)
    for pair in range(part // PAIR):
        for third, line in ((0, 2), (2, 3)):
            spot = (pair * 3 + third) * PAIR
            bias_ref[0:1, spot : spot + PAIR] = rows_ref[
                line : line + 1, lanes(place * part + pair * PAIR, PAIR)
            ]
    cols = fc1_ref.shape[1] // part
    small_ref[0:cols, :] = rows_ref[10 : 10 + cols, lanes(place * part, part)]
    for owner in range(part // shard):
        for line in range(cols):
            spot = (owner * cols + line) * shard
            fc1_ref[0:1, spot : spot + shard] = small_ref[
                line : line + 1, owner * shard : (owner + 1) * shard
            ]
    gain, shift, bias = rows_ref[0:1, :], rows_ref[1:2, :], bias_ref[0:1, :]
    for first in range(0, group, 2):
        span = slice(first * capacity, (first + 2) * capacity)
        inputs = jnp.concatenate([tokens[first][...].astype(F32), tokens[first + 1][...].astype(F32)])
        mean = jnp.mean(inputs, axis=-1, keepdims=True)
        centered = inputs - mean
        inverse = lax.rsqrt(jnp.mean(centered * centered, axis=-1, keepdims=True) + EPSILON)
        normed = (centered * inverse * gain + shift).astype(BF)
        normed_ref[span, :] = normed
        mean_ref[span, :] = mean
        inv_ref[span, :] = inverse
        out_ref[span, :] = (dot(normed, qkv_w[...], 1, 0) + bias).astype(BF)


def project(ids, tokens, pieces, hidden_part, ordered):
    capacity, width = tokens[0].shape
    group = len(tokens)
    length = group * capacity
    part = width // group
    return pl.pallas_call(
        lambda *refs: project_kernel(ordered, group, *refs),
        in_specs=[SMEM] + [VMEM] * (group + len(pieces)),
        out_specs=[VMEM] * 8,
        out_shape=[
            shaped((width, 3 * part), BF),
            shaped((width, part), BF),
            shaped((16, width), F32),
            shaped((length, width), BF),
            shaped((length, 3 * part), BF),
            shaped((length, 1), F32),
            shaped((length, 1), F32),
            shaped((1, hidden_part), F32),
        ],
        scratch_shapes=[
            pltpu.VMEM((width, EXTRA), F32),
            pltpu.VMEM((8, 3 * part), F32),
            pltpu.VMEM((8, part), F32),
        ],
        compiler_params=PARAMS,
        cost_estimate=pl.CostEstimate(
            flops=6 * length * width * part, bytes_accessed=12_000_000, transcendentals=0
        ),
        name="project",
    )(ids, *tokens, *pieces)


def query_chunks(length):
    step = 512
    return [(start, min(step, length - start)) for start in range(0, length, step)]


def attend_kernel(qkv_ref, bias_ref, out_ref, low_ref, lse_ref):
    length = qkv_ref.shape[0]
    key_bias = bias_ref[...]
    for head in range(2):
        keys = qkv_ref[:, PAIR + head * HD : PAIR + (head + 1) * HD]
        values = qkv_ref[:, 2 * PAIR + head * HD : 2 * PAIR + (head + 1) * HD]
        for start, size in query_chunks(length):
            queries = qkv_ref[start : start + size, head * HD : (head + 1) * HD]
            queries = queries * jnp.asarray(HD**-0.5, BF)
            scores = dot(keys, queries, 1, 1) + key_bias
            top = jnp.max(scores, axis=0, keepdims=True)
            expo = jnp.exp(scores - top)
            total = jnp.sum(expo, axis=0, keepdims=True)
            mixed = (dot(values, expo.astype(BF), 0, 0) / total).T
            out_ref[start : start + size, head * HD : (head + 1) * HD] = mixed
            low_ref[start : start + size, head * HD : (head + 1) * HD] = mixed.astype(BF)
            lse_ref[0, head : head + 1, start : start + size] = top + jnp.log(total)


def attend(qkv, key_bias):
    length, columns = qkv.shape
    pairs = columns // (3 * PAIR)
    return pl.pallas_call(
        attend_kernel,
        grid=(pairs,),
        in_specs=[
            pl.BlockSpec((length, 3 * PAIR), lambda p: (0, p)),
            pl.BlockSpec((length, 1), lambda p: (0, 0)),
        ],
        out_specs=[
            pl.BlockSpec((length, PAIR), lambda p: (0, p)),
            pl.BlockSpec((length, PAIR), lambda p: (0, p)),
            pl.BlockSpec((1, 2, length), lambda p: (p, 0, 0)),
        ],
        out_shape=[
            shaped((length, pairs * PAIR), F32),
            shaped((length, pairs * PAIR), BF),
            shaped((pairs, 2, length), F32),
        ],
        compiler_params=PARAMS,
        cost_estimate=pl.CostEstimate(
            flops=pairs * 2 * 4 * length * length * 256,
            bytes_accessed=length * columns * 4,
            transcendentals=pairs * 2 * length * length,
        ),
        name="attend",
    )(qkv, key_bias)


def attend_back_kernel(qkv_ref, bias_ref, att_ref, lse_ref, *rest):
    pieces, (out_ref, sums_ref, grad_ref) = rest[:-3], rest[-3:]
    length = qkv_ref.shape[0]
    size = pieces[0].shape[0]
    factor = HD**-0.5
    key_bias = bias_ref[...]
    for j, piece in enumerate(pieces):
        grad_ref[j * size : (j + 1) * size, :] = piece[...].astype(F32)
    for head in range(2):
        low, high = head * HD, (head + 1) * HD
        keys = qkv_ref[:, PAIR + low : PAIR + high]
        values = qkv_ref[:, 2 * PAIR + low : 2 * PAIR + high]
        key_grad = jnp.zeros((length, HD), F32)
        value_grad = jnp.zeros((length, HD), F32)
        for start, size in query_chunks(length):
            rows = slice(start, start + size)
            queries = qkv_ref[rows, low:high] * jnp.asarray(factor, BF)
            product = grad_ref[rows, low:high] * att_ref[rows, low:high]
            grads = grad_ref[rows, low:high].astype(BF)
            delta = jnp.sum(product.T, axis=0, keepdims=True)
            scores = dot(keys, queries, 1, 1) + key_bias
            probs = jnp.exp(scores - lse_ref[0, head : head + 1, rows])
            value_grad += dot(probs.astype(BF), grads, 1, 0)
            raw = (probs * (dot(values, grads, 1, 1) - delta)).astype(BF)
            key_grad += dot(raw, queries, 1, 0)
            query_grad = dot(keys, raw, 0, 0).T * factor
            out_ref[rows, low:high] = query_grad.astype(BF)
        out_ref[:, PAIR + low : PAIR + high] = key_grad.astype(BF)
        out_ref[:, 2 * PAIR + low : 2 * PAIR + high] = value_grad.astype(BF)
    sums_ref[0] = jnp.sum(out_ref[...].astype(F32), axis=0, keepdims=True)


def attend_back(qkv, key_bias, attended, lse, pieces):
    length, columns = qkv.shape
    pairs = columns // (3 * PAIR)
    size = pieces[0].shape[0]
    return pl.pallas_call(
        attend_back_kernel,
        grid=(pairs,),
        in_specs=[
            pl.BlockSpec((length, 3 * PAIR), lambda p: (0, p)),
            pl.BlockSpec((length, 1), lambda p: (0, 0)),
            pl.BlockSpec((length, PAIR), lambda p: (0, p)),
            pl.BlockSpec((1, 2, length), lambda p: (p, 0, 0)),
        ]
        + [pl.BlockSpec((size, PAIR), lambda p: (0, p))] * len(pieces),
        out_specs=[
            pl.BlockSpec((length, 3 * PAIR), lambda p: (0, p)),
            pl.BlockSpec((1, 1, 3 * PAIR), lambda p: (p, 0, 0)),
        ],
        out_shape=[shaped((length, columns), BF), shaped((pairs, 1, 3 * PAIR), F32)],
        scratch_shapes=[pltpu.VMEM((length, PAIR), F32)],
        compiler_params=PARAMS,
        cost_estimate=pl.CostEstimate(
            flops=pairs * 2 * 10 * length * length * 256,
            bytes_accessed=length * columns * 6,
            transcendentals=pairs * 2 * length * length,
        ),
        name="attend_back",
    )(qkv, key_bias, attended, lse, *pieces)


def middle_kernel(group, rows_ref, tokens_ref, *rest):
    parts, weights, (branch_ref, middle_ref, normed_ref, unit_ref, inv_ref) = (
        rest[:group], rest[group : 2 * group], rest[2 * group :]
    )
    branch = dot(parts[0][...], weights[0][...], 1, 1)
    for part, weight in zip(parts[1:], weights[1:]):
        branch = branch + dot(part[...], weight[...], 1, 1)
    branch = branch + rows_ref[4:5, :]
    branch_ref[...] = branch
    middle = tokens_ref[...].astype(F32) + rows_ref[5:6, :] * branch
    middle_ref[...] = middle
    unit, inverse = unit_rows(middle)
    unit_ref[...] = unit
    inv_ref[...] = inverse
    normed_ref[...] = (unit * rows_ref[6:7, :] + rows_ref[7:8, :]).astype(BF)


def middle_step(rows, tokens, parts, weights):
    length, width = tokens.shape
    group = len(parts)
    full = shaped((length, width), F32)
    return pl.pallas_call(
        lambda *refs: middle_kernel(group, *refs),
        in_specs=[VMEM] * (2 + 2 * group),
        out_specs=[VMEM] * 5,
        out_shape=[full, full, shaped((length, width), BF), full, shaped((length, 1), F32)],
        compiler_params=PARAMS,
        cost_estimate=pl.CostEstimate(
            flops=2 * length * width * width, bytes_accessed=8_000_000, transcendentals=0
        ),
        name="middle",
    )(rows, tokens, *parts, *weights)


def turn_kernel(group, terms, rows_ref, live_ref, cot_ref, unit_ref, inv_ref, branch_ref, *rest):
    backs, weights, outs = rest[:terms], rest[terms : terms + group], rest[terms + group :]
    middle_ref, grad_ref, sums_ref = outs[:3]
    norm_grad = backs[0][...].astype(F32)
    for ref in backs[1:]:
        norm_grad = norm_grad + ref[...].astype(F32)
    unit = unit_ref[...]
    out_grad = cot_ref[...].astype(F32) * live_ref[...]
    middle = out_grad + norm_back(norm_grad, unit, inv_ref[...], rows_ref[6:7, :])
    middle_ref[...] = middle
    low = (middle * rows_ref[5:6, :]).astype(BF)
    grad_ref[...] = low
    sums_ref[...] = jnp.zeros(sums_ref.shape, F32)
    sums_ref[0:1, :] = jnp.sum(low.astype(F32), axis=0, keepdims=True)
    sums_ref[1:2, :] = jnp.sum(middle * branch_ref[...], axis=0, keepdims=True)
    sums_ref[2:3, :] = jnp.sum(norm_grad * unit, axis=0, keepdims=True)
    sums_ref[3:4, :] = jnp.sum(norm_grad, axis=0, keepdims=True)
    for out, weight in zip(outs[3:], weights):
        out[...] = dot(low, weight[...], 1, 0).astype(BF)


def turn(rows, live, cotangent, unit, inverse, branch, backs, weights):
    length, width = cotangent.shape
    part = weights[0].shape[1]
    group = len(weights)
    return pl.pallas_call(
        lambda *refs: turn_kernel(group, len(backs), *refs),
        in_specs=[VMEM] * (6 + len(backs) + group),
        out_specs=[VMEM] * (3 + group),
        out_shape=[shaped((length, width), F32), shaped((length, width), BF), shaped((8, width), F32)]
        + [shaped((length, part), BF)] * group,
        compiler_params=PARAMS,
        cost_estimate=pl.CostEstimate(
            flops=2 * length * width * width, bytes_accessed=10_000_000, transcendentals=0
        ),
        name="turn",
    )(rows, live, cotangent, unit, inverse, branch, *backs, *weights)


def proj_weights_kernel(grad_ref, *rest):
    half = len(rest) // 2
    for part, out in zip(rest[:half], rest[half:]):
        out[...] = dot(grad_ref[...], part[...], 0, 0).astype(BF)


def proj_weights(grads, parts):
    length, width = grads.shape
    part = parts[0].shape[1]
    return pl.pallas_call(
        proj_weights_kernel,
        in_specs=[VMEM] * (1 + len(parts)),
        out_specs=[VMEM] * len(parts),
        out_shape=[shaped((width, part), BF)] * len(parts),
        compiler_params=PARAMS,
        cost_estimate=pl.CostEstimate(
            flops=2 * length * width * width, bytes_accessed=4_000_000, transcendentals=0
        ),
        name="proj_weights",
    )(grads, *parts)


def mlp_kernel(count, rows_ref, *rest):
    normed_in, cots, lives = rest[:count], rest[count : 2 * count], rest[2 * count : 3 * count]
    fc1_ref, fc2_ref, bias_ref = rest[3 * count : 3 * count + 3]
    backs = rest[3 * count + 3 : 4 * count + 3]
    normed_ref, grad_ref, act_ref, pre_ref, sums_ref, fbias_ref, back_acc = rest[4 * count + 3 :]
    step = pl.program_id(0)
    size = cots[0].shape[0]

    @pl.when(step == 0)
    def _():
        normed_ref[...] = jnp.concatenate([ref[...].astype(F32) for ref in normed_in]).astype(BF)
        scale = rows_ref[9:10, :]
        grads = [cot[...].astype(F32) * live[...] * scale for cot, live in zip(cots, lives)]
        grad_ref[...] = jnp.concatenate(grads).astype(BF)
        fbias_ref[...] = jnp.sum(grads[0].astype(BF).astype(F32), axis=0, keepdims=True)

    chunk = fc1_ref.shape[1] // 2
    for cols in (slice(0, chunk), slice(chunk, 2 * chunk)):
        pre = dot(normed_ref[...], fc1_ref[:, cols], 1, 0) + bias_ref[:, cols]
        act_grad = dot(grad_ref[...], fc2_ref[:, cols], 1, 0)
        cdf = 0.5 * (1.0 + lax.erf(pre * SQRT_HALF))
        act_ref[:, cols] = (pre * cdf).astype(BF)
        slope = cdf + pre * (jnp.exp(-0.5 * pre * pre) * INV_ROOT_TWO_PI)
        pre_grad = (act_grad * slope).astype(BF)
        pre_ref[:, cols] = pre_grad
        sums_ref[:, cols] = jnp.sum(pre_grad.astype(F32), axis=0, keepdims=True)
    back = dot(pre_ref[...], fc1_ref[...], 1, 1)

    @pl.when(step == 0)
    def _():
        back_acc[...] = back

    @pl.when(step == pl.num_programs(0) - 1)
    def _():
        whole = back_acc[...] + back
        for j, ref in enumerate(backs):
            ref[...] = whole[j * size : (j + 1) * size].astype(BF)


def mlp(rows, normed, cots, lives, weights, bias):
    size, width = normed[0].shape
    count = len(normed)
    length = count * size
    hidden = weights.shape[1] // 2
    step = hidden // 2

    def whole(*shape):
        return pl.BlockSpec(shape, lambda i: (0, 0))

    cols = pl.BlockSpec((length, step), lambda i: (0, i))
    return pl.pallas_call(
        lambda *refs: mlp_kernel(count, *refs),
        grid=(2,),
        in_specs=[whole(*rows.shape)]
        + [whole(size, width)] * (2 * count)
        + [whole(size, 1)] * count
        + [
            pl.BlockSpec((width, step), lambda i: (0, i)),
            pl.BlockSpec((width, step), lambda i: (0, 2 + i)),
            pl.BlockSpec((1, step), lambda i: (0, i)),
        ],
        out_specs=[whole(size, width)] * count
        + [whole(length, width)] * 2
        + [cols, cols, pl.BlockSpec((1, step), lambda i: (0, i)), whole(1, width)],
        out_shape=[shaped((size, width), BF)] * count
        + [shaped((length, width), BF)] * 2
        + [shaped((length, hidden), BF)] * 2
        + [shaped((1, hidden), F32), shaped((1, width), F32)],
        scratch_shapes=[pltpu.VMEM((length, width), F32)],
        compiler_params=PARAMS,
        cost_estimate=pl.CostEstimate(
            flops=6 * length * width * hidden,
            bytes_accessed=12_000_000,
            transcendentals=2 * length * hidden,
        ),
        name="mlp",
    )(rows, *normed, *cots, *lives, weights, weights, bias)


def mlp_weights_kernel(
    norm_a, norm_b, grad_a, grad_b, fc2_ref, pre_a, pre_b, act_a, act_b, out_ref, *branches
):
    hidden = pre_a.shape[1]
    first = dot(norm_a[...], pre_a[...], 0, 0) + dot(norm_b[...], pre_b[...], 0, 0)
    out_ref[:, :hidden] = first.astype(BF)
    second = dot(grad_a[...], act_a[...], 0, 0) + dot(grad_b[...], act_b[...], 0, 0)
    out_ref[:, hidden:] = second.astype(BF)
    count = len(branches) // 2
    size = branches[0].shape[0]
    for half, act in enumerate((act_a, act_b)):
        branch = dot(act[...], fc2_ref[...], 1, 1)
        for j in range(count):
            branches[half * count + j][...] = branch[j * size : (j + 1) * size].astype(BF)


def mlp_weights(normed, grads, pres, acts, weights, group):
    length, width = normed[0].shape
    hidden = pres[0].shape[1]
    size = 2 * length // group
    step = 256
    cols = pl.BlockSpec((length, step), lambda i: (0, i))
    whole = pl.BlockSpec((length, hidden), lambda i: (0, 0))
    return pl.pallas_call(
        mlp_weights_kernel,
        grid=(width // step,),
        in_specs=[cols] * 4 + [pl.BlockSpec((step, hidden), lambda i: (i, 1))] + [whole] * 4,
        out_specs=[pl.BlockSpec((step, 2 * hidden), lambda i: (i, 0))]
        + [pl.BlockSpec((size, step), lambda i: (0, i))] * group,
        out_shape=[shaped((width, 2 * hidden), BF)] + [shaped((size, width), BF)] * group,
        compiler_params=PARAMS,
        cost_estimate=pl.CostEstimate(
            flops=12 * length * width * hidden, bytes_accessed=20_000_000, transcendentals=0
        ),
        name="mlp_weights",
    )(*normed, *grads, weights, *pres, *acts)


def finish_kernel(rows_ref, live_ref, cot_ref, middle_ref, *rest):
    terms, (out_ref, sums_ref) = rest[:-2], rest[-2:]
    branch = terms[0][...].astype(F32)
    for ref in terms[1:]:
        branch = branch + ref[...].astype(F32)
    branch = branch + rows_ref[8:9, :]
    out_ref[...] = (middle_ref[...] + rows_ref[9:10, :] * branch).astype(BF)
    grads = cot_ref[...].astype(F32) * live_ref[...]
    sums_ref[...] = jnp.sum(grads * branch, axis=0, keepdims=True)


def finish(rows, live, cotangent, middle, terms):
    length, width = cotangent.shape
    return pl.pallas_call(
        finish_kernel,
        in_specs=[VMEM] * (4 + len(terms)),
        out_specs=[VMEM] * 2,
        out_shape=[shaped((length, width), BF), shaped((1, width), F32)],
        compiler_params=PARAMS,
        name="finish",
    )(rows, live, cotangent, middle, *terms)


def begin_kernel(rows_ref, tokens_ref, mean_ref, inv_ref, middle_ref, *rest):
    terms, out_ref = rest[:-1], rest[-1]
    grads = terms[0][...].astype(F32)
    for ref in terms[1:]:
        grads = grads + ref[...].astype(F32)
    inverse = inv_ref[...]
    unit = (tokens_ref[...].astype(F32) - mean_ref[...]) * inverse
    out_ref[...] = (middle_ref[...] + norm_back(grads, unit, inverse, rows_ref[0:1, :])).astype(BF)


def begin(rows, tokens, mean, inverse, middle_grad, terms):
    length, width = tokens.shape
    column = pl.BlockSpec((length, 1), lambda i: (0, 0))
    whole = pl.BlockSpec((length, width), lambda i: (0, 0))
    return pl.pallas_call(
        begin_kernel,
        grid=(1,),
        in_specs=[pl.BlockSpec(rows.shape, lambda i: (0, 0)), whole, column, column, whole]
        + [whole] * len(terms),
        out_specs=whole,
        out_shape=shaped((length, width), BF),
        compiler_params=PARAMS,
        name="begin",
    )(rows, tokens, mean, inverse, middle_grad, *terms)


def qkv_back_kernel(group, grad_ref, weight_ref, mean_ref, inv_ref, *rest):
    tokens, outs, sums_ref = rest[:group], rest[group:-1], rest[-1]
    size = tokens[0].shape[0]
    gain = shift = 0.0
    for first in range(0, group, 2):
        span = slice(first * size, (first + 2) * size)
        part = dot(grad_ref[span, :], weight_ref[...], 1, 1)
        inputs = jnp.concatenate([tokens[first][...].astype(F32), tokens[first + 1][...].astype(F32)])
        unit = (inputs - mean_ref[span, :]) * inv_ref[span, :]
        outs[first][...] = part[:size].astype(BF)
        outs[first + 1][...] = part[size:].astype(BF)
        gain = gain + jnp.sum(part * unit, axis=0, keepdims=True)
        shift = shift + jnp.sum(part, axis=0, keepdims=True)
    sums_ref[...] = jnp.zeros(sums_ref.shape, F32)
    sums_ref[0:1, :] = gain
    sums_ref[1:2, :] = shift


def qkv_back(qkv_grad, weight, tokens, mean, inverse):
    size, width = tokens[0].shape
    group = len(tokens)
    return pl.pallas_call(
        lambda *refs: qkv_back_kernel(group, *refs),
        in_specs=[VMEM] * (4 + group),
        out_specs=[VMEM] * (group + 1),
        out_shape=[shaped((size, width), BF)] * group + [shaped((8, width), F32)],
        compiler_params=PARAMS,
        cost_estimate=pl.CostEstimate(
            flops=2 * group * size * width * qkv_grad.shape[1],
            bytes_accessed=10_000_000,
            transcendentals=0,
        ),
        name="qkv_back",
    )(qkv_grad, weight, mean, inverse, *tokens)


def attn_weights_kernel(
    direct, shard, terms, ids_ref, normed_ref, grad_ref, norm1_ref, sums_ref, turn_ref, fbias_ref,
    scale2_ref, bias_a_ref, bias_b_ref, *rest,
):
    projs, outs = rest[:terms], rest[terms:-4]
    rows_ref, turned_ref, block_ref, small_ref = rest[-4:]
    place, row = ids_ref[0], ids_ref[1]
    width = normed_ref.shape[1]
    part = projs[0].shape[1]
    rows_ref[...] = jnp.zeros(rows_ref.shape, F32)
    rows_ref[0:2, :] = norm1_ref[0:2, :]
    for pair in range(part // PAIR):
        where = lanes(place * part + pair * PAIR, PAIR)
        rows_ref[2:3, where] = sums_ref[pair, :, :PAIR]
        rows_ref[3:4, where] = sums_ref[pair, :, 2 * PAIR :]
    rows_ref[4:8, :] = turn_ref[0:4, :]
    rows_ref[8:9, :] = fbias_ref[...]
    rows_ref[9:10, :] = scale2_ref[...]
    cols = bias_a_ref.shape[1] // part
    for owner in range(part // shard):
        for line in range(cols):
            spot = (owner * cols + line) * shard
            small_ref[line : line + 1, owner * shard : (owner + 1) * shard] = (
                bias_a_ref[0:1, spot : spot + shard] + bias_b_ref[0:1, spot : spot + shard]
            )
    rows_ref[10 : 10 + cols, lanes(place * part, part)] = small_ref[0:cols, :]
    turned_ref[...] = rows_ref[...].T
    step = block_ref.shape[0]
    for k in range(width // step):
        start = pl.multiple_of(((row >> 1) ^ k) * step, step) if direct else k * step
        cols = pl.ds(start, step)
        block_ref[:, : 3 * part] = dot(normed_ref[:, cols], grad_ref[...], 0, 0)
        proj = projs[0][cols, :].astype(F32)
        for ref in projs[1:]:
            proj = proj + ref[cols, :].astype(F32)
        block_ref[:, 3 * part : 4 * part] = proj
        block_ref[:, 4 * part :] = turned_ref[cols, :]
        if direct:
            size = step // 2
            side = row & 1
            outs[2 * k][...] = block_ref[pl.ds(pl.multiple_of(side * size, size), size), :].astype(BF)
            outs[2 * k + 1][...] = block_ref[
                pl.ds(pl.multiple_of((1 - side) * size, size), size), :
            ].astype(BF)
        else:
            outs[0][k * step : (k + 1) * step, :] = block_ref[...].astype(BF)


def attn_weights(ids, normed1, qkv_grad, sums, projs, blocks, shard):
    length, width = normed1.shape
    part = projs[0].shape[1]
    columns = 4 * part + EXTRA
    direct = blocks > 0
    step = 2 * (width // blocks) if direct else 256
    out_shape = [shaped((width // blocks, columns), BF)] * blocks if direct else [
        shaped((width, columns), BF)
    ]
    return pl.pallas_call(
        lambda *refs: attn_weights_kernel(direct, shard, len(projs), *refs),
        in_specs=[SMEM] + [VMEM] * (2 + len(sums) + len(projs)),
        out_specs=[VMEM] * len(out_shape),
        out_shape=out_shape,
        scratch_shapes=[
            pltpu.VMEM((EXTRA, width), F32),
            pltpu.VMEM((width, EXTRA), F32),
            pltpu.VMEM((step, columns), F32),
            pltpu.VMEM((8, part), F32),
        ],
        compiler_params=PARAMS,
        cost_estimate=pl.CostEstimate(
            flops=6 * length * width * part, bytes_accessed=12_000_000, transcendentals=0
        ),
        name="attn_weights",
    )(ids, normed1, qkv_grad, *sums, *projs)


def total(ids, terms, group):
    size, columns = terms[0].shape
    rows = size // group

    def kernel(ids_ref, *refs):
        ins, outs, sum_ref = refs[: len(terms)], refs[len(terms) : -1], refs[-1]
        value = ins[0][...].astype(F32)
        for ref in ins[1:]:
            value = value + ref[...].astype(F32)
        sum_ref[...] = value
        for k, out in enumerate(outs):
            start = pl.multiple_of((ids_ref[0] ^ k) * rows, rows)
            out[...] = sum_ref[pl.ds(start, rows), :].astype(BF)

    return pl.pallas_call(
        kernel,
        in_specs=[SMEM] + [VMEM] * len(terms),
        out_specs=[VMEM] * group,
        out_shape=[shaped((rows, columns), BF)] * group,
        scratch_shapes=[pltpu.VMEM((size, columns), F32)],
        compiler_params=PARAMS,
        name="total",
    )(ids, *terms)


def place_attn_kernel(ids_ref, *refs):
    group = len(refs) - 3
    blocks, (qkv_ref, proj_ref, extra_ref) = refs[:group], refs[group:]
    width = proj_ref.shape[1]
    part = width // group
    extra = jnp.zeros(extra_ref.shape[::-1], F32)
    for k, block in enumerate(blocks):
        source = ids_ref[0] ^ k
        for third in range(3):
            for pair in range(part // PAIR):
                spot = (pair * 3 + third) * PAIR
                where = lanes(third * width + source * part + pair * PAIR, PAIR)
                qkv_ref[:, where] = block[:, spot : spot + PAIR].astype(F32)
        proj_ref[:, lanes(source * part, part)] = block[:, 3 * part : 4 * part].astype(F32)
        extra = extra + block[:, 4 * part :].astype(F32)
    extra_ref[...] = extra.T


def place_attn(ids, blocks, width):
    rows = blocks[0].shape[0]
    return pl.pallas_call(
        place_attn_kernel,
        in_specs=[SMEM] + [VMEM] * len(blocks),
        out_specs=[VMEM] * 3,
        out_shape=[
            shaped((rows, 3 * width), F32),
            shaped((rows, width), F32),
            shaped((EXTRA, rows), F32),
        ],
        compiler_params=PARAMS,
        name="place_attn",
    )(ids, *blocks)


def place_mlp_kernel(ids_ref, *refs):
    group = len(refs) - 2
    blocks, (fc1_ref, fc2_ref) = refs[:group], refs[group:]
    part = fc1_ref.shape[1] // group
    for k, block in enumerate(blocks):
        where = lanes((ids_ref[0] ^ k) * part, part)
        fc1_ref[:, where] = block[:, :part].astype(F32)
        fc2_ref[:, where] = block[:, part:].astype(F32)


def place_mlp(ids, blocks, hidden):
    rows = blocks[0].shape[0]
    return pl.pallas_call(
        place_mlp_kernel,
        in_specs=[SMEM] + [VMEM] * len(blocks),
        out_specs=[VMEM] * 2,
        out_shape=[shaped((rows, hidden), F32)] * 2,
        compiler_params=PARAMS,
        name="place_mlp",
    )(ids, *blocks)


def local(tokens, counts, w_qkv, w_proj, w_fc1, fc1_bias, w_fc2, vectors, cotangent):
    _, capacity, width = tokens.shape
    hidden = w_fc1.shape[1]
    rows = w_qkv.shape[0]
    group, replicas = lax.axis_size("ctx"), lax.axis_size("dp")
    place, replica = lax.axis_index("ctx"), lax.axis_index("dp")
    ids = jnp.stack([place, replica]).astype(jnp.int32)
    head_width = width // group
    hidden_part = hidden // group
    bias_cols = hidden // width
    vector_count = vectors.shape[0]
    direct = replicas <= 8

    def swap(value, bit, axis="ctx"):
        size = group if axis == "ctx" else replicas
        return lax.ppermute(value, axis, [(i, i ^ bit) for i in range(size)])

    def after(value, *before):
        return lax.optimization_barrier((value,) + before)[0]

    def gather(own, *before):
        pieces = [own]
        for j in range(1, group):
            bit = j & -j
            source = pieces[j ^ bit]
            pieces.append(swap(after(source, *before) if j ^ bit else source, bit))
        return pieces

    def scatter(parts, *before, mids=None):
        pieces = {j: [part] for j, part in enumerate(parts)}

        def added(terms):
            if len(terms) == 1:
                return terms[0]
            return sum(term.astype(F32) for term in terms).astype(BF)

        bit = 1
        while bit < group:
            for j in sorted((j for j in pieces if j & bit), reverse=True):
                value = added(pieces.pop(j))
                if bit > 1:
                    if mids is not None:
                        mids.append(value)
                    value = after(value, *before)
                pieces[j ^ bit].append(swap(value, bit))
            bit *= 2
        return pieces[0]

    def split(whole):
        return [whole[j * capacity : (j + 1) * capacity] for j in range(whole.shape[0] // capacity)]

    def exchange(relative):
        return [relative[0]] + [swap(relative[k], k) for k in range(1, group)]

    def in_order(relative):
        stacked = jnp.stack(relative)
        return jnp.concatenate(
            [lax.dynamic_index_in_dim(stacked, place ^ s, 0, False) for s in range(group)], axis=0
        )

    cuts = cut(
        ids, counts, w_qkv, w_proj.T, w_fc1, w_fc2.T, vectors, fc1_bias.reshape(bias_cols, rows), group
    )
    first = exchange(cuts[:group])
    tokens_far = swap(after(tokens[0], *first), group // 2)
    if direct:
        shards = {0: jnp.concatenate(first, axis=0)}
        for m in range(replicas - 2, 0, -2):
            shards[m] = swap(shards[0], m, "dp")
        shards[1] = swap(shards[0], 1, "dp")
        arrived = [tokens_far] + [shards[m] for m in sorted(shards) if m]
        for m in range(3, replicas, 2):
            shards[m] = swap(after(shards[m - 1], *arrived), 1, "dp")
        first_pieces = [shards[m] for m in range(replicas)]
    else:
        first_pieces = [lax.all_gather(in_order(first), "dp", axis=0, tiled=True)]
        arrived = [tokens_far]
    tokens_pieces = [tokens[0]]
    for j in range(1, group):
        source = tokens_pieces[j ^ (j & -j)]
        if j == group // 2:
            tokens_pieces.append(tokens_far)
        else:
            tokens_pieces.append(swap(after(source, *arrived), j & -j))
    second = exchange([after(block, *arrived) for block in cuts[group:]])
    second_shard = in_order(second)
    second_all = lax.all_gather(second_shard, "dp", axis=0, tiled=True)

    count_column = 4 * head_width + vector_count + bias_cols
    live = []
    for block in first:
        piece = block[0, count_column : count_column + 2].astype(F32)
        bound = piece[0] * 128.0 + piece[1]
        slot = lax.broadcasted_iota(jnp.int32, (capacity, 1), 0).astype(F32)
        live.append((slot < bound).astype(F32))
    key_bias = jnp.where(jnp.concatenate(live, axis=0) > 0.0, 0.0, MASKED_SCORE).astype(F32)

    tokens_own = after(tokens[0], second_shard)
    (
        weight_qkv, weight_proj, vector_rows, normed1, qkv, mean1, inverse1, bias_fc1
    ) = project(
        ids, [tokens_own] + tokens_pieces[1:], first_pieces, hidden_part, 0 if direct else rows
    )

    cotangent_pieces = gather(after(cotangent[0], *second, *first_pieces), qkv)
    attended, attended_low, lse = attend(qkv, key_bias)
    projs = gather(weight_proj, attended_low)
    attended_own = exchange(split(attended_low))
    branch1, middle, normed2_own, unit2, inverse2 = middle_step(
        vector_rows, tokens[0], attended_own, projs
    )
    normed2 = gather(normed2_own)
    half = group // 2

    def feed(where, bias):
        return mlp(
            vector_rows, normed2[where], cotangent_pieces[where], live[where], second_all, bias
        )

    *backs_near, norm_near, grad_near, act_near, pre_near, sums_near, fbias = feed(
        slice(0, half), bias_fc1
    )
    *backs_far, norm_far, grad_far, act_far, pre_far, sums_far, _ = feed(
        slice(half, group), after(bias_fc1, sums_near)
    )
    mids = []
    norm2_terms = scatter(backs_near + backs_far, mids=mids)
    grad_mlp, *branches = mlp_weights(
        [norm_near, norm_far], [grad_near, grad_far], [after(pre_near, *mids), pre_far],
        [act_near, act_far], second_all, group,
    )
    owned_mlp = lax.psum_scatter(grad_mlp, "dp", scatter_dimension=0, tiled=True)

    middle_grad, branch_grad, turn_sums, *att_grads = turn(
        vector_rows, live[0], cotangent[0], unit2, inverse2, branch1, norm2_terms, projs
    )
    att_grads = exchange(att_grads)
    mids = []
    proj_terms = scatter(proj_weights(branch_grad, attended_own), mids=mids)
    branch2_terms = scatter(branches, *att_grads, mids=mids)
    qkv_grad, qkv_sums = attend_back(qkv, key_bias, attended, after(lse, *mids), att_grads)
    *norm1_parts, norm1_sums = qkv_back(qkv_grad, weight_qkv, tokens_pieces, mean1, inverse1)
    output, grad_scale2 = finish(vector_rows, live[0], cotangent[0], middle, branch2_terms)
    parts = attn_weights(
        ids, normed1, qkv_grad,
        [norm1_sums, qkv_sums, turn_sums, fbias, grad_scale2, sums_near, sums_far],
        proj_terms, replicas if direct else 0, rows,
    )
    if direct:
        terms, last = [], []
        for k in list(range(replicas // 2 - 1, -1, -1)):
            other = swap(after(parts[2 * k + 1], *last), 1, "dp")
            if k == 0:
                terms += [parts[0], other]
            else:
                summed = (parts[2 * k].astype(F32) + other.astype(F32)).astype(BF)
                terms.append(swap(summed, 2 * k, "dp"))
            last = [other]
        cuts_mlp = total(ids, [owned_mlp], group)
    else:
        owned_attn = lax.psum_scatter(parts[0], "dp", scatter_dimension=0, tiled=True)

        def relative(owned):
            blocks = owned.reshape(group, rows, -1)
            return [lax.dynamic_index_in_dim(blocks, place ^ k, 0, False) for k in range(group)]

        cuts_mlp = relative(owned_mlp)
    out_fc1, out_fc2 = place_mlp(ids, exchange(cuts_mlp), hidden)
    if direct:
        cuts_attn = total(after(ids, out_fc1), terms, group)
    else:
        cuts_attn = relative(owned_attn)
    input_grad = begin(
        vector_rows, tokens[0], mean1, inverse1, middle_grad, scatter(norm1_parts)
    )

    out_qkv, out_proj, out_extra = place_attn(ids, exchange(cuts_attn), width)
    return (
        output[None],
        input_grad[None],
        out_qkv,
        out_proj.T,
        out_fc1,
        out_extra[vector_count : vector_count + bias_cols].reshape(-1),
        out_fc2.T,
        out_extra[:vector_count],
    )


def solution(mesh):
    both = ("dp", "ctx")
    in_specs = (
        P("dp", "ctx", None),
        P("dp", "ctx"),
        P(both, None),
        P(None, both),
        P(both, None),
        P(both),
        P(None, both),
        P(None, both),
        P("dp", "ctx", None),
    )
    out_specs = (
        P("dp", "ctx", None),
        P("dp", "ctx", None),
        P(both, None),
        P(None, both),
        P(both, None),
        P(both),
        P(None, both),
        P(None, both),
    )
    return jax.shard_map(local, mesh=mesh, in_specs=in_specs, out_specs=out_specs, check_vma=False)
```

```python
import jax
import jax.numpy as jnp
from jax import lax
from jax.experimental import pallas as pl
from jax.experimental.pallas import tpu as pltpu
from jax.sharding import PartitionSpec as P

HD = 64
PAIR = 2 * HD
EXTRA = 128
EPSILON = 1e-06
MASKED_SCORE = -1e30
SQRT_HALF = 0.7071067811865476
INV_ROOT_TWO_PI = 0.3989422804014327
BF = jnp.bfloat16
F32 = jnp.float32
PARAMS = pltpu.CompilerParams(vmem_limit_bytes=60 * 1024 * 1024)
VMEM = pl.BlockSpec(memory_space=pltpu.VMEM)
SMEM = pl.BlockSpec(memory_space=pltpu.SMEM)


def shaped(shape, dtype):
    return jax.ShapeDtypeStruct(shape, dtype)


def dot(left, right, left_dim, right_dim):
    return lax.dot_general(
        left, right, (((left_dim,), (right_dim,)), ((), ())), preferred_element_type=F32
    )


def lanes(start, size):
    return pl.ds(pl.multiple_of(start, 128), size)


def unit_rows(inputs):
    centered = inputs - jnp.mean(inputs, axis=-1, keepdims=True)
    spread = jnp.mean(centered * centered, axis=-1, keepdims=True)
    inverse = lax.rsqrt(spread + EPSILON)
    return (centered * inverse, inverse)


def norm_back(grad_in, unit, inverse, gain):
    scaled = grad_in * gain
    inner = (
        scaled
        - jnp.mean(scaled, axis=-1, keepdims=True)
        - unit * jnp.mean(scaled * unit, axis=-1, keepdims=True)
    )
    return inner * inverse


def cut_kernel(ids_ref, count_ref, qkv_ref, proj_ref, fc1_ref, fc2_ref, vec_ref, bias_ref, *rest):
    outs, extra_ref = rest[:-1], rest[-1]
    group = len(outs) // 2
    place = ids_ref[0]
    width = proj_ref.shape[1]
    part = width // group
    hidden_part = fc1_ref.shape[1] // group
    vector_count, bias_cols = vec_ref.shape[0], bias_ref.shape[0]
    column = vector_count + bias_cols
    lane = lax.broadcasted_iota(jnp.int32, extra_ref.shape, 1)
    count = count_ref[0, 0]
    high = (count >> 7).astype(F32)
    low = (count & 127).astype(F32)
    extra_ref[...] = jnp.where(lane == column, high, jnp.where(lane == column + 1, low, 0.0))
    extra_ref[:, :vector_count] = vec_ref[...].astype(F32).T
    extra_ref[:, vector_count:column] = bias_ref[...].astype(F32).T
    extra = extra_ref[...].astype(BF)
    for k in range(group):
        target = place ^ k
        first, second = outs[k], outs[group + k]
        for third in range(3):
            for pair in range(part // PAIR):
                spot = (pair * 3 + third) * PAIR
                first[:, spot : spot + PAIR] = qkv_ref[
                    :, lanes(third * width + target * part + pair * PAIR, PAIR)
                ]
        first[:, 3 * part : 4 * part] = proj_ref[:, lanes(target * part, part)]
        first[:, 4 * part :] = extra
        second[:, :hidden_part] = fc1_ref[:, lanes(target * hidden_part, hidden_part)]
        second[:, hidden_part:] = fc2_ref[:, lanes(target * hidden_part, hidden_part)]


def cut(ids, counts, w_qkv, w_proj_t, w_fc1, w_fc2_t, vectors, bias, group):
    rows, width = w_proj_t.shape
    part, hidden_part = width // group, w_fc1.shape[1] // group
    return pl.pallas_call(
        cut_kernel,
        in_specs=[SMEM, SMEM] + [VMEM] * 6,
        out_specs=[VMEM] * (2 * group),
        out_shape=[shaped((rows, 4 * part + EXTRA), BF)] * group
        + [shaped((rows, 2 * hidden_part), BF)] * group,
        scratch_shapes=[pltpu.VMEM((rows, EXTRA), F32)],
        compiler_params=PARAMS,
        name="cut",
    )(ids, counts, w_qkv, w_proj_t, w_fc1, w_fc2_t, vectors, bias)


def project_kernel(ordered, group, count_column, ids_ref, *rest):
    tokens, blocks, rest = rest[:group], rest[group : 2 * group], rest[2 * group :]
    pieces, outs, lives, scratch = (
        rest[: -12 - group], rest[-12 - group : -3 - group], rest[-3 - group : -3], rest[-3:]
    )
    qkv_w, proj_w, rows_ref, normed_ref, out_ref, mean_ref, inv_ref, fc1_ref, key_ref = outs
    extra_ref, bias_ref, small_ref = scratch
    place, row = ids_ref[0], ids_ref[1]
    capacity, width = tokens[0].shape
    part = proj_w.shape[1]
    size = pieces[0].shape[0]

    def lay(block, start, count):
        where = pl.ds(start, count)
        qkv_w[where, :] = block[:, : 3 * part]
        proj_w[where, :] = block[:, 3 * part : 4 * part]
        extra_ref[where, :] = block[:, 4 * part :].astype(F32)

    if ordered:
        lay(pieces[0], 0, size)
        shard = ordered
    else:
        sub = shard = size // group
        for m, piece in enumerate(pieces):
            for j in range(group):
                start = (row ^ m) * size + (place ^ j) * sub
                lay(piece.at[j * sub : (j + 1) * sub], pl.multiple_of(start, sub), sub)
    slot = lax.broadcasted_iota(jnp.int32, (capacity, 1), 0).astype(F32)
    for j, (block, live_ref) in enumerate(zip(blocks, lives)):
        extra = block[:, 4 * part :].astype(F32)[0:1, :]
        bound = extra[:, count_column : count_column + 1] * 128.0
        bound = bound + extra[:, count_column + 1 : count_column + 2]
        live = jnp.where(slot < bound, 1.0, 0.0)
        live_ref[...] = live
        key_ref[j * capacity : (j + 1) * capacity, :] = (1.0 - live) * MASKED_SCORE
    turned = extra_ref[...].T
    rows_ref[...] = turned[: rows_ref.shape[0]]
    bias_ref[...] = jnp.zeros(bias_ref.shape, F32)
    for pair in range(part // PAIR):
        for third, line in ((0, 2), (2, 3)):
            spot = (pair * 3 + third) * PAIR
            bias_ref[0:1, spot : spot + PAIR] = rows_ref[
                line : line + 1, lanes(place * part + pair * PAIR, PAIR)
            ]
    cols = fc1_ref.shape[1] // part
    small_ref[0:cols, :] = rows_ref[10 : 10 + cols, lanes(place * part, part)]
    for owner in range(part // shard):
        for line in range(cols):
            spot = (owner * cols + line) * shard
            fc1_ref[0:1, spot : spot + shard] = small_ref[
                line : line + 1, owner * shard : (owner + 1) * shard
            ]
    gain, shift, bias = rows_ref[0:1, :], rows_ref[1:2, :], bias_ref[0:1, :]
    for first in range(0, group, 2):
        span = slice(first * capacity, (first + 2) * capacity)
        inputs = jnp.concatenate([tokens[first][...].astype(F32), tokens[first + 1][...].astype(F32)])
        mean = jnp.mean(inputs, axis=-1, keepdims=True)
        centered = inputs - mean
        inverse = lax.rsqrt(jnp.mean(centered * centered, axis=-1, keepdims=True) + EPSILON)
        normed = (centered * inverse * gain + shift).astype(BF)
        normed_ref[span, :] = normed
        mean_ref[span, :] = mean
        inv_ref[span, :] = inverse
        out_ref[span, :] = (dot(normed, qkv_w[...], 1, 0) + bias).astype(BF)


def project(ids, tokens, blocks, pieces, hidden_part, count_column, ordered):
    capacity, width = tokens[0].shape
    group = len(tokens)
    length = group * capacity
    part = width // group
    return pl.pallas_call(
        lambda *refs: project_kernel(ordered, group, count_column, *refs),
        in_specs=[SMEM] + [VMEM] * (2 * group + len(pieces)),
        out_specs=[VMEM] * (9 + group),
        out_shape=[
            shaped((width, 3 * part), BF),
            shaped((width, part), BF),
            shaped((16, width), F32),
            shaped((length, width), BF),
            shaped((length, 3 * part), BF),
            shaped((length, 1), F32),
            shaped((length, 1), F32),
            shaped((1, hidden_part), F32),
            shaped((length, 1), F32),
        ]
        + [shaped((capacity, 1), F32)] * group,
        scratch_shapes=[
            pltpu.VMEM((width, EXTRA), F32),
            pltpu.VMEM((8, 3 * part), F32),
            pltpu.VMEM((8, part), F32),
        ],
        compiler_params=PARAMS,
        cost_estimate=pl.CostEstimate(
            flops=6 * length * width * part, bytes_accessed=12_000_000, transcendentals=0
        ),
        name="project",
    )(ids, *tokens, *blocks, *pieces)


def query_chunks(length):
    step = 512
    return [(start, min(step, length - start)) for start in range(0, length, step)]


def attend_kernel(qkv_ref, bias_ref, out_ref, lse_ref, *lows):
    length = qkv_ref.shape[0]
    key_bias = bias_ref[...]
    for head in range(2):
        keys = qkv_ref[:, PAIR + head * HD : PAIR + (head + 1) * HD]
        values = qkv_ref[:, 2 * PAIR + head * HD : 2 * PAIR + (head + 1) * HD]
        for start, size in query_chunks(length):
            queries = qkv_ref[start : start + size, head * HD : (head + 1) * HD]
            queries = queries * jnp.asarray(HD**-0.5, BF)
            scores = dot(keys, queries, 1, 1) + key_bias
            top = jnp.max(scores, axis=0, keepdims=True)
            expo = jnp.exp(scores - top)
            total = jnp.sum(expo, axis=0, keepdims=True)
            mixed = (dot(values, expo.astype(BF), 0, 0) / total).T
            out_ref[start : start + size, head * HD : (head + 1) * HD] = mixed
            lse_ref[0, head : head + 1, start : start + size] = top + jnp.log(total)
    for j, low in enumerate(lows):
        size = low.shape[0]
        low[...] = out_ref[j * size : (j + 1) * size, :].astype(BF)


def attend(qkv, key_bias, group):
    length, columns = qkv.shape
    pairs = columns // (3 * PAIR)
    return pl.pallas_call(
        attend_kernel,
        grid=(pairs,),
        in_specs=[
            pl.BlockSpec((length, 3 * PAIR), lambda p: (0, p)),
            pl.BlockSpec((length, 1), lambda p: (0, 0)),
        ],
        out_specs=[
            pl.BlockSpec((length, PAIR), lambda p: (0, p)),
            pl.BlockSpec((1, 2, length), lambda p: (p, 0, 0)),
        ]
        + [pl.BlockSpec((length // group, PAIR), lambda p: (0, p))] * group,
        out_shape=[
            shaped((length, pairs * PAIR), F32),
            shaped((pairs, 2, length), F32),
        ]
        + [shaped((length // group, pairs * PAIR), BF)] * group,
        compiler_params=PARAMS,
        cost_estimate=pl.CostEstimate(
            flops=pairs * 2 * 4 * length * length * 256,
            bytes_accessed=length * columns * 4,
            transcendentals=pairs * 2 * length * length,
        ),
        name="attend",
    )(qkv, key_bias)


def attend_back_kernel(qkv_ref, bias_ref, att_ref, lse_ref, *rest):
    pieces, (out_ref, sums_ref, grad_ref) = rest[:-3], rest[-3:]
    length = qkv_ref.shape[0]
    size = pieces[0].shape[0]
    factor = HD**-0.5
    key_bias = bias_ref[...]
    for j, piece in enumerate(pieces):
        grad_ref[j * size : (j + 1) * size, :] = piece[...].astype(F32)
    for head in range(2):
        low, high = head * HD, (head + 1) * HD
        keys = qkv_ref[:, PAIR + low : PAIR + high]
        values = qkv_ref[:, 2 * PAIR + low : 2 * PAIR + high]
        key_grad = jnp.zeros((length, HD), F32)
        value_grad = jnp.zeros((length, HD), F32)
        for start, size in query_chunks(length):
            rows = slice(start, start + size)
            queries = qkv_ref[rows, low:high] * jnp.asarray(factor, BF)
            product = grad_ref[rows, low:high] * att_ref[rows, low:high]
            grads = grad_ref[rows, low:high].astype(BF)
            delta = jnp.sum(product.T, axis=0, keepdims=True)
            scores = dot(keys, queries, 1, 1) + key_bias
            probs = jnp.exp(scores - lse_ref[0, head : head + 1, rows])
            value_grad += dot(probs.astype(BF), grads, 1, 0)
            raw = (probs * (dot(values, grads, 1, 1) - delta)).astype(BF)
            key_grad += dot(raw, queries, 1, 0)
            query_grad = dot(keys, raw, 0, 0).T * factor
            out_ref[rows, low:high] = query_grad.astype(BF)
        out_ref[:, PAIR + low : PAIR + high] = key_grad.astype(BF)
        out_ref[:, 2 * PAIR + low : 2 * PAIR + high] = value_grad.astype(BF)
    sums_ref[0] = jnp.sum(out_ref[...].astype(F32), axis=0, keepdims=True)


def attend_back(qkv, key_bias, attended, lse, pieces):
    length, columns = qkv.shape
    pairs = columns // (3 * PAIR)
    size = pieces[0].shape[0]
    return pl.pallas_call(
        attend_back_kernel,
        grid=(pairs,),
        in_specs=[
            pl.BlockSpec((length, 3 * PAIR), lambda p: (0, p)),
            pl.BlockSpec((length, 1), lambda p: (0, 0)),
            pl.BlockSpec((length, PAIR), lambda p: (0, p)),
            pl.BlockSpec((1, 2, length), lambda p: (p, 0, 0)),
        ]
        + [pl.BlockSpec((size, PAIR), lambda p: (0, p))] * len(pieces),
        out_specs=[
            pl.BlockSpec((length, 3 * PAIR), lambda p: (0, p)),
            pl.BlockSpec((1, 1, 3 * PAIR), lambda p: (p, 0, 0)),
        ],
        out_shape=[shaped((length, columns), BF), shaped((pairs, 1, 3 * PAIR), F32)],
        scratch_shapes=[pltpu.VMEM((length, PAIR), F32)],
        compiler_params=PARAMS,
        cost_estimate=pl.CostEstimate(
            flops=pairs * 2 * 10 * length * length * 256,
            bytes_accessed=length * columns * 6,
            transcendentals=pairs * 2 * length * length,
        ),
        name="attend_back",
    )(qkv, key_bias, attended, lse, *pieces)


def middle_kernel(group, rows_ref, tokens_ref, *rest):
    parts, weights, (branch_ref, middle_ref, normed_ref, unit_ref, inv_ref) = (
        rest[:group], rest[group : 2 * group], rest[2 * group :]
    )
    branch = dot(parts[0][...], weights[0][...], 1, 1)
    for part, weight in zip(parts[1:], weights[1:]):
        branch = branch + dot(part[...], weight[...], 1, 1)
    branch = branch + rows_ref[4:5, :]
    branch_ref[...] = branch
    middle = tokens_ref[...].astype(F32) + rows_ref[5:6, :] * branch
    middle_ref[...] = middle
    unit, inverse = unit_rows(middle)
    unit_ref[...] = unit
    inv_ref[...] = inverse
    normed_ref[...] = (unit * rows_ref[6:7, :] + rows_ref[7:8, :]).astype(BF)


def middle_step(rows, tokens, parts, weights):
    length, width = tokens.shape
    group = len(parts)
    full = shaped((length, width), F32)
    return pl.pallas_call(
        lambda *refs: middle_kernel(group, *refs),
        in_specs=[VMEM] * (2 + 2 * group),
        out_specs=[VMEM] * 5,
        out_shape=[full, full, shaped((length, width), BF), full, shaped((length, 1), F32)],
        compiler_params=PARAMS,
        cost_estimate=pl.CostEstimate(
            flops=2 * length * width * width, bytes_accessed=8_000_000, transcendentals=0
        ),
        name="middle",
    )(rows, tokens, *parts, *weights)


def turn_kernel(group, terms, rows_ref, live_ref, cot_ref, unit_ref, inv_ref, branch_ref, *rest):
    backs, weights, outs = rest[:terms], rest[terms : terms + group], rest[terms + group :]
    middle_ref, grad_ref, sums_ref = outs[:3]
    norm_grad = backs[0][...].astype(F32)
    for ref in backs[1:]:
        norm_grad = norm_grad + ref[...].astype(F32)
    unit = unit_ref[...]
    out_grad = cot_ref[...].astype(F32) * live_ref[...]
    middle = out_grad + norm_back(norm_grad, unit, inv_ref[...], rows_ref[6:7, :])
    middle_ref[...] = middle
    low = (middle * rows_ref[5:6, :]).astype(BF)
    grad_ref[...] = low
    sums_ref[...] = jnp.zeros(sums_ref.shape, F32)
    sums_ref[0:1, :] = jnp.sum(low.astype(F32), axis=0, keepdims=True)
    sums_ref[1:2, :] = jnp.sum(middle * branch_ref[...], axis=0, keepdims=True)
    sums_ref[2:3, :] = jnp.sum(norm_grad * unit, axis=0, keepdims=True)
    sums_ref[3:4, :] = jnp.sum(norm_grad, axis=0, keepdims=True)
    for out, weight in zip(outs[3:], weights):
        out[...] = dot(low, weight[...], 1, 0).astype(BF)


def turn(rows, live, cotangent, unit, inverse, branch, backs, weights):
    length, width = cotangent.shape
    part = weights[0].shape[1]
    group = len(weights)
    return pl.pallas_call(
        lambda *refs: turn_kernel(group, len(backs), *refs),
        in_specs=[VMEM] * (6 + len(backs) + group),
        out_specs=[VMEM] * (3 + group),
        out_shape=[shaped((length, width), F32), shaped((length, width), BF), shaped((8, width), F32)]
        + [shaped((length, part), BF)] * group,
        compiler_params=PARAMS,
        cost_estimate=pl.CostEstimate(
            flops=2 * length * width * width, bytes_accessed=10_000_000, transcendentals=0
        ),
        name="turn",
    )(rows, live, cotangent, unit, inverse, branch, *backs, *weights)


def proj_weights_kernel(grad_ref, *rest):
    half = len(rest) // 2
    for part, out in zip(rest[:half], rest[half:]):
        out[...] = dot(grad_ref[...], part[...], 0, 0).astype(BF)


def proj_weights(grads, parts):
    length, width = grads.shape
    part = parts[0].shape[1]
    return pl.pallas_call(
        proj_weights_kernel,
        in_specs=[VMEM] * (1 + len(parts)),
        out_specs=[VMEM] * len(parts),
        out_shape=[shaped((width, part), BF)] * len(parts),
        compiler_params=PARAMS,
        cost_estimate=pl.CostEstimate(
            flops=2 * length * width * width, bytes_accessed=4_000_000, transcendentals=0
        ),
        name="proj_weights",
    )(grads, *parts)


def mlp_kernel(count, rows_ref, *rest):
    normed_in, cots, lives = rest[:count], rest[count : 2 * count], rest[2 * count : 3 * count]
    fc1_ref, fc2_ref, bias_ref = rest[3 * count : 3 * count + 3]
    backs = rest[3 * count + 3 : 4 * count + 3]
    (
        normed_ref, out_ref, act_ref, pre_ref, sums_ref, own_ref, grad_ref, back_acc
    ) = rest[4 * count + 3 :]
    step = pl.program_id(0)
    size = cots[0].shape[0]

    @pl.when(step == 0)
    def _():
        normed_ref[...] = jnp.concatenate([ref[...].astype(F32) for ref in normed_in]).astype(BF)
        scale = rows_ref[9:10, :]
        grads = [cot[...].astype(F32) * live[...] for cot, live in zip(cots, lives)]
        whole_grad = jnp.concatenate(grads)
        out_ref[...] = whole_grad.astype(BF)
        scaled = (whole_grad * scale).astype(BF)
        grad_ref[...] = scaled
        own_ref[0:1, :] = jnp.sum(scaled.astype(F32)[:size], axis=0, keepdims=True)
        own_ref[1:2, :] = jnp.sum(grads[0], axis=0, keepdims=True)

    chunk = fc1_ref.shape[1] // 2
    for cols in (slice(0, chunk), slice(chunk, 2 * chunk)):
        pre = dot(normed_ref[...], fc1_ref[:, cols], 1, 0) + bias_ref[:, cols]
        act_grad = dot(grad_ref[...], fc2_ref[:, cols], 1, 0)
        cdf = 0.5 * (1.0 + lax.erf(pre * SQRT_HALF))
        act_ref[:, cols] = (pre * cdf).astype(BF)
        slope = cdf + pre * (jnp.exp(-0.5 * pre * pre) * INV_ROOT_TWO_PI)
        pre_grad = (act_grad * slope).astype(BF)
        pre_ref[:, cols] = pre_grad
        sums_ref[:, cols] = jnp.sum(pre_grad.astype(F32), axis=0, keepdims=True)
    back = dot(pre_ref[...], fc1_ref[...], 1, 1)

    @pl.when(step == 0)
    def _():
        back_acc[...] = back

    @pl.when(step == pl.num_programs(0) - 1)
    def _():
        whole = back_acc[...] + back
        for j, ref in enumerate(backs):
            ref[...] = whole[j * size : (j + 1) * size].astype(BF)


def mlp(rows, normed, cots, lives, weights, bias):
    size, width = normed[0].shape
    count = len(normed)
    length = count * size
    hidden = weights.shape[1] // 2
    step = hidden // 2

    def whole(*shape):
        return pl.BlockSpec(shape, lambda i: (0, 0))

    cols = pl.BlockSpec((length, step), lambda i: (0, i))
    return pl.pallas_call(
        lambda *refs: mlp_kernel(count, *refs),
        grid=(2,),
        in_specs=[whole(*rows.shape)]
        + [whole(size, width)] * (2 * count)
        + [whole(size, 1)] * count
        + [
            pl.BlockSpec((width, step), lambda i: (0, i)),
            pl.BlockSpec((width, step), lambda i: (0, 2 + i)),
            pl.BlockSpec((1, step), lambda i: (0, i)),
        ],
        out_specs=[whole(size, width)] * count
        + [whole(length, width)] * 2
        + [cols, cols, pl.BlockSpec((1, step), lambda i: (0, i)), whole(8, width)],
        out_shape=[shaped((size, width), BF)] * count
        + [shaped((length, width), BF)] * 2
        + [shaped((length, hidden), BF)] * 2
        + [shaped((1, hidden), F32), shaped((8, width), F32)],
        scratch_shapes=[pltpu.VMEM((length, width), BF), pltpu.VMEM((length, width), F32)],
        compiler_params=PARAMS,
        cost_estimate=pl.CostEstimate(
            flops=6 * length * width * hidden,
            bytes_accessed=12_000_000,
            transcendentals=2 * length * hidden,
        ),
        name="mlp",
    )(rows, *normed, *cots, *lives, weights, weights, bias)


def mlp_weights_kernel(
    norm_a, norm_b, grad_a, grad_b, rows_ref, fc2_ref, pre_a, pre_b, act_a, act_b, own_ref,
    out_ref, scale2_ref, *branches
):
    hidden = pre_a.shape[1]
    first = dot(norm_a[...], pre_a[...], 0, 0) + dot(norm_b[...], pre_b[...], 0, 0)
    out_ref[:, :hidden] = first.astype(BF)
    outs = [grad_a[...].astype(F32), grad_b[...].astype(F32)]
    scaled = [(out * rows_ref[9:10, :]).astype(BF) for out in outs]
    second = dot(scaled[0], act_a[...], 0, 0) + dot(scaled[1], act_b[...], 0, 0)
    out_ref[:, hidden:] = second.astype(BF)
    scale2 = own_ref[1:2, :] * rows_ref[8:9, :]
    count = len(branches) // 2
    size = branches[0].shape[0]
    for half, act in enumerate((act_a, act_b)):
        branch = dot(act[...], fc2_ref[...], 1, 1)
        scale2 = scale2 + jnp.sum(outs[half] * branch, axis=0, keepdims=True)
        for j in range(count):
            branches[half * count + j][...] = branch[j * size : (j + 1) * size].astype(BF)
    scale2_ref[...] = scale2


def mlp_weights(rows, own, normed, grads, pres, acts, weights, group):
    length, width = normed[0].shape
    hidden = pres[0].shape[1]
    size = 2 * length // group
    step = 256
    cols = pl.BlockSpec((length, step), lambda i: (0, i))
    whole = pl.BlockSpec((length, hidden), lambda i: (0, 0))
    return pl.pallas_call(
        mlp_weights_kernel,
        grid=(width // step,),
        in_specs=[cols] * 4
        + [pl.BlockSpec((rows.shape[0], step), lambda i: (0, i))]
        + [pl.BlockSpec((step, hidden), lambda i: (i, 1))]
        + [whole] * 4
        + [pl.BlockSpec((own.shape[0], step), lambda i: (0, i))],
        out_specs=[pl.BlockSpec((step, 2 * hidden), lambda i: (i, 0))]
        + [pl.BlockSpec((1, step), lambda i: (0, i))]
        + [pl.BlockSpec((size, step), lambda i: (0, i))] * group,
        out_shape=[shaped((width, 2 * hidden), BF), shaped((1, width), F32)]
        + [shaped((size, width), BF)] * group,
        compiler_params=PARAMS,
        cost_estimate=pl.CostEstimate(
            flops=12 * length * width * hidden, bytes_accessed=20_000_000, transcendentals=0
        ),
        name="mlp_weights",
    )(*normed, *grads, rows, weights, *pres, *acts, own)


def finish_kernel(rows_ref, middle_ref, *rest):
    terms, out_ref = rest[:-1], rest[-1]
    branch = terms[0][...].astype(F32)
    for ref in terms[1:]:
        branch = branch + ref[...].astype(F32)
    branch = branch + rows_ref[8:9, :]
    out_ref[...] = (middle_ref[...] + rows_ref[9:10, :] * branch).astype(BF)


def finish(rows, middle, terms):
    return pl.pallas_call(
        finish_kernel,
        in_specs=[VMEM] * (2 + len(terms)),
        out_specs=VMEM,
        out_shape=shaped(middle.shape, BF),
        compiler_params=PARAMS,
        name="finish",
    )(rows, middle, *terms)


def begin_kernel(rows_ref, tokens_ref, mean_ref, inv_ref, middle_ref, *rest):
    terms, out_ref = rest[:-1], rest[-1]
    grads = terms[0][...].astype(F32)
    for ref in terms[1:]:
        grads = grads + ref[...].astype(F32)
    inverse = inv_ref[...]
    unit = (tokens_ref[...].astype(F32) - mean_ref[...]) * inverse
    out_ref[...] = (middle_ref[...] + norm_back(grads, unit, inverse, rows_ref[0:1, :])).astype(BF)


def begin(rows, tokens, mean, inverse, middle_grad, terms):
    length, width = tokens.shape
    column = pl.BlockSpec((length, 1), lambda i: (0, 0))
    whole = pl.BlockSpec((length, width), lambda i: (0, 0))
    return pl.pallas_call(
        begin_kernel,
        grid=(1,),
        in_specs=[pl.BlockSpec(rows.shape, lambda i: (0, 0)), whole, column, column, whole]
        + [whole] * len(terms),
        out_specs=whole,
        out_shape=shaped((length, width), BF),
        compiler_params=PARAMS,
        name="begin",
    )(rows, tokens, mean, inverse, middle_grad, *terms)


def qkv_back_kernel(group, grad_ref, weight_ref, mean_ref, inv_ref, *rest):
    tokens, outs, sums_ref = rest[:group], rest[group:-1], rest[-1]
    size = tokens[0].shape[0]
    gain = shift = 0.0
    for first in range(0, group, 2):
        span = slice(first * size, (first + 2) * size)
        part = dot(grad_ref[span, :], weight_ref[...], 1, 1)
        inputs = jnp.concatenate([tokens[first][...].astype(F32), tokens[first + 1][...].astype(F32)])
        unit = (inputs - mean_ref[span, :]) * inv_ref[span, :]
        outs[first][...] = part[:size].astype(BF)
        outs[first + 1][...] = part[size:].astype(BF)
        gain = gain + jnp.sum(part * unit, axis=0, keepdims=True)
        shift = shift + jnp.sum(part, axis=0, keepdims=True)
    sums_ref[...] = jnp.zeros(sums_ref.shape, F32)
    sums_ref[0:1, :] = gain
    sums_ref[1:2, :] = shift


def qkv_back(qkv_grad, weight, tokens, mean, inverse):
    size, width = tokens[0].shape
    group = len(tokens)
    return pl.pallas_call(
        lambda *refs: qkv_back_kernel(group, *refs),
        in_specs=[VMEM] * (4 + group),
        out_specs=[VMEM] * (group + 1),
        out_shape=[shaped((size, width), BF)] * group + [shaped((8, width), F32)],
        compiler_params=PARAMS,
        cost_estimate=pl.CostEstimate(
            flops=2 * group * size * width * qkv_grad.shape[1],
            bytes_accessed=10_000_000,
            transcendentals=0,
        ),
        name="qkv_back",
    )(qkv_grad, weight, mean, inverse, *tokens)


def attn_weights_kernel(
    direct, shard, terms, ids_ref, normed_ref, grad_ref, norm1_ref, sums_ref, turn_ref, fbias_ref,
    scale2_ref, bias_a_ref, bias_b_ref, *rest,
):
    projs, outs = rest[:terms], rest[terms:-4]
    rows_ref, turned_ref, block_ref, small_ref = rest[-4:]
    place, row = ids_ref[0], ids_ref[1]
    width = normed_ref.shape[1]
    part = projs[0].shape[1]
    rows_ref[...] = jnp.zeros(rows_ref.shape, F32)
    rows_ref[0:2, :] = norm1_ref[0:2, :]
    for pair in range(part // PAIR):
        where = lanes(place * part + pair * PAIR, PAIR)
        rows_ref[2:3, where] = sums_ref[pair, :, :PAIR]
        rows_ref[3:4, where] = sums_ref[pair, :, 2 * PAIR :]
    rows_ref[4:8, :] = turn_ref[0:4, :]
    rows_ref[8:9, :] = fbias_ref[0:1, :]
    rows_ref[9:10, :] = scale2_ref[...]
    cols = bias_a_ref.shape[1] // part
    for owner in range(part // shard):
        for line in range(cols):
            spot = (owner * cols + line) * shard
            small_ref[line : line + 1, owner * shard : (owner + 1) * shard] = (
                bias_a_ref[0:1, spot : spot + shard] + bias_b_ref[0:1, spot : spot + shard]
            )
    rows_ref[10 : 10 + cols, lanes(place * part, part)] = small_ref[0:cols, :]
    turned_ref[...] = rows_ref[...].T
    step = block_ref.shape[0]
    for k in range(width // step):
        start = pl.multiple_of(((row >> 1) ^ k) * step, step) if direct else k * step
        cols = pl.ds(start, step)
        block_ref[:, : 3 * part] = dot(normed_ref[:, cols], grad_ref[...], 0, 0)
        proj = projs[0][cols, :].astype(F32)
        for ref in projs[1:]:
            proj = proj + ref[cols, :].astype(F32)
        block_ref[:, 3 * part : 4 * part] = proj
        block_ref[:, 4 * part :] = turned_ref[cols, :]
        if direct:
            size = step // 2
            side = row & 1
            outs[2 * k][...] = block_ref[pl.ds(pl.multiple_of(side * size, size), size), :].astype(BF)
            outs[2 * k + 1][...] = block_ref[
                pl.ds(pl.multiple_of((1 - side) * size, size), size), :
            ].astype(BF)
        else:
            outs[0][k * step : (k + 1) * step, :] = block_ref[...].astype(BF)


def attn_weights(ids, normed1, qkv_grad, sums, projs, blocks, shard):
    length, width = normed1.shape
    part = projs[0].shape[1]
    columns = 4 * part + EXTRA
    direct = blocks > 0
    step = 2 * (width // blocks) if direct else 256
    out_shape = [shaped((width // blocks, columns), BF)] * blocks if direct else [
        shaped((width, columns), BF)
    ]
    return pl.pallas_call(
        lambda *refs: attn_weights_kernel(direct, shard, len(projs), *refs),
        in_specs=[SMEM] + [VMEM] * (2 + len(sums) + len(projs)),
        out_specs=[VMEM] * len(out_shape),
        out_shape=out_shape,
        scratch_shapes=[
            pltpu.VMEM((EXTRA, width), F32),
            pltpu.VMEM((width, EXTRA), F32),
            pltpu.VMEM((step, columns), F32),
            pltpu.VMEM((8, part), F32),
        ],
        compiler_params=PARAMS,
        cost_estimate=pl.CostEstimate(
            flops=6 * length * width * part, bytes_accessed=12_000_000, transcendentals=0
        ),
        name="attn_weights",
    )(ids, normed1, qkv_grad, *sums, *projs)


def total(ids, terms, group):
    size, columns = terms[0].shape
    rows = size // group

    def kernel(ids_ref, *refs):
        ins, outs, sum_ref = refs[: len(terms)], refs[len(terms) : -1], refs[-1]
        value = ins[0][...].astype(F32)
        for ref in ins[1:]:
            value = value + ref[...].astype(F32)
        sum_ref[...] = value
        for k, out in enumerate(outs):
            start = pl.multiple_of((ids_ref[0] ^ k) * rows, rows)
            out[...] = sum_ref[pl.ds(start, rows), :].astype(BF)

    return pl.pallas_call(
        kernel,
        in_specs=[SMEM] + [VMEM] * len(terms),
        out_specs=[VMEM] * group,
        out_shape=[shaped((rows, columns), BF)] * group,
        scratch_shapes=[pltpu.VMEM((size, columns), F32)],
        compiler_params=PARAMS,
        name="total",
    )(ids, *terms)


def place_attn_kernel(ids_ref, *refs):
    group = len(refs) - 4
    blocks, (qkv_ref, proj_ref, vec_ref, bias_ref) = refs[:group], refs[group:]
    width = proj_ref.shape[1]
    part = width // group
    extra = jnp.zeros((qkv_ref.shape[0], EXTRA), F32)
    for k, block in enumerate(blocks):
        source = ids_ref[0] ^ k
        for third in range(3):
            for pair in range(part // PAIR):
                spot = (pair * 3 + third) * PAIR
                where = lanes(third * width + source * part + pair * PAIR, PAIR)
                qkv_ref[:, where] = block[:, spot : spot + PAIR].astype(F32)
        proj_ref[:, lanes(source * part, part)] = block[:, 3 * part : 4 * part].astype(F32)
        extra = extra + block[:, 4 * part :].astype(F32)
    turned = extra.T
    count = vec_ref.shape[0]
    vec_ref[...] = turned[:count]
    bias_ref[...] = turned[count : count + bias_ref.shape[0]]


def place_attn(ids, blocks, width, vector_count, bias_cols):
    rows = blocks[0].shape[0]
    return pl.pallas_call(
        place_attn_kernel,
        in_specs=[SMEM] + [VMEM] * len(blocks),
        out_specs=[VMEM] * 4,
        out_shape=[
            shaped((rows, 3 * width), F32),
            shaped((rows, width), F32),
            shaped((vector_count, rows), F32),
            shaped((bias_cols, rows), F32),
        ],
        compiler_params=PARAMS,
        name="place_attn",
    )(ids, *blocks)


def place_mlp_kernel(ids_ref, *refs):
    group = len(refs) - 2
    blocks, (fc1_ref, fc2_ref) = refs[:group], refs[group:]
    part = fc1_ref.shape[1] // group
    for k, block in enumerate(blocks):
        where = lanes((ids_ref[0] ^ k) * part, part)
        fc1_ref[:, where] = block[:, :part].astype(F32)
        fc2_ref[:, where] = block[:, part:].astype(F32)


def place_mlp(ids, blocks, hidden):
    rows = blocks[0].shape[0]
    return pl.pallas_call(
        place_mlp_kernel,
        in_specs=[SMEM] + [VMEM] * len(blocks),
        out_specs=[VMEM] * 2,
        out_shape=[shaped((rows, hidden), F32)] * 2,
        compiler_params=PARAMS,
        name="place_mlp",
    )(ids, *blocks)


def local(tokens, counts, w_qkv, w_proj, w_fc1, fc1_bias, w_fc2, vectors, cotangent):
    _, capacity, width = tokens.shape
    hidden = w_fc1.shape[1]
    rows = w_qkv.shape[0]
    group, replicas = lax.axis_size("ctx"), lax.axis_size("dp")
    place, replica = lax.axis_index("ctx"), lax.axis_index("dp")
    ids = jnp.stack([place, replica]).astype(jnp.int32)
    head_width = width // group
    hidden_part = hidden // group
    bias_cols = hidden // width
    vector_count = vectors.shape[0]
    direct = replicas <= 8

    def swap(value, bit, axis="ctx"):
        size = group if axis == "ctx" else replicas
        return lax.ppermute(value, axis, [(i, i ^ bit) for i in range(size)])

    def after(value, *before):
        return lax.optimization_barrier((value,) + before)[0]

    def gather(own, *before):
        pieces = [own]
        for j in range(1, group):
            bit = j & -j
            source = pieces[j ^ bit]
            pieces.append(swap(after(source, *before) if j ^ bit else source, bit))
        return pieces

    def scatter(parts, *before, mids=None):
        pieces = {j: [part] for j, part in enumerate(parts)}

        def added(terms):
            if len(terms) == 1:
                return terms[0]
            return sum(term.astype(F32) for term in terms).astype(BF)

        bit = 1
        while bit < group:
            for j in sorted((j for j in pieces if j & bit), reverse=True):
                value = added(pieces.pop(j))
                if bit > 1:
                    if mids is not None:
                        mids.append(value)
                    value = after(value, *before)
                pieces[j ^ bit].append(swap(value, bit))
            bit *= 2
        return pieces[0]

    def exchange(relative):
        return [relative[0]] + [swap(relative[k], k) for k in range(1, group)]

    def in_order(relative):
        stacked = jnp.stack(relative)
        return jnp.concatenate(
            [lax.dynamic_index_in_dim(stacked, place ^ s, 0, False) for s in range(group)], axis=0
        )

    cuts = cut(
        ids, counts, w_qkv, w_proj.T, w_fc1, w_fc2.T, vectors, fc1_bias.reshape(bias_cols, rows), group
    )
    first = exchange(cuts[:group])
    tokens_far = swap(after(tokens[0], *first), group // 2)
    second = exchange([after(block, *first) for block in cuts[group:]])
    if direct:
        shards = {0: jnp.concatenate(first, axis=0)}
        for m in range(replicas - 2, 0, -2):
            shards[m] = swap(shards[0], m, "dp")
        arrived = [tokens_far] + [shards[m] for m in sorted(shards) if m] + second[1:]
        for m in range(1, replicas, 2):
            shards[m] = swap(after(shards[m - 1], *arrived), 1, "dp")
        first_pieces = [shards[m] for m in range(replicas)]
    else:
        first_pieces = [lax.all_gather(in_order(first), "dp", axis=0, tiled=True)]
        arrived = [tokens_far]
    tokens_pieces = [tokens[0]]
    for j in range(1, group):
        source = tokens_pieces[j ^ (j & -j)]
        if j == group // 2:
            tokens_pieces.append(tokens_far)
        else:
            tokens_pieces.append(swap(after(source, *arrived), j & -j))
    second_shard = after(in_order(second), *arrived)
    second_all = lax.all_gather(second_shard, "dp", axis=0, tiled=True)
    cotangent_far = swap(after(cotangent[0], *arrived), group // 2)

    tokens_own = after(tokens[0], second_shard, cotangent_far)
    count_column = vector_count + bias_cols
    (
        weight_qkv, weight_proj, vector_rows, normed1, qkv, mean1, inverse1, bias_fc1, key_bias,
        *live,
    ) = project(
        ids, [tokens_own] + tokens_pieces[1:], first, first_pieces, hidden_part, count_column,
        0 if direct else rows,
    )

    cotangent_pieces = [cotangent[0]]
    for j in range(1, group):
        source = cotangent_pieces[j ^ (j & -j)]
        if j == group // 2:
            cotangent_pieces.append(cotangent_far)
        else:
            cotangent_pieces.append(swap(after(source, qkv), j & -j))
    attended, lse, *attended_low = attend(qkv, key_bias, group)
    projs = gather(weight_proj, lse)
    attended_own = exchange(attended_low)
    branch1, middle, normed2_own, unit2, inverse2 = middle_step(
        vector_rows, tokens[0], attended_own, projs
    )
    normed2 = gather(normed2_own)
    half = group // 2

    def feed(where, bias):
        return mlp(
            vector_rows, normed2[where], cotangent_pieces[where], live[where], second_all, bias
        )

    *backs_near, norm_near, grad_near, act_near, pre_near, sums_near, own_sums = feed(
        slice(0, half), bias_fc1
    )
    *backs_far, norm_far, grad_far, act_far, pre_far, sums_far, _ = feed(
        slice(half, group), after(bias_fc1, sums_near)
    )
    mids = []
    norm2_terms = scatter(backs_near + backs_far, mids=mids)
    grad_mlp, grad_scale2, *branches = mlp_weights(
        vector_rows, own_sums, [norm_near, norm_far], [grad_near, grad_far], [after(pre_near, *mids), pre_far],
        [act_near, act_far], second_all, group,
    )
    owned_mlp = lax.psum_scatter(
        after(grad_mlp, *norm2_terms), "dp", scatter_dimension=0, tiled=True
    )

    middle_grad, branch_grad, turn_sums, *att_grads = turn(
        vector_rows, live[0], cotangent[0], unit2, inverse2, branch1, norm2_terms, projs
    )
    att_grads = exchange(att_grads)
    mids = []
    proj_terms = scatter(proj_weights(branch_grad, attended_own), mids=mids)
    branch2_terms = scatter(branches, *att_grads, mids=mids)
    qkv_grad, qkv_sums = attend_back(qkv, key_bias, attended, after(lse, *mids), att_grads)
    *norm1_parts, norm1_sums = qkv_back(qkv_grad, weight_qkv, tokens_pieces, mean1, inverse1)
    parts = attn_weights(
        ids, normed1, qkv_grad,
        [norm1_sums, qkv_sums, turn_sums, own_sums, grad_scale2, sums_near, sums_far],
        proj_terms, replicas if direct else 0, rows,
    )
    norm1_terms = scatter(norm1_parts)
    if direct:
        order = list(range(replicas // 2 - 1, -1, -1))
        others = []
        for k in order:
            others.append(swap(after(parts[2 * k + 1], *others[-2:-1]), 1, "dp"))
        terms = [parts[0], others[-1]]
        for k, other in zip(order[:-1], others):
            summed = (parts[2 * k].astype(F32) + other.astype(F32)).astype(BF)
            terms.append(swap(summed, 2 * k, "dp"))
        ids_late = after(ids, *others)
        cuts_mlp = total(ids_late, [owned_mlp], group)
    else:
        owned_attn = lax.psum_scatter(parts[0], "dp", scatter_dimension=0, tiled=True)

        def relative(owned):
            blocks = owned.reshape(group, rows, -1)
            return [lax.dynamic_index_in_dim(blocks, place ^ k, 0, False) for k in range(group)]

        cuts_mlp = relative(owned_mlp)
        ids_late = ids
    out_fc1, out_fc2 = place_mlp(ids, exchange(cuts_mlp), hidden)
    if direct:
        cuts_attn = total(after(ids, out_fc1, *norm1_terms, *branch2_terms), terms, group)
    else:
        cuts_attn = relative(owned_attn)

    input_grad = begin(
        vector_rows, after(tokens[0], *cuts_attn), mean1, inverse1, middle_grad, norm1_terms
    )
    output = finish(after(vector_rows, *cuts_attn), middle, branch2_terms)
    out_qkv, out_proj, out_vectors, out_bias = place_attn(
        ids, exchange(cuts_attn), width, vector_count, bias_cols
    )
    return (
        output[None],
        input_grad[None],
        out_qkv,
        out_proj.T,
        out_fc1,
        out_bias.reshape(-1),
        out_fc2.T,
        out_vectors,
    )


def solution(mesh):
    both = ("dp", "ctx")
    in_specs = (
        P("dp", "ctx", None),
        P("dp", "ctx"),
        P(both, None),
        P(None, both),
        P(both, None),
        P(both),
        P(None, both),
        P(None, both),
        P("dp", "ctx", None),
    )
    out_specs = (
        P("dp", "ctx", None),
        P("dp", "ctx", None),
        P(both, None),
        P(None, both),
        P(both, None),
        P(both),
        P(None, both),
        P(None, both),
    )
    return jax.shard_map(local, mesh=mesh, in_specs=in_specs, out_specs=out_specs, check_vma=False)
```

```python
import jax
import jax.numpy as jnp
from jax import lax
from jax.experimental import pallas as pl
from jax.experimental.pallas import tpu as pltpu
from jax.sharding import PartitionSpec as P

HD = 64
PAIR = 2 * HD
EXTRA = 128
EPSILON = 1e-06
MASKED_SCORE = -1e30
SQRT_HALF = 0.7071067811865476
INV_ROOT_TWO_PI = 0.3989422804014327
BF = jnp.bfloat16
F32 = jnp.float32
PARAMS = pltpu.CompilerParams(vmem_limit_bytes=60 * 1024 * 1024)
SMALL = pl.CostEstimate(flops=1_000_000_000, bytes_accessed=1_000_000, transcendentals=0)
VMEM = pl.BlockSpec(memory_space=pltpu.VMEM)
SMEM = pl.BlockSpec(memory_space=pltpu.SMEM)


def shaped(shape, dtype):
    return jax.ShapeDtypeStruct(shape, dtype)


def dot(left, right, left_dim, right_dim):
    return lax.dot_general(
        left, right, (((left_dim,), (right_dim,)), ((), ())), preferred_element_type=F32
    )


def lanes(start, size):
    return pl.ds(pl.multiple_of(start, 128), size)


def unit_rows(inputs):
    centered = inputs - jnp.mean(inputs, axis=-1, keepdims=True)
    spread = jnp.mean(centered * centered, axis=-1, keepdims=True)
    inverse = lax.rsqrt(spread + EPSILON)
    return (centered * inverse, inverse)


def norm_back(grad_in, unit, inverse, gain):
    scaled = grad_in * gain
    inner = (
        scaled
        - jnp.mean(scaled, axis=-1, keepdims=True)
        - unit * jnp.mean(scaled * unit, axis=-1, keepdims=True)
    )
    return inner * inverse


def cut_kernel(ids_ref, count_ref, qkv_ref, proj_ref, fc1_ref, fc2_ref, vec_ref, bias_ref, *rest):
    outs, (extra_ref, turn_ref) = rest[:-2], rest[-2:]
    group = len(outs) // 2
    place = ids_ref[0]
    width = proj_ref.shape[1]
    part = width // group
    hidden_part = fc1_ref.shape[1] // group
    vector_count, bias_cols = vec_ref.shape[0], bias_ref.shape[1] // vec_ref.shape[1]
    column = vector_count + bias_cols
    lane = lax.broadcasted_iota(jnp.int32, extra_ref.shape, 1)
    count = count_ref[0, 0]
    high = (count >> 7).astype(F32)
    low = (count & 127).astype(F32)
    extra_ref[...] = jnp.where(lane == column, high, jnp.where(lane == column + 1, low, 0.0))
    extra_ref[:, :vector_count] = vec_ref[...].astype(F32).T
    rows = qkv_ref.shape[0]
    for line in range(bias_cols):
        turn_ref[line : line + 1, :] = bias_ref[0:1, line * rows : (line + 1) * rows].astype(F32)
    extra_ref[:, vector_count:column] = turn_ref[0:bias_cols, :].T
    extra = extra_ref[...].astype(BF)
    for k in range(group):
        target = place ^ k
        first, second = outs[k], outs[group + k]
        for third in range(3):
            for pair in range(part // PAIR):
                spot = (pair * 3 + third) * PAIR
                first[:, spot : spot + PAIR] = qkv_ref[
                    :, lanes(third * width + target * part + pair * PAIR, PAIR)
                ]
        first[:, 3 * part : 4 * part] = proj_ref[:, lanes(target * part, part)]
        first[:, 4 * part :] = extra
        second[:, :hidden_part] = fc1_ref[:, lanes(target * hidden_part, hidden_part)]
        second[:, hidden_part:] = fc2_ref[:, lanes(target * hidden_part, hidden_part)]


def cut(ids, counts, w_qkv, w_proj_t, w_fc1, w_fc2_t, vectors, bias, group):
    rows, width = w_proj_t.shape
    part, hidden_part = width // group, w_fc1.shape[1] // group
    return pl.pallas_call(
        cut_kernel,
        in_specs=[SMEM, SMEM] + [VMEM] * 6,
        out_specs=[VMEM] * (2 * group),
        out_shape=[shaped((rows, 4 * part + EXTRA), BF)] * group
        + [shaped((rows, 2 * hidden_part), BF)] * group,
        scratch_shapes=[pltpu.VMEM((rows, EXTRA), F32), pltpu.VMEM((8, rows), F32)],
        compiler_params=PARAMS,
        name="cut",
    )(ids, counts, w_qkv, w_proj_t, w_fc1, w_fc2_t, vectors, bias)


def project_kernel(ordered, group, count_column, ids_ref, *rest):
    tokens, blocks, rest = rest[:group], rest[group : 2 * group], rest[2 * group :]
    pieces, outs, lives, scratch = (
        rest[: -12 - group], rest[-12 - group : -3 - group], rest[-3 - group : -3], rest[-3:]
    )
    qkv_w, proj_w, rows_ref, normed_ref, out_ref, mean_ref, inv_ref, fc1_ref, key_ref = outs
    extra_ref, bias_ref, small_ref = scratch
    place, row = ids_ref[0], ids_ref[1]
    capacity, width = tokens[0].shape
    part = proj_w.shape[1]
    size = pieces[0].shape[0]

    def lay(block, start, count):
        where = pl.ds(start, count)
        qkv_w[where, :] = block[:, : 3 * part]
        proj_w[where, :] = block[:, 3 * part : 4 * part]
        extra_ref[where, :] = block[:, 4 * part :].astype(F32)

    if ordered:
        lay(pieces[0], 0, size)
        shard = ordered
    else:
        sub = shard = size // group
        for m, piece in enumerate(pieces):
            for j in range(group):
                start = (row ^ m) * size + (place ^ j) * sub
                lay(piece.at[j * sub : (j + 1) * sub], pl.multiple_of(start, sub), sub)
    slot = lax.broadcasted_iota(jnp.int32, (capacity, 1), 0).astype(F32)
    for j, (block, live_ref) in enumerate(zip(blocks, lives)):
        extra = block[:, 4 * part :].astype(F32)[0:1, :]
        bound = extra[:, count_column : count_column + 1] * 128.0
        bound = bound + extra[:, count_column + 1 : count_column + 2]
        live = jnp.where(slot < bound, 1.0, 0.0)
        live_ref[...] = live
        key_ref[j * capacity : (j + 1) * capacity, :] = (1.0 - live) * MASKED_SCORE
    turned = extra_ref[...].T
    rows_ref[...] = turned[: rows_ref.shape[0]]
    bias_ref[...] = jnp.zeros(bias_ref.shape, F32)
    for pair in range(part // PAIR):
        for third, line in ((0, 2), (2, 3)):
            spot = (pair * 3 + third) * PAIR
            bias_ref[0:1, spot : spot + PAIR] = rows_ref[
                line : line + 1, lanes(place * part + pair * PAIR, PAIR)
            ]
    cols = fc1_ref.shape[1] // part
    small_ref[0:cols, :] = rows_ref[10 : 10 + cols, lanes(place * part, part)]
    for owner in range(part // shard):
        for line in range(cols):
            spot = (owner * cols + line) * shard
            fc1_ref[0:1, spot : spot + shard] = small_ref[
                line : line + 1, owner * shard : (owner + 1) * shard
            ]
    gain, shift, bias = rows_ref[0:1, :], rows_ref[1:2, :], bias_ref[0:1, :]
    for first in range(0, group, 2):
        span = slice(first * capacity, (first + 2) * capacity)
        inputs = jnp.concatenate([tokens[first][...].astype(F32), tokens[first + 1][...].astype(F32)])
        mean = jnp.mean(inputs, axis=-1, keepdims=True)
        centered = inputs - mean
        inverse = lax.rsqrt(jnp.mean(centered * centered, axis=-1, keepdims=True) + EPSILON)
        normed = (centered * inverse * gain + shift).astype(BF)
        normed_ref[span, :] = normed
        mean_ref[span, :] = mean
        inv_ref[span, :] = inverse
        out_ref[span, :] = (dot(normed, qkv_w[...], 1, 0) + bias).astype(BF)


def project(ids, tokens, blocks, pieces, hidden_part, count_column, ordered):
    capacity, width = tokens[0].shape
    group = len(tokens)
    length = group * capacity
    part = width // group
    return pl.pallas_call(
        lambda *refs: project_kernel(ordered, group, count_column, *refs),
        in_specs=[SMEM] + [VMEM] * (2 * group + len(pieces)),
        out_specs=[VMEM] * (9 + group),
        out_shape=[
            shaped((width, 3 * part), BF),
            shaped((width, part), BF),
            shaped((16, width), F32),
            shaped((length, width), BF),
            shaped((length, 3 * part), BF),
            shaped((length, 1), F32),
            shaped((length, 1), F32),
            shaped((1, hidden_part), F32),
            shaped((length, 1), F32),
        ]
        + [shaped((capacity, 1), F32)] * group,
        scratch_shapes=[
            pltpu.VMEM((width, EXTRA), F32),
            pltpu.VMEM((8, 3 * part), F32),
            pltpu.VMEM((8, part), F32),
        ],
        compiler_params=PARAMS,
        cost_estimate=SMALL,
        name="project",
    )(ids, *tokens, *blocks, *pieces)


def query_chunks(length):
    step = 512
    return [(start, min(step, length - start)) for start in range(0, length, step)]


def attend_kernel(qkv_ref, bias_ref, out_ref, lse_ref, *lows):
    length = qkv_ref.shape[0]
    key_bias = bias_ref[...]
    for head in range(2):
        keys = qkv_ref[:, PAIR + head * HD : PAIR + (head + 1) * HD]
        values = qkv_ref[:, 2 * PAIR + head * HD : 2 * PAIR + (head + 1) * HD]
        for start, size in query_chunks(length):
            queries = qkv_ref[start : start + size, head * HD : (head + 1) * HD]
            queries = queries * jnp.asarray(HD**-0.5, BF)
            scores = dot(keys, queries, 1, 1) + key_bias
            top = jnp.max(scores, axis=0, keepdims=True)
            expo = jnp.exp(scores - top)
            total = jnp.sum(expo, axis=0, keepdims=True)
            mixed = (dot(values, expo.astype(BF), 0, 0) / total).T
            out_ref[start : start + size, head * HD : (head + 1) * HD] = mixed
            lse_ref[0, head : head + 1, start : start + size] = top + jnp.log(total)
    for j, low in enumerate(lows):
        size = low.shape[0]
        low[...] = out_ref[j * size : (j + 1) * size, :].astype(BF)


def attend(qkv, key_bias, group):
    length, columns = qkv.shape
    pairs = columns // (3 * PAIR)
    return pl.pallas_call(
        attend_kernel,
        grid=(pairs,),
        in_specs=[
            pl.BlockSpec((length, 3 * PAIR), lambda p: (0, p)),
            pl.BlockSpec((length, 1), lambda p: (0, 0)),
        ],
        out_specs=[
            pl.BlockSpec((length, PAIR), lambda p: (0, p)),
            pl.BlockSpec((1, 2, length), lambda p: (p, 0, 0)),
        ]
        + [pl.BlockSpec((length // group, PAIR), lambda p: (0, p))] * group,
        out_shape=[
            shaped((length, pairs * PAIR), F32),
            shaped((pairs, 2, length), F32),
        ]
        + [shaped((length // group, pairs * PAIR), BF)] * group,
        compiler_params=PARAMS,
        cost_estimate=SMALL,
        name="attend",
    )(qkv, key_bias)


def attend_back_kernel(qkv_ref, bias_ref, att_ref, lse_ref, *rest):
    pieces, (out_ref, sums_ref, grad_ref) = rest[:-3], rest[-3:]
    length = qkv_ref.shape[0]
    size = pieces[0].shape[0]
    factor = HD**-0.5
    key_bias = bias_ref[...]
    for j, piece in enumerate(pieces):
        grad_ref[j * size : (j + 1) * size, :] = piece[...].astype(F32)
    for head in range(2):
        low, high = head * HD, (head + 1) * HD
        keys = qkv_ref[:, PAIR + low : PAIR + high]
        values = qkv_ref[:, 2 * PAIR + low : 2 * PAIR + high]
        key_grad = jnp.zeros((length, HD), F32)
        value_grad = jnp.zeros((length, HD), F32)
        for start, size in query_chunks(length):
            rows = slice(start, start + size)
            queries = qkv_ref[rows, low:high] * jnp.asarray(factor, BF)
            product = grad_ref[rows, low:high] * att_ref[rows, low:high]
            grads = grad_ref[rows, low:high].astype(BF)
            delta = jnp.sum(product.T, axis=0, keepdims=True)
            scores = dot(keys, queries, 1, 1) + key_bias
            probs = jnp.exp(scores - lse_ref[0, head : head + 1, rows])
            value_grad += dot(probs.astype(BF), grads, 1, 0)
            raw = (probs * (dot(values, grads, 1, 1) - delta)).astype(BF)
            key_grad += dot(raw, queries, 1, 0)
            query_grad = dot(keys, raw, 0, 0).T * factor
            out_ref[rows, low:high] = query_grad.astype(BF)
        out_ref[:, PAIR + low : PAIR + high] = key_grad.astype(BF)
        out_ref[:, 2 * PAIR + low : 2 * PAIR + high] = value_grad.astype(BF)
    sums_ref[0] = jnp.sum(out_ref[...].astype(F32), axis=0, keepdims=True)


def attend_back(qkv, key_bias, attended, lse, pieces):
    length, columns = qkv.shape
    pairs = columns // (3 * PAIR)
    size = pieces[0].shape[0]
    return pl.pallas_call(
        attend_back_kernel,
        grid=(pairs,),
        in_specs=[
            pl.BlockSpec((length, 3 * PAIR), lambda p: (0, p)),
            pl.BlockSpec((length, 1), lambda p: (0, 0)),
            pl.BlockSpec((length, PAIR), lambda p: (0, p)),
            pl.BlockSpec((1, 2, length), lambda p: (p, 0, 0)),
        ]
        + [pl.BlockSpec((size, PAIR), lambda p: (0, p))] * len(pieces),
        out_specs=[
            pl.BlockSpec((length, 3 * PAIR), lambda p: (0, p)),
            pl.BlockSpec((1, 1, 3 * PAIR), lambda p: (p, 0, 0)),
        ],
        out_shape=[shaped((length, columns), BF), shaped((pairs, 1, 3 * PAIR), F32)],
        scratch_shapes=[pltpu.VMEM((length, PAIR), F32)],
        compiler_params=PARAMS,
        cost_estimate=SMALL,
        name="attend_back",
    )(qkv, key_bias, attended, lse, *pieces)


def middle_kernel(group, rows_ref, tokens_ref, *rest):
    parts, weights, (branch_ref, middle_ref, normed_ref, unit_ref, inv_ref) = (
        rest[:group], rest[group : 2 * group], rest[2 * group :]
    )
    branch = dot(parts[0][...], weights[0][...], 1, 1)
    for part, weight in zip(parts[1:], weights[1:]):
        branch = branch + dot(part[...], weight[...], 1, 1)
    branch = branch + rows_ref[4:5, :]
    branch_ref[...] = branch
    middle = tokens_ref[...].astype(F32) + rows_ref[5:6, :] * branch
    middle_ref[...] = middle
    unit, inverse = unit_rows(middle)
    unit_ref[...] = unit
    inv_ref[...] = inverse
    normed_ref[...] = (unit * rows_ref[6:7, :] + rows_ref[7:8, :]).astype(BF)


def middle_step(rows, tokens, parts, weights):
    length, width = tokens.shape
    group = len(parts)
    full = shaped((length, width), F32)
    return pl.pallas_call(
        lambda *refs: middle_kernel(group, *refs),
        in_specs=[VMEM] * (2 + 2 * group),
        out_specs=[VMEM] * 5,
        out_shape=[full, full, shaped((length, width), BF), full, shaped((length, 1), F32)],
        compiler_params=PARAMS,
        cost_estimate=SMALL,
        name="middle",
    )(rows, tokens, *parts, *weights)


def turn_kernel(group, terms, rows_ref, live_ref, cot_ref, unit_ref, inv_ref, branch_ref, *rest):
    backs, weights, outs = rest[:terms], rest[terms : terms + group], rest[terms + group :]
    middle_ref, grad_ref, sums_ref = outs[:3]
    norm_grad = backs[0][...].astype(F32)
    for ref in backs[1:]:
        norm_grad = norm_grad + ref[...].astype(F32)
    unit = unit_ref[...]
    out_grad = cot_ref[...].astype(F32) * live_ref[...]
    middle = out_grad + norm_back(norm_grad, unit, inv_ref[...], rows_ref[6:7, :])
    middle_ref[...] = middle
    low = (middle * rows_ref[5:6, :]).astype(BF)
    grad_ref[...] = low
    sums_ref[...] = jnp.zeros(sums_ref.shape, F32)
    sums_ref[0:1, :] = jnp.sum(low.astype(F32), axis=0, keepdims=True)
    sums_ref[1:2, :] = jnp.sum(middle * branch_ref[...], axis=0, keepdims=True)
    sums_ref[2:3, :] = jnp.sum(norm_grad * unit, axis=0, keepdims=True)
    sums_ref[3:4, :] = jnp.sum(norm_grad, axis=0, keepdims=True)
    for out, weight in zip(outs[3:], weights):
        out[...] = dot(low, weight[...], 1, 0).astype(BF)


def turn(rows, live, cotangent, unit, inverse, branch, backs, weights):
    length, width = cotangent.shape
    part = weights[0].shape[1]
    group = len(weights)
    return pl.pallas_call(
        lambda *refs: turn_kernel(group, len(backs), *refs),
        in_specs=[VMEM] * (6 + len(backs) + group),
        out_specs=[VMEM] * (3 + group),
        out_shape=[shaped((length, width), F32), shaped((length, width), BF), shaped((8, width), F32)]
        + [shaped((length, part), BF)] * group,
        compiler_params=PARAMS,
        cost_estimate=SMALL,
        name="turn",
    )(rows, live, cotangent, unit, inverse, branch, *backs, *weights)


def proj_weights_kernel(grad_ref, *rest):
    half = len(rest) // 2
    for part, out in zip(rest[:half], rest[half:]):
        out[...] = dot(grad_ref[...], part[...], 0, 0).astype(BF)


def proj_weights(grads, parts):
    length, width = grads.shape
    part = parts[0].shape[1]
    return pl.pallas_call(
        proj_weights_kernel,
        in_specs=[VMEM] * (1 + len(parts)),
        out_specs=[VMEM] * len(parts),
        out_shape=[shaped((width, part), BF)] * len(parts),
        compiler_params=PARAMS,
        cost_estimate=SMALL,
        name="proj_weights",
    )(grads, *parts)


def mlp_kernel(count, shards, group, rows_ref, *rest):
    normed_in, cots, lives = rest[:count], rest[count : 2 * count], rest[2 * count : 3 * count]
    ids_ref, bias_ref = rest[3 * count : 3 * count + 2]
    rest = rest[3 * count + 2 :]
    pieces, backs, rest = rest[:shards], rest[shards : shards + count], rest[shards + count :]
    normed_ref, out_ref, act_ref, pre_ref, sums_ref, own_ref = rest[:6]
    if shards > 1:
        weight_ref, grad_ref, back_acc = rest[6:]
    else:
        weight_ref = pieces[0]
        grad_ref, back_acc = rest[6:]
    step = pl.program_id(0)
    size = cots[0].shape[0]

    @pl.when(step == 0)
    def _():
        if shards > 1:
            whole_size = pieces[0].shape[0]
            sub = whole_size // group
            for m, piece in enumerate(pieces):
                for j in range(group):
                    start = (ids_ref[1] ^ m) * whole_size + (ids_ref[0] ^ j) * sub
                    weight_ref[pl.ds(pl.multiple_of(start, sub), sub), :] = piece[
                        j * sub : (j + 1) * sub, :
                    ]
        normed_ref[...] = jnp.concatenate([ref[...].astype(F32) for ref in normed_in]).astype(BF)
        scale = rows_ref[9:10, :]
        grads = [cot[...].astype(F32) * live[...] for cot, live in zip(cots, lives)]
        whole_grad = jnp.concatenate(grads)
        out_ref[...] = whole_grad.astype(BF)
        scaled = (whole_grad * scale).astype(BF)
        grad_ref[...] = scaled
        own_ref[0:1, :] = jnp.sum(scaled.astype(F32)[:size], axis=0, keepdims=True)
        own_ref[1:2, :] = jnp.sum(grads[0], axis=0, keepdims=True)

    hidden = weight_ref.shape[1] // 2
    span = act_ref.shape[1]
    chunk = span // 2
    for cols in (slice(0, chunk), slice(chunk, 2 * chunk)):
        here = lanes(step * span + cols.start, chunk)
        there = lanes(hidden + step * span + cols.start, chunk)
        pre = dot(normed_ref[...], weight_ref[:, here], 1, 0) + bias_ref[:, cols]
        act_grad = dot(grad_ref[...], weight_ref[:, there], 1, 0)
        cdf = 0.5 * (1.0 + lax.erf(pre * SQRT_HALF))
        act_ref[:, cols] = (pre * cdf).astype(BF)
        slope = cdf + pre * (jnp.exp(-0.5 * pre * pre) * INV_ROOT_TWO_PI)
        pre_grad = (act_grad * slope).astype(BF)
        pre_ref[:, cols] = pre_grad
        sums_ref[:, cols] = jnp.sum(pre_grad.astype(F32), axis=0, keepdims=True)
    back = dot(pre_ref[...], weight_ref[:, lanes(step * span, span)], 1, 1)

    @pl.when(step == 0)
    def _():
        back_acc[...] = back

    @pl.when(step == pl.num_programs(0) - 1)
    def _():
        whole = back_acc[...] + back
        for j, ref in enumerate(backs):
            ref[...] = whole[j * size : (j + 1) * size].astype(BF)


def mlp(rows, normed, cots, lives, ids, bias, weights, group):
    size, width = normed[0].shape
    count, shards = len(normed), len(weights)
    length = count * size
    hidden = weights[0].shape[1] // 2
    laid = shards > 1
    step = hidden // 2

    def whole(*shape):
        return pl.BlockSpec(shape, lambda i: (0, 0))

    cols = pl.BlockSpec((length, step), lambda i: (0, i))
    return pl.pallas_call(
        lambda *refs: mlp_kernel(count, shards, group, *refs),
        grid=(2,),
        in_specs=[whole(*rows.shape)]
        + [whole(size, width)] * (2 * count)
        + [whole(size, 1)] * count
        + [SMEM, pl.BlockSpec((1, step), lambda i: (0, i))]
        + [whole(*piece.shape) for piece in weights],
        out_specs=[whole(size, width)] * count
        + [whole(length, width)] * 2
        + [cols, cols, pl.BlockSpec((1, step), lambda i: (0, i)), whole(8, width)]
        + [whole(width, 2 * hidden)] * laid,
        out_shape=[shaped((size, width), BF)] * count
        + [shaped((length, width), BF)] * 2
        + [shaped((length, hidden), BF)] * 2
        + [shaped((1, hidden), F32), shaped((8, width), F32)]
        + [shaped((width, 2 * hidden), BF)] * laid,
        scratch_shapes=[pltpu.VMEM((length, width), BF), pltpu.VMEM((length, width), F32)],
        compiler_params=PARAMS,
        cost_estimate=SMALL,
        name="mlp",
    )(rows, *normed, *cots, *lives, ids, bias, *weights)


def mlp_weights_kernel(
    direct, ids_ref, norm_a, norm_b, grad_a, grad_b, rows_ref, fc2_ref, pre_a, pre_b, act_a, act_b,
    own_ref, *rest
):
    keep_ref, send_ref, scale2_ref, *branches, out_ref = rest
    hidden = pre_a.shape[1]
    first = dot(norm_a[...], pre_a[...], 0, 0) + dot(norm_b[...], pre_b[...], 0, 0)
    out_ref[:, :hidden] = first
    outs = [grad_a[...].astype(F32), grad_b[...].astype(F32)]
    scaled = [(out * rows_ref[9:10, :]).astype(BF) for out in outs]
    second = dot(scaled[0], act_a[...], 0, 0) + dot(scaled[1], act_b[...], 0, 0)
    out_ref[:, hidden:] = second
    size = keep_ref.shape[0]
    if direct:
        side = ids_ref[1] & 1
        keep_ref[...] = out_ref[pl.ds(pl.multiple_of(side * size, size), size), :].astype(BF)
        other = pl.multiple_of((1 - side) * size, size)
        send_ref[...] = out_ref[pl.ds(other, size), :].astype(BF)
    else:
        keep_ref[...] = out_ref[:size, :].astype(BF)
        send_ref[...] = out_ref[size:, :].astype(BF)
    scale2 = own_ref[1:2, :] * rows_ref[8:9, :]
    count = len(branches) // 2
    size = branches[0].shape[0]
    for half, act in enumerate((act_a, act_b)):
        branch = dot(act[...], fc2_ref[...], 1, 1)
        scale2 = scale2 + jnp.sum(outs[half] * branch, axis=0, keepdims=True)
        for j in range(count):
            branches[half * count + j][...] = branch[j * size : (j + 1) * size].astype(BF)
    scale2_ref[...] = scale2


def mlp_weights(rows, own, normed, grads, pres, acts, weights, group, ids, direct):
    length, width = normed[0].shape
    hidden = pres[0].shape[1]
    size = 2 * length // group
    step = 256

    def at(i, ids_ref):
        return ((ids_ref[1] >> 1) ^ i) if direct else i

    cols = pl.BlockSpec((length, step), lambda i, ids_ref: (0, at(i, ids_ref)))
    whole = pl.BlockSpec((length, hidden), lambda i, ids_ref: (0, 0))

    def line(count):
        return pl.BlockSpec((count, step), lambda i, ids_ref: (0, at(i, ids_ref)))

    part = pl.BlockSpec((step // 2, 2 * hidden), lambda i, ids_ref: (i, 0))
    return pl.pallas_call(
        lambda *refs: mlp_weights_kernel(direct, *refs),
        grid_spec=pltpu.PrefetchScalarGridSpec(
            num_scalar_prefetch=1,
            grid=(width // step,),
            in_specs=[cols] * 4
            + [line(rows.shape[0])]
            + [pl.BlockSpec((step, hidden), lambda i, ids_ref: (at(i, ids_ref), 1))]
            + [whole] * 4
            + [line(own.shape[0])],
            out_specs=[part, part, line(1)] + [line(size)] * group,
            scratch_shapes=[pltpu.VMEM((step, 2 * hidden), F32)],
        ),
        out_shape=[shaped((width // 2, 2 * hidden), BF)] * 2
        + [shaped((1, width), F32)]
        + [shaped((size, width), BF)] * group,
        compiler_params=PARAMS,
        cost_estimate=SMALL,
        name="mlp_weights",
    )(ids, *normed, *grads, rows, weights, *pres, *acts, own)


def finish_kernel(rows_ref, middle_ref, *rest):
    terms, out_ref = rest[:-1], rest[-1]
    branch = terms[0][...].astype(F32)
    for ref in terms[1:]:
        branch = branch + ref[...].astype(F32)
    branch = branch + rows_ref[8:9, :]
    out_ref[...] = (middle_ref[...] + rows_ref[9:10, :] * branch).astype(BF)


def finish(rows, middle, terms):
    return pl.pallas_call(
        finish_kernel,
        in_specs=[VMEM] * (2 + len(terms)),
        out_specs=VMEM,
        out_shape=shaped(middle.shape, BF),
        compiler_params=PARAMS,
        name="finish",
    )(rows, middle, *terms)


def begin_kernel(rows_ref, tokens_ref, mean_ref, inv_ref, middle_ref, *rest):
    terms, out_ref = rest[:-1], rest[-1]
    grads = terms[0][...].astype(F32)
    for ref in terms[1:]:
        grads = grads + ref[...].astype(F32)
    inverse = inv_ref[...]
    unit = (tokens_ref[...].astype(F32) - mean_ref[...]) * inverse
    out_ref[...] = (middle_ref[...] + norm_back(grads, unit, inverse, rows_ref[0:1, :])).astype(BF)


def begin(rows, tokens, mean, inverse, middle_grad, terms):
    length, width = tokens.shape
    column = pl.BlockSpec((length, 1), lambda i: (0, 0))
    whole = pl.BlockSpec((length, width), lambda i: (0, 0))
    return pl.pallas_call(
        begin_kernel,
        grid=(1,),
        in_specs=[pl.BlockSpec(rows.shape, lambda i: (0, 0)), whole, column, column, whole]
        + [whole] * len(terms),
        out_specs=whole,
        out_shape=shaped((length, width), BF),
        compiler_params=PARAMS,
        name="begin",
    )(rows, tokens, mean, inverse, middle_grad, *terms)


def qkv_back_kernel(group, grad_ref, weight_ref, mean_ref, inv_ref, *rest):
    tokens, outs, sums_ref = rest[:group], rest[group:-1], rest[-1]
    size = tokens[0].shape[0]
    gain = shift = 0.0
    for first in range(0, group, 2):
        span = slice(first * size, (first + 2) * size)
        part = dot(grad_ref[span, :], weight_ref[...], 1, 1)
        inputs = jnp.concatenate([tokens[first][...].astype(F32), tokens[first + 1][...].astype(F32)])
        unit = (inputs - mean_ref[span, :]) * inv_ref[span, :]
        outs[first][...] = part[:size].astype(BF)
        outs[first + 1][...] = part[size:].astype(BF)
        gain = gain + jnp.sum(part * unit, axis=0, keepdims=True)
        shift = shift + jnp.sum(part, axis=0, keepdims=True)
    sums_ref[...] = jnp.zeros(sums_ref.shape, F32)
    sums_ref[0:1, :] = gain
    sums_ref[1:2, :] = shift


def qkv_back(qkv_grad, weight, tokens, mean, inverse):
    size, width = tokens[0].shape
    group = len(tokens)
    return pl.pallas_call(
        lambda *refs: qkv_back_kernel(group, *refs),
        in_specs=[VMEM] * (4 + group),
        out_specs=[VMEM] * (group + 1),
        out_shape=[shaped((size, width), BF)] * group + [shaped((8, width), F32)],
        compiler_params=PARAMS,
        cost_estimate=SMALL,
        name="qkv_back",
    )(qkv_grad, weight, mean, inverse, *tokens)


def attn_weights_kernel(
    direct, shard, terms, ids_ref, normed_ref, grad_ref, norm1_ref, sums_ref, turn_ref, fbias_ref,
    scale2_ref, bias_a_ref, bias_b_ref, *rest,
):
    projs, outs = rest[:terms], rest[terms:-4]
    rows_ref, turned_ref, block_ref, small_ref = rest[-4:]
    place, row = ids_ref[0], ids_ref[1]
    width = normed_ref.shape[1]
    part = projs[0].shape[1]
    rows_ref[...] = jnp.zeros(rows_ref.shape, F32)
    rows_ref[0:2, :] = norm1_ref[0:2, :]
    for pair in range(part // PAIR):
        where = lanes(place * part + pair * PAIR, PAIR)
        rows_ref[2:3, where] = sums_ref[pair, :, :PAIR]
        rows_ref[3:4, where] = sums_ref[pair, :, 2 * PAIR :]
    rows_ref[4:8, :] = turn_ref[0:4, :]
    rows_ref[8:9, :] = fbias_ref[0:1, :]
    rows_ref[9:10, :] = scale2_ref[...]
    cols = bias_a_ref.shape[1] // part
    for owner in range(part // shard):
        for line in range(cols):
            spot = (owner * cols + line) * shard
            small_ref[line : line + 1, owner * shard : (owner + 1) * shard] = (
                bias_a_ref[0:1, spot : spot + shard] + bias_b_ref[0:1, spot : spot + shard]
            )
    rows_ref[10 : 10 + cols, lanes(place * part, part)] = small_ref[0:cols, :]
    turned_ref[...] = rows_ref[...].T
    step = block_ref.shape[0]
    for k in range(width // step):
        start = pl.multiple_of(((row >> 1) ^ k) * step, step) if direct else k * step
        cols = pl.ds(start, step)
        block_ref[:, : 3 * part] = dot(normed_ref[:, cols], grad_ref[...], 0, 0)
        proj = projs[0][cols, :].astype(F32)
        for ref in projs[1:]:
            proj = proj + ref[cols, :].astype(F32)
        block_ref[:, 3 * part : 4 * part] = proj
        block_ref[:, 4 * part :] = turned_ref[cols, :]
        if direct:
            size = step // 2
            side = row & 1
            outs[2 * k][...] = block_ref[pl.ds(pl.multiple_of(side * size, size), size), :].astype(BF)
            outs[2 * k + 1][...] = block_ref[
                pl.ds(pl.multiple_of((1 - side) * size, size), size), :
            ].astype(BF)
        else:
            outs[0][k * step : (k + 1) * step, :] = block_ref[...].astype(BF)


def attn_weights(ids, normed1, qkv_grad, sums, projs, blocks, shard):
    length, width = normed1.shape
    part = projs[0].shape[1]
    columns = 4 * part + EXTRA
    direct = blocks > 0
    step = 2 * (width // blocks) if direct else 256
    out_shape = [shaped((width // blocks, columns), BF)] * blocks if direct else [
        shaped((width, columns), BF)
    ]
    return pl.pallas_call(
        lambda *refs: attn_weights_kernel(direct, shard, len(projs), *refs),
        in_specs=[SMEM] + [VMEM] * (2 + len(sums) + len(projs)),
        out_specs=[VMEM] * len(out_shape),
        out_shape=out_shape,
        scratch_shapes=[
            pltpu.VMEM((EXTRA, width), F32),
            pltpu.VMEM((width, EXTRA), F32),
            pltpu.VMEM((step, columns), F32),
            pltpu.VMEM((8, part), F32),
        ],
        compiler_params=PARAMS,
        cost_estimate=SMALL,
        name="attn_weights",
    )(ids, normed1, qkv_grad, *sums, *projs)


def total(ids, terms, group):
    size, columns = terms[0].shape
    rows = size // group

    def kernel(ids_ref, *refs):
        ins, outs, sum_ref = refs[: len(terms)], refs[len(terms) : -1], refs[-1]
        value = ins[0][...].astype(F32)
        for ref in ins[1:]:
            value = value + ref[...].astype(F32)
        sum_ref[...] = value
        for k, out in enumerate(outs):
            start = pl.multiple_of((ids_ref[0] ^ k) * rows, rows)
            out[...] = sum_ref[pl.ds(start, rows), :].astype(BF)

    return pl.pallas_call(
        kernel,
        in_specs=[SMEM] + [VMEM] * len(terms),
        out_specs=[VMEM] * group,
        out_shape=[shaped((rows, columns), BF)] * group,
        scratch_shapes=[pltpu.VMEM((size, columns), F32)],
        compiler_params=PARAMS,
        name="total",
    )(ids, *terms)


def place_attn_kernel(ids_ref, *refs):
    group = len(refs) - 4
    blocks, (qkv_ref, proj_ref, vec_ref, bias_ref) = refs[:group], refs[group:]
    width = proj_ref.shape[1]
    part = width // group
    extra = jnp.zeros((qkv_ref.shape[0], EXTRA), F32)
    for k, block in enumerate(blocks):
        source = ids_ref[0] ^ k
        for third in range(3):
            for pair in range(part // PAIR):
                spot = (pair * 3 + third) * PAIR
                where = lanes(third * width + source * part + pair * PAIR, PAIR)
                qkv_ref[:, where] = block[:, spot : spot + PAIR].astype(F32)
        proj_ref[:, lanes(source * part, part)] = block[:, 3 * part : 4 * part].astype(F32)
        extra = extra + block[:, 4 * part :].astype(F32)
    turned = extra.T
    count = vec_ref.shape[0]
    vec_ref[...] = turned[:count]
    rows = qkv_ref.shape[0]
    for line in range(bias_ref.shape[1] // rows):
        bias_ref[0:1, line * rows : (line + 1) * rows] = turned[count + line : count + line + 1]


def place_attn(ids, blocks, width, vector_count, bias_cols):
    rows = blocks[0].shape[0]
    return pl.pallas_call(
        place_attn_kernel,
        in_specs=[SMEM] + [VMEM] * len(blocks),
        out_specs=[VMEM] * 4,
        out_shape=[
            shaped((rows, 3 * width), F32),
            shaped((rows, width), F32),
            shaped((vector_count, rows), F32),
            shaped((1, bias_cols * rows), F32),
        ],
        compiler_params=PARAMS,
        name="place_attn",
    )(ids, *blocks)


def place_mlp_kernel(ids_ref, *refs):
    group = len(refs) - 2
    blocks, (fc1_ref, fc2_ref) = refs[:group], refs[group:]
    part = fc1_ref.shape[1] // group
    for k, block in enumerate(blocks):
        where = lanes((ids_ref[0] ^ k) * part, part)
        fc1_ref[:, where] = block[:, :part].astype(F32)
        fc2_ref[:, where] = block[:, part:].astype(F32)


def place_mlp(ids, blocks, hidden):
    rows = blocks[0].shape[0]
    return pl.pallas_call(
        place_mlp_kernel,
        in_specs=[SMEM] + [VMEM] * len(blocks),
        out_specs=[VMEM] * 2,
        out_shape=[shaped((rows, hidden), F32)] * 2,
        compiler_params=PARAMS,
        name="place_mlp",
    )(ids, *blocks)


def local(tokens, counts, w_qkv, w_proj, w_fc1, fc1_bias, w_fc2, vectors, cotangent):
    _, capacity, width = tokens.shape
    hidden = w_fc1.shape[1]
    rows = w_qkv.shape[0]
    group, replicas = lax.axis_size("ctx"), lax.axis_size("dp")
    place, replica = lax.axis_index("ctx"), lax.axis_index("dp")
    ids = jnp.stack([place, replica]).astype(jnp.int32)
    head_width = width // group
    hidden_part = hidden // group
    bias_cols = hidden // width
    vector_count = vectors.shape[0]
    direct = replicas <= 8

    def swap(value, bit, axis="ctx"):
        size = group if axis == "ctx" else replicas
        return lax.ppermute(value, axis, [(i, i ^ bit) for i in range(size)])

    def after(value, *before):
        return lax.optimization_barrier((value,) + before)[0]

    def gather(own, *before):
        pieces = [own]
        for j in range(1, group):
            bit = j & -j
            source = pieces[j ^ bit]
            pieces.append(swap(after(source, *before) if j ^ bit else source, bit))
        return pieces

    def scatter(parts, *before, mids=None, axis="ctx", scale=1, gates=None):
        pieces = {j: [part] for j, part in enumerate(parts)}

        def added(terms):
            if len(terms) == 1:
                return terms[0]
            return sum(term.astype(F32) for term in terms).astype(BF)

        bit = 1
        sent = []
        while bit < len(parts):
            for j in sorted((j for j in pieces if j & bit), reverse=True):
                value = added(pieces.pop(j))
                if bit > 1:
                    if mids is not None:
                        mids.append(value)
                    value = after(value, *before)
                elif axis == "dp":
                    value = after(value, *sent[-2:-1])
                if gates and bit in gates:
                    value = after(value, *gates[bit])
                sent.append(swap(value, bit * scale, axis))
                pieces[j ^ bit].append(sent[-1])
            bit *= 2
        return pieces[0]

    def exchange(relative):
        return [relative[0]] + [swap(relative[k], k) for k in range(1, group)]

    def in_order(relative):
        stacked = jnp.stack(relative)
        return jnp.concatenate(
            [lax.dynamic_index_in_dim(stacked, place ^ s, 0, False) for s in range(group)], axis=0
        )

    cuts = cut(
        ids, counts, w_qkv, w_proj.T, w_fc1, w_fc2.T, vectors, fc1_bias.reshape(1, -1), group
    )
    first = exchange(cuts[:group])
    tokens_far = swap(after(tokens[0], *first), group // 2)

    def widen(shards, *before):
        for m in range(2, replicas):
            low = m & -m
            if m ^ low:
                shards[m] = swap(after(shards[m ^ low], *before), low, "dp")

    if direct:
        shards = {0: jnp.concatenate(first, axis=0)}
        bits = [bit for bit in (4, 2, 1) if bit < replicas]
        for bit in bits:
            shards[bit] = swap(shards[0], bit, "dp")
        arrived = [tokens_far] + [shards[bit] for bit in bits]
        widen(shards, *arrived)
        first_pieces = [shards[m] for m in range(replicas)]
        arrived = arrived + [shards[m] for m in (3, 6) if m < replicas]
    else:
        first_pieces = [lax.all_gather(in_order(first), "dp", axis=0, tiled=True)]
        arrived = [tokens_far]
    second = exchange([after(block, *arrived) for block in cuts[group:]])
    tokens_pieces = [tokens[0]]
    for j in range(1, group):
        source = tokens_pieces[j ^ (j & -j)]
        if j == group // 2:
            tokens_pieces.append(tokens_far)
        else:
            tokens_pieces.append(swap(after(source, *arrived), j & -j))
    cotangent_far = swap(after(cotangent[0], *second), group // 2)
    if direct:
        shards = {0: after(jnp.concatenate(second, axis=0), first_pieces[-2])}
        for bit in bits:
            shards[bit] = swap(shards[0], bit, "dp")
        widen(shards)
        second_pieces = [shards[m] for m in range(replicas)]
        early, later = [shards[1], shards[2]], [shards[3], cotangent_far]
    else:
        early, later = [], [cotangent_far]
        second_pieces = [lax.all_gather(in_order(second), "dp", axis=0, tiled=True)]
    tokens_own = after(tokens[0], *early)
    count_column = vector_count + bias_cols
    (
        weight_qkv, weight_proj, vector_rows, normed1, qkv, mean1, inverse1, bias_fc1, key_bias,
        *live,
    ) = project(
        ids, [tokens_own] + tokens_pieces[1:], first, first_pieces, hidden_part, count_column,
        0 if direct else rows,
    )

    cotangent_pieces = [cotangent[0]]
    for j in range(1, group):
        source = cotangent_pieces[j ^ (j & -j)]
        if j == group // 2:
            cotangent_pieces.append(cotangent_far)
        else:
            cotangent_pieces.append(swap(after(source, qkv), j & -j))
    attended, lse, *attended_low = attend(after(qkv, *later), key_bias, group)
    projs = gather(weight_proj, lse)
    attended_own = exchange(attended_low)
    branch1, middle, normed2_own, unit2, inverse2 = middle_step(
        vector_rows, tokens[0], attended_own, projs
    )
    half = group // 2
    normed2 = [normed2_own]
    while len(normed2) < half:
        normed2 += [swap(piece, len(normed2)) for piece in normed2]

    def feed(where, pieces, weights):
        return mlp(
            vector_rows, pieces, cotangent_pieces[where], live[where], ids, bias_fc1, weights, group
        )

    near = list(feed(slice(0, half), normed2, second_pieces))
    if len(second_pieces) > 1:
        second_all = near.pop()
    else:
        second_all = second_pieces[0]
    *backs_near, norm_near, grad_near, act_near, pre_near, sums_near, own_sums = near
    normed2_far = [swap(normed2_own, half)]
    while len(normed2_far) < half:
        normed2_far += [
            swap(after(piece, sums_near), len(normed2_far)) for piece in normed2_far
        ]
    *backs_far, norm_far, grad_far, act_far, pre_far, sums_far, _ = feed(
        slice(half, group), normed2_far, [second_all]
    )
    mids = []
    norm2_terms = scatter(backs_near + backs_far, mids=mids)
    keep_mlp, send_mlp, grad_scale2, *branches = mlp_weights(
        vector_rows, own_sums, [norm_near, norm_far], [grad_near, grad_far], [after(pre_near, *mids), pre_far],
        [act_near, act_far], second_all, group, ids, direct,
    )
    other_mlp = None
    if direct:
        other_mlp = swap(after(send_mlp, *norm2_terms), 1, "dp")
    middle_grad, branch_grad, turn_sums, *att_grads = turn(
        vector_rows, live[0], cotangent[0], unit2, inverse2, branch1, norm2_terms, projs
    )
    att_grads = exchange(att_grads)
    mids = []
    proj_terms = scatter(proj_weights(branch_grad, attended_own), *att_grads, mids=mids)
    branch2_terms = scatter([after(part, *att_grads) for part in branches], *att_grads)
    qkv_grad, qkv_sums = attend_back(qkv, key_bias, attended, after(lse, *mids), att_grads)
    sums = []
    if direct:
        other = after(other_mlp, qkv_grad)
        size = group * rows
        blocks = [slice(k * size, (k + 1) * size) for k in range(replicas // 2)]
        sums = [
            (keep_mlp[block].astype(F32) + other[block].astype(F32)).astype(BF) for block in blocks
        ]
        owned_mlp = scatter(sums, axis="dp", scale=2)
    else:
        ordered = jnp.stack(
            [part.reshape(-1, 128, 2 * hidden_part) for part in (keep_mlp, send_mlp)], axis=1
        )
        owned_mlp = lax.psum_scatter(
            ordered.reshape(width, 2 * hidden_part), "dp", scatter_dimension=0, tiled=True
        )
    *norm1_parts, norm1_sums = qkv_back(after(qkv_grad, *sums), weight_qkv, tokens_pieces, mean1, inverse1)
    parts = attn_weights(
        ids, normed1, qkv_grad,
        [norm1_sums, qkv_sums, turn_sums, own_sums, grad_scale2, sums_near, sums_far],
        proj_terms, replicas if direct else 0, rows,
    )
    norm1_terms = scatter(norm1_parts)
    if direct:
        gates = {2: [owned_mlp[1], branch2_terms[-1]], 4: [owned_mlp[-1], norm1_terms[-1]]}
        terms = scatter(parts, axis="dp", gates=gates)
        cuts_mlp = total(after(ids, *terms), owned_mlp, group)
    else:
        owned_attn = lax.psum_scatter(parts[0], "dp", scatter_dimension=0, tiled=True)

        def relative(owned):
            blocks = owned.reshape(group, rows, -1)
            return [lax.dynamic_index_in_dim(blocks, place ^ k, 0, False) for k in range(group)]

        cuts_mlp = relative(owned_mlp)
    out_fc1, out_fc2 = place_mlp(ids, exchange(cuts_mlp), hidden)
    if direct:
        cuts_attn = total(ids, terms, group)
    else:
        cuts_attn = relative(owned_attn)

    input_grad = begin(
        vector_rows, after(tokens[0], *cuts_attn), mean1, inverse1, middle_grad, norm1_terms
    )
    output = finish(after(vector_rows, *cuts_attn), middle, branch2_terms)
    out_qkv, out_proj, out_vectors, out_bias = place_attn(
        ids, exchange(cuts_attn), width, vector_count, bias_cols
    )
    return (
        output[None],
        input_grad[None],
        out_qkv,
        out_proj.T,
        out_fc1,
        out_bias.reshape(-1),
        out_fc2.T,
        out_vectors,
    )


def solution(mesh):
    both = ("dp", "ctx")
    in_specs = (
        P("dp", "ctx", None),
        P("dp", "ctx"),
        P(both, None),
        P(None, both),
        P(both, None),
        P(both),
        P(None, both),
        P(None, both),
        P("dp", "ctx", None),
    )
    out_specs = (
        P("dp", "ctx", None),
        P("dp", "ctx", None),
        P(both, None),
        P(None, both),
        P(both, None),
        P(both),
        P(None, both),
        P(None, both),
    )
    return jax.shard_map(local, mesh=mesh, in_specs=in_specs, out_specs=out_specs, check_vma=False)
```

```python
import jax
import jax.numpy as jnp
from jax import lax
from jax.experimental import pallas as pl
from jax.experimental.pallas import tpu as pltpu
from jax.sharding import PartitionSpec as P

HD = 64
PAIR = 2 * HD
EXTRA = 128
EPSILON = 1e-06
MASKED_SCORE = -1e30
SQRT_HALF = 0.7071067811865476
INV_ROOT_TWO_PI = 0.3989422804014327
BF = jnp.bfloat16
F32 = jnp.float32
PARAMS = pltpu.CompilerParams(vmem_limit_bytes=60 * 1024 * 1024)
SMALL = pl.CostEstimate(flops=1_000_000_000, bytes_accessed=1_000_000, transcendentals=0)
VMEM = pl.BlockSpec(memory_space=pltpu.VMEM)
SMEM = pl.BlockSpec(memory_space=pltpu.SMEM)


def shaped(shape, dtype):
    return jax.ShapeDtypeStruct(shape, dtype)


def dot(left, right, left_dim, right_dim):
    return lax.dot_general(
        left, right, (((left_dim,), (right_dim,)), ((), ())), preferred_element_type=F32
    )


def lanes(start, size):
    return pl.ds(pl.multiple_of(start, 128), size)


def unit_rows(inputs):
    centered = inputs - jnp.mean(inputs, axis=-1, keepdims=True)
    spread = jnp.mean(centered * centered, axis=-1, keepdims=True)
    inverse = lax.rsqrt(spread + EPSILON)
    return (centered * inverse, inverse)


def norm_back(grad_in, unit, inverse, gain):
    scaled = grad_in * gain
    inner = (
        scaled
        - jnp.mean(scaled, axis=-1, keepdims=True)
        - unit * jnp.mean(scaled * unit, axis=-1, keepdims=True)
    )
    return inner * inverse


def cut_kernel(ids_ref, count_ref, qkv_ref, proj_ref, fc1_ref, fc2_ref, vec_ref, bias_ref, *rest):
    outs, (extra_ref, turn_ref) = rest[:-2], rest[-2:]
    group = len(outs) // 2
    place = ids_ref[0]
    width = proj_ref.shape[1]
    part = width // group
    hidden_part = fc1_ref.shape[1] // group
    vector_count, bias_cols = vec_ref.shape[0], bias_ref.shape[1] // vec_ref.shape[1]
    column = vector_count + bias_cols
    lane = lax.broadcasted_iota(jnp.int32, extra_ref.shape, 1)
    count = count_ref[0, 0]
    high = (count >> 7).astype(F32)
    low = (count & 127).astype(F32)
    extra_ref[...] = jnp.where(lane == column, high, jnp.where(lane == column + 1, low, 0.0))
    extra_ref[:, :vector_count] = vec_ref[...].astype(F32).T
    rows = qkv_ref.shape[0]
    for line in range(bias_cols):
        turn_ref[line : line + 1, :] = bias_ref[0:1, line * rows : (line + 1) * rows].astype(F32)
    extra_ref[:, vector_count:column] = turn_ref[0:bias_cols, :].T
    extra = extra_ref[...].astype(BF)
    for k in range(group):
        target = place ^ k
        first, second = outs[k], outs[group + k]
        for third in range(3):
            for pair in range(part // PAIR):
                spot = (pair * 3 + third) * PAIR
                first[:, spot : spot + PAIR] = qkv_ref[
                    :, lanes(third * width + target * part + pair * PAIR, PAIR)
                ]
        first[:, 3 * part : 4 * part] = proj_ref[:, lanes(target * part, part)]
        first[:, 4 * part :] = extra
        second[:, :hidden_part] = fc1_ref[:, lanes(target * hidden_part, hidden_part)]
        second[:, hidden_part:] = fc2_ref[:, lanes(target * hidden_part, hidden_part)]


def cut(ids, counts, w_qkv, w_proj_t, w_fc1, w_fc2_t, vectors, bias, group):
    rows, width = w_proj_t.shape
    part, hidden_part = width // group, w_fc1.shape[1] // group
    return pl.pallas_call(
        cut_kernel,
        in_specs=[SMEM, SMEM] + [VMEM] * 6,
        out_specs=[VMEM] * (2 * group),
        out_shape=[shaped((rows, 4 * part + EXTRA), BF)] * group
        + [shaped((rows, 2 * hidden_part), BF)] * group,
        scratch_shapes=[pltpu.VMEM((rows, EXTRA), F32), pltpu.VMEM((8, rows), F32)],
        compiler_params=PARAMS,
        name="cut",
    )(ids, counts, w_qkv, w_proj_t, w_fc1, w_fc2_t, vectors, bias)


def project_kernel(ordered, group, count_column, ids_ref, *rest):
    tokens, blocks, rest = rest[:group], rest[group : 2 * group], rest[2 * group :]
    pieces, outs, lives, scratch = (
        rest[: -12 - group], rest[-12 - group : -3 - group], rest[-3 - group : -3], rest[-3:]
    )
    qkv_w, proj_w, rows_ref, normed_ref, out_ref, mean_ref, inv_ref, fc1_ref, key_ref = outs
    extra_ref, bias_ref, small_ref = scratch
    place, row = ids_ref[0], ids_ref[1]
    capacity, width = tokens[0].shape
    part = proj_w.shape[1]
    size = pieces[0].shape[0]

    def lay(block, start, count):
        where = pl.ds(start, count)
        qkv_w[where, :] = block[:, : 3 * part]
        proj_w[where, :] = block[:, 3 * part : 4 * part]
        extra_ref[where, :] = block[:, 4 * part :].astype(F32)

    if ordered:
        lay(pieces[0], 0, size)
        shard = ordered
    else:
        sub = shard = size // group
        for m, piece in enumerate(pieces):
            for j in range(group):
                start = (row ^ m) * size + (place ^ j) * sub
                lay(piece.at[j * sub : (j + 1) * sub], pl.multiple_of(start, sub), sub)
    slot = lax.broadcasted_iota(jnp.int32, (capacity, 1), 0).astype(F32)
    for j, (block, live_ref) in enumerate(zip(blocks, lives)):
        extra = block[:, 4 * part :].astype(F32)[0:1, :]
        bound = extra[:, count_column : count_column + 1] * 128.0
        bound = bound + extra[:, count_column + 1 : count_column + 2]
        live = jnp.where(slot < bound, 1.0, 0.0)
        live_ref[...] = live
        key_ref[j * capacity : (j + 1) * capacity, :] = (1.0 - live) * MASKED_SCORE
    turned = extra_ref[...].T
    rows_ref[...] = turned[: rows_ref.shape[0]]
    bias_ref[...] = jnp.zeros(bias_ref.shape, F32)
    for pair in range(part // PAIR):
        for third, line in ((0, 2), (2, 3)):
            spot = (pair * 3 + third) * PAIR
            bias_ref[0:1, spot : spot + PAIR] = rows_ref[
                line : line + 1, lanes(place * part + pair * PAIR, PAIR)
            ]
    cols = fc1_ref.shape[1] // part
    small_ref[0:cols, :] = rows_ref[10 : 10 + cols, lanes(place * part, part)]
    for owner in range(part // shard):
        for line in range(cols):
            spot = (owner * cols + line) * shard
            fc1_ref[0:1, spot : spot + shard] = small_ref[
                line : line + 1, owner * shard : (owner + 1) * shard
            ]
    gain, shift, bias = rows_ref[0:1, :], rows_ref[1:2, :], bias_ref[0:1, :]
    for first in range(0, group, 2):
        span = slice(first * capacity, (first + 2) * capacity)
        inputs = jnp.concatenate([tokens[first][...].astype(F32), tokens[first + 1][...].astype(F32)])
        mean = jnp.mean(inputs, axis=-1, keepdims=True)
        centered = inputs - mean
        inverse = lax.rsqrt(jnp.mean(centered * centered, axis=-1, keepdims=True) + EPSILON)
        normed = (centered * inverse * gain + shift).astype(BF)
        normed_ref[span, :] = normed
        mean_ref[span, :] = mean
        inv_ref[span, :] = inverse
        out_ref[span, :] = (dot(normed, qkv_w[...], 1, 0) + bias).astype(BF)


def project(ids, tokens, blocks, pieces, hidden_part, count_column, ordered):
    capacity, width = tokens[0].shape
    group = len(tokens)
    length = group * capacity
    part = width // group
    return pl.pallas_call(
        lambda *refs: project_kernel(ordered, group, count_column, *refs),
        in_specs=[SMEM] + [VMEM] * (2 * group + len(pieces)),
        out_specs=[VMEM] * (9 + group),
        out_shape=[
            shaped((width, 3 * part), BF),
            shaped((width, part), BF),
            shaped((16, width), F32),
            shaped((length, width), BF),
            shaped((length, 3 * part), BF),
            shaped((length, 1), F32),
            shaped((length, 1), F32),
            shaped((1, hidden_part), F32),
            shaped((length, 1), F32),
        ]
        + [shaped((capacity, 1), F32)] * group,
        scratch_shapes=[
            pltpu.VMEM((width, EXTRA), F32),
            pltpu.VMEM((8, 3 * part), F32),
            pltpu.VMEM((8, part), F32),
        ],
        compiler_params=PARAMS,
        cost_estimate=SMALL,
        name="project",
    )(ids, *tokens, *blocks, *pieces)


def query_chunks(length):
    step = 512
    return [(start, min(step, length - start)) for start in range(0, length, step)]


def attend_kernel(qkv_ref, bias_ref, out_ref, lse_ref, *lows):
    length = qkv_ref.shape[0]
    key_bias = bias_ref[...]
    for head in range(2):
        keys = qkv_ref[:, PAIR + head * HD : PAIR + (head + 1) * HD]
        values = qkv_ref[:, 2 * PAIR + head * HD : 2 * PAIR + (head + 1) * HD]
        for start, size in query_chunks(length):
            queries = qkv_ref[start : start + size, head * HD : (head + 1) * HD]
            queries = queries * jnp.asarray(HD**-0.5, BF)
            scores = dot(keys, queries, 1, 1) + key_bias
            top = jnp.max(scores, axis=0, keepdims=True)
            expo = jnp.exp(scores - top)
            total = jnp.sum(expo, axis=0, keepdims=True)
            mixed = (dot(values, expo.astype(BF), 0, 0) / total).T
            out_ref[start : start + size, head * HD : (head + 1) * HD] = mixed
            lse_ref[0, head : head + 1, start : start + size] = top + jnp.log(total)
    for j, low in enumerate(lows):
        size = low.shape[0]
        low[...] = out_ref[j * size : (j + 1) * size, :].astype(BF)


def attend(qkv, key_bias, group):
    length, columns = qkv.shape
    pairs = columns // (3 * PAIR)
    return pl.pallas_call(
        attend_kernel,
        grid=(pairs,),
        in_specs=[
            pl.BlockSpec((length, 3 * PAIR), lambda p: (0, p)),
            pl.BlockSpec((length, 1), lambda p: (0, 0)),
        ],
        out_specs=[
            pl.BlockSpec((length, PAIR), lambda p: (0, p)),
            pl.BlockSpec((1, 2, length), lambda p: (p, 0, 0)),
        ]
        + [pl.BlockSpec((length // group, PAIR), lambda p: (0, p))] * group,
        out_shape=[
            shaped((length, pairs * PAIR), F32),
            shaped((pairs, 2, length), F32),
        ]
        + [shaped((length // group, pairs * PAIR), BF)] * group,
        compiler_params=PARAMS,
        cost_estimate=SMALL,
        name="attend",
    )(qkv, key_bias)


def attend_back_kernel(qkv_ref, bias_ref, att_ref, lse_ref, *rest):
    pieces, (out_ref, sums_ref, grad_ref) = rest[:-3], rest[-3:]
    length = qkv_ref.shape[0]
    size = pieces[0].shape[0]
    factor = HD**-0.5
    key_bias = bias_ref[...]
    for j, piece in enumerate(pieces):
        grad_ref[j * size : (j + 1) * size, :] = piece[...].astype(F32)
    for head in range(2):
        low, high = head * HD, (head + 1) * HD
        keys = qkv_ref[:, PAIR + low : PAIR + high]
        values = qkv_ref[:, 2 * PAIR + low : 2 * PAIR + high]
        key_grad = jnp.zeros((length, HD), F32)
        value_grad = jnp.zeros((length, HD), F32)
        for start, size in query_chunks(length):
            rows = slice(start, start + size)
            queries = qkv_ref[rows, low:high] * jnp.asarray(factor, BF)
            product = grad_ref[rows, low:high] * att_ref[rows, low:high]
            grads = grad_ref[rows, low:high].astype(BF)
            delta = jnp.sum(product.T, axis=0, keepdims=True)
            scores = dot(keys, queries, 1, 1) + key_bias
            probs = jnp.exp(scores - lse_ref[0, head : head + 1, rows])
            value_grad += dot(probs.astype(BF), grads, 1, 0)
            raw = (probs * (dot(values, grads, 1, 1) - delta)).astype(BF)
            key_grad += dot(raw, queries, 1, 0)
            query_grad = dot(keys, raw, 0, 0).T * factor
            out_ref[rows, low:high] = query_grad.astype(BF)
        out_ref[:, PAIR + low : PAIR + high] = key_grad.astype(BF)
        out_ref[:, 2 * PAIR + low : 2 * PAIR + high] = value_grad.astype(BF)
    sums_ref[0] = jnp.sum(out_ref[...].astype(F32), axis=0, keepdims=True)


def attend_back(qkv, key_bias, attended, lse, pieces):
    length, columns = qkv.shape
    pairs = columns // (3 * PAIR)
    size = pieces[0].shape[0]
    return pl.pallas_call(
        attend_back_kernel,
        grid=(pairs,),
        in_specs=[
            pl.BlockSpec((length, 3 * PAIR), lambda p: (0, p)),
            pl.BlockSpec((length, 1), lambda p: (0, 0)),
            pl.BlockSpec((length, PAIR), lambda p: (0, p)),
            pl.BlockSpec((1, 2, length), lambda p: (p, 0, 0)),
        ]
        + [pl.BlockSpec((size, PAIR), lambda p: (0, p))] * len(pieces),
        out_specs=[
            pl.BlockSpec((length, 3 * PAIR), lambda p: (0, p)),
            pl.BlockSpec((1, 1, 3 * PAIR), lambda p: (p, 0, 0)),
        ],
        out_shape=[shaped((length, columns), BF), shaped((pairs, 1, 3 * PAIR), F32)],
        scratch_shapes=[pltpu.VMEM((length, PAIR), F32)],
        compiler_params=PARAMS,
        cost_estimate=SMALL,
        name="attend_back",
    )(qkv, key_bias, attended, lse, *pieces)


def middle_kernel(group, rows_ref, tokens_ref, *rest):
    parts, weights, (branch_ref, middle_ref, normed_ref, unit_ref, inv_ref) = (
        rest[:group], rest[group : 2 * group], rest[2 * group :]
    )
    branch = dot(parts[0][...], weights[0][...], 1, 1)
    for part, weight in zip(parts[1:], weights[1:]):
        branch = branch + dot(part[...], weight[...], 1, 1)
    branch = branch + rows_ref[4:5, :]
    branch_ref[...] = branch
    middle = tokens_ref[...].astype(F32) + rows_ref[5:6, :] * branch
    middle_ref[...] = middle
    unit, inverse = unit_rows(middle)
    unit_ref[...] = unit
    inv_ref[...] = inverse
    normed_ref[...] = (unit * rows_ref[6:7, :] + rows_ref[7:8, :]).astype(BF)


def middle_step(rows, tokens, parts, weights):
    length, width = tokens.shape
    group = len(parts)
    full = shaped((length, width), F32)
    return pl.pallas_call(
        lambda *refs: middle_kernel(group, *refs),
        in_specs=[VMEM] * (2 + 2 * group),
        out_specs=[VMEM] * 5,
        out_shape=[full, full, shaped((length, width), BF), full, shaped((length, 1), F32)],
        compiler_params=PARAMS,
        cost_estimate=SMALL,
        name="middle",
    )(rows, tokens, *parts, *weights)


def turn_kernel(group, terms, rows_ref, live_ref, cot_ref, unit_ref, inv_ref, branch_ref, *rest):
    backs, weights, outs = rest[:terms], rest[terms : terms + group], rest[terms + group :]
    middle_ref, grad_ref, sums_ref = outs[:3]
    norm_grad = backs[0][...].astype(F32)
    for ref in backs[1:]:
        norm_grad = norm_grad + ref[...].astype(F32)
    unit = unit_ref[...]
    out_grad = cot_ref[...].astype(F32) * live_ref[...]
    middle = out_grad + norm_back(norm_grad, unit, inv_ref[...], rows_ref[6:7, :])
    middle_ref[...] = middle
    low = (middle * rows_ref[5:6, :]).astype(BF)
    grad_ref[...] = low
    sums_ref[...] = jnp.zeros(sums_ref.shape, F32)
    sums_ref[0:1, :] = jnp.sum(low.astype(F32), axis=0, keepdims=True)
    sums_ref[1:2, :] = jnp.sum(middle * branch_ref[...], axis=0, keepdims=True)
    sums_ref[2:3, :] = jnp.sum(norm_grad * unit, axis=0, keepdims=True)
    sums_ref[3:4, :] = jnp.sum(norm_grad, axis=0, keepdims=True)
    for out, weight in zip(outs[3:], weights):
        out[...] = dot(low, weight[...], 1, 0).astype(BF)


def turn(rows, live, cotangent, unit, inverse, branch, backs, weights):
    length, width = cotangent.shape
    part = weights[0].shape[1]
    group = len(weights)
    return pl.pallas_call(
        lambda *refs: turn_kernel(group, len(backs), *refs),
        in_specs=[VMEM] * (6 + len(backs) + group),
        out_specs=[VMEM] * (3 + group),
        out_shape=[shaped((length, width), F32), shaped((length, width), BF), shaped((8, width), F32)]
        + [shaped((length, part), BF)] * group,
        compiler_params=PARAMS,
        cost_estimate=SMALL,
        name="turn",
    )(rows, live, cotangent, unit, inverse, branch, *backs, *weights)


def proj_weights_kernel(grad_ref, *rest):
    half = len(rest) // 2
    for part, out in zip(rest[:half], rest[half:]):
        out[...] = dot(grad_ref[...], part[...], 0, 0).astype(BF)


def proj_weights(grads, parts):
    length, width = grads.shape
    part = parts[0].shape[1]
    return pl.pallas_call(
        proj_weights_kernel,
        in_specs=[VMEM] * (1 + len(parts)),
        out_specs=[VMEM] * len(parts),
        out_shape=[shaped((width, part), BF)] * len(parts),
        compiler_params=PARAMS,
        cost_estimate=SMALL,
        name="proj_weights",
    )(grads, *parts)


def mlp_kernel(count, shards, group, rows_ref, *rest):
    normed_in, cots, lives = rest[:count], rest[count : 2 * count], rest[2 * count : 3 * count]
    ids_ref, bias_ref = rest[3 * count : 3 * count + 2]
    rest = rest[3 * count + 2 :]
    pieces, backs, rest = rest[:shards], rest[shards : shards + count], rest[shards + count :]
    normed_ref, out_ref, act_ref, pre_ref, sums_ref, own_ref = rest[:6]
    if shards > 1:
        weight_ref, grad_ref, back_acc = rest[6:]
    else:
        weight_ref = pieces[0]
        grad_ref, back_acc = rest[6:]
    step = pl.program_id(0)
    size = cots[0].shape[0]

    @pl.when(step == 0)
    def _():
        if shards > 1:
            whole_size = pieces[0].shape[0]
            sub = whole_size // group
            for m, piece in enumerate(pieces):
                for j in range(group):
                    start = (ids_ref[1] ^ m) * whole_size + (ids_ref[0] ^ j) * sub
                    weight_ref[pl.ds(pl.multiple_of(start, sub), sub), :] = piece[
                        j * sub : (j + 1) * sub, :
                    ]
        normed_ref[...] = jnp.concatenate([ref[...].astype(F32) for ref in normed_in]).astype(BF)
        scale = rows_ref[9:10, :]
        grads = [cot[...].astype(F32) * live[...] for cot, live in zip(cots, lives)]
        whole_grad = jnp.concatenate(grads)
        out_ref[...] = whole_grad.astype(BF)
        scaled = (whole_grad * scale).astype(BF)
        grad_ref[...] = scaled
        own_ref[0:1, :] = jnp.sum(scaled.astype(F32)[:size], axis=0, keepdims=True)
        own_ref[1:2, :] = jnp.sum(grads[0], axis=0, keepdims=True)

    hidden = weight_ref.shape[1] // 2
    span = act_ref.shape[1]
    chunk = span // 2
    for cols in (slice(0, chunk), slice(chunk, 2 * chunk)):
        here = lanes(step * span + cols.start, chunk)
        there = lanes(hidden + step * span + cols.start, chunk)
        pre = dot(normed_ref[...], weight_ref[:, here], 1, 0) + bias_ref[:, cols]
        act_grad = dot(grad_ref[...], weight_ref[:, there], 1, 0)
        cdf = 0.5 * (1.0 + lax.erf(pre * SQRT_HALF))
        act_ref[:, cols] = (pre * cdf).astype(BF)
        slope = cdf + pre * (jnp.exp(-0.5 * pre * pre) * INV_ROOT_TWO_PI)
        pre_grad = (act_grad * slope).astype(BF)
        pre_ref[:, cols] = pre_grad
        sums_ref[:, cols] = jnp.sum(pre_grad.astype(F32), axis=0, keepdims=True)
    back = dot(pre_ref[...], weight_ref[:, lanes(step * span, span)], 1, 1)

    @pl.when(step == 0)
    def _():
        back_acc[...] = back

    @pl.when(step == pl.num_programs(0) - 1)
    def _():
        whole = back_acc[...] + back
        for j, ref in enumerate(backs):
            ref[...] = whole[j * size : (j + 1) * size].astype(BF)


def mlp(rows, normed, cots, lives, ids, bias, weights, group):
    size, width = normed[0].shape
    count, shards = len(normed), len(weights)
    length = count * size
    hidden = weights[0].shape[1] // 2
    laid = shards > 1
    step = hidden // 2

    def whole(*shape):
        return pl.BlockSpec(shape, lambda i: (0, 0))

    cols = pl.BlockSpec((length, step), lambda i: (0, i))
    return pl.pallas_call(
        lambda *refs: mlp_kernel(count, shards, group, *refs),
        grid=(2,),
        in_specs=[whole(*rows.shape)]
        + [whole(size, width)] * (2 * count)
        + [whole(size, 1)] * count
        + [SMEM, pl.BlockSpec((1, step), lambda i: (0, i))]
        + [whole(*piece.shape) for piece in weights],
        out_specs=[whole(size, width)] * count
        + [whole(length, width)] * 2
        + [cols, cols, pl.BlockSpec((1, step), lambda i: (0, i)), whole(8, width)]
        + [whole(width, 2 * hidden)] * laid,
        out_shape=[shaped((size, width), BF)] * count
        + [shaped((length, width), BF)] * 2
        + [shaped((length, hidden), BF)] * 2
        + [shaped((1, hidden), F32), shaped((8, width), F32)]
        + [shaped((width, 2 * hidden), BF)] * laid,
        scratch_shapes=[pltpu.VMEM((length, width), BF), pltpu.VMEM((length, width), F32)],
        compiler_params=PARAMS,
        cost_estimate=SMALL,
        name="mlp",
    )(rows, *normed, *cots, *lives, ids, bias, *weights)


def mlp_weights_kernel(
    direct, ids_ref, norm_a, norm_b, grad_a, grad_b, rows_ref, fc2_ref, pre_a, pre_b, act_a, act_b,
    own_ref, *rest
):
    keep_ref, send_ref, scale2_ref, *branches, out_ref = rest
    hidden = pre_a.shape[1]
    first = dot(norm_a[...], pre_a[...], 0, 0) + dot(norm_b[...], pre_b[...], 0, 0)
    size = keep_ref.shape[0]
    out_ref[0, :, :hidden] = first[:size].astype(BF)
    out_ref[1, :, :hidden] = first[size:].astype(BF)
    outs = [grad_a[...].astype(F32), grad_b[...].astype(F32)]
    scaled = [(out * rows_ref[9:10, :]).astype(BF) for out in outs]
    second = dot(scaled[0], act_a[...], 0, 0) + dot(scaled[1], act_b[...], 0, 0)
    out_ref[0, :, hidden:] = second[:size].astype(BF)
    out_ref[1, :, hidden:] = second[size:].astype(BF)
    side = (ids_ref[1] & 1) if direct else 0
    keep_ref[...] = out_ref[side]
    send_ref[...] = out_ref[1 - side]
    scale2 = own_ref[1:2, :] * rows_ref[8:9, :]
    count = len(branches) // 2
    size = branches[0].shape[0]
    for half, act in enumerate((act_a, act_b)):
        branch = dot(act[...], fc2_ref[...], 1, 1)
        scale2 = scale2 + jnp.sum(outs[half] * branch, axis=0, keepdims=True)
        for j in range(count):
            branches[half * count + j][...] = branch[j * size : (j + 1) * size].astype(BF)
    scale2_ref[...] = scale2


def mlp_weights(rows, own, normed, grads, pres, acts, weights, group, ids, direct):
    length, width = normed[0].shape
    hidden = pres[0].shape[1]
    size = 2 * length // group
    step = 256

    cols = pl.BlockSpec((length, step), lambda i, ids_ref: (0, i))
    whole = pl.BlockSpec((length, hidden), lambda i, ids_ref: (0, 0))

    def line(count):
        return pl.BlockSpec((count, step), lambda i, ids_ref: (0, i))

    part = pl.BlockSpec((step // 2, 2 * hidden), lambda i, ids_ref: (i, 0))
    return pl.pallas_call(
        lambda *refs: mlp_weights_kernel(direct, *refs),
        grid_spec=pltpu.PrefetchScalarGridSpec(
            num_scalar_prefetch=1,
            grid=(width // step,),
            in_specs=[cols] * 4
            + [line(rows.shape[0])]
            + [pl.BlockSpec((step, hidden), lambda i, ids_ref: (i, 1))]
            + [whole] * 4
            + [line(own.shape[0])],
            out_specs=[part, part, line(1)] + [line(size)] * group,
            scratch_shapes=[pltpu.VMEM((2, step // 2, 2 * hidden), BF)],
        ),
        out_shape=[shaped((width // 2, 2 * hidden), BF)] * 2
        + [shaped((1, width), F32)]
        + [shaped((size, width), BF)] * group,
        compiler_params=PARAMS,
        cost_estimate=SMALL,
        name="mlp_weights",
    )(ids, *normed, *grads, rows, weights, *pres, *acts, own)


def finish_kernel(rows_ref, middle_ref, *rest):
    terms, out_ref = rest[:-1], rest[-1]
    branch = terms[0][...].astype(F32)
    for ref in terms[1:]:
        branch = branch + ref[...].astype(F32)
    branch = branch + rows_ref[8:9, :]
    out_ref[...] = (middle_ref[...] + rows_ref[9:10, :] * branch).astype(BF)


def finish(rows, middle, terms):
    return pl.pallas_call(
        finish_kernel,
        in_specs=[VMEM] * (2 + len(terms)),
        out_specs=VMEM,
        out_shape=shaped(middle.shape, BF),
        compiler_params=PARAMS,
        name="finish",
    )(rows, middle, *terms)


def begin_kernel(rows_ref, tokens_ref, mean_ref, inv_ref, middle_ref, *rest):
    terms, out_ref = rest[:-1], rest[-1]
    grads = terms[0][...].astype(F32)
    for ref in terms[1:]:
        grads = grads + ref[...].astype(F32)
    inverse = inv_ref[...]
    unit = (tokens_ref[...].astype(F32) - mean_ref[...]) * inverse
    out_ref[...] = (middle_ref[...] + norm_back(grads, unit, inverse, rows_ref[0:1, :])).astype(BF)


def begin(rows, tokens, mean, inverse, middle_grad, terms):
    length, width = tokens.shape
    column = pl.BlockSpec((length, 1), lambda i: (0, 0))
    whole = pl.BlockSpec((length, width), lambda i: (0, 0))
    return pl.pallas_call(
        begin_kernel,
        grid=(1,),
        in_specs=[pl.BlockSpec(rows.shape, lambda i: (0, 0)), whole, column, column, whole]
        + [whole] * len(terms),
        out_specs=whole,
        out_shape=shaped((length, width), BF),
        compiler_params=PARAMS,
        name="begin",
    )(rows, tokens, mean, inverse, middle_grad, *terms)


def qkv_back_kernel(group, grad_ref, weight_ref, mean_ref, inv_ref, *rest):
    tokens, outs, sums_ref = rest[:group], rest[group:-1], rest[-1]
    size = tokens[0].shape[0]
    gain = shift = 0.0
    for first in range(0, group, 2):
        span = slice(first * size, (first + 2) * size)
        part = dot(grad_ref[span, :], weight_ref[...], 1, 1)
        inputs = jnp.concatenate([tokens[first][...].astype(F32), tokens[first + 1][...].astype(F32)])
        unit = (inputs - mean_ref[span, :]) * inv_ref[span, :]
        outs[first][...] = part[:size].astype(BF)
        outs[first + 1][...] = part[size:].astype(BF)
        gain = gain + jnp.sum(part * unit, axis=0, keepdims=True)
        shift = shift + jnp.sum(part, axis=0, keepdims=True)
    sums_ref[...] = jnp.zeros(sums_ref.shape, F32)
    sums_ref[0:1, :] = gain
    sums_ref[1:2, :] = shift


def qkv_back(qkv_grad, weight, tokens, mean, inverse):
    size, width = tokens[0].shape
    group = len(tokens)
    return pl.pallas_call(
        lambda *refs: qkv_back_kernel(group, *refs),
        in_specs=[VMEM] * (4 + group),
        out_specs=[VMEM] * (group + 1),
        out_shape=[shaped((size, width), BF)] * group + [shaped((8, width), F32)],
        compiler_params=PARAMS,
        cost_estimate=SMALL,
        name="qkv_back",
    )(qkv_grad, weight, mean, inverse, *tokens)


def attn_weights_kernel(
    direct, shard, terms, ids_ref, normed_ref, grad_ref, norm1_ref, sums_ref, turn_ref, fbias_ref,
    scale2_ref, bias_a_ref, bias_b_ref, *rest,
):
    projs, outs = rest[:terms], rest[terms:-5]
    rows_ref, turned_ref, block_ref, small_ref, stage_ref = rest[-5:]
    place, row = ids_ref[0], ids_ref[1]
    width = normed_ref.shape[1]
    part = projs[0].shape[1]
    rows_ref[...] = jnp.zeros(rows_ref.shape, F32)
    rows_ref[0:2, :] = norm1_ref[0:2, :]
    for pair in range(part // PAIR):
        where = lanes(place * part + pair * PAIR, PAIR)
        rows_ref[2:3, where] = sums_ref[pair, :, :PAIR]
        rows_ref[3:4, where] = sums_ref[pair, :, 2 * PAIR :]
    rows_ref[4:8, :] = turn_ref[0:4, :]
    rows_ref[8:9, :] = fbias_ref[0:1, :]
    rows_ref[9:10, :] = scale2_ref[...]
    cols = bias_a_ref.shape[1] // part
    for owner in range(part // shard):
        for line in range(cols):
            spot = (owner * cols + line) * shard
            small_ref[line : line + 1, owner * shard : (owner + 1) * shard] = (
                bias_a_ref[0:1, spot : spot + shard] + bias_b_ref[0:1, spot : spot + shard]
            )
    rows_ref[10 : 10 + cols, lanes(place * part, part)] = small_ref[0:cols, :]
    turned_ref[...] = rows_ref[...].T
    step = block_ref.shape[0]
    for k in range(width // step):
        start = pl.multiple_of(((row >> 1) ^ k) * step, step) if direct else k * step
        cols = pl.ds(start, step)
        block_ref[:, : 3 * part] = dot(normed_ref[:, cols], grad_ref[...], 0, 0)
        proj = projs[0][cols, :].astype(F32)
        for ref in projs[1:]:
            proj = proj + ref[cols, :].astype(F32)
        block_ref[:, 3 * part : 4 * part] = proj
        block_ref[:, 4 * part :] = turned_ref[cols, :]
        if direct:
            size = step // 2
            stage_ref[0] = block_ref[:size, :].astype(BF)
            stage_ref[1] = block_ref[size:, :].astype(BF)
            side = row & 1
            blocks = width // step
            outs[k][...] = stage_ref[side]
            spot = (k + 1) % 2 * size
            outs[blocks + (blocks - 1 - k) // 2][spot : spot + size, :] = stage_ref[1 - side]
        else:
            outs[0][k * step : (k + 1) * step, :] = block_ref[...].astype(BF)


def attn_weights(ids, normed1, qkv_grad, sums, projs, blocks, shard):
    length, width = normed1.shape
    part = projs[0].shape[1]
    columns = 4 * part + EXTRA
    direct = blocks > 0
    step = 2 * (width // blocks) if direct else 256
    out_shape = [shaped((width, columns), BF)]
    if direct:
        size = width // blocks
        out_shape = [shaped((size, columns), BF)] * (blocks // 2)
        out_shape += [shaped((2 * size, columns), BF)] * (blocks // 4)
    return pl.pallas_call(
        lambda *refs: attn_weights_kernel(direct, shard, len(projs), *refs),
        in_specs=[SMEM] + [VMEM] * (2 + len(sums) + len(projs)),
        out_specs=[VMEM] * len(out_shape),
        out_shape=out_shape,
        scratch_shapes=[
            pltpu.VMEM((EXTRA, width), F32),
            pltpu.VMEM((width, EXTRA), F32),
            pltpu.VMEM((step, columns), F32),
            pltpu.VMEM((8, part), F32),
            pltpu.VMEM((2, step // 2, columns), BF),
        ],
        compiler_params=PARAMS,
        cost_estimate=SMALL,
        name="attn_weights",
    )(ids, normed1, qkv_grad, *sums, *projs)


def total(ids, terms, group):
    size, columns = terms[0].shape
    rows = size // group

    def kernel(ids_ref, *refs):
        ins, outs, sum_ref = refs[: len(terms)], refs[len(terms) : -1], refs[-1]
        value = ins[0][...].astype(F32)
        for ref in ins[1:]:
            value = value + ref[...].astype(F32)
        sum_ref[...] = value
        for k, out in enumerate(outs):
            start = pl.multiple_of((ids_ref[0] ^ k) * rows, rows)
            out[...] = sum_ref[pl.ds(start, rows), :].astype(BF)

    return pl.pallas_call(
        kernel,
        in_specs=[SMEM] + [VMEM] * len(terms),
        out_specs=[VMEM] * group,
        out_shape=[shaped((rows, columns), BF)] * group,
        scratch_shapes=[pltpu.VMEM((size, columns), F32)],
        compiler_params=PARAMS,
        name="total",
    )(ids, *terms)


def place_attn_kernel(ids_ref, *refs):
    group = len(refs) - 4
    blocks, (qkv_ref, proj_ref, vec_ref, bias_ref) = refs[:group], refs[group:]
    width = proj_ref.shape[1]
    part = width // group
    extra = jnp.zeros((qkv_ref.shape[0], EXTRA), F32)
    for k, block in enumerate(blocks):
        source = ids_ref[0] ^ k
        for third in range(3):
            for pair in range(part // PAIR):
                spot = (pair * 3 + third) * PAIR
                where = lanes(third * width + source * part + pair * PAIR, PAIR)
                qkv_ref[:, where] = block[:, spot : spot + PAIR].astype(F32)
        proj_ref[:, lanes(source * part, part)] = block[:, 3 * part : 4 * part].astype(F32)
        extra = extra + block[:, 4 * part :].astype(F32)
    turned = extra.T
    count = vec_ref.shape[0]
    vec_ref[...] = turned[:count]
    rows = qkv_ref.shape[0]
    for line in range(bias_ref.shape[1] // rows):
        bias_ref[0:1, line * rows : (line + 1) * rows] = turned[count + line : count + line + 1]


def place_attn(ids, blocks, width, vector_count, bias_cols):
    rows = blocks[0].shape[0]
    return pl.pallas_call(
        place_attn_kernel,
        in_specs=[SMEM] + [VMEM] * len(blocks),
        out_specs=[VMEM] * 4,
        out_shape=[
            shaped((rows, 3 * width), F32),
            shaped((rows, width), F32),
            shaped((vector_count, rows), F32),
            shaped((1, bias_cols * rows), F32),
        ],
        compiler_params=PARAMS,
        name="place_attn",
    )(ids, *blocks)


def place_mlp_kernel(ids_ref, *refs):
    group = len(refs) - 2
    blocks, (fc1_ref, fc2_ref) = refs[:group], refs[group:]
    part = fc1_ref.shape[1] // group
    for k, block in enumerate(blocks):
        where = lanes((ids_ref[0] ^ k) * part, part)
        fc1_ref[:, where] = block[:, :part].astype(F32)
        fc2_ref[:, where] = block[:, part:].astype(F32)


def place_mlp(ids, blocks, hidden):
    rows = blocks[0].shape[0]
    return pl.pallas_call(
        place_mlp_kernel,
        in_specs=[SMEM] + [VMEM] * len(blocks),
        out_specs=[VMEM] * 2,
        out_shape=[shaped((rows, hidden), F32)] * 2,
        compiler_params=PARAMS,
        name="place_mlp",
    )(ids, *blocks)


def local(tokens, counts, w_qkv, w_proj, w_fc1, fc1_bias, w_fc2, vectors, cotangent):
    _, capacity, width = tokens.shape
    hidden = w_fc1.shape[1]
    rows = w_qkv.shape[0]
    group, replicas = lax.axis_size("ctx"), lax.axis_size("dp")
    place, replica = lax.axis_index("ctx"), lax.axis_index("dp")
    ids = jnp.stack([place, replica]).astype(jnp.int32)
    head_width = width // group
    hidden_part = hidden // group
    bias_cols = hidden // width
    vector_count = vectors.shape[0]
    direct = replicas == 8

    def swap(value, bit, axis="ctx"):
        size = group if axis == "ctx" else replicas
        return lax.ppermute(value, axis, [(i, i ^ bit) for i in range(size)])

    def after(value, *before):
        return lax.optimization_barrier((value,) + before)[0]

    def gather(own, *before):
        pieces = [own]
        for j in range(1, group):
            bit = j & -j
            source = pieces[j ^ bit]
            pieces.append(swap(after(source, *before) if j ^ bit else source, bit))
        return pieces

    def scatter(parts, *before, mids=None, axis="ctx", scale=1, gates=None):
        pieces = {j: [part] for j, part in enumerate(parts)}

        def added(terms):
            if len(terms) == 1:
                return terms[0]
            return sum(term.astype(F32) for term in terms).astype(BF)

        bit = 1
        sent = []
        while bit < len(parts):
            for j in sorted((j for j in pieces if j & bit), reverse=True):
                value = added(pieces.pop(j))
                if bit > 1:
                    if mids is not None:
                        mids.append(value)
                    value = after(value, *before)
                elif axis == "dp":
                    value = after(value, *sent[-2:-1])
                if gates and bit in gates:
                    value = after(value, *gates[bit])
                sent.append(swap(value, bit * scale, axis))
                pieces[j ^ bit].append(sent[-1])
            bit *= 2
        return pieces[0]

    def exchange(relative):
        return [relative[0]] + [swap(relative[k], k) for k in range(1, group)]

    def in_order(relative):
        stacked = jnp.stack(relative)
        return jnp.concatenate(
            [lax.dynamic_index_in_dim(stacked, place ^ s, 0, False) for s in range(group)], axis=0
        )

    cuts = cut(
        ids, counts, w_qkv, w_proj.T, w_fc1, w_fc2.T, vectors, fc1_bias.reshape(1, -1), group
    )
    first = exchange(cuts[:group])
    tokens_far = swap(after(tokens[0], *first), group // 2)

    def widen(shards, *before):
        for m in range(2, replicas):
            low = m & -m
            if m ^ low:
                shards[m] = swap(after(shards[m ^ low], *before), low, "dp")

    second = exchange([after(block, *first) for block in cuts[group:]])
    if direct:
        shards = {0: jnp.concatenate(first, axis=0)}
        for bit in (4, 2, 1):
            shards[bit] = swap(shards[0], bit, "dp")
        arrived = [tokens_far] + [shards[bit] for bit in (4, 2, 1)] + second[1:]
        widen(shards, *arrived)
        first_pieces = [shards[m] for m in range(replicas)]
    else:
        first_pieces = [lax.all_gather(in_order(first), "dp", axis=0, tiled=True)]
        arrived = [tokens_far]
    second_shard = after(in_order(second), *arrived)
    second_all = lax.all_gather(second_shard, "dp", axis=0, tiled=True)
    tokens_pieces = [tokens[0]]
    for j in range(1, group):
        source = tokens_pieces[j ^ (j & -j)]
        if j == group // 2:
            tokens_pieces.append(tokens_far)
        else:
            tokens_pieces.append(swap(after(source, *arrived), j & -j))
    cotangent_far = swap(after(cotangent[0], *arrived), group // 2)

    tokens_own = after(tokens[0], second_shard)
    count_column = vector_count + bias_cols
    (
        weight_qkv, weight_proj, vector_rows, normed1, qkv, mean1, inverse1, bias_fc1, key_bias,
        *live,
    ) = project(
        ids, [tokens_own] + tokens_pieces[1:], first, first_pieces, hidden_part, count_column,
        0 if direct else rows,
    )

    cotangent_pieces = [cotangent[0]]
    for j in range(1, group):
        source = cotangent_pieces[j ^ (j & -j)]
        if j == group // 2:
            cotangent_pieces.append(cotangent_far)
        else:
            cotangent_pieces.append(swap(after(source, qkv), j & -j))
    attended, lse, *attended_low = attend(after(qkv, cotangent_far), key_bias, group)
    projs = gather(weight_proj, lse)
    attended_own = exchange(attended_low)
    branch1, middle, normed2_own, unit2, inverse2 = middle_step(
        vector_rows, tokens[0], attended_own, projs
    )
    half = group // 2
    normed2 = [normed2_own]
    while len(normed2) < half:
        normed2 += [swap(piece, len(normed2)) for piece in normed2]

    def feed(where, pieces, weights):
        return mlp(
            vector_rows, pieces, cotangent_pieces[where], live[where], ids, bias_fc1, weights, group
        )

    *backs_near, norm_near, grad_near, act_near, pre_near, sums_near, own_sums = feed(
        slice(0, half), normed2, [second_all]
    )
    normed2_far = [swap(normed2_own, half)]
    while len(normed2_far) < half:
        normed2_far += [
            swap(after(piece, sums_near), len(normed2_far)) for piece in normed2_far
        ]
    *backs_far, norm_far, grad_far, act_far, pre_far, sums_far, _ = feed(
        slice(half, group), normed2_far, [second_all]
    )
    mids = []
    norm2_terms = scatter(backs_near + backs_far, mids=mids)
    keep_mlp, send_mlp, grad_scale2, *branches = mlp_weights(
        vector_rows, own_sums, [norm_near, norm_far], [grad_near, grad_far], [after(pre_near, *mids), pre_far],
        [act_near, act_far], second_all, group, ids, direct,
    )
    other_mlp = None
    if direct:
        other_mlp = swap(after(send_mlp, *norm2_terms), 1, "dp")
    middle_grad, branch_grad, turn_sums, *att_grads = turn(
        vector_rows, live[0], cotangent[0], unit2, inverse2, branch1, norm2_terms, projs
    )
    att_grads = exchange(att_grads)
    mids = []
    proj_terms = scatter(proj_weights(branch_grad, attended_own), *att_grads, mids=mids)
    branch2_terms = scatter(branches, *att_grads, mids=mids)
    qkv_grad, qkv_sums = attend_back(qkv, key_bias, attended, after(lse, *mids), att_grads)
    pending = [branch2_terms[-1], proj_terms[-1]]
    if direct:
        other = after(other_mlp, qkv_grad)
        summed = (keep_mlp.astype(F32) + other.astype(F32)).astype(BF)
        pending.append(summed)
        lines = [[side + 2 * z for z in range(replicas // 2)] for side in range(2)]
        owned_mlp = lax.psum_scatter(
            summed, "dp", scatter_dimension=0, tiled=True, axis_index_groups=lines
        )
    else:
        ordered = jnp.stack(
            [part.reshape(-1, 128, 2 * hidden_part) for part in (keep_mlp, send_mlp)], axis=1
        )
        owned_mlp = lax.psum_scatter(
            ordered.reshape(width, 2 * hidden_part), "dp", scatter_dimension=0, tiled=True
        )
    *norm1_parts, norm1_sums = qkv_back(after(qkv_grad, *pending), weight_qkv, tokens_pieces, mean1, inverse1)
    parts = attn_weights(
        ids, normed1, qkv_grad,
        [norm1_sums, qkv_sums, turn_sums, own_sums, grad_scale2, sums_near, sums_far],
        proj_terms, replicas if direct else 0, rows,
    )
    norm1_terms = scatter(norm1_parts)
    if direct:
        def add(left, right):
            return (left.astype(F32) + right.astype(F32)).astype(BF)

        keep0, keep1, keep2, keep3, send32, send10 = parts
        size = keep0.shape[0]
        other32 = swap(send32, 1, "dp")
        other10 = swap(after(send10, other32), 1, "dp")
        across = swap(add(keep3, other32[:size]), 2, "dp")
        far = swap(add(add(keep2, other32[size:]), across), 4, "dp")
        across0 = swap(add(keep1, other10[:size]), 2, "dp")
        terms = [add(keep0, other10[size:]), across0, far]
        settled = [across, across0]
        cuts_mlp = total(after(ids, *settled), [owned_mlp], group)
    else:
        owned_attn = lax.psum_scatter(parts[0], "dp", scatter_dimension=0, tiled=True)

        def relative(owned):
            blocks = owned.reshape(group, rows, -1)
            return [lax.dynamic_index_in_dim(blocks, place ^ k, 0, False) for k in range(group)]

        cuts_mlp = relative(owned_mlp)
        settled = []
    out_fc1, out_fc2 = place_mlp(ids, exchange(cuts_mlp), hidden)
    input_grad = begin(
        vector_rows, after(tokens[0], *settled), mean1, inverse1, middle_grad, norm1_terms
    )
    output = finish(after(vector_rows, *settled), middle, branch2_terms)
    if direct:
        cuts_attn = total(after(ids, input_grad, output, out_fc1), terms, group)
    else:
        cuts_attn = relative(owned_attn)

    out_qkv, out_proj, out_vectors, out_bias = place_attn(
        ids, exchange(cuts_attn), width, vector_count, bias_cols
    )
    return (
        output[None],
        input_grad[None],
        out_qkv,
        out_proj.T,
        out_fc1,
        out_bias.reshape(-1),
        out_fc2.T,
        out_vectors,
    )


def solution(mesh):
    both = ("dp", "ctx")
    in_specs = (
        P("dp", "ctx", None),
        P("dp", "ctx"),
        P(both, None),
        P(None, both),
        P(both, None),
        P(both),
        P(None, both),
        P(None, both),
        P("dp", "ctx", None),
    )
    out_specs = (
        P("dp", "ctx", None),
        P("dp", "ctx", None),
        P(both, None),
        P(None, both),
        P(both, None),
        P(both),
        P(None, both),
        P(None, both),
    )
    return jax.shard_map(local, mesh=mesh, in_specs=in_specs, out_specs=out_specs, check_vma=False)
```

```python
import jax
import jax.numpy as jnp
from jax import lax
from jax.experimental import pallas as pl
from jax.experimental.pallas import tpu as pltpu
from jax.sharding import PartitionSpec as P

HD = 64
PAIR = 2 * HD
EXTRA = 128
EPSILON = 1e-06
MASKED_SCORE = -1e30
SQRT_HALF = 0.7071067811865476
INV_ROOT_TWO_PI = 0.3989422804014327
BF = jnp.bfloat16
F32 = jnp.float32
PARAMS = pltpu.CompilerParams(vmem_limit_bytes=60 * 1024 * 1024)
SMALL = pl.CostEstimate(flops=1_000_000_000, bytes_accessed=1_000_000, transcendentals=0)
VMEM = pl.BlockSpec(memory_space=pltpu.VMEM)
SMEM = pl.BlockSpec(memory_space=pltpu.SMEM)


def shaped(shape, dtype):
    return jax.ShapeDtypeStruct(shape, dtype)


def dot(left, right, left_dim, right_dim):
    return lax.dot_general(
        left, right, (((left_dim,), (right_dim,)), ((), ())), preferred_element_type=F32
    )


def lanes(start, size):
    return pl.ds(pl.multiple_of(start, 128), size)


def unit_rows(inputs):
    centered = inputs - jnp.mean(inputs, axis=-1, keepdims=True)
    spread = jnp.mean(centered * centered, axis=-1, keepdims=True)
    inverse = lax.rsqrt(spread + EPSILON)
    return (centered * inverse, inverse)


def norm_back(grad_in, unit, inverse, gain):
    scaled = grad_in * gain
    inner = (
        scaled
        - jnp.mean(scaled, axis=-1, keepdims=True)
        - unit * jnp.mean(scaled * unit, axis=-1, keepdims=True)
    )
    return inner * inverse


def cut_kernel(ids_ref, count_ref, qkv_ref, proj_ref, fc1_ref, fc2_ref, vec_ref, bias_ref, *rest):
    outs, (extra_ref, turn_ref) = rest[:-2], rest[-2:]
    group = len(outs) // 2
    place = ids_ref[0]
    width = proj_ref.shape[1]
    part = width // group
    hidden_part = fc1_ref.shape[1] // group
    vector_count, bias_cols = vec_ref.shape[0], bias_ref.shape[1] // vec_ref.shape[1]
    column = vector_count + bias_cols
    lane = lax.broadcasted_iota(jnp.int32, extra_ref.shape, 1)
    count = count_ref[0, 0]
    high = (count >> 7).astype(F32)
    low = (count & 127).astype(F32)
    extra_ref[...] = jnp.where(lane == column, high, jnp.where(lane == column + 1, low, 0.0))
    extra_ref[:, :vector_count] = vec_ref[...].astype(F32).T
    rows = qkv_ref.shape[0]
    for line in range(bias_cols):
        turn_ref[line : line + 1, :] = bias_ref[0:1, line * rows : (line + 1) * rows].astype(F32)
    extra_ref[:, vector_count:column] = turn_ref[0:bias_cols, :].T
    extra = extra_ref[...].astype(BF)
    for k in range(group):
        target = place ^ k
        first, second = outs[k], outs[group + k]
        for third in range(3):
            for pair in range(part // PAIR):
                spot = (pair * 3 + third) * PAIR
                first[:, spot : spot + PAIR] = qkv_ref[
                    :, lanes(third * width + target * part + pair * PAIR, PAIR)
                ]
        first[:, 3 * part : 4 * part] = proj_ref[:, lanes(target * part, part)]
        first[:, 4 * part :] = extra
        second[:, :hidden_part] = fc1_ref[:, lanes(target * hidden_part, hidden_part)]
        second[:, hidden_part:] = fc2_ref[:, lanes(target * hidden_part, hidden_part)]


def cut(ids, counts, w_qkv, w_proj_t, w_fc1, w_fc2_t, vectors, bias, group):
    rows, width = w_proj_t.shape
    part, hidden_part = width // group, w_fc1.shape[1] // group
    return pl.pallas_call(
        cut_kernel,
        in_specs=[SMEM, SMEM] + [VMEM] * 6,
        out_specs=[VMEM] * (2 * group),
        out_shape=[shaped((rows, 4 * part + EXTRA), BF)] * group
        + [shaped((rows, 2 * hidden_part), BF)] * group,
        scratch_shapes=[pltpu.VMEM((rows, EXTRA), F32), pltpu.VMEM((8, rows), F32)],
        compiler_params=PARAMS,
        name="cut",
    )(ids, counts, w_qkv, w_proj_t, w_fc1, w_fc2_t, vectors, bias)


def project_kernel(ordered, group, count_column, ids_ref, *rest):
    tokens, blocks, rest = rest[:group], rest[group : 2 * group], rest[2 * group :]
    pieces, outs, lives, scratch = (
        rest[: -12 - group], rest[-12 - group : -3 - group], rest[-3 - group : -3], rest[-3:]
    )
    qkv_w, proj_w, rows_ref, normed_ref, out_ref, mean_ref, inv_ref, fc1_ref, key_ref = outs
    extra_ref, bias_ref, small_ref = scratch
    place, row = ids_ref[0], ids_ref[1]
    capacity, width = tokens[0].shape
    part = proj_w.shape[1]
    size = pieces[0].shape[0]

    def lay(block, start, count):
        where = pl.ds(start, count)
        qkv_w[where, :] = block[:, : 3 * part]
        proj_w[where, :] = block[:, 3 * part : 4 * part]
        extra_ref[where, :] = block[:, 4 * part :].astype(F32)

    if ordered:
        lay(pieces[0], 0, size)
        shard = ordered
    else:
        sub = shard = size // group
        for m, piece in enumerate(pieces):
            for j in range(group):
                start = (row ^ m) * size + (place ^ j) * sub
                lay(piece.at[j * sub : (j + 1) * sub], pl.multiple_of(start, sub), sub)
    slot = lax.broadcasted_iota(jnp.int32, (capacity, 1), 0).astype(F32)
    for j, (block, live_ref) in enumerate(zip(blocks, lives)):
        extra = block[:, 4 * part :].astype(F32)[0:1, :]
        bound = extra[:, count_column : count_column + 1] * 128.0
        bound = bound + extra[:, count_column + 1 : count_column + 2]
        live = jnp.where(slot < bound, 1.0, 0.0)
        live_ref[...] = live
        key_ref[j * capacity : (j + 1) * capacity, :] = (1.0 - live) * MASKED_SCORE
    turned = extra_ref[...].T
    rows_ref[...] = turned[: rows_ref.shape[0]]
    bias_ref[...] = jnp.zeros(bias_ref.shape, F32)
    for pair in range(part // PAIR):
        for third, line in ((0, 2), (2, 3)):
            spot = (pair * 3 + third) * PAIR
            bias_ref[0:1, spot : spot + PAIR] = rows_ref[
                line : line + 1, lanes(place * part + pair * PAIR, PAIR)
            ]
    cols = fc1_ref.shape[1] // part
    small_ref[0:cols, :] = rows_ref[10 : 10 + cols, lanes(place * part, part)]
    for owner in range(part // shard):
        for line in range(cols):
            spot = (owner * cols + line) * shard
            fc1_ref[0:1, spot : spot + shard] = small_ref[
                line : line + 1, owner * shard : (owner + 1) * shard
            ]
    gain, shift, bias = rows_ref[0:1, :], rows_ref[1:2, :], bias_ref[0:1, :]
    for first in range(0, group, 2):
        span = slice(first * capacity, (first + 2) * capacity)
        inputs = jnp.concatenate([tokens[first][...].astype(F32), tokens[first + 1][...].astype(F32)])
        mean = jnp.mean(inputs, axis=-1, keepdims=True)
        centered = inputs - mean
        inverse = lax.rsqrt(jnp.mean(centered * centered, axis=-1, keepdims=True) + EPSILON)
        normed = (centered * inverse * gain + shift).astype(BF)
        normed_ref[span, :] = normed
        mean_ref[span, :] = mean
        inv_ref[span, :] = inverse
        out_ref[span, :] = (dot(normed, qkv_w[...], 1, 0) + bias).astype(BF)


def project(ids, tokens, blocks, pieces, hidden_part, count_column, ordered):
    capacity, width = tokens[0].shape
    group = len(tokens)
    length = group * capacity
    part = width // group
    return pl.pallas_call(
        lambda *refs: project_kernel(ordered, group, count_column, *refs),
        in_specs=[SMEM] + [VMEM] * (2 * group + len(pieces)),
        out_specs=[VMEM] * (9 + group),
        out_shape=[
            shaped((width, 3 * part), BF),
            shaped((width, part), BF),
            shaped((16, width), F32),
            shaped((length, width), BF),
            shaped((length, 3 * part), BF),
            shaped((length, 1), F32),
            shaped((length, 1), F32),
            shaped((1, hidden_part), F32),
            shaped((length, 1), F32),
        ]
        + [shaped((capacity, 1), F32)] * group,
        scratch_shapes=[
            pltpu.VMEM((width, EXTRA), F32),
            pltpu.VMEM((8, 3 * part), F32),
            pltpu.VMEM((8, part), F32),
        ],
        compiler_params=PARAMS,
        cost_estimate=SMALL,
        name="project",
    )(ids, *tokens, *blocks, *pieces)


def query_chunks(length):
    step = 512
    return [(start, min(step, length - start)) for start in range(0, length, step)]


def attend_kernel(qkv_ref, bias_ref, out_ref, lse_ref, *lows):
    length = qkv_ref.shape[0]
    key_bias = bias_ref[...]
    for head in range(2):
        keys = qkv_ref[:, PAIR + head * HD : PAIR + (head + 1) * HD]
        values = qkv_ref[:, 2 * PAIR + head * HD : 2 * PAIR + (head + 1) * HD]
        for start, size in query_chunks(length):
            queries = qkv_ref[start : start + size, head * HD : (head + 1) * HD]
            queries = queries * jnp.asarray(HD**-0.5, BF)
            scores = dot(keys, queries, 1, 1) + key_bias
            top = jnp.max(scores, axis=0, keepdims=True)
            expo = jnp.exp(scores - top)
            total = jnp.sum(expo, axis=0, keepdims=True)
            mixed = (dot(values, expo.astype(BF), 0, 0) / total).T
            out_ref[start : start + size, head * HD : (head + 1) * HD] = mixed
            lse_ref[0, head : head + 1, start : start + size] = top + jnp.log(total)
    for j, low in enumerate(lows):
        size = low.shape[0]
        low[...] = out_ref[j * size : (j + 1) * size, :].astype(BF)


def attend(qkv, key_bias, group):
    length, columns = qkv.shape
    pairs = columns // (3 * PAIR)
    return pl.pallas_call(
        attend_kernel,
        grid=(pairs,),
        in_specs=[
            pl.BlockSpec((length, 3 * PAIR), lambda p: (0, p)),
            pl.BlockSpec((length, 1), lambda p: (0, 0)),
        ],
        out_specs=[
            pl.BlockSpec((length, PAIR), lambda p: (0, p)),
            pl.BlockSpec((1, 2, length), lambda p: (p, 0, 0)),
        ]
        + [pl.BlockSpec((length // group, PAIR), lambda p: (0, p))] * group,
        out_shape=[
            shaped((length, pairs * PAIR), F32),
            shaped((pairs, 2, length), F32),
        ]
        + [shaped((length // group, pairs * PAIR), BF)] * group,
        compiler_params=PARAMS,
        cost_estimate=SMALL,
        name="attend",
    )(qkv, key_bias)


def attend_back_kernel(qkv_ref, bias_ref, att_ref, lse_ref, *rest):
    pieces, (out_ref, sums_ref, grad_ref) = rest[:-3], rest[-3:]
    length = qkv_ref.shape[0]
    size = pieces[0].shape[0]
    factor = HD**-0.5
    key_bias = bias_ref[...]
    for j, piece in enumerate(pieces):
        grad_ref[j * size : (j + 1) * size, :] = piece[...].astype(F32)
    for head in range(2):
        low, high = head * HD, (head + 1) * HD
        keys = qkv_ref[:, PAIR + low : PAIR + high]
        values = qkv_ref[:, 2 * PAIR + low : 2 * PAIR + high]
        key_grad = jnp.zeros((length, HD), F32)
        value_grad = jnp.zeros((length, HD), F32)
        for start, size in query_chunks(length):
            rows = slice(start, start + size)
            queries = qkv_ref[rows, low:high] * jnp.asarray(factor, BF)
            product = grad_ref[rows, low:high] * att_ref[rows, low:high]
            grads = grad_ref[rows, low:high].astype(BF)
            delta = jnp.sum(product.T, axis=0, keepdims=True)
            scores = dot(keys, queries, 1, 1) + key_bias
            probs = jnp.exp(scores - lse_ref[0, head : head + 1, rows])
            value_grad += dot(probs.astype(BF), grads, 1, 0)
            raw = (probs * (dot(values, grads, 1, 1) - delta)).astype(BF)
            key_grad += dot(raw, queries, 1, 0)
            query_grad = dot(keys, raw, 0, 0).T * factor
            out_ref[rows, low:high] = query_grad.astype(BF)
        out_ref[:, PAIR + low : PAIR + high] = key_grad.astype(BF)
        out_ref[:, 2 * PAIR + low : 2 * PAIR + high] = value_grad.astype(BF)
    sums_ref[0] = jnp.sum(out_ref[...].astype(F32), axis=0, keepdims=True)


def attend_back(qkv, key_bias, attended, lse, pieces):
    length, columns = qkv.shape
    pairs = columns // (3 * PAIR)
    size = pieces[0].shape[0]
    return pl.pallas_call(
        attend_back_kernel,
        grid=(pairs,),
        in_specs=[
            pl.BlockSpec((length, 3 * PAIR), lambda p: (0, p)),
            pl.BlockSpec((length, 1), lambda p: (0, 0)),
            pl.BlockSpec((length, PAIR), lambda p: (0, p)),
            pl.BlockSpec((1, 2, length), lambda p: (p, 0, 0)),
        ]
        + [pl.BlockSpec((size, PAIR), lambda p: (0, p))] * len(pieces),
        out_specs=[
            pl.BlockSpec((length, 3 * PAIR), lambda p: (0, p)),
            pl.BlockSpec((1, 1, 3 * PAIR), lambda p: (p, 0, 0)),
        ],
        out_shape=[shaped((length, columns), BF), shaped((pairs, 1, 3 * PAIR), F32)],
        scratch_shapes=[pltpu.VMEM((length, PAIR), F32)],
        compiler_params=PARAMS,
        cost_estimate=SMALL,
        name="attend_back",
    )(qkv, key_bias, attended, lse, *pieces)


def middle_kernel(group, rows_ref, tokens_ref, *rest):
    parts, weights, (branch_ref, middle_ref, normed_ref, unit_ref, inv_ref) = (
        rest[:group], rest[group : 2 * group], rest[2 * group :]
    )
    branch = dot(parts[0][...], weights[0][...], 1, 1)
    for part, weight in zip(parts[1:], weights[1:]):
        branch = branch + dot(part[...], weight[...], 1, 1)
    branch = branch + rows_ref[4:5, :]
    branch_ref[...] = branch
    middle = tokens_ref[...].astype(F32) + rows_ref[5:6, :] * branch
    middle_ref[...] = middle
    unit, inverse = unit_rows(middle)
    unit_ref[...] = unit
    inv_ref[...] = inverse
    normed_ref[...] = (unit * rows_ref[6:7, :] + rows_ref[7:8, :]).astype(BF)


def middle_step(rows, tokens, parts, weights):
    length, width = tokens.shape
    group = len(parts)
    full = shaped((length, width), F32)
    return pl.pallas_call(
        lambda *refs: middle_kernel(group, *refs),
        in_specs=[VMEM] * (2 + 2 * group),
        out_specs=[VMEM] * 5,
        out_shape=[full, full, shaped((length, width), BF), full, shaped((length, 1), F32)],
        compiler_params=PARAMS,
        cost_estimate=SMALL,
        name="middle",
    )(rows, tokens, *parts, *weights)


def turn_kernel(group, terms, rows_ref, live_ref, cot_ref, unit_ref, inv_ref, branch_ref, *rest):
    backs, weights, outs = rest[:terms], rest[terms : terms + group], rest[terms + group :]
    middle_ref, grad_ref, sums_ref = outs[:3]
    norm_grad = backs[0][...].astype(F32)
    for ref in backs[1:]:
        norm_grad = norm_grad + ref[...].astype(F32)
    unit = unit_ref[...]
    out_grad = cot_ref[...].astype(F32) * live_ref[...]
    middle = out_grad + norm_back(norm_grad, unit, inv_ref[...], rows_ref[6:7, :])
    middle_ref[...] = middle
    low = (middle * rows_ref[5:6, :]).astype(BF)
    grad_ref[...] = low
    sums_ref[...] = jnp.zeros(sums_ref.shape, F32)
    sums_ref[0:1, :] = jnp.sum(low.astype(F32), axis=0, keepdims=True)
    sums_ref[1:2, :] = jnp.sum(middle * branch_ref[...], axis=0, keepdims=True)
    sums_ref[2:3, :] = jnp.sum(norm_grad * unit, axis=0, keepdims=True)
    sums_ref[3:4, :] = jnp.sum(norm_grad, axis=0, keepdims=True)
    for out, weight in zip(outs[3:], weights):
        out[...] = dot(low, weight[...], 1, 0).astype(BF)


def turn(rows, live, cotangent, unit, inverse, branch, backs, weights):
    length, width = cotangent.shape
    part = weights[0].shape[1]
    group = len(weights)
    return pl.pallas_call(
        lambda *refs: turn_kernel(group, len(backs), *refs),
        in_specs=[VMEM] * (6 + len(backs) + group),
        out_specs=[VMEM] * (3 + group),
        out_shape=[shaped((length, width), F32), shaped((length, width), BF), shaped((8, width), F32)]
        + [shaped((length, part), BF)] * group,
        compiler_params=PARAMS,
        cost_estimate=SMALL,
        name="turn",
    )(rows, live, cotangent, unit, inverse, branch, *backs, *weights)


def proj_weights_kernel(grad_ref, *rest):
    half = len(rest) // 2
    for part, out in zip(rest[:half], rest[half:]):
        out[...] = dot(grad_ref[...], part[...], 0, 0).astype(BF)


def proj_weights(grads, parts):
    length, width = grads.shape
    part = parts[0].shape[1]
    return pl.pallas_call(
        proj_weights_kernel,
        in_specs=[VMEM] * (1 + len(parts)),
        out_specs=[VMEM] * len(parts),
        out_shape=[shaped((width, part), BF)] * len(parts),
        compiler_params=PARAMS,
        cost_estimate=SMALL,
        name="proj_weights",
    )(grads, *parts)


def mlp_kernel(count, shards, group, rows_ref, *rest):
    normed_in, cots, lives = rest[:count], rest[count : 2 * count], rest[2 * count : 3 * count]
    ids_ref, bias_ref = rest[3 * count : 3 * count + 2]
    rest = rest[3 * count + 2 :]
    pieces, backs, rest = rest[:shards], rest[shards : shards + count], rest[shards + count :]
    normed_ref, out_ref, act_ref, pre_ref, sums_ref, own_ref = rest[:6]
    if shards > 1:
        weight_ref, grad_ref, back_acc = rest[6:]
    else:
        weight_ref = pieces[0]
        grad_ref, back_acc = rest[6:]
    step = pl.program_id(0)
    size = cots[0].shape[0]

    @pl.when(step == 0)
    def _():
        if shards > 1:
            whole_size = pieces[0].shape[0]
            sub = whole_size // group
            for m, piece in enumerate(pieces):
                for j in range(group):
                    start = (ids_ref[1] ^ m) * whole_size + (ids_ref[0] ^ j) * sub
                    weight_ref[pl.ds(pl.multiple_of(start, sub), sub), :] = piece[
                        j * sub : (j + 1) * sub, :
                    ]
        normed_ref[...] = jnp.concatenate([ref[...].astype(F32) for ref in normed_in]).astype(BF)
        scale = rows_ref[9:10, :]
        grads = [cot[...].astype(F32) * live[...] for cot, live in zip(cots, lives)]
        whole_grad = jnp.concatenate(grads)
        out_ref[...] = whole_grad.astype(BF)
        scaled = (whole_grad * scale).astype(BF)
        grad_ref[...] = scaled
        own_ref[0:1, :] = jnp.sum(scaled.astype(F32)[:size], axis=0, keepdims=True)
        own_ref[1:2, :] = jnp.sum(grads[0], axis=0, keepdims=True)

    hidden = weight_ref.shape[1] // 2
    span = act_ref.shape[1]
    chunk = span // 2
    for cols in (slice(0, chunk), slice(chunk, 2 * chunk)):
        here = lanes(step * span + cols.start, chunk)
        there = lanes(hidden + step * span + cols.start, chunk)
        pre = dot(normed_ref[...], weight_ref[:, here], 1, 0) + bias_ref[:, cols]
        act_grad = dot(grad_ref[...], weight_ref[:, there], 1, 0)
        cdf = 0.5 * (1.0 + lax.erf(pre * SQRT_HALF))
        act_ref[:, cols] = (pre * cdf).astype(BF)
        slope = cdf + pre * (jnp.exp(-0.5 * pre * pre) * INV_ROOT_TWO_PI)
        pre_grad = (act_grad * slope).astype(BF)
        pre_ref[:, cols] = pre_grad
        sums_ref[:, cols] = jnp.sum(pre_grad.astype(F32), axis=0, keepdims=True)
    back = dot(pre_ref[...], weight_ref[:, lanes(step * span, span)], 1, 1)

    @pl.when(step == 0)
    def _():
        back_acc[...] = back

    @pl.when(step == pl.num_programs(0) - 1)
    def _():
        whole = back_acc[...] + back
        for j, ref in enumerate(backs):
            ref[...] = whole[j * size : (j + 1) * size].astype(BF)


def mlp(rows, normed, cots, lives, ids, bias, weights, group):
    size, width = normed[0].shape
    count, shards = len(normed), len(weights)
    length = count * size
    hidden = weights[0].shape[1] // 2
    laid = shards > 1
    step = hidden // 2

    def whole(*shape):
        return pl.BlockSpec(shape, lambda i: (0, 0))

    cols = pl.BlockSpec((length, step), lambda i: (0, i))
    return pl.pallas_call(
        lambda *refs: mlp_kernel(count, shards, group, *refs),
        grid=(2,),
        in_specs=[whole(*rows.shape)]
        + [whole(size, width)] * (2 * count)
        + [whole(size, 1)] * count
        + [SMEM, pl.BlockSpec((1, step), lambda i: (0, i))]
        + [whole(*piece.shape) for piece in weights],
        out_specs=[whole(size, width)] * count
        + [whole(length, width)] * 2
        + [cols, cols, pl.BlockSpec((1, step), lambda i: (0, i)), whole(8, width)]
        + [whole(width, 2 * hidden)] * laid,
        out_shape=[shaped((size, width), BF)] * count
        + [shaped((length, width), BF)] * 2
        + [shaped((length, hidden), BF)] * 2
        + [shaped((1, hidden), F32), shaped((8, width), F32)]
        + [shaped((width, 2 * hidden), BF)] * laid,
        scratch_shapes=[pltpu.VMEM((length, width), BF), pltpu.VMEM((length, width), F32)],
        compiler_params=PARAMS,
        cost_estimate=SMALL,
        name="mlp",
    )(rows, *normed, *cots, *lives, ids, bias, *weights)


def mlp_weights_kernel(
    direct, ids_ref, norm_a, norm_b, grad_a, grad_b, rows_ref, fc2_ref, pre_a, pre_b, act_a, act_b,
    own_ref, *rest
):
    keep_ref, send_ref, scale2_ref, *branches, out_ref = rest
    hidden = pre_a.shape[1]
    first = dot(norm_a[...], pre_a[...], 0, 0) + dot(norm_b[...], pre_b[...], 0, 0)
    size = keep_ref.shape[0]
    out_ref[0, :, :hidden] = first[:size].astype(BF)
    out_ref[1, :, :hidden] = first[size:].astype(BF)
    outs = [grad_a[...].astype(F32), grad_b[...].astype(F32)]
    scaled = [(out * rows_ref[9:10, :]).astype(BF) for out in outs]
    second = dot(scaled[0], act_a[...], 0, 0) + dot(scaled[1], act_b[...], 0, 0)
    out_ref[0, :, hidden:] = second[:size].astype(BF)
    out_ref[1, :, hidden:] = second[size:].astype(BF)
    side = (ids_ref[1] & 1) if direct else 0
    keep_ref[...] = out_ref[side]
    send_ref[...] = out_ref[1 - side]
    scale2 = own_ref[1:2, :] * rows_ref[8:9, :]
    count = len(branches) // 2
    size = branches[0].shape[0]
    for half, act in enumerate((act_a, act_b)):
        branch = dot(act[...], fc2_ref[...], 1, 1)
        scale2 = scale2 + jnp.sum(outs[half] * branch, axis=0, keepdims=True)
        for j in range(count):
            branches[half * count + j][...] = branch[j * size : (j + 1) * size].astype(BF)
    scale2_ref[...] = scale2


def mlp_weights(rows, own, normed, grads, pres, acts, weights, group, ids, direct):
    length, width = normed[0].shape
    hidden = pres[0].shape[1]
    size = 2 * length // group
    step = 256

    cols = pl.BlockSpec((length, step), lambda i, ids_ref: (0, i))
    whole = pl.BlockSpec((length, hidden), lambda i, ids_ref: (0, 0))

    def line(count):
        return pl.BlockSpec((count, step), lambda i, ids_ref: (0, i))

    part = pl.BlockSpec((step // 2, 2 * hidden), lambda i, ids_ref: (i, 0))
    return pl.pallas_call(
        lambda *refs: mlp_weights_kernel(direct, *refs),
        grid_spec=pltpu.PrefetchScalarGridSpec(
            num_scalar_prefetch=1,
            grid=(width // step,),
            in_specs=[cols] * 4
            + [line(rows.shape[0])]
            + [pl.BlockSpec((step, hidden), lambda i, ids_ref: (i, 1))]
            + [whole] * 4
            + [line(own.shape[0])],
            out_specs=[part, part, line(1)] + [line(size)] * group,
            scratch_shapes=[pltpu.VMEM((2, step // 2, 2 * hidden), BF)],
        ),
        out_shape=[shaped((width // 2, 2 * hidden), BF)] * 2
        + [shaped((1, width), F32)]
        + [shaped((size, width), BF)] * group,
        compiler_params=PARAMS,
        cost_estimate=SMALL,
        name="mlp_weights",
    )(ids, *normed, *grads, rows, weights, *pres, *acts, own)


def finish_kernel(rows_ref, middle_ref, *rest):
    terms, out_ref = rest[:-1], rest[-1]
    branch = terms[0][...].astype(F32)
    for ref in terms[1:]:
        branch = branch + ref[...].astype(F32)
    branch = branch + rows_ref[8:9, :]
    out_ref[...] = (middle_ref[...] + rows_ref[9:10, :] * branch).astype(BF)


def finish(rows, middle, terms):
    return pl.pallas_call(
        finish_kernel,
        in_specs=[VMEM] * (2 + len(terms)),
        out_specs=VMEM,
        out_shape=shaped(middle.shape, BF),
        compiler_params=PARAMS,
        name="finish",
    )(rows, middle, *terms)


def begin_kernel(rows_ref, tokens_ref, mean_ref, inv_ref, middle_ref, *rest):
    terms, out_ref = rest[:-1], rest[-1]
    grads = terms[0][...].astype(F32)
    for ref in terms[1:]:
        grads = grads + ref[...].astype(F32)
    inverse = inv_ref[...]
    unit = (tokens_ref[...].astype(F32) - mean_ref[...]) * inverse
    out_ref[...] = (middle_ref[...] + norm_back(grads, unit, inverse, rows_ref[0:1, :])).astype(BF)


def begin(rows, tokens, mean, inverse, middle_grad, terms):
    length, width = tokens.shape
    column = pl.BlockSpec((length, 1), lambda i: (0, 0))
    whole = pl.BlockSpec((length, width), lambda i: (0, 0))
    return pl.pallas_call(
        begin_kernel,
        grid=(1,),
        in_specs=[pl.BlockSpec(rows.shape, lambda i: (0, 0)), whole, column, column, whole]
        + [whole] * len(terms),
        out_specs=whole,
        out_shape=shaped((length, width), BF),
        compiler_params=PARAMS,
        name="begin",
    )(rows, tokens, mean, inverse, middle_grad, *terms)


def qkv_back_kernel(group, grad_ref, weight_ref, mean_ref, inv_ref, *rest):
    tokens, outs, sums_ref = rest[:group], rest[group:-1], rest[-1]
    size = tokens[0].shape[0]
    gain = shift = 0.0
    for first in range(0, group, 2):
        span = slice(first * size, (first + 2) * size)
        part = dot(grad_ref[span, :], weight_ref[...], 1, 1)
        inputs = jnp.concatenate([tokens[first][...].astype(F32), tokens[first + 1][...].astype(F32)])
        unit = (inputs - mean_ref[span, :]) * inv_ref[span, :]
        outs[first][...] = part[:size].astype(BF)
        outs[first + 1][...] = part[size:].astype(BF)
        gain = gain + jnp.sum(part * unit, axis=0, keepdims=True)
        shift = shift + jnp.sum(part, axis=0, keepdims=True)
    sums_ref[...] = jnp.zeros(sums_ref.shape, F32)
    sums_ref[0:1, :] = gain
    sums_ref[1:2, :] = shift


def qkv_back(qkv_grad, weight, tokens, mean, inverse):
    size, width = tokens[0].shape
    group = len(tokens)
    return pl.pallas_call(
        lambda *refs: qkv_back_kernel(group, *refs),
        in_specs=[VMEM] * (4 + group),
        out_specs=[VMEM] * (group + 1),
        out_shape=[shaped((size, width), BF)] * group + [shaped((8, width), F32)],
        compiler_params=PARAMS,
        cost_estimate=SMALL,
        name="qkv_back",
    )(qkv_grad, weight, mean, inverse, *tokens)


def attn_weights_kernel(
    direct, shard, terms, ids_ref, normed_ref, grad_ref, norm1_ref, sums_ref, turn_ref, fbias_ref,
    scale2_ref, bias_a_ref, bias_b_ref, *rest,
):
    projs, outs = rest[:terms], rest[terms:-5]
    rows_ref, turned_ref, block_ref, small_ref, stage_ref = rest[-5:]
    place, row = ids_ref[0], ids_ref[1]
    width = normed_ref.shape[1]
    part = projs[0].shape[1]
    rows_ref[...] = jnp.zeros(rows_ref.shape, F32)
    rows_ref[0:2, :] = norm1_ref[0:2, :]
    for pair in range(part // PAIR):
        where = lanes(place * part + pair * PAIR, PAIR)
        rows_ref[2:3, where] = sums_ref[pair, :, :PAIR]
        rows_ref[3:4, where] = sums_ref[pair, :, 2 * PAIR :]
    rows_ref[4:8, :] = turn_ref[0:4, :]
    rows_ref[8:9, :] = fbias_ref[0:1, :]
    rows_ref[9:10, :] = scale2_ref[...]
    cols = bias_a_ref.shape[1] // part
    for owner in range(part // shard):
        for line in range(cols):
            spot = (owner * cols + line) * shard
            small_ref[line : line + 1, owner * shard : (owner + 1) * shard] = (
                bias_a_ref[0:1, spot : spot + shard] + bias_b_ref[0:1, spot : spot + shard]
            )
    rows_ref[10 : 10 + cols, lanes(place * part, part)] = small_ref[0:cols, :]
    turned_ref[...] = rows_ref[...].T
    step = block_ref.shape[0]
    for k in range(width // step):
        start = pl.multiple_of(((row >> 1) ^ k) * step, step) if direct else k * step
        cols = pl.ds(start, step)
        block_ref[:, : 3 * part] = dot(normed_ref[:, cols], grad_ref[...], 0, 0)
        proj = projs[0][cols, :].astype(F32)
        for ref in projs[1:]:
            proj = proj + ref[cols, :].astype(F32)
        block_ref[:, 3 * part : 4 * part] = proj
        block_ref[:, 4 * part :] = turned_ref[cols, :]
        if direct:
            size = step // 2
            stage_ref[0] = block_ref[:size, :].astype(BF)
            stage_ref[1] = block_ref[size:, :].astype(BF)
            side = row & 1
            blocks = width // step
            outs[k][...] = stage_ref[side]
            spot = (k + 1) % 2 * size
            outs[blocks + (blocks - 1 - k) // 2][spot : spot + size, :] = stage_ref[1 - side]
        else:
            outs[0][k * step : (k + 1) * step, :] = block_ref[...].astype(BF)


def attn_weights(ids, normed1, qkv_grad, sums, projs, blocks, shard):
    length, width = normed1.shape
    part = projs[0].shape[1]
    columns = 4 * part + EXTRA
    direct = blocks > 0
    step = 2 * (width // blocks) if direct else 256
    out_shape = [shaped((width, columns), BF)]
    if direct:
        size = width // blocks
        out_shape = [shaped((size, columns), BF)] * (blocks // 2)
        out_shape += [shaped((2 * size, columns), BF)] * (blocks // 4)
    return pl.pallas_call(
        lambda *refs: attn_weights_kernel(direct, shard, len(projs), *refs),
        in_specs=[SMEM] + [VMEM] * (2 + len(sums) + len(projs)),
        out_specs=[VMEM] * len(out_shape),
        out_shape=out_shape,
        scratch_shapes=[
            pltpu.VMEM((EXTRA, width), F32),
            pltpu.VMEM((width, EXTRA), F32),
            pltpu.VMEM((step, columns), F32),
            pltpu.VMEM((8, part), F32),
            pltpu.VMEM((2, step // 2, columns), BF),
        ],
        compiler_params=PARAMS,
        cost_estimate=SMALL,
        name="attn_weights",
    )(ids, normed1, qkv_grad, *sums, *projs)


def total(ids, terms, group):
    size, columns = terms[0].shape
    rows = size // group

    def kernel(ids_ref, *refs):
        ins, outs, sum_ref = refs[: len(terms)], refs[len(terms) : -1], refs[-1]
        value = ins[0][...].astype(F32)
        for ref in ins[1:]:
            value = value + ref[...].astype(F32)
        sum_ref[...] = value
        for k, out in enumerate(outs):
            start = pl.multiple_of((ids_ref[0] ^ k) * rows, rows)
            out[...] = sum_ref[pl.ds(start, rows), :].astype(BF)

    return pl.pallas_call(
        kernel,
        in_specs=[SMEM] + [VMEM] * len(terms),
        out_specs=[VMEM] * group,
        out_shape=[shaped((rows, columns), BF)] * group,
        scratch_shapes=[pltpu.VMEM((size, columns), F32)],
        compiler_params=PARAMS,
        name="total",
    )(ids, *terms)


def place_attn_kernel(ids_ref, *refs):
    group = len(refs) - 4
    blocks, (qkv_ref, proj_ref, vec_ref, bias_ref) = refs[:group], refs[group:]
    width = proj_ref.shape[1]
    part = width // group
    extra = jnp.zeros((qkv_ref.shape[0], EXTRA), F32)
    for k, block in enumerate(blocks):
        source = ids_ref[0] ^ k
        for third in range(3):
            for pair in range(part // PAIR):
                spot = (pair * 3 + third) * PAIR
                where = lanes(third * width + source * part + pair * PAIR, PAIR)
                qkv_ref[:, where] = block[:, spot : spot + PAIR].astype(F32)
        proj_ref[:, lanes(source * part, part)] = block[:, 3 * part : 4 * part].astype(F32)
        extra = extra + block[:, 4 * part :].astype(F32)
    turned = extra.T
    count = vec_ref.shape[0]
    vec_ref[...] = turned[:count]
    rows = qkv_ref.shape[0]
    for line in range(bias_ref.shape[1] // rows):
        bias_ref[0:1, line * rows : (line + 1) * rows] = turned[count + line : count + line + 1]


def place_attn(ids, blocks, width, vector_count, bias_cols):
    rows = blocks[0].shape[0]
    return pl.pallas_call(
        place_attn_kernel,
        in_specs=[SMEM] + [VMEM] * len(blocks),
        out_specs=[VMEM] * 4,
        out_shape=[
            shaped((rows, 3 * width), F32),
            shaped((rows, width), F32),
            shaped((vector_count, rows), F32),
            shaped((1, bias_cols * rows), F32),
        ],
        compiler_params=PARAMS,
        name="place_attn",
    )(ids, *blocks)


def place_mlp_kernel(ids_ref, *refs):
    group = len(refs) - 2
    blocks, (fc1_ref, fc2_ref) = refs[:group], refs[group:]
    part = fc1_ref.shape[1] // group
    for k, block in enumerate(blocks):
        where = lanes((ids_ref[0] ^ k) * part, part)
        fc1_ref[:, where] = block[:, :part].astype(F32)
        fc2_ref[:, where] = block[:, part:].astype(F32)


def place_mlp(ids, blocks, hidden):
    rows = blocks[0].shape[0]
    return pl.pallas_call(
        place_mlp_kernel,
        in_specs=[SMEM] + [VMEM] * len(blocks),
        out_specs=[VMEM] * 2,
        out_shape=[shaped((rows, hidden), F32)] * 2,
        compiler_params=PARAMS,
        name="place_mlp",
    )(ids, *blocks)


def local(tokens, counts, w_qkv, w_proj, w_fc1, fc1_bias, w_fc2, vectors, cotangent):
    _, capacity, width = tokens.shape
    hidden = w_fc1.shape[1]
    rows = w_qkv.shape[0]
    group, replicas = lax.axis_size("ctx"), lax.axis_size("dp")
    place, replica = lax.axis_index("ctx"), lax.axis_index("dp")
    ids = jnp.stack([place, replica]).astype(jnp.int32)
    head_width = width // group
    hidden_part = hidden // group
    bias_cols = hidden // width
    vector_count = vectors.shape[0]
    direct = replicas == 8

    def swap(value, bit, axis="ctx"):
        size = group if axis == "ctx" else replicas
        return lax.ppermute(value, axis, [(i, i ^ bit) for i in range(size)])

    def after(value, *before):
        return lax.optimization_barrier((value,) + before)[0]

    def gather(own, *before):
        pieces = [own]
        for j in range(1, group):
            bit = j & -j
            source = pieces[j ^ bit]
            pieces.append(swap(after(source, *before) if j ^ bit else source, bit))
        return pieces

    def scatter(parts, *before, mids=None, axis="ctx", scale=1, gates=None):
        pieces = {j: [part] for j, part in enumerate(parts)}

        def added(terms):
            if len(terms) == 1:
                return terms[0]
            return sum(term.astype(F32) for term in terms).astype(BF)

        bit = 1
        sent = []
        while bit < len(parts):
            for j in sorted((j for j in pieces if j & bit), reverse=True):
                value = added(pieces.pop(j))
                if bit > 1:
                    if mids is not None:
                        mids.append(value)
                    value = after(value, *before)
                elif axis == "dp":
                    value = after(value, *sent[-2:-1])
                if gates and bit in gates:
                    value = after(value, *gates[bit])
                sent.append(swap(value, bit * scale, axis))
                pieces[j ^ bit].append(sent[-1])
            bit *= 2
        return pieces[0]

    def exchange(relative):
        return [relative[0]] + [swap(relative[k], k) for k in range(1, group)]

    def in_order(relative):
        stacked = jnp.stack(relative)
        return jnp.concatenate(
            [lax.dynamic_index_in_dim(stacked, place ^ s, 0, False) for s in range(group)], axis=0
        )

    cuts = cut(
        ids, counts, w_qkv, w_proj.T, w_fc1, w_fc2.T, vectors, fc1_bias.reshape(1, -1), group
    )
    first = exchange(cuts[:group])
    tokens_far = swap(after(tokens[0], *first), group // 2)

    def widen(shards, *before):
        for m in range(2, replicas):
            low = m & -m
            if m ^ low:
                shards[m] = swap(after(shards[m ^ low], *before), low, "dp")

    second = exchange([after(block, *first) for block in cuts[group:]])
    if direct:
        shards = {0: jnp.concatenate(first, axis=0)}
        for bit in (4, 2, 1):
            shards[bit] = swap(shards[0], bit, "dp")
        arrived = [shards[bit] for bit in (4, 2, 1)] + second[1:]
        widen(shards, *arrived)
        shards[7] = swap(after(shards[6], tokens_far), 1, "dp")
        first_pieces = [shards[m] for m in range(replicas)]
        nearly = [shards[6], shards[3], shards[5]]
    else:
        first_pieces = [lax.all_gather(in_order(first), "dp", axis=0, tiled=True)]
        arrived = nearly = [tokens_far]
    second_shard = after(in_order(second), *arrived)
    second_all = lax.all_gather(second_shard, "dp", axis=0, tiled=True)
    tokens_pieces = [tokens[0]]
    for j in range(1, group):
        source = tokens_pieces[j ^ (j & -j)]
        if j == group // 2:
            tokens_pieces.append(tokens_far)
        else:
            tokens_pieces.append(swap(after(source, *nearly), j & -j))
    cotangent_far = swap(after(cotangent[0], *arrived), group // 2)

    tokens_own = after(tokens[0], second_shard)
    count_column = vector_count + bias_cols
    (
        weight_qkv, weight_proj, vector_rows, normed1, qkv, mean1, inverse1, bias_fc1, key_bias,
        *live,
    ) = project(
        ids, [tokens_own] + tokens_pieces[1:], first, first_pieces, hidden_part, count_column,
        0 if direct else rows,
    )

    cotangent_pieces = [cotangent[0]]
    for j in range(1, group):
        source = cotangent_pieces[j ^ (j & -j)]
        if j == group // 2:
            cotangent_pieces.append(cotangent_far)
        else:
            cotangent_pieces.append(swap(after(source, qkv), j & -j))
    attended, lse, *attended_low = attend(after(qkv, cotangent_far), key_bias, group)
    projs = gather(weight_proj, lse)
    attended_own = exchange(attended_low)
    branch1, middle, normed2_own, unit2, inverse2 = middle_step(
        vector_rows, tokens[0], attended_own, projs
    )
    half = group // 2
    normed2 = [normed2_own]
    while len(normed2) < half:
        normed2 += [swap(piece, len(normed2)) for piece in normed2]

    def feed(where, pieces, weights):
        return mlp(
            vector_rows, pieces, cotangent_pieces[where], live[where], ids, bias_fc1, weights, group
        )

    *backs_near, norm_near, grad_near, act_near, pre_near, sums_near, own_sums = feed(
        slice(0, half), normed2, [second_all]
    )
    normed2_far = [swap(normed2_own, half)]
    while len(normed2_far) < half:
        normed2_far += [
            swap(after(piece, sums_near), len(normed2_far)) for piece in normed2_far
        ]
    *backs_far, norm_far, grad_far, act_far, pre_far, sums_far, _ = feed(
        slice(half, group), normed2_far, [second_all]
    )
    mids = []
    norm2_terms = scatter(backs_near + backs_far, mids=mids)
    keep_mlp, send_mlp, grad_scale2, *branches = mlp_weights(
        vector_rows, own_sums, [norm_near, norm_far], [grad_near, grad_far], [after(pre_near, *mids), pre_far],
        [act_near, act_far], second_all, group, ids, direct,
    )
    other_mlp = None
    if direct:
        other_mlp = swap(after(send_mlp, *norm2_terms), 1, "dp")
    middle_grad, branch_grad, turn_sums, *att_grads = turn(
        vector_rows, live[0], cotangent[0], unit2, inverse2, branch1, norm2_terms, projs
    )
    att_grads = exchange(att_grads)
    mids = []
    proj_terms = scatter(proj_weights(branch_grad, attended_own), *att_grads, mids=mids)
    branch2_terms = scatter(branches, *att_grads)
    qkv_grad, qkv_sums = attend_back(qkv, key_bias, attended, after(lse, *mids), att_grads)
    pending = []
    if direct:
        other = after(other_mlp, qkv_grad)
        summed = (keep_mlp.astype(F32) + other.astype(F32)).astype(BF)
        pending.append(summed)
        lines = [[side + 2 * z for z in range(replicas // 2)] for side in range(2)]
        owned_mlp = lax.psum_scatter(
            summed, "dp", scatter_dimension=0, tiled=True, axis_index_groups=lines
        )
    else:
        ordered = jnp.stack(
            [part.reshape(-1, 128, 2 * hidden_part) for part in (keep_mlp, send_mlp)], axis=1
        )
        owned_mlp = lax.psum_scatter(
            ordered.reshape(width, 2 * hidden_part), "dp", scatter_dimension=0, tiled=True
        )
    *norm1_parts, norm1_sums = qkv_back(after(qkv_grad, *pending), weight_qkv, tokens_pieces, mean1, inverse1)
    parts = attn_weights(
        ids, normed1, qkv_grad,
        [norm1_sums, qkv_sums, turn_sums, own_sums, grad_scale2, sums_near, sums_far],
        proj_terms, replicas if direct else 0, rows,
    )
    norm1_terms = scatter(norm1_parts)
    if direct:
        def add(left, right):
            return (left.astype(F32) + right.astype(F32)).astype(BF)

        keep0, keep1, keep2, keep3, send32, send10 = parts
        size = keep0.shape[0]
        other32 = swap(send32, 1, "dp")
        other10 = swap(after(send10, other32), 1, "dp")
        across = swap(add(keep3, other32[:size]), 2, "dp")
        far = swap(add(add(keep2, other32[size:]), across), 4, "dp")
        across0 = swap(add(keep1, other10[:size]), 2, "dp")
        terms = [add(keep0, other10[size:]), across0, far]
        settled = [across]
        cuts_mlp = total(after(ids, *settled), [owned_mlp], group)
    else:
        owned_attn = lax.psum_scatter(parts[0], "dp", scatter_dimension=0, tiled=True)

        def relative(owned):
            blocks = owned.reshape(group, rows, -1)
            return [lax.dynamic_index_in_dim(blocks, place ^ k, 0, False) for k in range(group)]

        cuts_mlp = relative(owned_mlp)
        settled = []
    out_fc1, out_fc2 = place_mlp(ids, exchange(cuts_mlp), hidden)
    input_grad = begin(
        vector_rows, after(tokens[0], *settled), mean1, inverse1, middle_grad, norm1_terms
    )
    output = finish(after(vector_rows, *settled), middle, branch2_terms)
    if direct:
        cuts_attn = total(after(ids, input_grad, output, out_fc1), terms, group)
    else:
        cuts_attn = relative(owned_attn)

    out_qkv, out_proj, out_vectors, out_bias = place_attn(
        ids, exchange(cuts_attn), width, vector_count, bias_cols
    )
    return (
        output[None],
        input_grad[None],
        out_qkv,
        out_proj.T,
        out_fc1,
        out_bias.reshape(-1),
        out_fc2.T,
        out_vectors,
    )


def solution(mesh):
    both = ("dp", "ctx")
    in_specs = (
        P("dp", "ctx", None),
        P("dp", "ctx"),
        P(both, None),
        P(None, both),
        P(both, None),
        P(both),
        P(None, both),
        P(None, both),
        P("dp", "ctx", None),
    )
    out_specs = (
        P("dp", "ctx", None),
        P("dp", "ctx", None),
        P(both, None),
        P(None, both),
        P(both, None),
        P(both),
        P(None, both),
        P(None, both),
    )
    return jax.shard_map(local, mesh=mesh, in_specs=in_specs, out_specs=out_specs, check_vma=False)
```

```python
import jax
import jax.numpy as jnp
from jax import lax
from jax.experimental import pallas as pl
from jax.experimental.pallas import tpu as pltpu
from jax.sharding import PartitionSpec as P

HD = 64
PAIR = 2 * HD
EXTRA = 128
EPSILON = 1e-06
MASKED_SCORE = -1e30
SQRT_HALF = 0.7071067811865476
INV_ROOT_TWO_PI = 0.3989422804014327
BF = jnp.bfloat16
F32 = jnp.float32
PARAMS = pltpu.CompilerParams(vmem_limit_bytes=60 * 1024 * 1024)
SMALL = pl.CostEstimate(flops=1_000_000_000, bytes_accessed=1_000_000, transcendentals=0)
VMEM = pl.BlockSpec(memory_space=pltpu.VMEM)
SMEM = pl.BlockSpec(memory_space=pltpu.SMEM)


def shaped(shape, dtype):
    return jax.ShapeDtypeStruct(shape, dtype)


def dot(left, right, left_dim, right_dim):
    return lax.dot_general(
        left, right, (((left_dim,), (right_dim,)), ((), ())), preferred_element_type=F32
    )


def lanes(start, size):
    return pl.ds(pl.multiple_of(start, 128), size)


def unit_rows(inputs):
    centered = inputs - jnp.mean(inputs, axis=-1, keepdims=True)
    spread = jnp.mean(centered * centered, axis=-1, keepdims=True)
    inverse = lax.rsqrt(spread + EPSILON)
    return (centered * inverse, inverse)


def norm_back(grad_in, unit, inverse, gain):
    scaled = grad_in * gain
    inner = (
        scaled
        - jnp.mean(scaled, axis=-1, keepdims=True)
        - unit * jnp.mean(scaled * unit, axis=-1, keepdims=True)
    )
    return inner * inverse


def cut_kernel(ids_ref, count_ref, qkv_ref, proj_ref, fc1_ref, fc2_ref, vec_ref, bias_ref, *rest):
    outs, (extra_ref, turn_ref) = rest[:-2], rest[-2:]
    group = len(outs) // 2
    place = ids_ref[0]
    width = proj_ref.shape[1]
    part = width // group
    hidden_part = fc1_ref.shape[1] // group
    vector_count, bias_cols = vec_ref.shape[0], bias_ref.shape[1] // vec_ref.shape[1]
    column = vector_count + bias_cols
    lane = lax.broadcasted_iota(jnp.int32, extra_ref.shape, 1)
    count = count_ref[0, 0]
    high = (count >> 7).astype(F32)
    low = (count & 127).astype(F32)
    extra_ref[...] = jnp.where(lane == column, high, jnp.where(lane == column + 1, low, 0.0))
    extra_ref[:, :vector_count] = vec_ref[...].astype(F32).T
    rows = qkv_ref.shape[0]
    for line in range(bias_cols):
        turn_ref[line : line + 1, :] = bias_ref[0:1, line * rows : (line + 1) * rows].astype(F32)
    extra_ref[:, vector_count:column] = turn_ref[0:bias_cols, :].T
    extra = extra_ref[...].astype(BF)
    for k in range(group):
        target = place ^ k
        first, second = outs[k], outs[group + k]
        for third in range(3):
            for pair in range(part // PAIR):
                spot = (pair * 3 + third) * PAIR
                first[:, spot : spot + PAIR] = qkv_ref[
                    :, lanes(third * width + target * part + pair * PAIR, PAIR)
                ]
        first[:, 3 * part : 4 * part] = proj_ref[:, lanes(target * part, part)]
        first[:, 4 * part :] = extra
        second[:, :hidden_part] = fc1_ref[:, lanes(target * hidden_part, hidden_part)]
        second[:, hidden_part:] = fc2_ref[:, lanes(target * hidden_part, hidden_part)]


def cut(ids, counts, w_qkv, w_proj_t, w_fc1, w_fc2_t, vectors, bias, group):
    rows, width = w_proj_t.shape
    part, hidden_part = width // group, w_fc1.shape[1] // group
    return pl.pallas_call(
        cut_kernel,
        in_specs=[SMEM, SMEM] + [VMEM] * 6,
        out_specs=[VMEM] * (2 * group),
        out_shape=[shaped((rows, 4 * part + EXTRA), BF)] * group
        + [shaped((rows, 2 * hidden_part), BF)] * group,
        scratch_shapes=[pltpu.VMEM((rows, EXTRA), F32), pltpu.VMEM((8, rows), F32)],
        compiler_params=PARAMS,
        name="cut",
    )(ids, counts, w_qkv, w_proj_t, w_fc1, w_fc2_t, vectors, bias)


def project_kernel(ordered, group, count_column, ids_ref, *rest):
    tokens, blocks, rest = rest[:group], rest[group : 2 * group], rest[2 * group :]
    pieces, outs, lives, scratch = (
        rest[: -12 - group], rest[-12 - group : -3 - group], rest[-3 - group : -3], rest[-3:]
    )
    qkv_w, proj_w, rows_ref, normed_ref, out_ref, mean_ref, inv_ref, fc1_ref, key_ref = outs
    extra_ref, bias_ref, small_ref = scratch
    place, row = ids_ref[0], ids_ref[1]
    capacity, width = tokens[0].shape
    part = proj_w.shape[1]
    size = pieces[0].shape[0]

    def lay(block, start, count):
        where = pl.ds(start, count)
        qkv_w[where, :] = block[:, : 3 * part]
        proj_w[where, :] = block[:, 3 * part : 4 * part]
        extra_ref[where, :] = block[:, 4 * part :].astype(F32)

    if ordered:
        lay(pieces[0], 0, size)
        shard = ordered
    else:
        sub = shard = size // group
        for m, piece in enumerate(pieces):
            for j in range(group):
                start = (row ^ m) * size + (place ^ j) * sub
                lay(piece.at[j * sub : (j + 1) * sub], pl.multiple_of(start, sub), sub)
    slot = lax.broadcasted_iota(jnp.int32, (capacity, 1), 0).astype(F32)
    for j, (block, live_ref) in enumerate(zip(blocks, lives)):
        extra = block[:, 4 * part :].astype(F32)[0:1, :]
        bound = extra[:, count_column : count_column + 1] * 128.0
        bound = bound + extra[:, count_column + 1 : count_column + 2]
        live = jnp.where(slot < bound, 1.0, 0.0)
        live_ref[...] = live
        key_ref[j * capacity : (j + 1) * capacity, :] = (1.0 - live) * MASKED_SCORE
    turned = extra_ref[...].T
    rows_ref[...] = turned[: rows_ref.shape[0]]
    bias_ref[...] = jnp.zeros(bias_ref.shape, F32)
    for pair in range(part // PAIR):
        for third, line in ((0, 2), (2, 3)):
            spot = (pair * 3 + third) * PAIR
            bias_ref[0:1, spot : spot + PAIR] = rows_ref[
                line : line + 1, lanes(place * part + pair * PAIR, PAIR)
            ]
    cols = fc1_ref.shape[1] // part
    small_ref[0:cols, :] = rows_ref[10 : 10 + cols, lanes(place * part, part)]
    for owner in range(part // shard):
        for line in range(cols):
            spot = (owner * cols + line) * shard
            fc1_ref[0:1, spot : spot + shard] = small_ref[
                line : line + 1, owner * shard : (owner + 1) * shard
            ]
    gain, shift, bias = rows_ref[0:1, :], rows_ref[1:2, :], bias_ref[0:1, :]
    for first in range(0, group, 2):
        span = slice(first * capacity, (first + 2) * capacity)
        inputs = jnp.concatenate([tokens[first][...].astype(F32), tokens[first + 1][...].astype(F32)])
        mean = jnp.mean(inputs, axis=-1, keepdims=True)
        centered = inputs - mean
        inverse = lax.rsqrt(jnp.mean(centered * centered, axis=-1, keepdims=True) + EPSILON)
        normed = (centered * inverse * gain + shift).astype(BF)
        normed_ref[span, :] = normed
        mean_ref[span, :] = mean
        inv_ref[span, :] = inverse
        out_ref[span, :] = (dot(normed, qkv_w[...], 1, 0) + bias).astype(BF)


def project(ids, tokens, blocks, pieces, hidden_part, count_column, ordered):
    capacity, width = tokens[0].shape
    group = len(tokens)
    length = group * capacity
    part = width // group
    return pl.pallas_call(
        lambda *refs: project_kernel(ordered, group, count_column, *refs),
        in_specs=[SMEM] + [VMEM] * (2 * group + len(pieces)),
        out_specs=[VMEM] * (9 + group),
        out_shape=[
            shaped((width, 3 * part), BF),
            shaped((width, part), BF),
            shaped((16, width), F32),
            shaped((length, width), BF),
            shaped((length, 3 * part), BF),
            shaped((length, 1), F32),
            shaped((length, 1), F32),
            shaped((1, hidden_part), F32),
            shaped((length, 1), F32),
        ]
        + [shaped((capacity, 1), F32)] * group,
        scratch_shapes=[
            pltpu.VMEM((width, EXTRA), F32),
            pltpu.VMEM((8, 3 * part), F32),
            pltpu.VMEM((8, part), F32),
        ],
        compiler_params=PARAMS,
        cost_estimate=SMALL,
        name="project",
    )(ids, *tokens, *blocks, *pieces)


def query_chunks(length):
    step = 512
    return [(start, min(step, length - start)) for start in range(0, length, step)]


def attend_kernel(qkv_ref, bias_ref, out_ref, lse_ref, *lows):
    length = qkv_ref.shape[0]
    key_bias = bias_ref[...]
    for head in range(2):
        keys = qkv_ref[:, PAIR + head * HD : PAIR + (head + 1) * HD]
        values = qkv_ref[:, 2 * PAIR + head * HD : 2 * PAIR + (head + 1) * HD]
        for start, size in query_chunks(length):
            queries = qkv_ref[start : start + size, head * HD : (head + 1) * HD]
            queries = queries * jnp.asarray(HD**-0.5, BF)
            scores = dot(keys, queries, 1, 1) + key_bias
            top = jnp.max(scores, axis=0, keepdims=True)
            expo = jnp.exp(scores - top)
            total = jnp.sum(expo, axis=0, keepdims=True)
            mixed = (dot(values, expo.astype(BF), 0, 0) / total).T
            out_ref[start : start + size, head * HD : (head + 1) * HD] = mixed
            lse_ref[0, head : head + 1, start : start + size] = top + jnp.log(total)
    for j, low in enumerate(lows):
        size = low.shape[0]
        low[...] = out_ref[j * size : (j + 1) * size, :].astype(BF)


def attend(qkv, key_bias, group):
    length, columns = qkv.shape
    pairs = columns // (3 * PAIR)
    return pl.pallas_call(
        attend_kernel,
        grid=(pairs,),
        in_specs=[
            pl.BlockSpec((length, 3 * PAIR), lambda p: (0, p)),
            pl.BlockSpec((length, 1), lambda p: (0, 0)),
        ],
        out_specs=[
            pl.BlockSpec((length, PAIR), lambda p: (0, p)),
            pl.BlockSpec((1, 2, length), lambda p: (p, 0, 0)),
        ]
        + [pl.BlockSpec((length // group, PAIR), lambda p: (0, p))] * group,
        out_shape=[
            shaped((length, pairs * PAIR), F32),
            shaped((pairs, 2, length), F32),
        ]
        + [shaped((length // group, pairs * PAIR), BF)] * group,
        compiler_params=PARAMS,
        cost_estimate=SMALL,
        name="attend",
    )(qkv, key_bias)


def attend_back_kernel(qkv_ref, bias_ref, att_ref, lse_ref, *rest):
    pieces, (out_ref, sums_ref, grad_ref) = rest[:-3], rest[-3:]
    length = qkv_ref.shape[0]
    size = pieces[0].shape[0]
    factor = HD**-0.5
    key_bias = bias_ref[...]
    for j, piece in enumerate(pieces):
        grad_ref[j * size : (j + 1) * size, :] = piece[...].astype(F32)
    for head in range(2):
        low, high = head * HD, (head + 1) * HD
        keys = qkv_ref[:, PAIR + low : PAIR + high]
        values = qkv_ref[:, 2 * PAIR + low : 2 * PAIR + high]
        key_grad = jnp.zeros((length, HD), F32)
        value_grad = jnp.zeros((length, HD), F32)
        for start, size in query_chunks(length):
            rows = slice(start, start + size)
            queries = qkv_ref[rows, low:high] * jnp.asarray(factor, BF)
            product = grad_ref[rows, low:high] * att_ref[rows, low:high]
            grads = grad_ref[rows, low:high].astype(BF)
            delta = jnp.sum(product.T, axis=0, keepdims=True)
            scores = dot(keys, queries, 1, 1) + key_bias
            probs = jnp.exp(scores - lse_ref[0, head : head + 1, rows])
            value_grad += dot(probs.astype(BF), grads, 1, 0)
            raw = (probs * (dot(values, grads, 1, 1) - delta)).astype(BF)
            key_grad += dot(raw, queries, 1, 0)
            query_grad = dot(keys, raw, 0, 0).T * factor
            out_ref[rows, low:high] = query_grad.astype(BF)
        out_ref[:, PAIR + low : PAIR + high] = key_grad.astype(BF)
        out_ref[:, 2 * PAIR + low : 2 * PAIR + high] = value_grad.astype(BF)
    sums_ref[0] = jnp.sum(out_ref[...].astype(F32), axis=0, keepdims=True)


def attend_back(qkv, key_bias, attended, lse, pieces):
    length, columns = qkv.shape
    pairs = columns // (3 * PAIR)
    size = pieces[0].shape[0]
    return pl.pallas_call(
        attend_back_kernel,
        grid=(pairs,),
        in_specs=[
            pl.BlockSpec((length, 3 * PAIR), lambda p: (0, p)),
            pl.BlockSpec((length, 1), lambda p: (0, 0)),
            pl.BlockSpec((length, PAIR), lambda p: (0, p)),
            pl.BlockSpec((1, 2, length), lambda p: (p, 0, 0)),
        ]
        + [pl.BlockSpec((size, PAIR), lambda p: (0, p))] * len(pieces),
        out_specs=[
            pl.BlockSpec((length, 3 * PAIR), lambda p: (0, p)),
            pl.BlockSpec((1, 1, 3 * PAIR), lambda p: (p, 0, 0)),
        ],
        out_shape=[shaped((length, columns), BF), shaped((pairs, 1, 3 * PAIR), F32)],
        scratch_shapes=[pltpu.VMEM((length, PAIR), F32)],
        compiler_params=PARAMS,
        cost_estimate=SMALL,
        name="attend_back",
    )(qkv, key_bias, attended, lse, *pieces)


def middle_kernel(group, rows_ref, tokens_ref, *rest):
    parts, weights, (branch_ref, middle_ref, normed_ref, unit_ref, inv_ref) = (
        rest[:group], rest[group : 2 * group], rest[2 * group :]
    )
    branch = dot(parts[0][...], weights[0][...], 1, 1)
    for part, weight in zip(parts[1:], weights[1:]):
        branch = branch + dot(part[...], weight[...], 1, 1)
    branch = branch + rows_ref[4:5, :]
    branch_ref[...] = branch
    middle = tokens_ref[...].astype(F32) + rows_ref[5:6, :] * branch
    middle_ref[...] = middle
    unit, inverse = unit_rows(middle)
    unit_ref[...] = unit
    inv_ref[...] = inverse
    normed_ref[...] = (unit * rows_ref[6:7, :] + rows_ref[7:8, :]).astype(BF)


def middle_step(rows, tokens, parts, weights):
    length, width = tokens.shape
    group = len(parts)
    full = shaped((length, width), F32)
    return pl.pallas_call(
        lambda *refs: middle_kernel(group, *refs),
        in_specs=[VMEM] * (2 + 2 * group),
        out_specs=[VMEM] * 5,
        out_shape=[full, full, shaped((length, width), BF), full, shaped((length, 1), F32)],
        compiler_params=PARAMS,
        cost_estimate=SMALL,
        name="middle",
    )(rows, tokens, *parts, *weights)


def turn_kernel(group, terms, rows_ref, live_ref, cot_ref, unit_ref, inv_ref, branch_ref, *rest):
    backs, weights, outs = rest[:terms], rest[terms : terms + group], rest[terms + group :]
    middle_ref, grad_ref, sums_ref = outs[:3]
    norm_grad = backs[0][...].astype(F32)
    for ref in backs[1:]:
        norm_grad = norm_grad + ref[...].astype(F32)
    unit = unit_ref[...]
    out_grad = cot_ref[...].astype(F32) * live_ref[...]
    middle = out_grad + norm_back(norm_grad, unit, inv_ref[...], rows_ref[6:7, :])
    middle_ref[...] = middle
    low = (middle * rows_ref[5:6, :]).astype(BF)
    grad_ref[...] = low
    sums_ref[...] = jnp.zeros(sums_ref.shape, F32)
    sums_ref[0:1, :] = jnp.sum(low.astype(F32), axis=0, keepdims=True)
    sums_ref[1:2, :] = jnp.sum(middle * branch_ref[...], axis=0, keepdims=True)
    sums_ref[2:3, :] = jnp.sum(norm_grad * unit, axis=0, keepdims=True)
    sums_ref[3:4, :] = jnp.sum(norm_grad, axis=0, keepdims=True)
    for out, weight in zip(outs[3:], weights):
        out[...] = dot(low, weight[...], 1, 0).astype(BF)


def turn(rows, live, cotangent, unit, inverse, branch, backs, weights):
    length, width = cotangent.shape
    part = weights[0].shape[1]
    group = len(weights)
    return pl.pallas_call(
        lambda *refs: turn_kernel(group, len(backs), *refs),
        in_specs=[VMEM] * (6 + len(backs) + group),
        out_specs=[VMEM] * (3 + group),
        out_shape=[shaped((length, width), F32), shaped((length, width), BF), shaped((8, width), F32)]
        + [shaped((length, part), BF)] * group,
        compiler_params=PARAMS,
        cost_estimate=SMALL,
        name="turn",
    )(rows, live, cotangent, unit, inverse, branch, *backs, *weights)


def proj_weights_kernel(grad_ref, *rest):
    half = len(rest) // 2
    for part, out in zip(rest[:half], rest[half:]):
        out[...] = dot(grad_ref[...], part[...], 0, 0).astype(BF)


def proj_weights(grads, parts):
    length, width = grads.shape
    part = parts[0].shape[1]
    return pl.pallas_call(
        proj_weights_kernel,
        in_specs=[VMEM] * (1 + len(parts)),
        out_specs=[VMEM] * len(parts),
        out_shape=[shaped((width, part), BF)] * len(parts),
        compiler_params=PARAMS,
        cost_estimate=SMALL,
        name="proj_weights",
    )(grads, *parts)


def mlp_kernel(count, shards, group, rows_ref, *rest):
    normed_in, cots, lives = rest[:count], rest[count : 2 * count], rest[2 * count : 3 * count]
    ids_ref, bias_ref = rest[3 * count : 3 * count + 2]
    rest = rest[3 * count + 2 :]
    pieces, backs, rest = rest[:shards], rest[shards : shards + count], rest[shards + count :]
    normed_ref, out_ref, act_ref, pre_ref, sums_ref, own_ref = rest[:6]
    if shards > 1:
        weight_ref, grad_ref, back_acc = rest[6:]
    else:
        weight_ref = pieces[0]
        grad_ref, back_acc = rest[6:]
    step = pl.program_id(0)
    size = cots[0].shape[0]

    @pl.when(step == 0)
    def _():
        if shards > 1:
            whole_size = pieces[0].shape[0]
            sub = whole_size // group
            for m, piece in enumerate(pieces):
                for j in range(group):
                    start = (ids_ref[1] ^ m) * whole_size + (ids_ref[0] ^ j) * sub
                    weight_ref[pl.ds(pl.multiple_of(start, sub), sub), :] = piece[
                        j * sub : (j + 1) * sub, :
                    ]
        normed_ref[...] = jnp.concatenate([ref[...].astype(F32) for ref in normed_in]).astype(BF)
        scale = rows_ref[9:10, :]
        grads = [cot[...].astype(F32) * live[...] for cot, live in zip(cots, lives)]
        whole_grad = jnp.concatenate(grads)
        out_ref[...] = whole_grad.astype(BF)
        scaled = (whole_grad * scale).astype(BF)
        grad_ref[...] = scaled
        own_ref[0:1, :] = jnp.sum(scaled.astype(F32)[:size], axis=0, keepdims=True)
        own_ref[1:2, :] = jnp.sum(grads[0], axis=0, keepdims=True)

    hidden = weight_ref.shape[1] // 2
    span = act_ref.shape[1]
    chunk = span // 2
    for cols in (slice(0, chunk), slice(chunk, 2 * chunk)):
        here = lanes(step * span + cols.start, chunk)
        there = lanes(hidden + step * span + cols.start, chunk)
        pre = dot(normed_ref[...], weight_ref[:, here], 1, 0) + bias_ref[:, cols]
        act_grad = dot(grad_ref[...], weight_ref[:, there], 1, 0)
        cdf = 0.5 * (1.0 + lax.erf(pre * SQRT_HALF))
        act_ref[:, cols] = (pre * cdf).astype(BF)
        slope = cdf + pre * (jnp.exp(-0.5 * pre * pre) * INV_ROOT_TWO_PI)
        pre_grad = (act_grad * slope).astype(BF)
        pre_ref[:, cols] = pre_grad
        sums_ref[:, cols] = jnp.sum(pre_grad.astype(F32), axis=0, keepdims=True)
    back = dot(pre_ref[...], weight_ref[:, lanes(step * span, span)], 1, 1)

    @pl.when(step == 0)
    def _():
        back_acc[...] = back

    @pl.when(step == pl.num_programs(0) - 1)
    def _():
        whole = back_acc[...] + back
        for j, ref in enumerate(backs):
            ref[...] = whole[j * size : (j + 1) * size].astype(BF)


def mlp(rows, normed, cots, lives, ids, bias, weights, group):
    size, width = normed[0].shape
    count, shards = len(normed), len(weights)
    length = count * size
    hidden = weights[0].shape[1] // 2
    laid = shards > 1
    step = hidden // 2

    def whole(*shape):
        return pl.BlockSpec(shape, lambda i: (0, 0))

    cols = pl.BlockSpec((length, step), lambda i: (0, i))
    return pl.pallas_call(
        lambda *refs: mlp_kernel(count, shards, group, *refs),
        grid=(2,),
        in_specs=[whole(*rows.shape)]
        + [whole(size, width)] * (2 * count)
        + [whole(size, 1)] * count
        + [SMEM, pl.BlockSpec((1, step), lambda i: (0, i))]
        + [whole(*piece.shape) for piece in weights],
        out_specs=[whole(size, width)] * count
        + [whole(length, width)] * 2
        + [cols, cols, pl.BlockSpec((1, step), lambda i: (0, i)), whole(8, width)]
        + [whole(width, 2 * hidden)] * laid,
        out_shape=[shaped((size, width), BF)] * count
        + [shaped((length, width), BF)] * 2
        + [shaped((length, hidden), BF)] * 2
        + [shaped((1, hidden), F32), shaped((8, width), F32)]
        + [shaped((width, 2 * hidden), BF)] * laid,
        scratch_shapes=[pltpu.VMEM((length, width), BF), pltpu.VMEM((length, width), F32)],
        compiler_params=PARAMS,
        cost_estimate=SMALL,
        name="mlp",
    )(rows, *normed, *cots, *lives, ids, bias, *weights)


def mlp_weights_kernel(
    direct, ids_ref, norm_a, norm_b, grad_a, grad_b, rows_ref, fc2_ref, pre_a, pre_b, act_a, act_b,
    own_ref, *rest
):
    keep_ref, send_ref, scale2_ref, *branches, out_ref = rest
    hidden = pre_a.shape[1]
    first = dot(norm_a[...], pre_a[...], 0, 0) + dot(norm_b[...], pre_b[...], 0, 0)
    size = keep_ref.shape[0]
    out_ref[0, :, :hidden] = first[:size].astype(BF)
    out_ref[1, :, :hidden] = first[size:].astype(BF)
    outs = [grad_a[...].astype(F32), grad_b[...].astype(F32)]
    scaled = [(out * rows_ref[9:10, :]).astype(BF) for out in outs]
    second = dot(scaled[0], act_a[...], 0, 0) + dot(scaled[1], act_b[...], 0, 0)
    out_ref[0, :, hidden:] = second[:size].astype(BF)
    out_ref[1, :, hidden:] = second[size:].astype(BF)
    side = (ids_ref[1] & 1) if direct else 0
    keep_ref[...] = out_ref[side]
    send_ref[...] = out_ref[1 - side]
    scale2 = own_ref[1:2, :] * rows_ref[8:9, :]
    count = len(branches) // 2
    size = branches[0].shape[0]
    for half, act in enumerate((act_a, act_b)):
        branch = dot(act[...], fc2_ref[...], 1, 1)
        scale2 = scale2 + jnp.sum(outs[half] * branch, axis=0, keepdims=True)
        for j in range(count):
            branches[half * count + j][...] = branch[j * size : (j + 1) * size].astype(BF)
    scale2_ref[...] = scale2


def mlp_weights(rows, own, normed, grads, pres, acts, weights, group, ids, direct):
    length, width = normed[0].shape
    hidden = pres[0].shape[1]
    size = 2 * length // group
    step = 256

    cols = pl.BlockSpec((length, step), lambda i, ids_ref: (0, i))
    whole = pl.BlockSpec((length, hidden), lambda i, ids_ref: (0, 0))

    def line(count):
        return pl.BlockSpec((count, step), lambda i, ids_ref: (0, i))

    part = pl.BlockSpec((step // 2, 2 * hidden), lambda i, ids_ref: (i, 0))
    return pl.pallas_call(
        lambda *refs: mlp_weights_kernel(direct, *refs),
        grid_spec=pltpu.PrefetchScalarGridSpec(
            num_scalar_prefetch=1,
            grid=(width // step,),
            in_specs=[cols] * 4
            + [line(rows.shape[0])]
            + [pl.BlockSpec((step, hidden), lambda i, ids_ref: (i, 1))]
            + [whole] * 4
            + [line(own.shape[0])],
            out_specs=[part, part, line(1)] + [line(size)] * group,
            scratch_shapes=[pltpu.VMEM((2, step // 2, 2 * hidden), BF)],
        ),
        out_shape=[shaped((width // 2, 2 * hidden), BF)] * 2
        + [shaped((1, width), F32)]
        + [shaped((size, width), BF)] * group,
        compiler_params=PARAMS,
        cost_estimate=SMALL,
        name="mlp_weights",
    )(ids, *normed, *grads, rows, weights, *pres, *acts, own)


def finish_kernel(rows_ref, middle_ref, *rest):
    terms, out_ref = rest[:-1], rest[-1]
    branch = terms[0][...].astype(F32)
    for ref in terms[1:]:
        branch = branch + ref[...].astype(F32)
    branch = branch + rows_ref[8:9, :]
    out_ref[...] = (middle_ref[...] + rows_ref[9:10, :] * branch).astype(BF)


def finish(rows, middle, terms):
    return pl.pallas_call(
        finish_kernel,
        in_specs=[VMEM] * (2 + len(terms)),
        out_specs=VMEM,
        out_shape=shaped(middle.shape, BF),
        compiler_params=PARAMS,
        name="finish",
    )(rows, middle, *terms)


def begin_kernel(rows_ref, tokens_ref, mean_ref, inv_ref, middle_ref, *rest):
    terms, out_ref = rest[:-1], rest[-1]
    grads = terms[0][...].astype(F32)
    for ref in terms[1:]:
        grads = grads + ref[...].astype(F32)
    inverse = inv_ref[...]
    unit = (tokens_ref[...].astype(F32) - mean_ref[...]) * inverse
    out_ref[...] = (middle_ref[...] + norm_back(grads, unit, inverse, rows_ref[0:1, :])).astype(BF)


def begin(rows, tokens, mean, inverse, middle_grad, terms):
    length, width = tokens.shape
    column = pl.BlockSpec((length, 1), lambda i: (0, 0))
    whole = pl.BlockSpec((length, width), lambda i: (0, 0))
    return pl.pallas_call(
        begin_kernel,
        grid=(1,),
        in_specs=[pl.BlockSpec(rows.shape, lambda i: (0, 0)), whole, column, column, whole]
        + [whole] * len(terms),
        out_specs=whole,
        out_shape=shaped((length, width), BF),
        compiler_params=PARAMS,
        name="begin",
    )(rows, tokens, mean, inverse, middle_grad, *terms)


def qkv_back_kernel(group, grad_ref, weight_ref, mean_ref, inv_ref, *rest):
    tokens, outs, sums_ref = rest[:group], rest[group:-1], rest[-1]
    size = tokens[0].shape[0]
    gain = shift = 0.0
    for first in range(0, group, 2):
        span = slice(first * size, (first + 2) * size)
        part = dot(grad_ref[span, :], weight_ref[...], 1, 1)
        inputs = jnp.concatenate([tokens[first][...].astype(F32), tokens[first + 1][...].astype(F32)])
        unit = (inputs - mean_ref[span, :]) * inv_ref[span, :]
        outs[first][...] = part[:size].astype(BF)
        outs[first + 1][...] = part[size:].astype(BF)
        gain = gain + jnp.sum(part * unit, axis=0, keepdims=True)
        shift = shift + jnp.sum(part, axis=0, keepdims=True)
    sums_ref[...] = jnp.zeros(sums_ref.shape, F32)
    sums_ref[0:1, :] = gain
    sums_ref[1:2, :] = shift


def qkv_back(qkv_grad, weight, tokens, mean, inverse):
    size, width = tokens[0].shape
    group = len(tokens)
    return pl.pallas_call(
        lambda *refs: qkv_back_kernel(group, *refs),
        in_specs=[VMEM] * (4 + group),
        out_specs=[VMEM] * (group + 1),
        out_shape=[shaped((size, width), BF)] * group + [shaped((8, width), F32)],
        compiler_params=PARAMS,
        cost_estimate=SMALL,
        name="qkv_back",
    )(qkv_grad, weight, mean, inverse, *tokens)


def attn_weights_kernel(
    direct, shard, terms, ids_ref, normed_ref, grad_ref, norm1_ref, sums_ref, turn_ref, fbias_ref,
    scale2_ref, bias_a_ref, bias_b_ref, *rest,
):
    projs, outs = rest[:terms], rest[terms:-5]
    rows_ref, turned_ref, block_ref, small_ref, stage_ref = rest[-5:]
    place, row = ids_ref[0], ids_ref[1]
    width = normed_ref.shape[1]
    part = projs[0].shape[1]
    rows_ref[...] = jnp.zeros(rows_ref.shape, F32)
    rows_ref[0:2, :] = norm1_ref[0:2, :]
    for pair in range(part // PAIR):
        where = lanes(place * part + pair * PAIR, PAIR)
        rows_ref[2:3, where] = sums_ref[pair, :, :PAIR]
        rows_ref[3:4, where] = sums_ref[pair, :, 2 * PAIR :]
    rows_ref[4:8, :] = turn_ref[0:4, :]
    rows_ref[8:9, :] = fbias_ref[0:1, :]
    rows_ref[9:10, :] = scale2_ref[...]
    cols = bias_a_ref.shape[1] // part
    for owner in range(part // shard):
        for line in range(cols):
            spot = (owner * cols + line) * shard
            small_ref[line : line + 1, owner * shard : (owner + 1) * shard] = (
                bias_a_ref[0:1, spot : spot + shard] + bias_b_ref[0:1, spot : spot + shard]
            )
    rows_ref[10 : 10 + cols, lanes(place * part, part)] = small_ref[0:cols, :]
    turned_ref[...] = rows_ref[...].T
    step = block_ref.shape[0]
    for k in range(width // step):
        start = pl.multiple_of(((row >> 1) ^ k) * step, step) if direct else k * step
        cols = pl.ds(start, step)
        block_ref[:, : 3 * part] = dot(normed_ref[:, cols], grad_ref[...], 0, 0)
        proj = projs[0][cols, :].astype(F32)
        for ref in projs[1:]:
            proj = proj + ref[cols, :].astype(F32)
        block_ref[:, 3 * part : 4 * part] = proj
        block_ref[:, 4 * part :] = turned_ref[cols, :]
        if direct:
            size = step // 2
            stage_ref[0] = block_ref[:size, :].astype(BF)
            stage_ref[1] = block_ref[size:, :].astype(BF)
            side = row & 1
            blocks = width // step
            outs[k][...] = stage_ref[side]
            spot = (k + 1) % 2 * size
            outs[blocks + (blocks - 1 - k) // 2][spot : spot + size, :] = stage_ref[1 - side]
        else:
            outs[0][k * step : (k + 1) * step, :] = block_ref[...].astype(BF)


def attn_weights(ids, normed1, qkv_grad, sums, projs, blocks, shard):
    length, width = normed1.shape
    part = projs[0].shape[1]
    columns = 4 * part + EXTRA
    direct = blocks > 0
    step = 2 * (width // blocks) if direct else 256
    out_shape = [shaped((width, columns), BF)]
    if direct:
        size = width // blocks
        out_shape = [shaped((size, columns), BF)] * (blocks // 2)
        out_shape += [shaped((2 * size, columns), BF)] * (blocks // 4)
    return pl.pallas_call(
        lambda *refs: attn_weights_kernel(direct, shard, len(projs), *refs),
        in_specs=[SMEM] + [VMEM] * (2 + len(sums) + len(projs)),
        out_specs=[VMEM] * len(out_shape),
        out_shape=out_shape,
        scratch_shapes=[
            pltpu.VMEM((EXTRA, width), F32),
            pltpu.VMEM((width, EXTRA), F32),
            pltpu.VMEM((step, columns), F32),
            pltpu.VMEM((8, part), F32),
            pltpu.VMEM((2, step // 2, columns), BF),
        ],
        compiler_params=PARAMS,
        cost_estimate=SMALL,
        name="attn_weights",
    )(ids, normed1, qkv_grad, *sums, *projs)


def total(ids, terms, group):
    size, columns = terms[0].shape
    rows = size // group

    def kernel(ids_ref, *refs):
        ins, outs, sum_ref = refs[: len(terms)], refs[len(terms) : -1], refs[-1]
        value = ins[0][...].astype(F32)
        for ref in ins[1:]:
            value = value + ref[...].astype(F32)
        sum_ref[...] = value
        for k, out in enumerate(outs):
            start = pl.multiple_of((ids_ref[0] ^ k) * rows, rows)
            out[...] = sum_ref[pl.ds(start, rows), :].astype(BF)

    return pl.pallas_call(
        kernel,
        in_specs=[SMEM] + [VMEM] * len(terms),
        out_specs=[VMEM] * group,
        out_shape=[shaped((rows, columns), BF)] * group,
        scratch_shapes=[pltpu.VMEM((size, columns), F32)],
        compiler_params=PARAMS,
        name="total",
    )(ids, *terms)


def place_attn_kernel(ids_ref, *refs):
    group = len(refs) - 4
    blocks, (qkv_ref, proj_ref, vec_ref, bias_ref) = refs[:group], refs[group:]
    width = proj_ref.shape[1]
    part = width // group
    extra = jnp.zeros((qkv_ref.shape[0], EXTRA), F32)
    for k, block in enumerate(blocks):
        source = ids_ref[0] ^ k
        for third in range(3):
            for pair in range(part // PAIR):
                spot = (pair * 3 + third) * PAIR
                where = lanes(third * width + source * part + pair * PAIR, PAIR)
                qkv_ref[:, where] = block[:, spot : spot + PAIR].astype(F32)
        proj_ref[:, lanes(source * part, part)] = block[:, 3 * part : 4 * part].astype(F32)
        extra = extra + block[:, 4 * part :].astype(F32)
    turned = extra.T
    count = vec_ref.shape[0]
    vec_ref[...] = turned[:count]
    rows = qkv_ref.shape[0]
    for line in range(bias_ref.shape[1] // rows):
        bias_ref[0:1, line * rows : (line + 1) * rows] = turned[count + line : count + line + 1]


def place_attn(ids, blocks, width, vector_count, bias_cols):
    rows = blocks[0].shape[0]
    return pl.pallas_call(
        place_attn_kernel,
        in_specs=[SMEM] + [VMEM] * len(blocks),
        out_specs=[VMEM] * 4,
        out_shape=[
            shaped((rows, 3 * width), F32),
            shaped((rows, width), F32),
            shaped((vector_count, rows), F32),
            shaped((1, bias_cols * rows), F32),
        ],
        compiler_params=PARAMS,
        name="place_attn",
    )(ids, *blocks)


def place_mlp_kernel(ids_ref, *refs):
    group = len(refs) - 2
    blocks, (fc1_ref, fc2_ref) = refs[:group], refs[group:]
    part = fc1_ref.shape[1] // group
    for k, block in enumerate(blocks):
        where = lanes((ids_ref[0] ^ k) * part, part)
        fc1_ref[:, where] = block[:, :part].astype(F32)
        fc2_ref[:, where] = block[:, part:].astype(F32)


def place_mlp(ids, blocks, hidden):
    rows = blocks[0].shape[0]
    return pl.pallas_call(
        place_mlp_kernel,
        in_specs=[SMEM] + [VMEM] * len(blocks),
        out_specs=[VMEM] * 2,
        out_shape=[shaped((rows, hidden), F32)] * 2,
        compiler_params=PARAMS,
        name="place_mlp",
    )(ids, *blocks)


def local(tokens, counts, w_qkv, w_proj, w_fc1, fc1_bias, w_fc2, vectors, cotangent):
    _, capacity, width = tokens.shape
    hidden = w_fc1.shape[1]
    rows = w_qkv.shape[0]
    group, replicas = lax.axis_size("ctx"), lax.axis_size("dp")
    place, replica = lax.axis_index("ctx"), lax.axis_index("dp")
    ids = jnp.stack([place, replica]).astype(jnp.int32)
    head_width = width // group
    hidden_part = hidden // group
    bias_cols = hidden // width
    vector_count = vectors.shape[0]
    direct = replicas == 8

    def swap(value, bit, axis="ctx"):
        size = group if axis == "ctx" else replicas
        return lax.ppermute(value, axis, [(i, i ^ bit) for i in range(size)])

    def after(value, *before):
        return lax.optimization_barrier((value,) + before)[0]

    def gather(own, *before):
        pieces = [own]
        for j in range(1, group):
            bit = j & -j
            source = pieces[j ^ bit]
            pieces.append(swap(after(source, *before) if j ^ bit else source, bit))
        return pieces

    def scatter(parts, *before, mids=None, axis="ctx", scale=1, gates=None):
        pieces = {j: [part] for j, part in enumerate(parts)}

        def added(terms):
            if len(terms) == 1:
                return terms[0]
            return sum(term.astype(F32) for term in terms).astype(BF)

        bit = 1
        sent = []
        while bit < len(parts):
            for j in sorted((j for j in pieces if j & bit), reverse=True):
                value = added(pieces.pop(j))
                if bit > 1:
                    if mids is not None:
                        mids.append(value)
                    value = after(value, *before)
                elif axis == "dp":
                    value = after(value, *sent[-2:-1])
                if gates and bit in gates:
                    value = after(value, *gates[bit])
                sent.append(swap(value, bit * scale, axis))
                pieces[j ^ bit].append(sent[-1])
            bit *= 2
        return pieces[0]

    def exchange(relative):
        return [relative[0]] + [swap(relative[k], k) for k in range(1, group)]

    def in_order(relative):
        stacked = jnp.stack(relative)
        return jnp.concatenate(
            [lax.dynamic_index_in_dim(stacked, place ^ s, 0, False) for s in range(group)], axis=0
        )

    cuts = cut(
        ids, counts, w_qkv, w_proj.T, w_fc1, w_fc2.T, vectors, fc1_bias.reshape(1, -1), group
    )
    first = exchange(cuts[:group])
    tokens_far = swap(after(tokens[0], *first), group // 2)

    def widen(shards, *before):
        for m in range(2, replicas):
            low = m & -m
            if m ^ low:
                shards[m] = swap(after(shards[m ^ low], *before), low, "dp")

    second = exchange([after(block, *first) for block in cuts[group:]])
    if direct:
        shards = {0: jnp.concatenate(first, axis=0)}
        for bit in (4, 2, 1):
            shards[bit] = swap(shards[0], bit, "dp")
        arrived = [shards[bit] for bit in (4, 2, 1)] + second[1:]
        widen(shards, *arrived)
        first_pieces = [shards[m] for m in range(replicas)]
        nearly = [shards[3], shards[5], shards[7]]
    else:
        first_pieces = [lax.all_gather(in_order(first), "dp", axis=0, tiled=True)]
        arrived = nearly = [tokens_far]
    second_shard = after(in_order(second), *arrived)
    second_all = lax.all_gather(second_shard, "dp", axis=0, tiled=True)
    tokens_pieces = [tokens[0]]
    for j in range(1, group):
        source = tokens_pieces[j ^ (j & -j)]
        if j == group // 2:
            tokens_pieces.append(tokens_far)
        else:
            tokens_pieces.append(swap(after(source, *nearly), j & -j))
    cotangent_far = swap(after(cotangent[0], *arrived), group // 2)

    tokens_own = after(tokens[0], second_shard)
    count_column = vector_count + bias_cols
    (
        weight_qkv, weight_proj, vector_rows, normed1, qkv, mean1, inverse1, bias_fc1, key_bias,
        *live,
    ) = project(
        ids, [tokens_own] + tokens_pieces[1:], first, first_pieces, hidden_part, count_column,
        0 if direct else rows,
    )

    cotangent_pieces = [cotangent[0]]
    for j in range(1, group):
        source = cotangent_pieces[j ^ (j & -j)]
        if j == group // 2:
            cotangent_pieces.append(cotangent_far)
        else:
            cotangent_pieces.append(swap(after(source, qkv), j & -j))
    attended, lse, *attended_low = attend(after(qkv, cotangent_far), key_bias, group)
    projs = gather(weight_proj, lse)
    attended_own = exchange(attended_low)
    branch1, middle, normed2_own, unit2, inverse2 = middle_step(
        vector_rows, tokens[0], attended_own, projs
    )
    half = group // 2
    normed2 = [normed2_own]
    while len(normed2) < half:
        normed2 += [swap(piece, len(normed2)) for piece in normed2]

    def feed(where, pieces, weights):
        return mlp(
            vector_rows, pieces, cotangent_pieces[where], live[where], ids, bias_fc1, weights, group
        )

    *backs_near, norm_near, grad_near, act_near, pre_near, sums_near, own_sums = feed(
        slice(0, half), normed2, [second_all]
    )
    normed2_far = [swap(normed2_own, half)]
    while len(normed2_far) < half:
        normed2_far += [
            swap(after(piece, sums_near), len(normed2_far)) for piece in normed2_far
        ]
    *backs_far, norm_far, grad_far, act_far, pre_far, sums_far, _ = feed(
        slice(half, group), normed2_far, [second_all]
    )
    mids = []
    norm2_terms = scatter(backs_near + backs_far, mids=mids)
    keep_mlp, send_mlp, grad_scale2, *branches = mlp_weights(
        vector_rows, own_sums, [norm_near, norm_far], [grad_near, grad_far], [after(pre_near, *mids), pre_far],
        [act_near, act_far], second_all, group, ids, direct,
    )
    other_mlp = None
    if direct:
        other_mlp = swap(after(send_mlp, *norm2_terms), 1, "dp")
    middle_grad, branch_grad, turn_sums, *att_grads = turn(
        vector_rows, live[0], cotangent[0], unit2, inverse2, branch1, norm2_terms, projs
    )
    att_grads = exchange(att_grads)
    mids = []
    proj_terms = scatter(proj_weights(branch_grad, attended_own), *att_grads, mids=mids)
    branch2_mids = []
    branch2_terms = scatter(branches, *att_grads, mids=branch2_mids)
    qkv_grad, qkv_sums = attend_back(qkv, key_bias, attended, after(lse, *mids), att_grads)
    *norm1_parts, norm1_sums = qkv_back(qkv_grad, weight_qkv, tokens_pieces, mean1, inverse1)
    if direct:
        other = after(other_mlp, norm1_sums)
        summed = (keep_mlp.astype(F32) + other.astype(F32)).astype(BF)
        lines = [[side + 2 * z for z in range(replicas // 2)] for side in range(2)]
        owned_mlp = lax.psum_scatter(
            summed, "dp", scatter_dimension=0, tiled=True, axis_index_groups=lines
        )
    else:
        ordered = jnp.stack(
            [part.reshape(-1, 128, 2 * hidden_part) for part in (keep_mlp, send_mlp)], axis=1
        )
        owned_mlp = lax.psum_scatter(
            ordered.reshape(width, 2 * hidden_part), "dp", scatter_dimension=0, tiled=True
        )
    before = branch2_mids + ([summed] if direct else [])
    parts = attn_weights(
        ids, after(normed1, *before), qkv_grad,
        [norm1_sums, qkv_sums, turn_sums, own_sums, grad_scale2, sums_near, sums_far],
        proj_terms, replicas if direct else 0, rows,
    )
    norm1_terms = scatter(norm1_parts)
    if direct:
        def add(left, right):
            return (left.astype(F32) + right.astype(F32)).astype(BF)

        keep0, keep1, keep2, keep3, send32, send10 = parts
        size = keep0.shape[0]
        other32 = swap(send32, 1, "dp")
        other10 = swap(after(send10, other32, branch2_terms[-1]), 1, "dp")
        across = swap(add(keep3, other32[:size]), 2, "dp")
        near2 = add(add(keep2, other32[size:]), across)
        far = swap(after(near2, norm1_terms[-1]), 4, "dp")
        across0 = swap(add(keep1, other10[:size]), 2, "dp")
        terms = [add(keep0, other10[size:]), across0, far]
        settled = [across]
        cuts_mlp = total(after(ids, *settled), [owned_mlp], group)
    else:
        owned_attn = lax.psum_scatter(parts[0], "dp", scatter_dimension=0, tiled=True)

        def relative(owned):
            blocks = owned.reshape(group, rows, -1)
            return [lax.dynamic_index_in_dim(blocks, place ^ k, 0, False) for k in range(group)]

        cuts_mlp = relative(owned_mlp)
        settled = []
    out_fc1, out_fc2 = place_mlp(ids, exchange(cuts_mlp), hidden)
    input_grad = begin(
        vector_rows, after(tokens[0], *settled), mean1, inverse1, middle_grad, norm1_terms
    )
    output = finish(after(vector_rows, *settled), middle, branch2_terms)
    if direct:
        cuts_attn = total(after(ids, input_grad, output, out_fc1), terms, group)
    else:
        cuts_attn = relative(owned_attn)

    out_qkv, out_proj, out_vectors, out_bias = place_attn(
        ids, exchange(cuts_attn), width, vector_count, bias_cols
    )
    return (
        output[None],
        input_grad[None],
        out_qkv,
        out_proj.T,
        out_fc1,
        out_bias.reshape(-1),
        out_fc2.T,
        out_vectors,
    )


def solution(mesh):
    both = ("dp", "ctx")
    in_specs = (
        P("dp", "ctx", None),
        P("dp", "ctx"),
        P(both, None),
        P(None, both),
        P(both, None),
        P(both),
        P(None, both),
        P(None, both),
        P("dp", "ctx", None),
    )
    out_specs = (
        P("dp", "ctx", None),
        P("dp", "ctx", None),
        P(both, None),
        P(None, both),
        P(both, None),
        P(both),
        P(None, both),
        P(None, both),
    )
    return jax.shard_map(local, mesh=mesh, in_specs=in_specs, out_specs=out_specs, check_vma=False)
```

```python
import jax
import jax.numpy as jnp
from jax import lax
from jax.experimental import pallas as pl
from jax.experimental.pallas import tpu as pltpu
from jax.sharding import PartitionSpec as P

HD = 64
PAIR = 2 * HD
EXTRA = 128
EPSILON = 1e-06
MASKED_SCORE = -1e30
SQRT_HALF = 0.7071067811865476
INV_ROOT_TWO_PI = 0.3989422804014327
BF = jnp.bfloat16
F32 = jnp.float32
PARAMS = pltpu.CompilerParams(vmem_limit_bytes=60 * 1024 * 1024)
SMALL = pl.CostEstimate(flops=1_000_000_000, bytes_accessed=1_000_000, transcendentals=0)
VMEM = pl.BlockSpec(memory_space=pltpu.VMEM)
SMEM = pl.BlockSpec(memory_space=pltpu.SMEM)


def shaped(shape, dtype):
    return jax.ShapeDtypeStruct(shape, dtype)


def dot(left, right, left_dim, right_dim):
    return lax.dot_general(
        left, right, (((left_dim,), (right_dim,)), ((), ())), preferred_element_type=F32
    )


def lanes(start, size):
    return pl.ds(pl.multiple_of(start, 128), size)


def unit_rows(inputs):
    centered = inputs - jnp.mean(inputs, axis=-1, keepdims=True)
    spread = jnp.mean(centered * centered, axis=-1, keepdims=True)
    inverse = lax.rsqrt(spread + EPSILON)
    return (centered * inverse, inverse)


def norm_back(grad_in, unit, inverse, gain):
    scaled = grad_in * gain
    inner = (
        scaled
        - jnp.mean(scaled, axis=-1, keepdims=True)
        - unit * jnp.mean(scaled * unit, axis=-1, keepdims=True)
    )
    return inner * inverse


def cut_kernel(ids_ref, count_ref, qkv_ref, proj_ref, fc1_ref, fc2_ref, vec_ref, bias_ref, *rest):
    outs, (extra_ref, turn_ref) = rest[:-2], rest[-2:]
    group = len(outs) // 2
    place = ids_ref[0]
    width = proj_ref.shape[1]
    part = width // group
    hidden_part = fc1_ref.shape[1] // group
    vector_count, bias_cols = vec_ref.shape[0], bias_ref.shape[1] // vec_ref.shape[1]
    column = vector_count + bias_cols
    lane = lax.broadcasted_iota(jnp.int32, extra_ref.shape, 1)
    count = count_ref[0, 0]
    high = (count >> 7).astype(F32)
    low = (count & 127).astype(F32)
    extra_ref[...] = jnp.where(lane == column, high, jnp.where(lane == column + 1, low, 0.0))
    extra_ref[:, :vector_count] = vec_ref[...].astype(F32).T
    rows = qkv_ref.shape[0]
    for line in range(bias_cols):
        turn_ref[line : line + 1, :] = bias_ref[0:1, line * rows : (line + 1) * rows].astype(F32)
    extra_ref[:, vector_count:column] = turn_ref[0:bias_cols, :].T
    extra = extra_ref[...].astype(BF)
    for k in range(group):
        target = place ^ k
        first, second = outs[k], outs[group + k]
        for third in range(3):
            for pair in range(part // PAIR):
                spot = (pair * 3 + third) * PAIR
                first[:, spot : spot + PAIR] = qkv_ref[
                    :, lanes(third * width + target * part + pair * PAIR, PAIR)
                ]
        first[:, 3 * part : 4 * part] = proj_ref[:, lanes(target * part, part)]
        first[:, 4 * part :] = extra
        second[:, :hidden_part] = fc1_ref[:, lanes(target * hidden_part, hidden_part)]
        second[:, hidden_part:] = fc2_ref[:, lanes(target * hidden_part, hidden_part)]


def cut(ids, counts, w_qkv, w_proj_t, w_fc1, w_fc2_t, vectors, bias, group):
    rows, width = w_proj_t.shape
    part, hidden_part = width // group, w_fc1.shape[1] // group
    return pl.pallas_call(
        cut_kernel,
        in_specs=[SMEM, SMEM] + [VMEM] * 6,
        out_specs=[VMEM] * (2 * group),
        out_shape=[shaped((rows, 4 * part + EXTRA), BF)] * group
        + [shaped((rows, 2 * hidden_part), BF)] * group,
        scratch_shapes=[pltpu.VMEM((rows, EXTRA), F32), pltpu.VMEM((8, rows), F32)],
        compiler_params=PARAMS,
        name="cut",
    )(ids, counts, w_qkv, w_proj_t, w_fc1, w_fc2_t, vectors, bias)


def project_kernel(ordered, group, count_column, ids_ref, *rest):
    tokens, blocks, rest = rest[:group], rest[group : 2 * group], rest[2 * group :]
    pieces, outs, lives, scratch = (
        rest[: -12 - group], rest[-12 - group : -3 - group], rest[-3 - group : -3], rest[-3:]
    )
    qkv_w, proj_w, rows_ref, normed_ref, out_ref, mean_ref, inv_ref, fc1_ref, key_ref = outs
    extra_ref, bias_ref, small_ref = scratch
    place, row = ids_ref[0], ids_ref[1]
    capacity, width = tokens[0].shape
    part = proj_w.shape[1]
    size = pieces[0].shape[0]

    def lay(block, start, count):
        where = pl.ds(start, count)
        qkv_w[where, :] = block[:, : 3 * part]
        proj_w[where, :] = block[:, 3 * part : 4 * part]
        extra_ref[where, :] = block[:, 4 * part :].astype(F32)

    if ordered:
        lay(pieces[0], 0, size)
        shard = ordered
    else:
        sub = shard = size // group
        for m, piece in enumerate(pieces):
            for j in range(group):
                start = (row ^ m) * size + (place ^ j) * sub
                lay(piece.at[j * sub : (j + 1) * sub], pl.multiple_of(start, sub), sub)
    slot = lax.broadcasted_iota(jnp.int32, (capacity, 1), 0).astype(F32)
    for j, (block, live_ref) in enumerate(zip(blocks, lives)):
        extra = block[:, 4 * part :].astype(F32)[0:1, :]
        bound = extra[:, count_column : count_column + 1] * 128.0
        bound = bound + extra[:, count_column + 1 : count_column + 2]
        live = jnp.where(slot < bound, 1.0, 0.0)
        live_ref[...] = live
        key_ref[j * capacity : (j + 1) * capacity, :] = (1.0 - live) * MASKED_SCORE
    turned = extra_ref[...].T
    rows_ref[...] = turned[: rows_ref.shape[0]]
    bias_ref[...] = jnp.zeros(bias_ref.shape, F32)
    for pair in range(part // PAIR):
        for third, line in ((0, 2), (2, 3)):
            spot = (pair * 3 + third) * PAIR
            bias_ref[0:1, spot : spot + PAIR] = rows_ref[
                line : line + 1, lanes(place * part + pair * PAIR, PAIR)
            ]
    cols = fc1_ref.shape[1] // part
    small_ref[0:cols, :] = rows_ref[10 : 10 + cols, lanes(place * part, part)]
    for owner in range(part // shard):
        for line in range(cols):
            spot = (owner * cols + line) * shard
            fc1_ref[0:1, spot : spot + shard] = small_ref[
                line : line + 1, owner * shard : (owner + 1) * shard
            ]
    gain, shift, bias = rows_ref[0:1, :], rows_ref[1:2, :], bias_ref[0:1, :]
    for first in range(0, group, 2):
        span = slice(first * capacity, (first + 2) * capacity)
        inputs = jnp.concatenate([tokens[first][...].astype(F32), tokens[first + 1][...].astype(F32)])
        mean = jnp.mean(inputs, axis=-1, keepdims=True)
        centered = inputs - mean
        inverse = lax.rsqrt(jnp.mean(centered * centered, axis=-1, keepdims=True) + EPSILON)
        normed = (centered * inverse * gain + shift).astype(BF)
        normed_ref[span, :] = normed
        mean_ref[span, :] = mean
        inv_ref[span, :] = inverse
        out_ref[span, :] = (dot(normed, qkv_w[...], 1, 0) + bias).astype(BF)


def project(ids, tokens, blocks, pieces, hidden_part, count_column, ordered):
    capacity, width = tokens[0].shape
    group = len(tokens)
    length = group * capacity
    part = width // group
    return pl.pallas_call(
        lambda *refs: project_kernel(ordered, group, count_column, *refs),
        in_specs=[SMEM] + [VMEM] * (2 * group + len(pieces)),
        out_specs=[VMEM] * (9 + group),
        out_shape=[
            shaped((width, 3 * part), BF),
            shaped((width, part), BF),
            shaped((16, width), F32),
            shaped((length, width), BF),
            shaped((length, 3 * part), BF),
            shaped((length, 1), F32),
            shaped((length, 1), F32),
            shaped((1, hidden_part), F32),
            shaped((length, 1), F32),
        ]
        + [shaped((capacity, 1), F32)] * group,
        scratch_shapes=[
            pltpu.VMEM((width, EXTRA), F32),
            pltpu.VMEM((8, 3 * part), F32),
            pltpu.VMEM((8, part), F32),
        ],
        compiler_params=PARAMS,
        cost_estimate=SMALL,
        name="project",
    )(ids, *tokens, *blocks, *pieces)


def query_chunks(length):
    step = 512
    return [(start, min(step, length - start)) for start in range(0, length, step)]


def attend_kernel(qkv_ref, bias_ref, out_ref, lse_ref, *lows):
    length = qkv_ref.shape[0]
    key_bias = bias_ref[...]
    for head in range(2):
        keys = qkv_ref[:, PAIR + head * HD : PAIR + (head + 1) * HD]
        values = qkv_ref[:, 2 * PAIR + head * HD : 2 * PAIR + (head + 1) * HD]
        for start, size in query_chunks(length):
            queries = qkv_ref[start : start + size, head * HD : (head + 1) * HD]
            queries = queries * jnp.asarray(HD**-0.5, BF)
            scores = dot(keys, queries, 1, 1) + key_bias
            top = jnp.max(scores, axis=0, keepdims=True)
            expo = jnp.exp(scores - top)
            total = jnp.sum(expo, axis=0, keepdims=True)
            mixed = (dot(values, expo.astype(BF), 0, 0) / total).T
            out_ref[start : start + size, head * HD : (head + 1) * HD] = mixed
            lse_ref[0, head : head + 1, start : start + size] = top + jnp.log(total)
    for j, low in enumerate(lows):
        size = low.shape[0]
        low[...] = out_ref[j * size : (j + 1) * size, :].astype(BF)


def attend(qkv, key_bias, group):
    length, columns = qkv.shape
    pairs = columns // (3 * PAIR)
    return pl.pallas_call(
        attend_kernel,
        grid=(pairs,),
        in_specs=[
            pl.BlockSpec((length, 3 * PAIR), lambda p: (0, p)),
            pl.BlockSpec((length, 1), lambda p: (0, 0)),
        ],
        out_specs=[
            pl.BlockSpec((length, PAIR), lambda p: (0, p)),
            pl.BlockSpec((1, 2, length), lambda p: (p, 0, 0)),
        ]
        + [pl.BlockSpec((length // group, PAIR), lambda p: (0, p))] * group,
        out_shape=[
            shaped((length, pairs * PAIR), F32),
            shaped((pairs, 2, length), F32),
        ]
        + [shaped((length // group, pairs * PAIR), BF)] * group,
        compiler_params=PARAMS,
        cost_estimate=SMALL,
        name="attend",
    )(qkv, key_bias)


def attend_back_kernel(qkv_ref, bias_ref, att_ref, lse_ref, *rest):
    pieces, (out_ref, sums_ref, grad_ref) = rest[:-3], rest[-3:]
    length = qkv_ref.shape[0]
    size = pieces[0].shape[0]
    factor = HD**-0.5
    key_bias = bias_ref[...]
    for j, piece in enumerate(pieces):
        grad_ref[j * size : (j + 1) * size, :] = piece[...].astype(F32)
    for head in range(2):
        low, high = head * HD, (head + 1) * HD
        keys = qkv_ref[:, PAIR + low : PAIR + high]
        values = qkv_ref[:, 2 * PAIR + low : 2 * PAIR + high]
        key_grad = jnp.zeros((length, HD), F32)
        value_grad = jnp.zeros((length, HD), F32)
        for start, size in query_chunks(length):
            rows = slice(start, start + size)
            queries = qkv_ref[rows, low:high] * jnp.asarray(factor, BF)
            product = grad_ref[rows, low:high] * att_ref[rows, low:high]
            grads = grad_ref[rows, low:high].astype(BF)
            delta = jnp.sum(product.T, axis=0, keepdims=True)
            scores = dot(keys, queries, 1, 1) + key_bias
            probs = jnp.exp(scores - lse_ref[0, head : head + 1, rows])
            value_grad += dot(probs.astype(BF), grads, 1, 0)
            raw = (probs * (dot(values, grads, 1, 1) - delta)).astype(BF)
            key_grad += dot(raw, queries, 1, 0)
            query_grad = dot(keys, raw, 0, 0).T * factor
            out_ref[rows, low:high] = query_grad.astype(BF)
        out_ref[:, PAIR + low : PAIR + high] = key_grad.astype(BF)
        out_ref[:, 2 * PAIR + low : 2 * PAIR + high] = value_grad.astype(BF)
    sums_ref[0] = jnp.sum(out_ref[...].astype(F32), axis=0, keepdims=True)


def attend_back(qkv, key_bias, attended, lse, pieces):
    length, columns = qkv.shape
    pairs = columns // (3 * PAIR)
    size = pieces[0].shape[0]
    return pl.pallas_call(
        attend_back_kernel,
        grid=(pairs,),
        in_specs=[
            pl.BlockSpec((length, 3 * PAIR), lambda p: (0, p)),
            pl.BlockSpec((length, 1), lambda p: (0, 0)),
            pl.BlockSpec((length, PAIR), lambda p: (0, p)),
            pl.BlockSpec((1, 2, length), lambda p: (p, 0, 0)),
        ]
        + [pl.BlockSpec((size, PAIR), lambda p: (0, p))] * len(pieces),
        out_specs=[
            pl.BlockSpec((length, 3 * PAIR), lambda p: (0, p)),
            pl.BlockSpec((1, 1, 3 * PAIR), lambda p: (p, 0, 0)),
        ],
        out_shape=[shaped((length, columns), BF), shaped((pairs, 1, 3 * PAIR), F32)],
        scratch_shapes=[pltpu.VMEM((length, PAIR), F32)],
        compiler_params=PARAMS,
        cost_estimate=SMALL,
        name="attend_back",
    )(qkv, key_bias, attended, lse, *pieces)


def middle_kernel(group, rows_ref, tokens_ref, *rest):
    parts, weights, (branch_ref, middle_ref, normed_ref, unit_ref, inv_ref) = (
        rest[:group], rest[group : 2 * group], rest[2 * group :]
    )
    branch = dot(parts[0][...], weights[0][...], 1, 1)
    for part, weight in zip(parts[1:], weights[1:]):
        branch = branch + dot(part[...], weight[...], 1, 1)
    branch = branch + rows_ref[4:5, :]
    branch_ref[...] = branch
    middle = tokens_ref[...].astype(F32) + rows_ref[5:6, :] * branch
    middle_ref[...] = middle
    unit, inverse = unit_rows(middle)
    unit_ref[...] = unit
    inv_ref[...] = inverse
    normed_ref[...] = (unit * rows_ref[6:7, :] + rows_ref[7:8, :]).astype(BF)


def middle_step(rows, tokens, parts, weights):
    length, width = tokens.shape
    group = len(parts)
    full = shaped((length, width), F32)
    return pl.pallas_call(
        lambda *refs: middle_kernel(group, *refs),
        in_specs=[VMEM] * (2 + 2 * group),
        out_specs=[VMEM] * 5,
        out_shape=[full, full, shaped((length, width), BF), full, shaped((length, 1), F32)],
        compiler_params=PARAMS,
        cost_estimate=SMALL,
        name="middle",
    )(rows, tokens, *parts, *weights)


def turn_kernel(group, terms, rows_ref, live_ref, cot_ref, unit_ref, inv_ref, branch_ref, *rest):
    backs, weights, outs = rest[:terms], rest[terms : terms + group], rest[terms + group :]
    middle_ref, grad_ref, sums_ref = outs[:3]
    norm_grad = backs[0][...].astype(F32)
    for ref in backs[1:]:
        norm_grad = norm_grad + ref[...].astype(F32)
    unit = unit_ref[...]
    out_grad = cot_ref[...].astype(F32) * live_ref[...]
    middle = out_grad + norm_back(norm_grad, unit, inv_ref[...], rows_ref[6:7, :])
    middle_ref[...] = middle
    low = (middle * rows_ref[5:6, :]).astype(BF)
    grad_ref[...] = low
    sums_ref[...] = jnp.zeros(sums_ref.shape, F32)
    sums_ref[0:1, :] = jnp.sum(low.astype(F32), axis=0, keepdims=True)
    sums_ref[1:2, :] = jnp.sum(middle * branch_ref[...], axis=0, keepdims=True)
    sums_ref[2:3, :] = jnp.sum(norm_grad * unit, axis=0, keepdims=True)
    sums_ref[3:4, :] = jnp.sum(norm_grad, axis=0, keepdims=True)
    for out, weight in zip(outs[3:], weights):
        out[...] = dot(low, weight[...], 1, 0).astype(BF)


def turn(rows, live, cotangent, unit, inverse, branch, backs, weights):
    length, width = cotangent.shape
    part = weights[0].shape[1]
    group = len(weights)
    return pl.pallas_call(
        lambda *refs: turn_kernel(group, len(backs), *refs),
        in_specs=[VMEM] * (6 + len(backs) + group),
        out_specs=[VMEM] * (3 + group),
        out_shape=[shaped((length, width), F32), shaped((length, width), BF), shaped((8, width), F32)]
        + [shaped((length, part), BF)] * group,
        compiler_params=PARAMS,
        cost_estimate=SMALL,
        name="turn",
    )(rows, live, cotangent, unit, inverse, branch, *backs, *weights)


def proj_weights_kernel(ids_ref, grad_ref, *rest):
    parts, out_ref = rest[:-1], rest[-1]
    for j, part in enumerate(parts):
        out_ref[ids_ref[0] ^ j] = dot(grad_ref[...], part[...], 0, 0).astype(BF)


def proj_weights(ids, grads, parts):
    width = grads.shape[1]
    part = parts[0].shape[1]
    return pl.pallas_call(
        proj_weights_kernel,
        in_specs=[SMEM] + [VMEM] * (1 + len(parts)),
        out_specs=VMEM,
        out_shape=shaped((len(parts), width, part), BF),
        compiler_params=PARAMS,
        cost_estimate=SMALL,
        name="proj_weights",
    )(ids, grads, *parts)


def mlp_kernel(count, shards, group, rows_ref, *rest):
    normed_in, cots, lives = rest[:count], rest[count : 2 * count], rest[2 * count : 3 * count]
    ids_ref, bias_ref = rest[3 * count : 3 * count + 2]
    rest = rest[3 * count + 2 :]
    pieces, backs, rest = rest[:shards], rest[shards : shards + count], rest[shards + count :]
    normed_ref, out_ref, act_ref, pre_ref, sums_ref, own_ref = rest[:6]
    if shards > 1:
        weight_ref, grad_ref, back_acc = rest[6:]
    else:
        weight_ref = pieces[0]
        grad_ref, back_acc = rest[6:]
    step = pl.program_id(0)
    size = cots[0].shape[0]

    @pl.when(step == 0)
    def _():
        if shards > 1:
            whole_size = pieces[0].shape[0]
            sub = whole_size // group
            for m, piece in enumerate(pieces):
                for j in range(group):
                    start = (ids_ref[1] ^ m) * whole_size + (ids_ref[0] ^ j) * sub
                    weight_ref[pl.ds(pl.multiple_of(start, sub), sub), :] = piece[
                        j * sub : (j + 1) * sub, :
                    ]
        normed_ref[...] = jnp.concatenate([ref[...].astype(F32) for ref in normed_in]).astype(BF)
        scale = rows_ref[9:10, :]
        grads = [cot[...].astype(F32) * live[...] for cot, live in zip(cots, lives)]
        whole_grad = jnp.concatenate(grads)
        out_ref[...] = whole_grad.astype(BF)
        scaled = (whole_grad * scale).astype(BF)
        grad_ref[...] = scaled
        own_ref[0:1, :] = jnp.sum(scaled.astype(F32)[:size], axis=0, keepdims=True)
        own_ref[1:2, :] = jnp.sum(grads[0], axis=0, keepdims=True)

    hidden = weight_ref.shape[1] // 2
    span = act_ref.shape[1]
    chunk = span // 2
    for cols in (slice(0, chunk), slice(chunk, 2 * chunk)):
        here = lanes(step * span + cols.start, chunk)
        there = lanes(hidden + step * span + cols.start, chunk)
        pre = dot(normed_ref[...], weight_ref[:, here], 1, 0) + bias_ref[:, cols]
        act_grad = dot(grad_ref[...], weight_ref[:, there], 1, 0)
        cdf = 0.5 * (1.0 + lax.erf(pre * SQRT_HALF))
        act_ref[:, cols] = (pre * cdf).astype(BF)
        slope = cdf + pre * (jnp.exp(-0.5 * pre * pre) * INV_ROOT_TWO_PI)
        pre_grad = (act_grad * slope).astype(BF)
        pre_ref[:, cols] = pre_grad
        sums_ref[:, cols] = jnp.sum(pre_grad.astype(F32), axis=0, keepdims=True)
    back = dot(pre_ref[...], weight_ref[:, lanes(step * span, span)], 1, 1)

    @pl.when(step == 0)
    def _():
        back_acc[...] = back

    @pl.when(step == pl.num_programs(0) - 1)
    def _():
        whole = back_acc[...] + back
        for j, ref in enumerate(backs):
            ref[...] = whole[j * size : (j + 1) * size].astype(BF)


def mlp(rows, normed, cots, lives, ids, bias, weights, group):
    size, width = normed[0].shape
    count, shards = len(normed), len(weights)
    length = count * size
    hidden = weights[0].shape[1] // 2
    laid = shards > 1
    step = hidden // 2

    def whole(*shape):
        return pl.BlockSpec(shape, lambda i: (0, 0))

    cols = pl.BlockSpec((length, step), lambda i: (0, i))
    return pl.pallas_call(
        lambda *refs: mlp_kernel(count, shards, group, *refs),
        grid=(2,),
        in_specs=[whole(*rows.shape)]
        + [whole(size, width)] * (2 * count)
        + [whole(size, 1)] * count
        + [SMEM, pl.BlockSpec((1, step), lambda i: (0, i))]
        + [whole(*piece.shape) for piece in weights],
        out_specs=[whole(size, width)] * count
        + [whole(length, width)] * 2
        + [cols, cols, pl.BlockSpec((1, step), lambda i: (0, i)), whole(8, width)]
        + [whole(width, 2 * hidden)] * laid,
        out_shape=[shaped((size, width), BF)] * count
        + [shaped((length, width), BF)] * 2
        + [shaped((length, hidden), BF)] * 2
        + [shaped((1, hidden), F32), shaped((8, width), F32)]
        + [shaped((width, 2 * hidden), BF)] * laid,
        scratch_shapes=[pltpu.VMEM((length, width), BF), pltpu.VMEM((length, width), F32)],
        compiler_params=PARAMS,
        cost_estimate=SMALL,
        name="mlp",
    )(rows, *normed, *cots, *lives, ids, bias, *weights)


def mlp_weights_kernel(
    direct, ids_ref, norm_a, norm_b, grad_a, grad_b, rows_ref, fc2_ref, pre_a, pre_b, act_a, act_b,
    own_ref, *rest
):
    keep_ref, send_ref, scale2_ref, *branches, out_ref = rest
    hidden = pre_a.shape[1]
    first = dot(norm_a[...], pre_a[...], 0, 0) + dot(norm_b[...], pre_b[...], 0, 0)
    size = keep_ref.shape[0]
    out_ref[0, :, :hidden] = first[:size].astype(BF)
    out_ref[1, :, :hidden] = first[size:].astype(BF)
    outs = [grad_a[...].astype(F32), grad_b[...].astype(F32)]
    scaled = [(out * rows_ref[9:10, :]).astype(BF) for out in outs]
    second = dot(scaled[0], act_a[...], 0, 0) + dot(scaled[1], act_b[...], 0, 0)
    out_ref[0, :, hidden:] = second[:size].astype(BF)
    out_ref[1, :, hidden:] = second[size:].astype(BF)
    side = (ids_ref[1] & 1) if direct else 0
    keep_ref[...] = out_ref[side]
    send_ref[...] = out_ref[1 - side]
    scale2 = own_ref[1:2, :] * rows_ref[8:9, :]
    count = len(branches) // 2
    size = branches[0].shape[0]
    for half, act in enumerate((act_a, act_b)):
        branch = dot(act[...], fc2_ref[...], 1, 1)
        scale2 = scale2 + jnp.sum(outs[half] * branch, axis=0, keepdims=True)
        for j in range(count):
            branches[half * count + j][...] = branch[j * size : (j + 1) * size].astype(BF)
    scale2_ref[...] = scale2


def mlp_weights(rows, own, normed, grads, pres, acts, weights, group, ids, direct):
    length, width = normed[0].shape
    hidden = pres[0].shape[1]
    size = 2 * length // group
    step = 256

    cols = pl.BlockSpec((length, step), lambda i, ids_ref: (0, i))
    whole = pl.BlockSpec((length, hidden), lambda i, ids_ref: (0, 0))

    def line(count):
        return pl.BlockSpec((count, step), lambda i, ids_ref: (0, i))

    part = pl.BlockSpec((step // 2, 2 * hidden), lambda i, ids_ref: (i, 0))
    return pl.pallas_call(
        lambda *refs: mlp_weights_kernel(direct, *refs),
        grid_spec=pltpu.PrefetchScalarGridSpec(
            num_scalar_prefetch=1,
            grid=(width // step,),
            in_specs=[cols] * 4
            + [line(rows.shape[0])]
            + [pl.BlockSpec((step, hidden), lambda i, ids_ref: (i, 1))]
            + [whole] * 4
            + [line(own.shape[0])],
            out_specs=[part, part, line(1)] + [line(size)] * group,
            scratch_shapes=[pltpu.VMEM((2, step // 2, 2 * hidden), BF)],
        ),
        out_shape=[shaped((width // 2, 2 * hidden), BF)] * 2
        + [shaped((1, width), F32)]
        + [shaped((size, width), BF)] * group,
        compiler_params=PARAMS,
        cost_estimate=SMALL,
        name="mlp_weights",
    )(ids, *normed, *grads, rows, weights, *pres, *acts, own)


def finish_kernel(rows_ref, middle_ref, *rest):
    terms, out_ref = rest[:-1], rest[-1]
    branch = terms[0][...].astype(F32)
    for ref in terms[1:]:
        branch = branch + ref[...].astype(F32)
    branch = branch + rows_ref[8:9, :]
    out_ref[...] = (middle_ref[...] + rows_ref[9:10, :] * branch).astype(BF)


def finish(rows, middle, terms):
    return pl.pallas_call(
        finish_kernel,
        in_specs=[VMEM] * (2 + len(terms)),
        out_specs=VMEM,
        out_shape=shaped(middle.shape, BF),
        compiler_params=PARAMS,
        name="finish",
    )(rows, middle, *terms)


def begin_kernel(rows_ref, tokens_ref, mean_ref, inv_ref, middle_ref, *rest):
    terms, out_ref = rest[:-1], rest[-1]
    grads = terms[0][...].astype(F32)
    for ref in terms[1:]:
        grads = grads + ref[...].astype(F32)
    inverse = inv_ref[...]
    unit = (tokens_ref[...].astype(F32) - mean_ref[...]) * inverse
    out_ref[...] = (middle_ref[...] + norm_back(grads, unit, inverse, rows_ref[0:1, :])).astype(BF)


def begin(rows, tokens, mean, inverse, middle_grad, terms):
    length, width = tokens.shape
    column = pl.BlockSpec((length, 1), lambda i: (0, 0))
    whole = pl.BlockSpec((length, width), lambda i: (0, 0))
    return pl.pallas_call(
        begin_kernel,
        grid=(1,),
        in_specs=[pl.BlockSpec(rows.shape, lambda i: (0, 0)), whole, column, column, whole]
        + [whole] * len(terms),
        out_specs=whole,
        out_shape=shaped((length, width), BF),
        compiler_params=PARAMS,
        name="begin",
    )(rows, tokens, mean, inverse, middle_grad, *terms)


def qkv_back_kernel(group, grad_ref, weight_ref, mean_ref, inv_ref, *rest):
    tokens, outs, sums_ref = rest[:group], rest[group:-1], rest[-1]
    size = tokens[0].shape[0]
    gain = shift = 0.0
    for first in range(0, group, 2):
        span = slice(first * size, (first + 2) * size)
        part = dot(grad_ref[span, :], weight_ref[...], 1, 1)
        inputs = jnp.concatenate([tokens[first][...].astype(F32), tokens[first + 1][...].astype(F32)])
        unit = (inputs - mean_ref[span, :]) * inv_ref[span, :]
        outs[first][...] = part[:size].astype(BF)
        outs[first + 1][...] = part[size:].astype(BF)
        gain = gain + jnp.sum(part * unit, axis=0, keepdims=True)
        shift = shift + jnp.sum(part, axis=0, keepdims=True)
    sums_ref[...] = jnp.zeros(sums_ref.shape, F32)
    sums_ref[0:1, :] = gain
    sums_ref[1:2, :] = shift


def qkv_back(qkv_grad, weight, tokens, mean, inverse):
    size, width = tokens[0].shape
    group = len(tokens)
    return pl.pallas_call(
        lambda *refs: qkv_back_kernel(group, *refs),
        in_specs=[VMEM] * (4 + group),
        out_specs=[VMEM] * (group + 1),
        out_shape=[shaped((size, width), BF)] * group + [shaped((8, width), F32)],
        compiler_params=PARAMS,
        cost_estimate=SMALL,
        name="qkv_back",
    )(qkv_grad, weight, mean, inverse, *tokens)


def attn_weights_kernel(
    direct, shard, terms, ids_ref, normed_ref, grad_ref, norm1_ref, sums_ref, turn_ref, fbias_ref,
    scale2_ref, bias_a_ref, bias_b_ref, *rest,
):
    projs, outs = rest[:terms], rest[terms:-5]
    rows_ref, turned_ref, block_ref, small_ref, stage_ref = rest[-5:]
    place, row = ids_ref[0], ids_ref[1]
    width = normed_ref.shape[1]
    part = projs[0].shape[1]
    rows_ref[...] = jnp.zeros(rows_ref.shape, F32)
    rows_ref[0:2, :] = norm1_ref[0:2, :]
    for pair in range(part // PAIR):
        where = lanes(place * part + pair * PAIR, PAIR)
        rows_ref[2:3, where] = sums_ref[pair, :, :PAIR]
        rows_ref[3:4, where] = sums_ref[pair, :, 2 * PAIR :]
    rows_ref[4:8, :] = turn_ref[0:4, :]
    rows_ref[8:9, :] = fbias_ref[0:1, :]
    rows_ref[9:10, :] = scale2_ref[...]
    cols = bias_a_ref.shape[1] // part
    for owner in range(part // shard):
        for line in range(cols):
            spot = (owner * cols + line) * shard
            small_ref[line : line + 1, owner * shard : (owner + 1) * shard] = (
                bias_a_ref[0:1, spot : spot + shard] + bias_b_ref[0:1, spot : spot + shard]
            )
    rows_ref[10 : 10 + cols, lanes(place * part, part)] = small_ref[0:cols, :]
    turned_ref[...] = rows_ref[...].T
    step = block_ref.shape[0]
    for k in range(width // step):
        start = pl.multiple_of(((row >> 1) ^ k) * step, step) if direct else k * step
        cols = pl.ds(start, step)
        block_ref[:, : 3 * part] = dot(normed_ref[:, cols], grad_ref[...], 0, 0)
        proj = projs[0][cols, :].astype(F32)
        for ref in projs[1:]:
            proj = proj + ref[cols, :].astype(F32)
        block_ref[:, 3 * part : 4 * part] = proj
        block_ref[:, 4 * part :] = turned_ref[cols, :]
        if direct:
            size = step // 2
            stage_ref[0] = block_ref[:size, :].astype(BF)
            stage_ref[1] = block_ref[size:, :].astype(BF)
            side = row & 1
            blocks = width // step
            outs[k][...] = stage_ref[side]
            spot = (k + 1) % 2 * size
            outs[blocks + (blocks - 1 - k) // 2][spot : spot + size, :] = stage_ref[1 - side]
        else:
            outs[0][k * step : (k + 1) * step, :] = block_ref[...].astype(BF)


def attn_weights(ids, normed1, qkv_grad, sums, projs, blocks, shard):
    length, width = normed1.shape
    part = projs[0].shape[1]
    columns = 4 * part + EXTRA
    direct = blocks > 0
    step = 2 * (width // blocks) if direct else 256
    out_shape = [shaped((width, columns), BF)]
    if direct:
        size = width // blocks
        out_shape = [shaped((size, columns), BF)] * (blocks // 2)
        out_shape += [shaped((2 * size, columns), BF)] * (blocks // 4)
    return pl.pallas_call(
        lambda *refs: attn_weights_kernel(direct, shard, len(projs), *refs),
        in_specs=[SMEM] + [VMEM] * (2 + len(sums) + len(projs)),
        out_specs=[VMEM] * len(out_shape),
        out_shape=out_shape,
        scratch_shapes=[
            pltpu.VMEM((EXTRA, width), F32),
            pltpu.VMEM((width, EXTRA), F32),
            pltpu.VMEM((step, columns), F32),
            pltpu.VMEM((8, part), F32),
            pltpu.VMEM((2, step // 2, columns), BF),
        ],
        compiler_params=PARAMS,
        cost_estimate=SMALL,
        name="attn_weights",
    )(ids, normed1, qkv_grad, *sums, *projs)


def total(ids, terms, group):
    size, columns = terms[0].shape
    rows = size // group

    def kernel(ids_ref, *refs):
        ins, outs, sum_ref = refs[: len(terms)], refs[len(terms) : -1], refs[-1]
        value = ins[0][...].astype(F32)
        for ref in ins[1:]:
            value = value + ref[...].astype(F32)
        sum_ref[...] = value
        for k, out in enumerate(outs):
            start = pl.multiple_of((ids_ref[0] ^ k) * rows, rows)
            out[...] = sum_ref[pl.ds(start, rows), :].astype(BF)

    return pl.pallas_call(
        kernel,
        in_specs=[SMEM] + [VMEM] * len(terms),
        out_specs=[VMEM] * group,
        out_shape=[shaped((rows, columns), BF)] * group,
        scratch_shapes=[pltpu.VMEM((size, columns), F32)],
        compiler_params=PARAMS,
        name="total",
    )(ids, *terms)


def place_attn_kernel(ids_ref, *refs):
    group = len(refs) - 4
    blocks, (qkv_ref, proj_ref, vec_ref, bias_ref) = refs[:group], refs[group:]
    width = proj_ref.shape[1]
    part = width // group
    extra = jnp.zeros((qkv_ref.shape[0], EXTRA), F32)
    for k, block in enumerate(blocks):
        source = ids_ref[0] ^ k
        for third in range(3):
            for pair in range(part // PAIR):
                spot = (pair * 3 + third) * PAIR
                where = lanes(third * width + source * part + pair * PAIR, PAIR)
                qkv_ref[:, where] = block[:, spot : spot + PAIR].astype(F32)
        proj_ref[:, lanes(source * part, part)] = block[:, 3 * part : 4 * part].astype(F32)
        extra = extra + block[:, 4 * part :].astype(F32)
    turned = extra.T
    count = vec_ref.shape[0]
    vec_ref[...] = turned[:count]
    rows = qkv_ref.shape[0]
    for line in range(bias_ref.shape[1] // rows):
        bias_ref[0:1, line * rows : (line + 1) * rows] = turned[count + line : count + line + 1]


def place_attn(ids, blocks, width, vector_count, bias_cols):
    rows = blocks[0].shape[0]
    return pl.pallas_call(
        place_attn_kernel,
        in_specs=[SMEM] + [VMEM] * len(blocks),
        out_specs=[VMEM] * 4,
        out_shape=[
            shaped((rows, 3 * width), F32),
            shaped((rows, width), F32),
            shaped((vector_count, rows), F32),
            shaped((1, bias_cols * rows), F32),
        ],
        compiler_params=PARAMS,
        name="place_attn",
    )(ids, *blocks)


def place_mlp_kernel(ids_ref, *refs):
    group = len(refs) - 2
    blocks, (fc1_ref, fc2_ref) = refs[:group], refs[group:]
    part = fc1_ref.shape[1] // group
    for k, block in enumerate(blocks):
        where = lanes((ids_ref[0] ^ k) * part, part)
        fc1_ref[:, where] = block[:, :part].astype(F32)
        fc2_ref[:, where] = block[:, part:].astype(F32)


def place_mlp(ids, blocks, hidden):
    rows = blocks[0].shape[0]
    return pl.pallas_call(
        place_mlp_kernel,
        in_specs=[SMEM] + [VMEM] * len(blocks),
        out_specs=[VMEM] * 2,
        out_shape=[shaped((rows, hidden), F32)] * 2,
        compiler_params=PARAMS,
        name="place_mlp",
    )(ids, *blocks)


def local(tokens, counts, w_qkv, w_proj, w_fc1, fc1_bias, w_fc2, vectors, cotangent):
    _, capacity, width = tokens.shape
    hidden = w_fc1.shape[1]
    rows = w_qkv.shape[0]
    group, replicas = lax.axis_size("ctx"), lax.axis_size("dp")
    place, replica = lax.axis_index("ctx"), lax.axis_index("dp")
    ids = jnp.stack([place, replica]).astype(jnp.int32)
    head_width = width // group
    hidden_part = hidden // group
    bias_cols = hidden // width
    vector_count = vectors.shape[0]
    direct = replicas == 8

    def swap(value, bit, axis="ctx"):
        size = group if axis == "ctx" else replicas
        return lax.ppermute(value, axis, [(i, i ^ bit) for i in range(size)])

    def after(value, *before):
        return lax.optimization_barrier((value,) + before)[0]

    def gather(own, *before):
        pieces = [own]
        for j in range(1, group):
            bit = j & -j
            source = pieces[j ^ bit]
            pieces.append(swap(after(source, *before) if j ^ bit else source, bit))
        return pieces

    def scatter(parts, *before, mids=None, axis="ctx", scale=1, gates=None):
        pieces = {j: [part] for j, part in enumerate(parts)}

        def added(terms):
            if len(terms) == 1:
                return terms[0]
            return sum(term.astype(F32) for term in terms).astype(BF)

        bit = 1
        sent = []
        while bit < len(parts):
            for j in sorted((j for j in pieces if j & bit), reverse=True):
                value = added(pieces.pop(j))
                if bit > 1:
                    if mids is not None:
                        mids.append(value)
                    value = after(value, *before)
                elif axis == "dp":
                    value = after(value, *sent[-2:-1])
                if gates and bit in gates:
                    value = after(value, *gates[bit])
                sent.append(swap(value, bit * scale, axis))
                pieces[j ^ bit].append(sent[-1])
            bit *= 2
        return pieces[0]

    def exchange(relative):
        return [relative[0]] + [swap(relative[k], k) for k in range(1, group)]

    def in_order(relative):
        stacked = jnp.stack(relative)
        return jnp.concatenate(
            [lax.dynamic_index_in_dim(stacked, place ^ s, 0, False) for s in range(group)], axis=0
        )

    cuts = cut(
        ids, counts, w_qkv, w_proj.T, w_fc1, w_fc2.T, vectors, fc1_bias.reshape(1, -1), group
    )
    first = exchange(cuts[:group])
    tokens_far = swap(after(tokens[0], *first), group // 2)

    def widen(shards, *before):
        for m in range(2, replicas):
            low = m & -m
            if m ^ low:
                shards[m] = swap(after(shards[m ^ low], *before), low, "dp")

    second = exchange([after(block, *first) for block in cuts[group:]])
    if direct:
        shards = {0: jnp.concatenate(first, axis=0)}
        for bit in (4, 2, 1):
            shards[bit] = swap(shards[0], bit, "dp")
        arrived = [shards[bit] for bit in (4, 2, 1)] + second[1:]
        widen(shards, *arrived)
        first_pieces = [shards[m] for m in range(replicas)]
        nearly = [shards[3], shards[5], shards[7]]
    else:
        first_pieces = [lax.all_gather(in_order(first), "dp", axis=0, tiled=True)]
        arrived = nearly = [tokens_far]
    second_shard = after(in_order(second), *arrived)
    second_all = lax.all_gather(second_shard, "dp", axis=0, tiled=True)
    cotangent_far = swap(after(cotangent[0], *arrived), group // 2)
    nearly = nearly + [cotangent_far]
    tokens_pieces = [tokens[0]]
    for j in range(1, group):
        source = tokens_pieces[j ^ (j & -j)]
        if j == group // 2:
            tokens_pieces.append(tokens_far)
        else:
            tokens_pieces.append(swap(after(source, *nearly), j & -j))
    tokens_own = after(tokens[0], second_shard)
    count_column = vector_count + bias_cols
    (
        weight_qkv, weight_proj, vector_rows, normed1, qkv, mean1, inverse1, bias_fc1, key_bias,
        *live,
    ) = project(
        ids, [tokens_own] + tokens_pieces[1:], first, first_pieces, hidden_part, count_column,
        0 if direct else rows,
    )

    cotangent_pieces = [cotangent[0]]
    for j in range(1, group):
        source = cotangent_pieces[j ^ (j & -j)]
        if j == group // 2:
            cotangent_pieces.append(cotangent_far)
        else:
            cotangent_pieces.append(swap(after(source, qkv), j & -j))
    attended, lse, *attended_low = attend(qkv, key_bias, group)
    projs = gather(weight_proj, lse)
    attended_own = exchange(attended_low)
    branch1, middle, normed2_own, unit2, inverse2 = middle_step(
        vector_rows, tokens[0], attended_own, projs
    )
    half = group // 2
    normed2 = [normed2_own]
    while len(normed2) < half:
        normed2 += [swap(piece, len(normed2)) for piece in normed2]

    def feed(where, pieces, weights):
        return mlp(
            vector_rows, pieces, cotangent_pieces[where], live[where], ids, bias_fc1, weights, group
        )

    *backs_near, norm_near, grad_near, act_near, pre_near, sums_near, own_sums = feed(
        slice(0, half), normed2, [second_all]
    )
    normed2_far = [swap(normed2_own, half)]
    while len(normed2_far) < half:
        normed2_far += [
            swap(after(piece, sums_near), len(normed2_far)) for piece in normed2_far
        ]
    *backs_far, norm_far, grad_far, act_far, pre_far, sums_far, _ = feed(
        slice(half, group), normed2_far, [second_all]
    )
    mids = []
    norm2_terms = scatter(backs_near + backs_far, mids=mids)
    keep_mlp, send_mlp, grad_scale2, *branches = mlp_weights(
        vector_rows, own_sums, [norm_near, norm_far], [grad_near, grad_far], [after(pre_near, *mids), pre_far],
        [act_near, act_far], second_all, group, ids, direct,
    )
    other_mlp = None
    if direct:
        other_mlp = swap(after(send_mlp, *norm2_terms), 1, "dp")
    middle_grad, branch_grad, turn_sums, *att_grads = turn(
        vector_rows, live[0], cotangent[0], unit2, inverse2, branch1, norm2_terms, projs
    )
    att_grads = exchange(att_grads)
    proj_parts = proj_weights(ids, branch_grad, attended_own).reshape(group * width, -1)
    proj_grad = lax.psum_scatter(
        after(proj_parts, *att_grads), "ctx", scatter_dimension=0, tiled=True
    )
    branch2_mids = []
    branch2_terms = scatter(branches, *att_grads, mids=branch2_mids)
    qkv_grad, qkv_sums = attend_back(qkv, key_bias, attended, after(lse, proj_parts), att_grads)
    if direct:
        other = after(other_mlp, qkv_grad)
        summed = (keep_mlp.astype(F32) + other.astype(F32)).astype(BF)
        lines = [[side + 2 * z for z in range(replicas // 2)] for side in range(2)]
        owned_mlp = lax.psum_scatter(
            summed, "dp", scatter_dimension=0, tiled=True, axis_index_groups=lines
        )
    else:
        ordered = jnp.stack(
            [part.reshape(-1, 128, 2 * hidden_part) for part in (keep_mlp, send_mlp)], axis=1
        )
        owned_mlp = lax.psum_scatter(
            ordered.reshape(width, 2 * hidden_part), "dp", scatter_dimension=0, tiled=True
        )
    *norm1_parts, norm1_sums = qkv_back(after(qkv_grad, summed) if direct else qkv_grad, weight_qkv, tokens_pieces, mean1, inverse1)
    before = branch2_mids
    parts = attn_weights(
        ids, after(normed1, *before), qkv_grad,
        [norm1_sums, qkv_sums, turn_sums, own_sums, grad_scale2, sums_near, sums_far],
        [proj_grad], replicas if direct else 0, rows,
    )
    norm1_terms = scatter(norm1_parts)
    if direct:
        def add(left, right):
            return (left.astype(F32) + right.astype(F32)).astype(BF)

        keep0, keep1, keep2, keep3, send32, send10 = parts
        size = keep0.shape[0]
        other32 = swap(send32, 1, "dp")
        other10 = swap(after(send10, other32, branch2_terms[-1]), 1, "dp")
        across = swap(add(keep3, other32[:size]), 2, "dp")
        near2 = add(add(keep2, other32[size:]), across)
        far = swap(after(near2, norm1_terms[-1]), 4, "dp")
        across0 = swap(add(keep1, other10[:size]), 2, "dp")
        terms = [add(keep0, other10[size:]), across0, far]
        settled = [across]
        cuts_mlp = total(after(ids, *settled), [owned_mlp], group)
    else:
        owned_attn = lax.psum_scatter(parts[0], "dp", scatter_dimension=0, tiled=True)

        def relative(owned):
            blocks = owned.reshape(group, rows, -1)
            return [lax.dynamic_index_in_dim(blocks, place ^ k, 0, False) for k in range(group)]

        cuts_mlp = relative(owned_mlp)
        settled = []
    out_fc1, out_fc2 = place_mlp(ids, exchange(cuts_mlp), hidden)
    input_grad = begin(
        vector_rows, after(tokens[0], *settled), mean1, inverse1, middle_grad, norm1_terms
    )
    output = finish(after(vector_rows, *settled), middle, branch2_terms)
    if direct:
        cuts_attn = total(after(ids, input_grad, output, out_fc1), terms, group)
    else:
        cuts_attn = relative(owned_attn)

    out_qkv, out_proj, out_vectors, out_bias = place_attn(
        ids, exchange(cuts_attn), width, vector_count, bias_cols
    )
    return (
        output[None],
        input_grad[None],
        out_qkv,
        out_proj.T,
        out_fc1,
        out_bias.reshape(-1),
        out_fc2.T,
        out_vectors,
    )


def solution(mesh):
    both = ("dp", "ctx")
    in_specs = (
        P("dp", "ctx", None),
        P("dp", "ctx"),
        P(both, None),
        P(None, both),
        P(both, None),
        P(both),
        P(None, both),
        P(None, both),
        P("dp", "ctx", None),
    )
    out_specs = (
        P("dp", "ctx", None),
        P("dp", "ctx", None),
        P(both, None),
        P(None, both),
        P(both, None),
        P(both),
        P(None, both),
        P(None, both),
    )
    return jax.shard_map(local, mesh=mesh, in_specs=in_specs, out_specs=out_specs, check_vma=False)
```

```python
import jax
import jax.numpy as jnp
from jax import lax
from jax.experimental import pallas as pl
from jax.experimental.pallas import tpu as pltpu
from jax.sharding import PartitionSpec as P

HD = 64
PAIR = 2 * HD
EXTRA = 128
EPSILON = 1e-06
MASKED_SCORE = -1e30
SQRT_HALF = 0.7071067811865476
INV_ROOT_TWO_PI = 0.3989422804014327
BF = jnp.bfloat16
F32 = jnp.float32
PARAMS = pltpu.CompilerParams(vmem_limit_bytes=60 * 1024 * 1024)
SMALL = pl.CostEstimate(flops=1_000_000_000, bytes_accessed=1_000_000, transcendentals=0)
VMEM = pl.BlockSpec(memory_space=pltpu.VMEM)
SMEM = pl.BlockSpec(memory_space=pltpu.SMEM)


def shaped(shape, dtype):
    return jax.ShapeDtypeStruct(shape, dtype)


def dot(left, right, left_dim, right_dim):
    return lax.dot_general(
        left, right, (((left_dim,), (right_dim,)), ((), ())), preferred_element_type=F32
    )


def lanes(start, size):
    return pl.ds(pl.multiple_of(start, 128), size)


def unit_rows(inputs):
    centered = inputs - jnp.mean(inputs, axis=-1, keepdims=True)
    spread = jnp.mean(centered * centered, axis=-1, keepdims=True)
    inverse = lax.rsqrt(spread + EPSILON)
    return (centered * inverse, inverse)


def norm_back(grad_in, unit, inverse, gain):
    scaled = grad_in * gain
    inner = (
        scaled
        - jnp.mean(scaled, axis=-1, keepdims=True)
        - unit * jnp.mean(scaled * unit, axis=-1, keepdims=True)
    )
    return inner * inverse


def cut_kernel(ids_ref, count_ref, qkv_ref, proj_ref, fc1_ref, fc2_ref, vec_ref, bias_ref, *rest):
    outs, (extra_ref, turn_ref) = rest[:-2], rest[-2:]
    group = len(outs) // 2
    place = ids_ref[0]
    width = proj_ref.shape[1]
    part = width // group
    hidden_part = fc1_ref.shape[1] // group
    vector_count, bias_cols = vec_ref.shape[0], bias_ref.shape[1] // vec_ref.shape[1]
    column = vector_count + bias_cols
    lane = lax.broadcasted_iota(jnp.int32, extra_ref.shape, 1)
    count = count_ref[0, 0]
    high = (count >> 7).astype(F32)
    low = (count & 127).astype(F32)
    extra_ref[...] = jnp.where(lane == column, high, jnp.where(lane == column + 1, low, 0.0))
    extra_ref[:, :vector_count] = vec_ref[...].astype(F32).T
    rows = qkv_ref.shape[0]
    for line in range(bias_cols):
        turn_ref[line : line + 1, :] = bias_ref[0:1, line * rows : (line + 1) * rows].astype(F32)
    extra_ref[:, vector_count:column] = turn_ref[0:bias_cols, :].T
    extra = extra_ref[...].astype(BF)
    for k in range(group):
        target = place ^ k
        first, second = outs[k], outs[group + k]
        for third in range(3):
            for pair in range(part // PAIR):
                spot = (pair * 3 + third) * PAIR
                first[:, spot : spot + PAIR] = qkv_ref[
                    :, lanes(third * width + target * part + pair * PAIR, PAIR)
                ]
        first[:, 3 * part : 4 * part] = proj_ref[:, lanes(target * part, part)]
        first[:, 4 * part :] = extra
        second[:, :hidden_part] = fc1_ref[:, lanes(target * hidden_part, hidden_part)]
        second[:, hidden_part:] = fc2_ref[:, lanes(target * hidden_part, hidden_part)]


def cut(ids, counts, w_qkv, w_proj_t, w_fc1, w_fc2_t, vectors, bias, group):
    rows, width = w_proj_t.shape
    part, hidden_part = width // group, w_fc1.shape[1] // group
    return pl.pallas_call(
        cut_kernel,
        in_specs=[SMEM, SMEM] + [VMEM] * 6,
        out_specs=[VMEM] * (2 * group),
        out_shape=[shaped((rows, 4 * part + EXTRA), BF)] * group
        + [shaped((rows, 2 * hidden_part), BF)] * group,
        scratch_shapes=[pltpu.VMEM((rows, EXTRA), F32), pltpu.VMEM((8, rows), F32)],
        compiler_params=PARAMS,
        name="cut",
    )(ids, counts, w_qkv, w_proj_t, w_fc1, w_fc2_t, vectors, bias)


def project_kernel(ordered, group, count_column, ids_ref, *rest):
    tokens, blocks, rest = rest[:group], rest[group : 2 * group], rest[2 * group :]
    pieces, outs, lives, scratch = (
        rest[: -12 - group], rest[-12 - group : -3 - group], rest[-3 - group : -3], rest[-3:]
    )
    qkv_w, proj_w, rows_ref, normed_ref, out_ref, mean_ref, inv_ref, fc1_ref, key_ref = outs
    extra_ref, bias_ref, small_ref = scratch
    place, row = ids_ref[0], ids_ref[1]
    capacity, width = tokens[0].shape
    part = proj_w.shape[1]
    size = pieces[0].shape[0]

    def lay(block, start, count):
        where = pl.ds(start, count)
        qkv_w[where, :] = block[:, : 3 * part]
        proj_w[where, :] = block[:, 3 * part : 4 * part]
        extra_ref[where, :] = block[:, 4 * part :].astype(F32)

    if ordered:
        lay(pieces[0], 0, size)
        shard = ordered
    else:
        sub = shard = size // group
        for m, piece in enumerate(pieces):
            for j in range(group):
                start = (row ^ m) * size + (place ^ j) * sub
                lay(piece.at[j * sub : (j + 1) * sub], pl.multiple_of(start, sub), sub)
    slot = lax.broadcasted_iota(jnp.int32, (capacity, 1), 0).astype(F32)
    for j, (block, live_ref) in enumerate(zip(blocks, lives)):
        extra = block[:, 4 * part :].astype(F32)[0:1, :]
        bound = extra[:, count_column : count_column + 1] * 128.0
        bound = bound + extra[:, count_column + 1 : count_column + 2]
        live = jnp.where(slot < bound, 1.0, 0.0)
        live_ref[...] = live
        key_ref[j * capacity : (j + 1) * capacity, :] = (1.0 - live) * MASKED_SCORE
    turned = extra_ref[...].T
    rows_ref[...] = turned[: rows_ref.shape[0]]
    bias_ref[...] = jnp.zeros(bias_ref.shape, F32)
    for pair in range(part // PAIR):
        for third, line in ((0, 2), (2, 3)):
            spot = (pair * 3 + third) * PAIR
            bias_ref[0:1, spot : spot + PAIR] = rows_ref[
                line : line + 1, lanes(place * part + pair * PAIR, PAIR)
            ]
    cols = fc1_ref.shape[1] // part
    small_ref[0:cols, :] = rows_ref[10 : 10 + cols, lanes(place * part, part)]
    for owner in range(part // shard):
        for line in range(cols):
            spot = (owner * cols + line) * shard
            fc1_ref[0:1, spot : spot + shard] = small_ref[
                line : line + 1, owner * shard : (owner + 1) * shard
            ]
    gain, shift, bias = rows_ref[0:1, :], rows_ref[1:2, :], bias_ref[0:1, :]
    for first in range(0, group, 2):
        span = slice(first * capacity, (first + 2) * capacity)
        inputs = jnp.concatenate([tokens[first][...].astype(F32), tokens[first + 1][...].astype(F32)])
        mean = jnp.mean(inputs, axis=-1, keepdims=True)
        centered = inputs - mean
        inverse = lax.rsqrt(jnp.mean(centered * centered, axis=-1, keepdims=True) + EPSILON)
        normed = (centered * inverse * gain + shift).astype(BF)
        normed_ref[span, :] = normed
        mean_ref[span, :] = mean
        inv_ref[span, :] = inverse
        out_ref[span, :] = (dot(normed, qkv_w[...], 1, 0) + bias).astype(BF)


def project(ids, tokens, blocks, pieces, hidden_part, count_column, ordered):
    capacity, width = tokens[0].shape
    group = len(tokens)
    length = group * capacity
    part = width // group
    return pl.pallas_call(
        lambda *refs: project_kernel(ordered, group, count_column, *refs),
        in_specs=[SMEM] + [VMEM] * (2 * group + len(pieces)),
        out_specs=[VMEM] * (9 + group),
        out_shape=[
            shaped((width, 3 * part), BF),
            shaped((width, part), BF),
            shaped((16, width), F32),
            shaped((length, width), BF),
            shaped((length, 3 * part), BF),
            shaped((length, 1), F32),
            shaped((length, 1), F32),
            shaped((1, hidden_part), F32),
            shaped((length, 1), F32),
        ]
        + [shaped((capacity, 1), F32)] * group,
        scratch_shapes=[
            pltpu.VMEM((width, EXTRA), F32),
            pltpu.VMEM((8, 3 * part), F32),
            pltpu.VMEM((8, part), F32),
        ],
        compiler_params=PARAMS,
        cost_estimate=SMALL,
        name="project",
    )(ids, *tokens, *blocks, *pieces)


def query_chunks(length):
    step = 512
    return [(start, min(step, length - start)) for start in range(0, length, step)]


def attend_kernel(qkv_ref, bias_ref, out_ref, lse_ref, *lows):
    length = qkv_ref.shape[0]
    key_bias = bias_ref[...]
    for head in range(2):
        keys = qkv_ref[:, PAIR + head * HD : PAIR + (head + 1) * HD]
        values = qkv_ref[:, 2 * PAIR + head * HD : 2 * PAIR + (head + 1) * HD]
        for start, size in query_chunks(length):
            queries = qkv_ref[start : start + size, head * HD : (head + 1) * HD]
            queries = queries * jnp.asarray(HD**-0.5, BF)
            scores = dot(keys, queries, 1, 1) + key_bias
            top = jnp.max(scores, axis=0, keepdims=True)
            expo = jnp.exp(scores - top)
            total = jnp.sum(expo, axis=0, keepdims=True)
            mixed = (dot(values, expo.astype(BF), 0, 0) / total).T
            out_ref[start : start + size, head * HD : (head + 1) * HD] = mixed
            lse_ref[0, head : head + 1, start : start + size] = top + jnp.log(total)
    for j, low in enumerate(lows):
        size = low.shape[0]
        low[...] = out_ref[j * size : (j + 1) * size, :].astype(BF)


def attend(qkv, key_bias, group):
    length, columns = qkv.shape
    pairs = columns // (3 * PAIR)
    return pl.pallas_call(
        attend_kernel,
        grid=(pairs,),
        in_specs=[
            pl.BlockSpec((length, 3 * PAIR), lambda p: (0, p)),
            pl.BlockSpec((length, 1), lambda p: (0, 0)),
        ],
        out_specs=[
            pl.BlockSpec((length, PAIR), lambda p: (0, p)),
            pl.BlockSpec((1, 2, length), lambda p: (p, 0, 0)),
        ]
        + [pl.BlockSpec((length // group, PAIR), lambda p: (0, p))] * group,
        out_shape=[
            shaped((length, pairs * PAIR), F32),
            shaped((pairs, 2, length), F32),
        ]
        + [shaped((length // group, pairs * PAIR), BF)] * group,
        compiler_params=PARAMS,
        cost_estimate=SMALL,
        name="attend",
    )(qkv, key_bias)


def attend_back_kernel(qkv_ref, bias_ref, att_ref, lse_ref, *rest):
    pieces, (out_ref, sums_ref, grad_ref) = rest[:-3], rest[-3:]
    length = qkv_ref.shape[0]
    size = pieces[0].shape[0]
    factor = HD**-0.5
    key_bias = bias_ref[...]
    for j, piece in enumerate(pieces):
        grad_ref[j * size : (j + 1) * size, :] = piece[...].astype(F32)
    for head in range(2):
        low, high = head * HD, (head + 1) * HD
        keys = qkv_ref[:, PAIR + low : PAIR + high]
        values = qkv_ref[:, 2 * PAIR + low : 2 * PAIR + high]
        key_grad = jnp.zeros((length, HD), F32)
        value_grad = jnp.zeros((length, HD), F32)
        for start, size in query_chunks(length):
            rows = slice(start, start + size)
            queries = qkv_ref[rows, low:high] * jnp.asarray(factor, BF)
            product = grad_ref[rows, low:high] * att_ref[rows, low:high]
            grads = grad_ref[rows, low:high].astype(BF)
            delta = jnp.sum(product.T, axis=0, keepdims=True)
            scores = dot(keys, queries, 1, 1) + key_bias
            probs = jnp.exp(scores - lse_ref[0, head : head + 1, rows])
            value_grad += dot(probs.astype(BF), grads, 1, 0)
            raw = (probs * (dot(values, grads, 1, 1) - delta)).astype(BF)
            key_grad += dot(raw, queries, 1, 0)
            query_grad = dot(keys, raw, 0, 0).T * factor
            out_ref[rows, low:high] = query_grad.astype(BF)
        out_ref[:, PAIR + low : PAIR + high] = key_grad.astype(BF)
        out_ref[:, 2 * PAIR + low : 2 * PAIR + high] = value_grad.astype(BF)
    sums_ref[0] = jnp.sum(out_ref[...].astype(F32), axis=0, keepdims=True)


def attend_back(qkv, key_bias, attended, lse, pieces):
    length, columns = qkv.shape
    pairs = columns // (3 * PAIR)
    size = pieces[0].shape[0]
    return pl.pallas_call(
        attend_back_kernel,
        grid=(pairs,),
        in_specs=[
            pl.BlockSpec((length, 3 * PAIR), lambda p: (0, p)),
            pl.BlockSpec((length, 1), lambda p: (0, 0)),
            pl.BlockSpec((length, PAIR), lambda p: (0, p)),
            pl.BlockSpec((1, 2, length), lambda p: (p, 0, 0)),
        ]
        + [pl.BlockSpec((size, PAIR), lambda p: (0, p))] * len(pieces),
        out_specs=[
            pl.BlockSpec((length, 3 * PAIR), lambda p: (0, p)),
            pl.BlockSpec((1, 1, 3 * PAIR), lambda p: (p, 0, 0)),
        ],
        out_shape=[shaped((length, columns), BF), shaped((pairs, 1, 3 * PAIR), F32)],
        scratch_shapes=[pltpu.VMEM((length, PAIR), F32)],
        compiler_params=PARAMS,
        cost_estimate=SMALL,
        name="attend_back",
    )(qkv, key_bias, attended, lse, *pieces)


def middle_kernel(group, rows_ref, tokens_ref, *rest):
    parts, weights, (branch_ref, middle_ref, normed_ref, unit_ref, inv_ref) = (
        rest[:group], rest[group : 2 * group], rest[2 * group :]
    )
    branch = dot(parts[0][...], weights[0][...], 1, 1)
    for part, weight in zip(parts[1:], weights[1:]):
        branch = branch + dot(part[...], weight[...], 1, 1)
    branch = branch + rows_ref[4:5, :]
    branch_ref[...] = branch
    middle = tokens_ref[...].astype(F32) + rows_ref[5:6, :] * branch
    middle_ref[...] = middle
    unit, inverse = unit_rows(middle)
    unit_ref[...] = unit
    inv_ref[...] = inverse
    normed_ref[...] = (unit * rows_ref[6:7, :] + rows_ref[7:8, :]).astype(BF)


def middle_step(rows, tokens, parts, weights):
    length, width = tokens.shape
    group = len(parts)
    full = shaped((length, width), F32)
    return pl.pallas_call(
        lambda *refs: middle_kernel(group, *refs),
        in_specs=[VMEM] * (2 + 2 * group),
        out_specs=[VMEM] * 5,
        out_shape=[full, full, shaped((length, width), BF), full, shaped((length, 1), F32)],
        compiler_params=PARAMS,
        cost_estimate=SMALL,
        name="middle",
    )(rows, tokens, *parts, *weights)


def turn_kernel(group, terms, rows_ref, live_ref, cot_ref, unit_ref, inv_ref, branch_ref, *rest):
    backs, weights, outs = rest[:terms], rest[terms : terms + group], rest[terms + group :]
    middle_ref, grad_ref, sums_ref = outs[:3]
    norm_grad = backs[0][...].astype(F32)
    for ref in backs[1:]:
        norm_grad = norm_grad + ref[...].astype(F32)
    unit = unit_ref[...]
    out_grad = cot_ref[...].astype(F32) * live_ref[...]
    middle = out_grad + norm_back(norm_grad, unit, inv_ref[...], rows_ref[6:7, :])
    middle_ref[...] = middle
    low = (middle * rows_ref[5:6, :]).astype(BF)
    grad_ref[...] = low
    sums_ref[...] = jnp.zeros(sums_ref.shape, F32)
    sums_ref[0:1, :] = jnp.sum(low.astype(F32), axis=0, keepdims=True)
    sums_ref[1:2, :] = jnp.sum(middle * branch_ref[...], axis=0, keepdims=True)
    sums_ref[2:3, :] = jnp.sum(norm_grad * unit, axis=0, keepdims=True)
    sums_ref[3:4, :] = jnp.sum(norm_grad, axis=0, keepdims=True)
    for out, weight in zip(outs[3:], weights):
        out[...] = dot(low, weight[...], 1, 0).astype(BF)


def turn(rows, live, cotangent, unit, inverse, branch, backs, weights):
    length, width = cotangent.shape
    part = weights[0].shape[1]
    group = len(weights)
    return pl.pallas_call(
        lambda *refs: turn_kernel(group, len(backs), *refs),
        in_specs=[VMEM] * (6 + len(backs) + group),
        out_specs=[VMEM] * (3 + group),
        out_shape=[shaped((length, width), F32), shaped((length, width), BF), shaped((8, width), F32)]
        + [shaped((length, part), BF)] * group,
        compiler_params=PARAMS,
        cost_estimate=SMALL,
        name="turn",
    )(rows, live, cotangent, unit, inverse, branch, *backs, *weights)


def proj_weights_kernel(ids_ref, grad_ref, *rest):
    parts, out_ref = rest[:-1], rest[-1]
    for j, part in enumerate(parts):
        out_ref[ids_ref[0] ^ j] = dot(grad_ref[...], part[...], 0, 0).astype(BF)


def proj_weights(ids, grads, parts):
    width = grads.shape[1]
    part = parts[0].shape[1]
    return pl.pallas_call(
        proj_weights_kernel,
        in_specs=[SMEM] + [VMEM] * (1 + len(parts)),
        out_specs=VMEM,
        out_shape=shaped((len(parts), width, part), BF),
        compiler_params=PARAMS,
        cost_estimate=SMALL,
        name="proj_weights",
    )(ids, grads, *parts)


def mlp_kernel(count, shards, group, rows_ref, *rest):
    normed_in, cots, lives = rest[:count], rest[count : 2 * count], rest[2 * count : 3 * count]
    ids_ref, bias_ref = rest[3 * count : 3 * count + 2]
    rest = rest[3 * count + 2 :]
    pieces, backs, rest = rest[:shards], rest[shards : shards + count], rest[shards + count :]
    normed_ref, out_ref, act_ref, pre_ref, sums_ref, own_ref = rest[:6]
    if shards > 1:
        weight_ref, grad_ref, back_acc = rest[6:]
    else:
        weight_ref = pieces[0]
        grad_ref, back_acc = rest[6:]
    step = pl.program_id(0)
    size = cots[0].shape[0]

    @pl.when(step == 0)
    def _():
        if shards > 1:
            whole_size = pieces[0].shape[0]
            sub = whole_size // group
            for m, piece in enumerate(pieces):
                for j in range(group):
                    start = (ids_ref[1] ^ m) * whole_size + (ids_ref[0] ^ j) * sub
                    weight_ref[pl.ds(pl.multiple_of(start, sub), sub), :] = piece[
                        j * sub : (j + 1) * sub, :
                    ]
        normed_ref[...] = jnp.concatenate([ref[...].astype(F32) for ref in normed_in]).astype(BF)
        scale = rows_ref[9:10, :]
        grads = [cot[...].astype(F32) * live[...] for cot, live in zip(cots, lives)]
        whole_grad = jnp.concatenate(grads)
        out_ref[...] = whole_grad.astype(BF)
        scaled = (whole_grad * scale).astype(BF)
        grad_ref[...] = scaled
        own_ref[0:1, :] = jnp.sum(scaled.astype(F32)[:size], axis=0, keepdims=True)
        own_ref[1:2, :] = jnp.sum(grads[0], axis=0, keepdims=True)

    hidden = weight_ref.shape[1] // 2
    span = act_ref.shape[1]
    chunk = span // 2
    for cols in (slice(0, chunk), slice(chunk, 2 * chunk)):
        here = lanes(step * span + cols.start, chunk)
        there = lanes(hidden + step * span + cols.start, chunk)
        pre = dot(normed_ref[...], weight_ref[:, here], 1, 0) + bias_ref[:, cols]
        act_grad = dot(grad_ref[...], weight_ref[:, there], 1, 0)
        cdf = 0.5 * (1.0 + lax.erf(pre * SQRT_HALF))
        act_ref[:, cols] = (pre * cdf).astype(BF)
        slope = cdf + pre * (jnp.exp(-0.5 * pre * pre) * INV_ROOT_TWO_PI)
        pre_grad = (act_grad * slope).astype(BF)
        pre_ref[:, cols] = pre_grad
        sums_ref[:, cols] = jnp.sum(pre_grad.astype(F32), axis=0, keepdims=True)
    back = dot(pre_ref[...], weight_ref[:, lanes(step * span, span)], 1, 1)

    @pl.when(step == 0)
    def _():
        back_acc[...] = back

    @pl.when(step == pl.num_programs(0) - 1)
    def _():
        whole = back_acc[...] + back
        for j, ref in enumerate(backs):
            ref[...] = whole[j * size : (j + 1) * size].astype(BF)


def mlp(rows, normed, cots, lives, ids, bias, weights, group):
    size, width = normed[0].shape
    count, shards = len(normed), len(weights)
    length = count * size
    hidden = weights[0].shape[1] // 2
    laid = shards > 1
    step = hidden // 2

    def whole(*shape):
        return pl.BlockSpec(shape, lambda i: (0, 0))

    cols = pl.BlockSpec((length, step), lambda i: (0, i))
    return pl.pallas_call(
        lambda *refs: mlp_kernel(count, shards, group, *refs),
        grid=(2,),
        in_specs=[whole(*rows.shape)]
        + [whole(size, width)] * (2 * count)
        + [whole(size, 1)] * count
        + [SMEM, pl.BlockSpec((1, step), lambda i: (0, i))]
        + [whole(*piece.shape) for piece in weights],
        out_specs=[whole(size, width)] * count
        + [whole(length, width)] * 2
        + [cols, cols, pl.BlockSpec((1, step), lambda i: (0, i)), whole(8, width)]
        + [whole(width, 2 * hidden)] * laid,
        out_shape=[shaped((size, width), BF)] * count
        + [shaped((length, width), BF)] * 2
        + [shaped((length, hidden), BF)] * 2
        + [shaped((1, hidden), F32), shaped((8, width), F32)]
        + [shaped((width, 2 * hidden), BF)] * laid,
        scratch_shapes=[pltpu.VMEM((length, width), BF), pltpu.VMEM((length, width), F32)],
        compiler_params=PARAMS,
        cost_estimate=SMALL,
        name="mlp",
    )(rows, *normed, *cots, *lives, ids, bias, *weights)


def mlp_weights_kernel(
    direct, ids_ref, norm_a, norm_b, grad_a, grad_b, rows_ref, fc2_ref, pre_a, pre_b, act_a, act_b,
    own_ref, *rest
):
    keep_ref, send_ref, scale2_ref, *branches, out_ref = rest
    hidden = pre_a.shape[1]
    first = dot(norm_a[...], pre_a[...], 0, 0) + dot(norm_b[...], pre_b[...], 0, 0)
    size = keep_ref.shape[0]
    out_ref[0, :, :hidden] = first[:size].astype(BF)
    out_ref[1, :, :hidden] = first[size:].astype(BF)
    outs = [grad_a[...].astype(F32), grad_b[...].astype(F32)]
    scaled = [(out * rows_ref[9:10, :]).astype(BF) for out in outs]
    second = dot(scaled[0], act_a[...], 0, 0) + dot(scaled[1], act_b[...], 0, 0)
    out_ref[0, :, hidden:] = second[:size].astype(BF)
    out_ref[1, :, hidden:] = second[size:].astype(BF)
    side = (ids_ref[1] & 1) if direct else 0
    keep_ref[...] = out_ref[side]
    send_ref[...] = out_ref[1 - side]
    scale2 = own_ref[1:2, :] * rows_ref[8:9, :]
    count = len(branches) // 2
    size = branches[0].shape[0]
    for half, act in enumerate((act_a, act_b)):
        branch = dot(act[...], fc2_ref[...], 1, 1)
        scale2 = scale2 + jnp.sum(outs[half] * branch, axis=0, keepdims=True)
        for j in range(count):
            branches[half * count + j][...] = branch[j * size : (j + 1) * size].astype(BF)
    scale2_ref[...] = scale2


def mlp_weights(rows, own, normed, grads, pres, acts, weights, group, ids, direct):
    length, width = normed[0].shape
    hidden = pres[0].shape[1]
    size = 2 * length // group
    step = 256

    cols = pl.BlockSpec((length, step), lambda i, ids_ref: (0, i))
    whole = pl.BlockSpec((length, hidden), lambda i, ids_ref: (0, 0))

    def line(count):
        return pl.BlockSpec((count, step), lambda i, ids_ref: (0, i))

    part = pl.BlockSpec((step // 2, 2 * hidden), lambda i, ids_ref: (i, 0))
    return pl.pallas_call(
        lambda *refs: mlp_weights_kernel(direct, *refs),
        grid_spec=pltpu.PrefetchScalarGridSpec(
            num_scalar_prefetch=1,
            grid=(width // step,),
            in_specs=[cols] * 4
            + [line(rows.shape[0])]
            + [pl.BlockSpec((step, hidden), lambda i, ids_ref: (i, 1))]
            + [whole] * 4
            + [line(own.shape[0])],
            out_specs=[part, part, line(1)] + [line(size)] * group,
            scratch_shapes=[pltpu.VMEM((2, step // 2, 2 * hidden), BF)],
        ),
        out_shape=[shaped((width // 2, 2 * hidden), BF)] * 2
        + [shaped((1, width), F32)]
        + [shaped((size, width), BF)] * group,
        compiler_params=PARAMS,
        cost_estimate=SMALL,
        name="mlp_weights",
    )(ids, *normed, *grads, rows, weights, *pres, *acts, own)


def finish_kernel(rows_ref, middle_ref, *rest):
    terms, out_ref = rest[:-1], rest[-1]
    branch = terms[0][...].astype(F32)
    for ref in terms[1:]:
        branch = branch + ref[...].astype(F32)
    branch = branch + rows_ref[8:9, :]
    out_ref[...] = (middle_ref[...] + rows_ref[9:10, :] * branch).astype(BF)


def finish(rows, middle, terms):
    return pl.pallas_call(
        finish_kernel,
        in_specs=[VMEM] * (2 + len(terms)),
        out_specs=VMEM,
        out_shape=shaped(middle.shape, BF),
        compiler_params=PARAMS,
        name="finish",
    )(rows, middle, *terms)


def begin_kernel(rows_ref, tokens_ref, mean_ref, inv_ref, middle_ref, *rest):
    terms, out_ref = rest[:-1], rest[-1]
    grads = terms[0][...].astype(F32)
    for ref in terms[1:]:
        grads = grads + ref[...].astype(F32)
    inverse = inv_ref[...]
    unit = (tokens_ref[...].astype(F32) - mean_ref[...]) * inverse
    out_ref[...] = (middle_ref[...] + norm_back(grads, unit, inverse, rows_ref[0:1, :])).astype(BF)


def begin(rows, tokens, mean, inverse, middle_grad, terms):
    length, width = tokens.shape
    column = pl.BlockSpec((length, 1), lambda i: (0, 0))
    whole = pl.BlockSpec((length, width), lambda i: (0, 0))
    return pl.pallas_call(
        begin_kernel,
        grid=(1,),
        in_specs=[pl.BlockSpec(rows.shape, lambda i: (0, 0)), whole, column, column, whole]
        + [whole] * len(terms),
        out_specs=whole,
        out_shape=shaped((length, width), BF),
        compiler_params=PARAMS,
        name="begin",
    )(rows, tokens, mean, inverse, middle_grad, *terms)


def qkv_back_kernel(group, grad_ref, weight_ref, mean_ref, inv_ref, *rest):
    tokens, outs, sums_ref = rest[:group], rest[group:-1], rest[-1]
    size = tokens[0].shape[0]
    gain = shift = 0.0
    for first in range(0, group, 2):
        span = slice(first * size, (first + 2) * size)
        part = dot(grad_ref[span, :], weight_ref[...], 1, 1)
        inputs = jnp.concatenate([tokens[first][...].astype(F32), tokens[first + 1][...].astype(F32)])
        unit = (inputs - mean_ref[span, :]) * inv_ref[span, :]
        outs[first][...] = part[:size].astype(BF)
        outs[first + 1][...] = part[size:].astype(BF)
        gain = gain + jnp.sum(part * unit, axis=0, keepdims=True)
        shift = shift + jnp.sum(part, axis=0, keepdims=True)
    sums_ref[...] = jnp.zeros(sums_ref.shape, F32)
    sums_ref[0:1, :] = gain
    sums_ref[1:2, :] = shift


def qkv_back(qkv_grad, weight, tokens, mean, inverse):
    size, width = tokens[0].shape
    group = len(tokens)
    return pl.pallas_call(
        lambda *refs: qkv_back_kernel(group, *refs),
        in_specs=[VMEM] * (4 + group),
        out_specs=[VMEM] * (group + 1),
        out_shape=[shaped((size, width), BF)] * group + [shaped((8, width), F32)],
        compiler_params=PARAMS,
        cost_estimate=SMALL,
        name="qkv_back",
    )(qkv_grad, weight, mean, inverse, *tokens)


def attn_weights_kernel(
    direct, shard, terms, ids_ref, normed_ref, grad_ref, norm1_ref, sums_ref, turn_ref, fbias_ref,
    scale2_ref, bias_a_ref, bias_b_ref, *rest,
):
    projs, outs = rest[:terms], rest[terms:-5]
    rows_ref, turned_ref, block_ref, small_ref, stage_ref = rest[-5:]
    place, row = ids_ref[0], ids_ref[1]
    width = normed_ref.shape[1]
    part = projs[0].shape[1]
    rows_ref[...] = jnp.zeros(rows_ref.shape, F32)
    rows_ref[0:2, :] = norm1_ref[0:2, :]
    for pair in range(part // PAIR):
        where = lanes(place * part + pair * PAIR, PAIR)
        rows_ref[2:3, where] = sums_ref[pair, :, :PAIR]
        rows_ref[3:4, where] = sums_ref[pair, :, 2 * PAIR :]
    rows_ref[4:8, :] = turn_ref[0:4, :]
    rows_ref[8:9, :] = fbias_ref[0:1, :]
    rows_ref[9:10, :] = scale2_ref[...]
    cols = bias_a_ref.shape[1] // part
    for owner in range(part // shard):
        for line in range(cols):
            spot = (owner * cols + line) * shard
            small_ref[line : line + 1, owner * shard : (owner + 1) * shard] = (
                bias_a_ref[0:1, spot : spot + shard] + bias_b_ref[0:1, spot : spot + shard]
            )
    rows_ref[10 : 10 + cols, lanes(place * part, part)] = small_ref[0:cols, :]
    turned_ref[...] = rows_ref[...].T
    step = block_ref.shape[0]
    for k in range(width // step):
        start = pl.multiple_of(((row >> 1) ^ k) * step, step) if direct else k * step
        cols = pl.ds(start, step)
        block_ref[:, : 3 * part] = dot(normed_ref[:, cols], grad_ref[...], 0, 0)
        proj = projs[0][cols, :].astype(F32)
        for ref in projs[1:]:
            proj = proj + ref[cols, :].astype(F32)
        block_ref[:, 3 * part : 4 * part] = proj
        block_ref[:, 4 * part :] = turned_ref[cols, :]
        if direct:
            size = step // 2
            stage_ref[0] = block_ref[:size, :].astype(BF)
            stage_ref[1] = block_ref[size:, :].astype(BF)
            side = row & 1
            blocks = width // step
            outs[k][...] = stage_ref[side]
            spot = (k + 1) % 2 * size
            outs[blocks + (blocks - 1 - k) // 2][spot : spot + size, :] = stage_ref[1 - side]
        else:
            outs[0][k * step : (k + 1) * step, :] = block_ref[...].astype(BF)


def attn_weights(ids, normed1, qkv_grad, sums, projs, blocks, shard):
    length, width = normed1.shape
    part = projs[0].shape[1]
    columns = 4 * part + EXTRA
    direct = blocks > 0
    step = 2 * (width // blocks) if direct else 256
    out_shape = [shaped((width, columns), BF)]
    if direct:
        size = width // blocks
        out_shape = [shaped((size, columns), BF)] * (blocks // 2)
        out_shape += [shaped((2 * size, columns), BF)] * (blocks // 4)
    return pl.pallas_call(
        lambda *refs: attn_weights_kernel(direct, shard, len(projs), *refs),
        in_specs=[SMEM] + [VMEM] * (2 + len(sums) + len(projs)),
        out_specs=[VMEM] * len(out_shape),
        out_shape=out_shape,
        scratch_shapes=[
            pltpu.VMEM((EXTRA, width), F32),
            pltpu.VMEM((width, EXTRA), F32),
            pltpu.VMEM((step, columns), F32),
            pltpu.VMEM((8, part), F32),
            pltpu.VMEM((2, step // 2, columns), BF),
        ],
        compiler_params=PARAMS,
        cost_estimate=SMALL,
        name="attn_weights",
    )(ids, normed1, qkv_grad, *sums, *projs)


def total(ids, terms, group):
    size, columns = terms[0].shape
    rows = size // group

    def kernel(ids_ref, *refs):
        ins, outs, sum_ref = refs[: len(terms)], refs[len(terms) : -1], refs[-1]
        value = ins[0][...].astype(F32)
        for ref in ins[1:]:
            value = value + ref[...].astype(F32)
        sum_ref[...] = value
        for k, out in enumerate(outs):
            start = pl.multiple_of((ids_ref[0] ^ k) * rows, rows)
            out[...] = sum_ref[pl.ds(start, rows), :].astype(BF)

    return pl.pallas_call(
        kernel,
        in_specs=[SMEM] + [VMEM] * len(terms),
        out_specs=[VMEM] * group,
        out_shape=[shaped((rows, columns), BF)] * group,
        scratch_shapes=[pltpu.VMEM((size, columns), F32)],
        compiler_params=PARAMS,
        name="total",
    )(ids, *terms)


def place_attn_kernel(ids_ref, *refs):
    group = len(refs) - 4
    blocks, (qkv_ref, proj_ref, vec_ref, bias_ref) = refs[:group], refs[group:]
    width = proj_ref.shape[1]
    part = width // group
    extra = jnp.zeros((qkv_ref.shape[0], EXTRA), F32)
    for k, block in enumerate(blocks):
        source = ids_ref[0] ^ k
        for third in range(3):
            for pair in range(part // PAIR):
                spot = (pair * 3 + third) * PAIR
                where = lanes(third * width + source * part + pair * PAIR, PAIR)
                qkv_ref[:, where] = block[:, spot : spot + PAIR].astype(F32)
        proj_ref[:, lanes(source * part, part)] = block[:, 3 * part : 4 * part].astype(F32)
        extra = extra + block[:, 4 * part :].astype(F32)
    turned = extra.T
    count = vec_ref.shape[0]
    vec_ref[...] = turned[:count]
    rows = qkv_ref.shape[0]
    for line in range(bias_ref.shape[1] // rows):
        bias_ref[0:1, line * rows : (line + 1) * rows] = turned[count + line : count + line + 1]


def place_attn(ids, blocks, width, vector_count, bias_cols):
    rows = blocks[0].shape[0]
    return pl.pallas_call(
        place_attn_kernel,
        in_specs=[SMEM] + [VMEM] * len(blocks),
        out_specs=[VMEM] * 4,
        out_shape=[
            shaped((rows, 3 * width), F32),
            shaped((rows, width), F32),
            shaped((vector_count, rows), F32),
            shaped((1, bias_cols * rows), F32),
        ],
        compiler_params=PARAMS,
        name="place_attn",
    )(ids, *blocks)


def place_mlp_kernel(ids_ref, *refs):
    group = len(refs) - 2
    blocks, (fc1_ref, fc2_ref) = refs[:group], refs[group:]
    part = fc1_ref.shape[1] // group
    for k, block in enumerate(blocks):
        where = lanes((ids_ref[0] ^ k) * part, part)
        fc1_ref[:, where] = block[:, :part].astype(F32)
        fc2_ref[:, where] = block[:, part:].astype(F32)


def place_mlp(ids, blocks, hidden):
    rows = blocks[0].shape[0]
    return pl.pallas_call(
        place_mlp_kernel,
        in_specs=[SMEM] + [VMEM] * len(blocks),
        out_specs=[VMEM] * 2,
        out_shape=[shaped((rows, hidden), F32)] * 2,
        compiler_params=PARAMS,
        name="place_mlp",
    )(ids, *blocks)


def local(tokens, counts, w_qkv, w_proj, w_fc1, fc1_bias, w_fc2, vectors, cotangent):
    _, capacity, width = tokens.shape
    hidden = w_fc1.shape[1]
    rows = w_qkv.shape[0]
    group, replicas = lax.axis_size("ctx"), lax.axis_size("dp")
    place, replica = lax.axis_index("ctx"), lax.axis_index("dp")
    ids = jnp.stack([place, replica]).astype(jnp.int32)
    head_width = width // group
    hidden_part = hidden // group
    bias_cols = hidden // width
    vector_count = vectors.shape[0]
    direct = replicas == 8

    def swap(value, bit, axis="ctx"):
        size = group if axis == "ctx" else replicas
        return lax.ppermute(value, axis, [(i, i ^ bit) for i in range(size)])

    def after(value, *before):
        return lax.optimization_barrier((value,) + before)[0]

    def gather(own, *before):
        pieces = [own]
        for j in range(1, group):
            bit = j & -j
            source = pieces[j ^ bit]
            pieces.append(swap(after(source, *before) if j ^ bit else source, bit))
        return pieces

    def scatter(parts, *before, mids=None, axis="ctx", scale=1, gates=None):
        pieces = {j: [part] for j, part in enumerate(parts)}

        def added(terms):
            if len(terms) == 1:
                return terms[0]
            return sum(term.astype(F32) for term in terms).astype(BF)

        bit = 1
        sent = []
        while bit < len(parts):
            for j in sorted((j for j in pieces if j & bit), reverse=True):
                value = added(pieces.pop(j))
                if bit > 1:
                    if mids is not None:
                        mids.append(value)
                    value = after(value, *before)
                elif axis == "dp":
                    value = after(value, *sent[-2:-1])
                if gates and bit in gates:
                    value = after(value, *gates[bit])
                sent.append(swap(value, bit * scale, axis))
                pieces[j ^ bit].append(sent[-1])
            bit *= 2
        return pieces[0]

    def exchange(relative):
        return [relative[0]] + [swap(relative[k], k) for k in range(1, group)]

    def in_order(relative):
        stacked = jnp.stack(relative)
        return jnp.concatenate(
            [lax.dynamic_index_in_dim(stacked, place ^ s, 0, False) for s in range(group)], axis=0
        )

    cuts = cut(
        ids, counts, w_qkv, w_proj.T, w_fc1, w_fc2.T, vectors, fc1_bias.reshape(1, -1), group
    )
    first = exchange(cuts[:group])
    tokens_far = swap(after(tokens[0], *first), group // 2)

    def widen(shards, *before):
        for m in range(2, replicas):
            low = m & -m
            if m ^ low:
                shards[m] = swap(after(shards[m ^ low], *before), low, "dp")

    second = exchange([after(block, *first) for block in cuts[group:]])
    if direct:
        shards = {0: jnp.concatenate(first, axis=0)}
        for bit in (4, 2, 1):
            shards[bit] = swap(shards[0], bit, "dp")
        arrived = [shards[bit] for bit in (4, 2, 1)] + second[1:]
        widen(shards, *arrived)
        first_pieces = [shards[m] for m in range(replicas)]
        nearly = [shards[3], shards[5], shards[7]]
    else:
        first_pieces = [lax.all_gather(in_order(first), "dp", axis=0, tiled=True)]
        arrived = nearly = [tokens_far]
    second_shard = after(in_order(second), *arrived)
    second_all = lax.all_gather(second_shard, "dp", axis=0, tiled=True)
    cotangent_far = swap(after(cotangent[0], *arrived), group // 2)
    nearly = nearly + [cotangent_far]
    tokens_pieces = [tokens[0]]
    for j in range(1, group):
        source = tokens_pieces[j ^ (j & -j)]
        if j == group // 2:
            tokens_pieces.append(tokens_far)
        else:
            tokens_pieces.append(swap(after(source, *nearly), j & -j))
    tokens_own = after(tokens[0], second_shard)
    count_column = vector_count + bias_cols
    (
        weight_qkv, weight_proj, vector_rows, normed1, qkv, mean1, inverse1, bias_fc1, key_bias,
        *live,
    ) = project(
        ids, [tokens_own] + tokens_pieces[1:], first, first_pieces, hidden_part, count_column,
        0 if direct else rows,
    )

    cotangent_pieces = [cotangent[0]]
    for j in range(1, group):
        source = cotangent_pieces[j ^ (j & -j)]
        if j == group // 2:
            cotangent_pieces.append(cotangent_far)
        else:
            cotangent_pieces.append(swap(after(source, qkv), j & -j))
    attended, lse, *attended_low = attend(qkv, key_bias, group)
    projs = gather(weight_proj, lse)
    attended_own = exchange(attended_low)
    branch1, middle, normed2_own, unit2, inverse2 = middle_step(
        vector_rows, tokens[0], attended_own, projs
    )
    half = group // 2
    normed2 = [normed2_own]
    while len(normed2) < half:
        normed2 += [swap(piece, len(normed2)) for piece in normed2]

    def feed(where, pieces, weights):
        return mlp(
            vector_rows, pieces, cotangent_pieces[where], live[where], ids, bias_fc1, weights, group
        )

    *backs_near, norm_near, grad_near, act_near, pre_near, sums_near, own_sums = feed(
        slice(0, half), normed2, [second_all]
    )
    normed2_far = [swap(normed2_own, half)]
    while len(normed2_far) < half:
        normed2_far += [
            swap(after(piece, sums_near), len(normed2_far)) for piece in normed2_far
        ]
    *backs_far, norm_far, grad_far, act_far, pre_far, sums_far, _ = feed(
        slice(half, group), normed2_far, [second_all]
    )
    mids = []
    norm2_terms = scatter(backs_near + backs_far, mids=mids)
    keep_mlp, send_mlp, grad_scale2, *branches = mlp_weights(
        vector_rows, own_sums, [norm_near, norm_far], [grad_near, grad_far], [after(pre_near, *mids), pre_far],
        [act_near, act_far], second_all, group, ids, direct,
    )
    other_mlp = None
    if direct:
        other_mlp = swap(after(send_mlp, *norm2_terms), 1, "dp")
    middle_grad, branch_grad, turn_sums, *att_grads = turn(
        after(vector_rows, grad_scale2), live[0], cotangent[0], unit2, inverse2, branch1, norm2_terms, projs
    )
    att_grads = exchange(att_grads)
    proj_parts = proj_weights(ids, branch_grad, attended_own).reshape(group * width, -1)
    proj_grad = lax.psum_scatter(
        after(proj_parts, *att_grads), "ctx", scatter_dimension=0, tiled=True
    )
    branch2_mids = []
    branch2_terms = scatter(branches, *att_grads, mids=branch2_mids)
    qkv_grad, qkv_sums = attend_back(qkv, key_bias, attended, after(lse, proj_parts), att_grads)
    if direct:
        other = after(other_mlp, qkv_grad)
        summed = (keep_mlp.astype(F32) + other.astype(F32)).astype(BF)
        lines = [[side + 2 * z for z in range(replicas // 2)] for side in range(2)]
        owned_mlp = lax.psum_scatter(
            summed, "dp", scatter_dimension=0, tiled=True, axis_index_groups=lines
        )
    else:
        ordered = jnp.stack(
            [part.reshape(-1, 128, 2 * hidden_part) for part in (keep_mlp, send_mlp)], axis=1
        )
        owned_mlp = lax.psum_scatter(
            ordered.reshape(width, 2 * hidden_part), "dp", scatter_dimension=0, tiled=True
        )
    *norm1_parts, norm1_sums = qkv_back(after(qkv_grad, summed) if direct else qkv_grad, weight_qkv, tokens_pieces, mean1, inverse1)
    before = branch2_mids
    parts = attn_weights(
        ids, after(normed1, *before), qkv_grad,
        [norm1_sums, qkv_sums, turn_sums, own_sums, grad_scale2, sums_near, sums_far],
        [proj_grad], replicas if direct else 0, rows,
    )
    norm1_terms = scatter(norm1_parts)
    if direct:
        def add(left, right):
            return (left.astype(F32) + right.astype(F32)).astype(BF)

        keep0, keep1, keep2, keep3, send32, send10 = parts
        size = keep0.shape[0]
        other32 = swap(send32, 1, "dp")
        other10 = swap(after(send10, other32, branch2_terms[-1]), 1, "dp")
        across = swap(add(keep3, other32[:size]), 2, "dp")
        near2 = add(add(keep2, other32[size:]), across)
        far = swap(after(near2, norm1_terms[-1]), 4, "dp")
        across0 = swap(add(keep1, other10[:size]), 2, "dp")
        terms = [add(keep0, other10[size:]), across0, far]
        settled = [across]
        cuts_mlp = total(after(ids, *settled), [owned_mlp], group)
    else:
        owned_attn = lax.psum_scatter(parts[0], "dp", scatter_dimension=0, tiled=True)

        def relative(owned):
            blocks = owned.reshape(group, rows, -1)
            return [lax.dynamic_index_in_dim(blocks, place ^ k, 0, False) for k in range(group)]

        cuts_mlp = relative(owned_mlp)
        settled = []
    out_fc1, out_fc2 = place_mlp(ids, exchange(cuts_mlp), hidden)
    input_grad = begin(
        vector_rows, after(tokens[0], *settled), mean1, inverse1, middle_grad, norm1_terms
    )
    output = finish(after(vector_rows, *settled), middle, branch2_terms)
    if direct:
        cuts_attn = total(after(ids, input_grad, output, out_fc1), terms, group)
    else:
        cuts_attn = relative(owned_attn)

    out_qkv, out_proj, out_vectors, out_bias = place_attn(
        ids, exchange(cuts_attn), width, vector_count, bias_cols
    )
    return (
        output[None],
        input_grad[None],
        out_qkv,
        out_proj.T,
        out_fc1,
        out_bias.reshape(-1),
        out_fc2.T,
        out_vectors,
    )


def solution(mesh):
    both = ("dp", "ctx")
    in_specs = (
        P("dp", "ctx", None),
        P("dp", "ctx"),
        P(both, None),
        P(None, both),
        P(both, None),
        P(both),
        P(None, both),
        P(None, both),
        P("dp", "ctx", None),
    )
    out_specs = (
        P("dp", "ctx", None),
        P("dp", "ctx", None),
        P(both, None),
        P(None, both),
        P(both, None),
        P(both),
        P(None, both),
        P(None, both),
    )
    return jax.shard_map(local, mesh=mesh, in_specs=in_specs, out_specs=out_specs, check_vma=False)
```

```python
import jax
import jax.numpy as jnp
from jax import lax
from jax.experimental import pallas as pl
from jax.experimental.pallas import tpu as pltpu
from jax.sharding import PartitionSpec as P

HD = 64
PAIR = 2 * HD
EXTRA = 128
EPSILON = 1e-06
MASKED_SCORE = -1e30
SQRT_HALF = 0.7071067811865476
INV_ROOT_TWO_PI = 0.3989422804014327
BF = jnp.bfloat16
F32 = jnp.float32
PARAMS = pltpu.CompilerParams(vmem_limit_bytes=60 * 1024 * 1024)
SMALL = pl.CostEstimate(flops=1_000_000_000, bytes_accessed=1_000_000, transcendentals=0)
TINY = pl.CostEstimate(flops=1_000, bytes_accessed=1_000, transcendentals=0)
VMEM = pl.BlockSpec(memory_space=pltpu.VMEM)
SMEM = pl.BlockSpec(memory_space=pltpu.SMEM)


def shaped(shape, dtype):
    return jax.ShapeDtypeStruct(shape, dtype)


def dot(left, right, left_dim, right_dim):
    return lax.dot_general(
        left, right, (((left_dim,), (right_dim,)), ((), ())), preferred_element_type=F32
    )


def lanes(start, size):
    return pl.ds(pl.multiple_of(start, 128), size)


def unit_rows(inputs):
    centered = inputs - jnp.mean(inputs, axis=-1, keepdims=True)
    spread = jnp.mean(centered * centered, axis=-1, keepdims=True)
    inverse = lax.rsqrt(spread + EPSILON)
    return (centered * inverse, inverse)


def norm_back(grad_in, unit, inverse, gain):
    scaled = grad_in * gain
    inner = (
        scaled
        - jnp.mean(scaled, axis=-1, keepdims=True)
        - unit * jnp.mean(scaled * unit, axis=-1, keepdims=True)
    )
    return inner * inverse


def cut_kernel(ids_ref, count_ref, qkv_ref, proj_ref, fc1_ref, fc2_ref, vec_ref, bias_ref, *rest):
    outs, (extra_ref, turn_ref) = rest[:-2], rest[-2:]
    group = len(outs) // 2
    place = ids_ref[0]
    width = proj_ref.shape[1]
    part = width // group
    hidden_part = fc1_ref.shape[1] // group
    vector_count, bias_cols = vec_ref.shape[0], bias_ref.shape[1] // vec_ref.shape[1]
    column = vector_count + bias_cols
    lane = lax.broadcasted_iota(jnp.int32, extra_ref.shape, 1)
    count = count_ref[0, 0]
    high = (count >> 7).astype(F32)
    low = (count & 127).astype(F32)
    extra_ref[...] = jnp.where(lane == column, high, jnp.where(lane == column + 1, low, 0.0))
    extra_ref[:, :vector_count] = vec_ref[...].astype(F32).T
    rows = qkv_ref.shape[0]
    for line in range(bias_cols):
        turn_ref[line : line + 1, :] = bias_ref[0:1, line * rows : (line + 1) * rows].astype(F32)
    extra_ref[:, vector_count:column] = turn_ref[0:bias_cols, :].T
    extra = extra_ref[...].astype(BF)
    for k in range(group):
        target = place ^ k
        first, second = outs[k], outs[group + k]
        for third in range(3):
            for pair in range(part // PAIR):
                spot = (pair * 3 + third) * PAIR
                first[:, spot : spot + PAIR] = qkv_ref[
                    :, lanes(third * width + target * part + pair * PAIR, PAIR)
                ]
        first[:, 3 * part : 4 * part] = proj_ref[:, lanes(target * part, part)]
        first[:, 4 * part :] = extra
        second[:, :hidden_part] = fc1_ref[:, lanes(target * hidden_part, hidden_part)]
        second[:, hidden_part:] = fc2_ref[:, lanes(target * hidden_part, hidden_part)]


def cut(ids, counts, w_qkv, w_proj_t, w_fc1, w_fc2_t, vectors, bias, group):
    rows, width = w_proj_t.shape
    part, hidden_part = width // group, w_fc1.shape[1] // group
    return pl.pallas_call(
        cut_kernel,
        in_specs=[SMEM, SMEM] + [VMEM] * 6,
        out_specs=[VMEM] * (2 * group),
        out_shape=[shaped((rows, 4 * part + EXTRA), BF)] * group
        + [shaped((rows, 2 * hidden_part), BF)] * group,
        scratch_shapes=[pltpu.VMEM((rows, EXTRA), F32), pltpu.VMEM((8, rows), F32)],
        compiler_params=PARAMS,
        name="cut",
    )(ids, counts, w_qkv, w_proj_t, w_fc1, w_fc2_t, vectors, bias)


def project_kernel(ordered, group, count_column, ids_ref, *rest):
    tokens, blocks, rest = rest[:group], rest[group : 2 * group], rest[2 * group :]
    pieces, outs, lives, scratch = (
        rest[: -12 - group], rest[-12 - group : -3 - group], rest[-3 - group : -3], rest[-3:]
    )
    qkv_w, proj_w, rows_ref, normed_ref, out_ref, mean_ref, inv_ref, fc1_ref, key_ref = outs
    extra_ref, bias_ref, small_ref = scratch
    place, row = ids_ref[0], ids_ref[1]
    capacity, width = tokens[0].shape
    part = proj_w.shape[1]
    size = pieces[0].shape[0]

    def lay(block, start, count):
        where = pl.ds(start, count)
        qkv_w[where, :] = block[:, : 3 * part]
        proj_w[where, :] = block[:, 3 * part : 4 * part]
        extra_ref[where, :] = block[:, 4 * part :].astype(F32)

    if ordered:
        lay(pieces[0], 0, size)
        shard = ordered
    else:
        sub = shard = size // group
        for m, piece in enumerate(pieces):
            for j in range(group):
                start = (row ^ m) * size + (place ^ j) * sub
                lay(piece.at[j * sub : (j + 1) * sub], pl.multiple_of(start, sub), sub)
    slot = lax.broadcasted_iota(jnp.int32, (capacity, 1), 0).astype(F32)
    for j, (block, live_ref) in enumerate(zip(blocks, lives)):
        extra = block[:, 4 * part :].astype(F32)[0:1, :]
        bound = extra[:, count_column : count_column + 1] * 128.0
        bound = bound + extra[:, count_column + 1 : count_column + 2]
        live = jnp.where(slot < bound, 1.0, 0.0)
        live_ref[...] = live
        key_ref[j * capacity : (j + 1) * capacity, :] = (1.0 - live) * MASKED_SCORE
    turned = extra_ref[...].T
    rows_ref[...] = turned[: rows_ref.shape[0]]
    bias_ref[...] = jnp.zeros(bias_ref.shape, F32)
    for pair in range(part // PAIR):
        for third, line in ((0, 2), (2, 3)):
            spot = (pair * 3 + third) * PAIR
            bias_ref[0:1, spot : spot + PAIR] = rows_ref[
                line : line + 1, lanes(place * part + pair * PAIR, PAIR)
            ]
    cols = fc1_ref.shape[1] // part
    small_ref[0:cols, :] = rows_ref[10 : 10 + cols, lanes(place * part, part)]
    for owner in range(part // shard):
        for line in range(cols):
            spot = (owner * cols + line) * shard
            fc1_ref[0:1, spot : spot + shard] = small_ref[
                line : line + 1, owner * shard : (owner + 1) * shard
            ]
    gain, shift, bias = rows_ref[0:1, :], rows_ref[1:2, :], bias_ref[0:1, :]
    for first in range(0, group, 2):
        span = slice(first * capacity, (first + 2) * capacity)
        inputs = jnp.concatenate([tokens[first][...].astype(F32), tokens[first + 1][...].astype(F32)])
        mean = jnp.mean(inputs, axis=-1, keepdims=True)
        centered = inputs - mean
        inverse = lax.rsqrt(jnp.mean(centered * centered, axis=-1, keepdims=True) + EPSILON)
        normed = (centered * inverse * gain + shift).astype(BF)
        normed_ref[span, :] = normed
        mean_ref[span, :] = mean
        inv_ref[span, :] = inverse
        out_ref[span, :] = (dot(normed, qkv_w[...], 1, 0) + bias).astype(BF)


def project(ids, tokens, blocks, pieces, hidden_part, count_column, ordered):
    capacity, width = tokens[0].shape
    group = len(tokens)
    length = group * capacity
    part = width // group
    return pl.pallas_call(
        lambda *refs: project_kernel(ordered, group, count_column, *refs),
        in_specs=[SMEM] + [VMEM] * (2 * group + len(pieces)),
        out_specs=[VMEM] * (9 + group),
        out_shape=[
            shaped((width, 3 * part), BF),
            shaped((width, part), BF),
            shaped((16, width), F32),
            shaped((length, width), BF),
            shaped((length, 3 * part), BF),
            shaped((length, 1), F32),
            shaped((length, 1), F32),
            shaped((1, hidden_part), F32),
            shaped((length, 1), F32),
        ]
        + [shaped((capacity, 1), F32)] * group,
        scratch_shapes=[
            pltpu.VMEM((width, EXTRA), F32),
            pltpu.VMEM((8, 3 * part), F32),
            pltpu.VMEM((8, part), F32),
        ],
        compiler_params=PARAMS,
        cost_estimate=SMALL,
        name="project",
    )(ids, *tokens, *blocks, *pieces)


def query_chunks(length):
    step = 512
    return [(start, min(step, length - start)) for start in range(0, length, step)]


def attend_kernel(qkv_ref, bias_ref, out_ref, lse_ref, *lows):
    length = qkv_ref.shape[0]
    key_bias = bias_ref[...]
    for head in range(2):
        keys = qkv_ref[:, PAIR + head * HD : PAIR + (head + 1) * HD]
        values = qkv_ref[:, 2 * PAIR + head * HD : 2 * PAIR + (head + 1) * HD]
        for start, size in query_chunks(length):
            queries = qkv_ref[start : start + size, head * HD : (head + 1) * HD]
            queries = queries * jnp.asarray(HD**-0.5, BF)
            scores = dot(keys, queries, 1, 1) + key_bias
            top = jnp.max(scores, axis=0, keepdims=True)
            expo = jnp.exp(scores - top)
            total = jnp.sum(expo, axis=0, keepdims=True)
            mixed = (dot(values, expo.astype(BF), 0, 0) / total).T
            out_ref[start : start + size, head * HD : (head + 1) * HD] = mixed
            lse_ref[0, head : head + 1, start : start + size] = top + jnp.log(total)
    for j, low in enumerate(lows):
        size = low.shape[0]
        low[...] = out_ref[j * size : (j + 1) * size, :].astype(BF)


def attend(qkv, key_bias, group):
    length, columns = qkv.shape
    pairs = columns // (3 * PAIR)
    return pl.pallas_call(
        attend_kernel,
        grid=(pairs,),
        in_specs=[
            pl.BlockSpec((length, 3 * PAIR), lambda p: (0, p)),
            pl.BlockSpec((length, 1), lambda p: (0, 0)),
        ],
        out_specs=[
            pl.BlockSpec((length, PAIR), lambda p: (0, p)),
            pl.BlockSpec((1, 2, length), lambda p: (p, 0, 0)),
        ]
        + [pl.BlockSpec((length // group, PAIR), lambda p: (0, p))] * group,
        out_shape=[
            shaped((length, pairs * PAIR), F32),
            shaped((pairs, 2, length), F32),
        ]
        + [shaped((length // group, pairs * PAIR), BF)] * group,
        compiler_params=PARAMS,
        cost_estimate=SMALL,
        name="attend",
    )(qkv, key_bias)


def attend_back_kernel(qkv_ref, bias_ref, att_ref, lse_ref, *rest):
    pieces, (out_ref, sums_ref, grad_ref) = rest[:-3], rest[-3:]
    length = qkv_ref.shape[0]
    size = pieces[0].shape[0]
    factor = HD**-0.5
    key_bias = bias_ref[...]
    for j, piece in enumerate(pieces):
        grad_ref[j * size : (j + 1) * size, :] = piece[...].astype(F32)
    for head in range(2):
        low, high = head * HD, (head + 1) * HD
        keys = qkv_ref[:, PAIR + low : PAIR + high]
        values = qkv_ref[:, 2 * PAIR + low : 2 * PAIR + high]
        key_grad = jnp.zeros((length, HD), F32)
        value_grad = jnp.zeros((length, HD), F32)
        for start, size in query_chunks(length):
            rows = slice(start, start + size)
            queries = qkv_ref[rows, low:high] * jnp.asarray(factor, BF)
            product = grad_ref[rows, low:high] * att_ref[rows, low:high]
            grads = grad_ref[rows, low:high].astype(BF)
            delta = jnp.sum(product.T, axis=0, keepdims=True)
            scores = dot(keys, queries, 1, 1) + key_bias
            probs = jnp.exp(scores - lse_ref[0, head : head + 1, rows])
            value_grad += dot(probs.astype(BF), grads, 1, 0)
            raw = (probs * (dot(values, grads, 1, 1) - delta)).astype(BF)
            key_grad += dot(raw, queries, 1, 0)
            query_grad = dot(keys, raw, 0, 0).T * factor
            out_ref[rows, low:high] = query_grad.astype(BF)
        out_ref[:, PAIR + low : PAIR + high] = key_grad.astype(BF)
        out_ref[:, 2 * PAIR + low : 2 * PAIR + high] = value_grad.astype(BF)
    sums_ref[0] = jnp.sum(out_ref[...].astype(F32), axis=0, keepdims=True)


def attend_back(qkv, key_bias, attended, lse, pieces):
    length, columns = qkv.shape
    pairs = columns // (3 * PAIR)
    size = pieces[0].shape[0]
    return pl.pallas_call(
        attend_back_kernel,
        grid=(pairs,),
        in_specs=[
            pl.BlockSpec((length, 3 * PAIR), lambda p: (0, p)),
            pl.BlockSpec((length, 1), lambda p: (0, 0)),
            pl.BlockSpec((length, PAIR), lambda p: (0, p)),
            pl.BlockSpec((1, 2, length), lambda p: (p, 0, 0)),
        ]
        + [pl.BlockSpec((size, PAIR), lambda p: (0, p))] * len(pieces),
        out_specs=[
            pl.BlockSpec((length, 3 * PAIR), lambda p: (0, p)),
            pl.BlockSpec((1, 1, 3 * PAIR), lambda p: (p, 0, 0)),
        ],
        out_shape=[shaped((length, columns), BF), shaped((pairs, 1, 3 * PAIR), F32)],
        scratch_shapes=[pltpu.VMEM((length, PAIR), F32)],
        compiler_params=PARAMS,
        cost_estimate=TINY,
        name="attend_back",
    )(qkv, key_bias, attended, lse, *pieces)


def middle_kernel(group, rows_ref, tokens_ref, *rest):
    parts, weights, (branch_ref, middle_ref, normed_ref, unit_ref, inv_ref) = (
        rest[:group], rest[group : 2 * group], rest[2 * group :]
    )
    branch = dot(parts[0][...], weights[0][...], 1, 1)
    for part, weight in zip(parts[1:], weights[1:]):
        branch = branch + dot(part[...], weight[...], 1, 1)
    branch = branch + rows_ref[4:5, :]
    branch_ref[...] = branch
    middle = tokens_ref[...].astype(F32) + rows_ref[5:6, :] * branch
    middle_ref[...] = middle
    unit, inverse = unit_rows(middle)
    unit_ref[...] = unit
    inv_ref[...] = inverse
    normed_ref[...] = (unit * rows_ref[6:7, :] + rows_ref[7:8, :]).astype(BF)


def middle_step(rows, tokens, parts, weights):
    length, width = tokens.shape
    group = len(parts)
    full = shaped((length, width), F32)
    return pl.pallas_call(
        lambda *refs: middle_kernel(group, *refs),
        in_specs=[VMEM] * (2 + 2 * group),
        out_specs=[VMEM] * 5,
        out_shape=[full, full, shaped((length, width), BF), full, shaped((length, 1), F32)],
        compiler_params=PARAMS,
        cost_estimate=SMALL,
        name="middle",
    )(rows, tokens, *parts, *weights)


def turn_kernel(group, terms, rows_ref, live_ref, cot_ref, unit_ref, inv_ref, branch_ref, *rest):
    backs, weights, outs = rest[:terms], rest[terms : terms + group], rest[terms + group :]
    middle_ref, grad_ref, sums_ref = outs[:3]
    norm_grad = backs[0][...].astype(F32)
    for ref in backs[1:]:
        norm_grad = norm_grad + ref[...].astype(F32)
    unit = unit_ref[...]
    out_grad = cot_ref[...].astype(F32) * live_ref[...]
    middle = out_grad + norm_back(norm_grad, unit, inv_ref[...], rows_ref[6:7, :])
    middle_ref[...] = middle
    low = (middle * rows_ref[5:6, :]).astype(BF)
    grad_ref[...] = low
    sums_ref[...] = jnp.zeros(sums_ref.shape, F32)
    sums_ref[0:1, :] = jnp.sum(low.astype(F32), axis=0, keepdims=True)
    sums_ref[1:2, :] = jnp.sum(middle * branch_ref[...], axis=0, keepdims=True)
    sums_ref[2:3, :] = jnp.sum(norm_grad * unit, axis=0, keepdims=True)
    sums_ref[3:4, :] = jnp.sum(norm_grad, axis=0, keepdims=True)
    for out, weight in zip(outs[3:], weights):
        out[...] = dot(low, weight[...], 1, 0).astype(BF)


def turn(rows, live, cotangent, unit, inverse, branch, backs, weights):
    length, width = cotangent.shape
    part = weights[0].shape[1]
    group = len(weights)
    return pl.pallas_call(
        lambda *refs: turn_kernel(group, len(backs), *refs),
        in_specs=[VMEM] * (6 + len(backs) + group),
        out_specs=[VMEM] * (3 + group),
        out_shape=[shaped((length, width), F32), shaped((length, width), BF), shaped((8, width), F32)]
        + [shaped((length, part), BF)] * group,
        compiler_params=PARAMS,
        cost_estimate=TINY,
        name="turn",
    )(rows, live, cotangent, unit, inverse, branch, *backs, *weights)


def proj_weights_kernel(ids_ref, grad_ref, *rest):
    parts, out_ref = rest[:-1], rest[-1]
    for j, part in enumerate(parts):
        out_ref[ids_ref[0] ^ j] = dot(grad_ref[...], part[...], 0, 0).astype(BF)


def proj_weights(ids, grads, parts):
    width = grads.shape[1]
    part = parts[0].shape[1]
    return pl.pallas_call(
        proj_weights_kernel,
        in_specs=[SMEM] + [VMEM] * (1 + len(parts)),
        out_specs=VMEM,
        out_shape=shaped((len(parts), width, part), BF),
        compiler_params=PARAMS,
        cost_estimate=TINY,
        name="proj_weights",
    )(ids, grads, *parts)


def mlp_kernel(count, shards, group, rows_ref, *rest):
    normed_in, cots, lives = rest[:count], rest[count : 2 * count], rest[2 * count : 3 * count]
    ids_ref, bias_ref = rest[3 * count : 3 * count + 2]
    rest = rest[3 * count + 2 :]
    pieces, backs, rest = rest[:shards], rest[shards : shards + count], rest[shards + count :]
    normed_ref, out_ref, act_ref, pre_ref, sums_ref, own_ref = rest[:6]
    if shards > 1:
        weight_ref, grad_ref, back_acc = rest[6:]
    else:
        weight_ref = pieces[0]
        grad_ref, back_acc = rest[6:]
    step = pl.program_id(0)
    size = cots[0].shape[0]

    @pl.when(step == 0)
    def _():
        if shards > 1:
            whole_size = pieces[0].shape[0]
            sub = whole_size // group
            for m, piece in enumerate(pieces):
                for j in range(group):
                    start = (ids_ref[1] ^ m) * whole_size + (ids_ref[0] ^ j) * sub
                    weight_ref[pl.ds(pl.multiple_of(start, sub), sub), :] = piece[
                        j * sub : (j + 1) * sub, :
                    ]
        normed_ref[...] = jnp.concatenate([ref[...].astype(F32) for ref in normed_in]).astype(BF)
        scale = rows_ref[9:10, :]
        grads = [cot[...].astype(F32) * live[...] for cot, live in zip(cots, lives)]
        whole_grad = jnp.concatenate(grads)
        out_ref[...] = whole_grad.astype(BF)
        scaled = (whole_grad * scale).astype(BF)
        grad_ref[...] = scaled
        own_ref[0:1, :] = jnp.sum(scaled.astype(F32)[:size], axis=0, keepdims=True)
        own_ref[1:2, :] = jnp.sum(grads[0], axis=0, keepdims=True)

    hidden = weight_ref.shape[1] // 2
    span = act_ref.shape[1]
    chunk = span // 2
    for cols in (slice(0, chunk), slice(chunk, 2 * chunk)):
        here = lanes(step * span + cols.start, chunk)
        there = lanes(hidden + step * span + cols.start, chunk)
        pre = dot(normed_ref[...], weight_ref[:, here], 1, 0) + bias_ref[:, cols]
        act_grad = dot(grad_ref[...], weight_ref[:, there], 1, 0)
        cdf = 0.5 * (1.0 + lax.erf(pre * SQRT_HALF))
        act_ref[:, cols] = (pre * cdf).astype(BF)
        slope = cdf + pre * (jnp.exp(-0.5 * pre * pre) * INV_ROOT_TWO_PI)
        pre_grad = (act_grad * slope).astype(BF)
        pre_ref[:, cols] = pre_grad
        sums_ref[:, cols] = jnp.sum(pre_grad.astype(F32), axis=0, keepdims=True)
    back = dot(pre_ref[...], weight_ref[:, lanes(step * span, span)], 1, 1)

    @pl.when(step == 0)
    def _():
        back_acc[...] = back

    @pl.when(step == pl.num_programs(0) - 1)
    def _():
        whole = back_acc[...] + back
        for j, ref in enumerate(backs):
            ref[...] = whole[j * size : (j + 1) * size].astype(BF)


def mlp(rows, normed, cots, lives, ids, bias, weights, group):
    size, width = normed[0].shape
    count, shards = len(normed), len(weights)
    length = count * size
    hidden = weights[0].shape[1] // 2
    laid = shards > 1
    step = hidden // 2

    def whole(*shape):
        return pl.BlockSpec(shape, lambda i: (0, 0))

    cols = pl.BlockSpec((length, step), lambda i: (0, i))
    return pl.pallas_call(
        lambda *refs: mlp_kernel(count, shards, group, *refs),
        grid=(2,),
        in_specs=[whole(*rows.shape)]
        + [whole(size, width)] * (2 * count)
        + [whole(size, 1)] * count
        + [SMEM, pl.BlockSpec((1, step), lambda i: (0, i))]
        + [whole(*piece.shape) for piece in weights],
        out_specs=[whole(size, width)] * count
        + [whole(length, width)] * 2
        + [cols, cols, pl.BlockSpec((1, step), lambda i: (0, i)), whole(8, width)]
        + [whole(width, 2 * hidden)] * laid,
        out_shape=[shaped((size, width), BF)] * count
        + [shaped((length, width), BF)] * 2
        + [shaped((length, hidden), BF)] * 2
        + [shaped((1, hidden), F32), shaped((8, width), F32)]
        + [shaped((width, 2 * hidden), BF)] * laid,
        scratch_shapes=[pltpu.VMEM((length, width), BF), pltpu.VMEM((length, width), F32)],
        compiler_params=PARAMS,
        cost_estimate=SMALL,
        name="mlp",
    )(rows, *normed, *cots, *lives, ids, bias, *weights)


def mlp_weights_kernel(
    direct, ids_ref, norm_a, norm_b, grad_a, grad_b, rows_ref, fc2_ref, pre_a, pre_b, act_a, act_b,
    own_ref, *rest
):
    keep_ref, send_ref, scale2_ref, *branches, out_ref = rest
    hidden = pre_a.shape[1]
    first = dot(norm_a[...], pre_a[...], 0, 0) + dot(norm_b[...], pre_b[...], 0, 0)
    size = keep_ref.shape[0]
    out_ref[0, :, :hidden] = first[:size].astype(BF)
    out_ref[1, :, :hidden] = first[size:].astype(BF)
    outs = [grad_a[...].astype(F32), grad_b[...].astype(F32)]
    scaled = [(out * rows_ref[9:10, :]).astype(BF) for out in outs]
    second = dot(scaled[0], act_a[...], 0, 0) + dot(scaled[1], act_b[...], 0, 0)
    out_ref[0, :, hidden:] = second[:size].astype(BF)
    out_ref[1, :, hidden:] = second[size:].astype(BF)
    side = (ids_ref[1] & 1) if direct else 0
    keep_ref[...] = out_ref[side]
    send_ref[...] = out_ref[1 - side]
    scale2 = own_ref[1:2, :] * rows_ref[8:9, :]
    count = len(branches) // 2
    size = branches[0].shape[0]
    for half, act in enumerate((act_a, act_b)):
        branch = dot(act[...], fc2_ref[...], 1, 1)
        scale2 = scale2 + jnp.sum(outs[half] * branch, axis=0, keepdims=True)
        for j in range(count):
            branches[half * count + j][...] = branch[j * size : (j + 1) * size].astype(BF)
    scale2_ref[...] = scale2


def mlp_weights(rows, own, normed, grads, pres, acts, weights, group, ids, direct):
    length, width = normed[0].shape
    hidden = pres[0].shape[1]
    size = 2 * length // group
    step = 256

    cols = pl.BlockSpec((length, step), lambda i, ids_ref: (0, i))
    whole = pl.BlockSpec((length, hidden), lambda i, ids_ref: (0, 0))

    def line(count):
        return pl.BlockSpec((count, step), lambda i, ids_ref: (0, i))

    part = pl.BlockSpec((step // 2, 2 * hidden), lambda i, ids_ref: (i, 0))
    return pl.pallas_call(
        lambda *refs: mlp_weights_kernel(direct, *refs),
        grid_spec=pltpu.PrefetchScalarGridSpec(
            num_scalar_prefetch=1,
            grid=(width // step,),
            in_specs=[cols] * 4
            + [line(rows.shape[0])]
            + [pl.BlockSpec((step, hidden), lambda i, ids_ref: (i, 1))]
            + [whole] * 4
            + [line(own.shape[0])],
            out_specs=[part, part, line(1)] + [line(size)] * group,
            scratch_shapes=[pltpu.VMEM((2, step // 2, 2 * hidden), BF)],
        ),
        out_shape=[shaped((width // 2, 2 * hidden), BF)] * 2
        + [shaped((1, width), F32)]
        + [shaped((size, width), BF)] * group,
        compiler_params=PARAMS,
        cost_estimate=SMALL,
        name="mlp_weights",
    )(ids, *normed, *grads, rows, weights, *pres, *acts, own)


def finish_kernel(rows_ref, middle_ref, *rest):
    terms, out_ref = rest[:-1], rest[-1]
    branch = terms[0][...].astype(F32)
    for ref in terms[1:]:
        branch = branch + ref[...].astype(F32)
    branch = branch + rows_ref[8:9, :]
    out_ref[...] = (middle_ref[...] + rows_ref[9:10, :] * branch).astype(BF)


def finish(rows, middle, terms):
    return pl.pallas_call(
        finish_kernel,
        in_specs=[VMEM] * (2 + len(terms)),
        out_specs=VMEM,
        out_shape=shaped(middle.shape, BF),
        compiler_params=PARAMS,
        name="finish",
    )(rows, middle, *terms)


def begin_kernel(rows_ref, tokens_ref, mean_ref, inv_ref, middle_ref, *rest):
    terms, out_ref = rest[:-1], rest[-1]
    grads = terms[0][...].astype(F32)
    for ref in terms[1:]:
        grads = grads + ref[...].astype(F32)
    inverse = inv_ref[...]
    unit = (tokens_ref[...].astype(F32) - mean_ref[...]) * inverse
    out_ref[...] = (middle_ref[...] + norm_back(grads, unit, inverse, rows_ref[0:1, :])).astype(BF)


def begin(rows, tokens, mean, inverse, middle_grad, terms):
    length, width = tokens.shape
    column = pl.BlockSpec((length, 1), lambda i: (0, 0))
    whole = pl.BlockSpec((length, width), lambda i: (0, 0))
    return pl.pallas_call(
        begin_kernel,
        grid=(1,),
        in_specs=[pl.BlockSpec(rows.shape, lambda i: (0, 0)), whole, column, column, whole]
        + [whole] * len(terms),
        out_specs=whole,
        out_shape=shaped((length, width), BF),
        compiler_params=PARAMS,
        name="begin",
    )(rows, tokens, mean, inverse, middle_grad, *terms)


def qkv_back_kernel(group, grad_ref, weight_ref, mean_ref, inv_ref, *rest):
    tokens, outs, sums_ref = rest[:group], rest[group:-1], rest[-1]
    size = tokens[0].shape[0]
    gain = shift = 0.0
    for first in range(0, group, 2):
        span = slice(first * size, (first + 2) * size)
        part = dot(grad_ref[span, :], weight_ref[...], 1, 1)
        inputs = jnp.concatenate([tokens[first][...].astype(F32), tokens[first + 1][...].astype(F32)])
        unit = (inputs - mean_ref[span, :]) * inv_ref[span, :]
        outs[first][...] = part[:size].astype(BF)
        outs[first + 1][...] = part[size:].astype(BF)
        gain = gain + jnp.sum(part * unit, axis=0, keepdims=True)
        shift = shift + jnp.sum(part, axis=0, keepdims=True)
    sums_ref[...] = jnp.zeros(sums_ref.shape, F32)
    sums_ref[0:1, :] = gain
    sums_ref[1:2, :] = shift


def qkv_back(qkv_grad, weight, tokens, mean, inverse):
    size, width = tokens[0].shape
    group = len(tokens)
    return pl.pallas_call(
        lambda *refs: qkv_back_kernel(group, *refs),
        in_specs=[VMEM] * (4 + group),
        out_specs=[VMEM] * (group + 1),
        out_shape=[shaped((size, width), BF)] * group + [shaped((8, width), F32)],
        compiler_params=PARAMS,
        cost_estimate=TINY,
        name="qkv_back",
    )(qkv_grad, weight, mean, inverse, *tokens)


def attn_weights_kernel(
    direct, shard, terms, ids_ref, normed_ref, grad_ref, norm1_ref, sums_ref, turn_ref, fbias_ref,
    scale2_ref, bias_a_ref, bias_b_ref, *rest,
):
    projs, outs = rest[:terms], rest[terms:-5]
    rows_ref, turned_ref, block_ref, small_ref, stage_ref = rest[-5:]
    place, row = ids_ref[0], ids_ref[1]
    width = normed_ref.shape[1]
    part = projs[0].shape[1]
    rows_ref[...] = jnp.zeros(rows_ref.shape, F32)
    rows_ref[0:2, :] = norm1_ref[0:2, :]
    for pair in range(part // PAIR):
        where = lanes(place * part + pair * PAIR, PAIR)
        rows_ref[2:3, where] = sums_ref[pair, :, :PAIR]
        rows_ref[3:4, where] = sums_ref[pair, :, 2 * PAIR :]
    rows_ref[4:8, :] = turn_ref[0:4, :]
    rows_ref[8:9, :] = fbias_ref[0:1, :]
    rows_ref[9:10, :] = scale2_ref[...]
    cols = bias_a_ref.shape[1] // part
    for owner in range(part // shard):
        for line in range(cols):
            spot = (owner * cols + line) * shard
            small_ref[line : line + 1, owner * shard : (owner + 1) * shard] = (
                bias_a_ref[0:1, spot : spot + shard] + bias_b_ref[0:1, spot : spot + shard]
            )
    rows_ref[10 : 10 + cols, lanes(place * part, part)] = small_ref[0:cols, :]
    turned_ref[...] = rows_ref[...].T
    step = block_ref.shape[0]
    for k in range(width // step):
        start = pl.multiple_of(((row >> 1) ^ k) * step, step) if direct else k * step
        cols = pl.ds(start, step)
        block_ref[:, : 3 * part] = dot(normed_ref[:, cols], grad_ref[...], 0, 0)
        proj = projs[0][cols, :].astype(F32)
        for ref in projs[1:]:
            proj = proj + ref[cols, :].astype(F32)
        block_ref[:, 3 * part : 4 * part] = proj
        block_ref[:, 4 * part :] = turned_ref[cols, :]
        if direct:
            size = step // 2
            stage_ref[0] = block_ref[:size, :].astype(BF)
            stage_ref[1] = block_ref[size:, :].astype(BF)
            side = row & 1
            blocks = width // step
            outs[k][...] = stage_ref[side]
            spot = (k + 1) % 2 * size
            outs[blocks + (blocks - 1 - k) // 2][spot : spot + size, :] = stage_ref[1 - side]
        else:
            outs[0][k * step : (k + 1) * step, :] = block_ref[...].astype(BF)


def attn_weights(ids, normed1, qkv_grad, sums, projs, blocks, shard):
    length, width = normed1.shape
    part = projs[0].shape[1]
    columns = 4 * part + EXTRA
    direct = blocks > 0
    step = 2 * (width // blocks) if direct else 256
    out_shape = [shaped((width, columns), BF)]
    if direct:
        size = width // blocks
        out_shape = [shaped((size, columns), BF)] * (blocks // 2)
        out_shape += [shaped((2 * size, columns), BF)] * (blocks // 4)
    return pl.pallas_call(
        lambda *refs: attn_weights_kernel(direct, shard, len(projs), *refs),
        in_specs=[SMEM] + [VMEM] * (2 + len(sums) + len(projs)),
        out_specs=[VMEM] * len(out_shape),
        out_shape=out_shape,
        scratch_shapes=[
            pltpu.VMEM((EXTRA, width), F32),
            pltpu.VMEM((width, EXTRA), F32),
            pltpu.VMEM((step, columns), F32),
            pltpu.VMEM((8, part), F32),
            pltpu.VMEM((2, step // 2, columns), BF),
        ],
        compiler_params=PARAMS,
        cost_estimate=SMALL,
        name="attn_weights",
    )(ids, normed1, qkv_grad, *sums, *projs)


def total(ids, terms, group):
    size, columns = terms[0].shape
    rows = size // group

    def kernel(ids_ref, *refs):
        ins, outs, sum_ref = refs[: len(terms)], refs[len(terms) : -1], refs[-1]
        value = ins[0][...].astype(F32)
        for ref in ins[1:]:
            value = value + ref[...].astype(F32)
        sum_ref[...] = value
        for k, out in enumerate(outs):
            start = pl.multiple_of((ids_ref[0] ^ k) * rows, rows)
            out[...] = sum_ref[pl.ds(start, rows), :].astype(BF)

    return pl.pallas_call(
        kernel,
        in_specs=[SMEM] + [VMEM] * len(terms),
        out_specs=[VMEM] * group,
        out_shape=[shaped((rows, columns), BF)] * group,
        scratch_shapes=[pltpu.VMEM((size, columns), F32)],
        compiler_params=PARAMS,
        name="total",
    )(ids, *terms)


def place_attn_kernel(ids_ref, *refs):
    group = len(refs) - 4
    blocks, (qkv_ref, proj_ref, vec_ref, bias_ref) = refs[:group], refs[group:]
    width = proj_ref.shape[1]
    part = width // group
    extra = jnp.zeros((qkv_ref.shape[0], EXTRA), F32)
    for k, block in enumerate(blocks):
        source = ids_ref[0] ^ k
        for third in range(3):
            for pair in range(part // PAIR):
                spot = (pair * 3 + third) * PAIR
                where = lanes(third * width + source * part + pair * PAIR, PAIR)
                qkv_ref[:, where] = block[:, spot : spot + PAIR].astype(F32)
        proj_ref[:, lanes(source * part, part)] = block[:, 3 * part : 4 * part].astype(F32)
        extra = extra + block[:, 4 * part :].astype(F32)
    turned = extra.T
    count = vec_ref.shape[0]
    vec_ref[...] = turned[:count]
    rows = qkv_ref.shape[0]
    for line in range(bias_ref.shape[1] // rows):
        bias_ref[0:1, line * rows : (line + 1) * rows] = turned[count + line : count + line + 1]


def place_attn(ids, blocks, width, vector_count, bias_cols):
    rows = blocks[0].shape[0]
    return pl.pallas_call(
        place_attn_kernel,
        in_specs=[SMEM] + [VMEM] * len(blocks),
        out_specs=[VMEM] * 4,
        out_shape=[
            shaped((rows, 3 * width), F32),
            shaped((rows, width), F32),
            shaped((vector_count, rows), F32),
            shaped((1, bias_cols * rows), F32),
        ],
        compiler_params=PARAMS,
        name="place_attn",
    )(ids, *blocks)


def place_mlp_kernel(ids_ref, *refs):
    group = len(refs) - 2
    blocks, (fc1_ref, fc2_ref) = refs[:group], refs[group:]
    part = fc1_ref.shape[1] // group
    for k, block in enumerate(blocks):
        where = lanes((ids_ref[0] ^ k) * part, part)
        fc1_ref[:, where] = block[:, :part].astype(F32)
        fc2_ref[:, where] = block[:, part:].astype(F32)


def place_mlp(ids, blocks, hidden):
    rows = blocks[0].shape[0]
    return pl.pallas_call(
        place_mlp_kernel,
        in_specs=[SMEM] + [VMEM] * len(blocks),
        out_specs=[VMEM] * 2,
        out_shape=[shaped((rows, hidden), F32)] * 2,
        compiler_params=PARAMS,
        name="place_mlp",
    )(ids, *blocks)


def local(tokens, counts, w_qkv, w_proj, w_fc1, fc1_bias, w_fc2, vectors, cotangent):
    _, capacity, width = tokens.shape
    hidden = w_fc1.shape[1]
    rows = w_qkv.shape[0]
    group, replicas = lax.axis_size("ctx"), lax.axis_size("dp")
    place, replica = lax.axis_index("ctx"), lax.axis_index("dp")
    ids = jnp.stack([place, replica]).astype(jnp.int32)
    head_width = width // group
    hidden_part = hidden // group
    bias_cols = hidden // width
    vector_count = vectors.shape[0]
    direct = replicas == 8

    def swap(value, bit, axis="ctx"):
        size = group if axis == "ctx" else replicas
        return lax.ppermute(value, axis, [(i, i ^ bit) for i in range(size)])

    def after(value, *before):
        return lax.optimization_barrier((value,) + before)[0]

    def gather(own, *before):
        pieces = [own]
        for j in range(1, group):
            bit = j & -j
            source = pieces[j ^ bit]
            pieces.append(swap(after(source, *before) if j ^ bit else source, bit))
        return pieces

    def scatter(parts, *before, mids=None, axis="ctx", scale=1, gates=None):
        pieces = {j: [part] for j, part in enumerate(parts)}

        def added(terms):
            if len(terms) == 1:
                return terms[0]
            return sum(term.astype(F32) for term in terms).astype(BF)

        bit = 1
        sent = []
        while bit < len(parts):
            for j in sorted((j for j in pieces if j & bit), reverse=True):
                value = added(pieces.pop(j))
                if bit > 1:
                    if mids is not None:
                        mids.append(value)
                    value = after(value, *before)
                elif axis == "dp":
                    value = after(value, *sent[-2:-1])
                if gates and bit in gates:
                    value = after(value, *gates[bit])
                sent.append(swap(value, bit * scale, axis))
                pieces[j ^ bit].append(sent[-1])
            bit *= 2
        return pieces[0]

    def exchange(relative):
        return [relative[0]] + [swap(relative[k], k) for k in range(1, group)]

    def in_order(relative):
        stacked = jnp.stack(relative)
        return jnp.concatenate(
            [lax.dynamic_index_in_dim(stacked, place ^ s, 0, False) for s in range(group)], axis=0
        )

    cuts = cut(
        ids, counts, w_qkv, w_proj.T, w_fc1, w_fc2.T, vectors, fc1_bias.reshape(1, -1), group
    )
    first = exchange(cuts[:group])
    tokens_far = swap(after(tokens[0], *first), group // 2)

    def widen(shards, *before):
        for m in range(2, replicas):
            low = m & -m
            if m ^ low:
                shards[m] = swap(after(shards[m ^ low], *before), low, "dp")

    second = exchange([after(block, *first) for block in cuts[group:]])
    if direct:
        shards = {0: jnp.concatenate(first, axis=0)}
        for bit in (4, 2, 1):
            shards[bit] = swap(shards[0], bit, "dp")
        arrived = [shards[bit] for bit in (4, 2, 1)] + second[1:]
        widen(shards, *arrived)
        first_pieces = [shards[m] for m in range(replicas)]
        nearly = [shards[3], shards[5], shards[7]]
    else:
        first_pieces = [lax.all_gather(in_order(first), "dp", axis=0, tiled=True)]
        arrived = nearly = [tokens_far]
    second_shard = after(in_order(second), *arrived)
    second_all = lax.all_gather(second_shard, "dp", axis=0, tiled=True)
    cotangent_far = swap(after(cotangent[0], *arrived), group // 2)
    nearly = nearly + [cotangent_far]
    tokens_pieces = [tokens[0]]
    for j in range(1, group):
        source = tokens_pieces[j ^ (j & -j)]
        if j == group // 2:
            tokens_pieces.append(tokens_far)
        else:
            tokens_pieces.append(swap(after(source, *nearly), j & -j))
    tokens_own = after(tokens[0], second_shard)
    count_column = vector_count + bias_cols
    (
        weight_qkv, weight_proj, vector_rows, normed1, qkv, mean1, inverse1, bias_fc1, key_bias,
        *live,
    ) = project(
        ids, [tokens_own] + tokens_pieces[1:], first, first_pieces, hidden_part, count_column,
        0 if direct else rows,
    )

    cotangent_pieces = [cotangent[0]]
    for j in range(1, group):
        source = cotangent_pieces[j ^ (j & -j)]
        if j == group // 2:
            cotangent_pieces.append(cotangent_far)
        else:
            cotangent_pieces.append(swap(after(source, qkv), j & -j))
    attended, lse, *attended_low = attend(qkv, key_bias, group)
    projs = gather(weight_proj, lse)
    attended_own = exchange(attended_low)
    branch1, middle, normed2_own, unit2, inverse2 = middle_step(
        vector_rows, tokens[0], attended_own, projs
    )
    half = group // 2
    normed2 = [normed2_own]
    while len(normed2) < half:
        normed2 += [swap(piece, len(normed2)) for piece in normed2]

    def feed(where, pieces, weights):
        return mlp(
            vector_rows, pieces, cotangent_pieces[where], live[where], ids, bias_fc1, weights, group
        )

    *backs_near, norm_near, grad_near, act_near, pre_near, sums_near, own_sums = feed(
        slice(0, half), normed2, [second_all]
    )
    normed2_far = [swap(normed2_own, half)]
    while len(normed2_far) < half:
        normed2_far += [
            swap(after(piece, sums_near), len(normed2_far)) for piece in normed2_far
        ]
    *backs_far, norm_far, grad_far, act_far, pre_far, sums_far, _ = feed(
        slice(half, group), normed2_far, [second_all]
    )
    mids = []
    norm2_terms = scatter(backs_near + backs_far, mids=mids)
    keep_mlp, send_mlp, grad_scale2, *branches = mlp_weights(
        vector_rows, own_sums, [norm_near, norm_far], [grad_near, grad_far], [after(pre_near, *mids), pre_far],
        [act_near, act_far], second_all, group, ids, direct,
    )
    other_mlp = None
    if direct:
        other_mlp = swap(after(send_mlp, *norm2_terms), 1, "dp")
    middle_grad, branch_grad, turn_sums, *att_grads = turn(
        after(vector_rows, grad_scale2), live[0], cotangent[0], unit2, inverse2, branch1, norm2_terms, projs
    )
    att_grads = exchange(att_grads)
    proj_parts = proj_weights(ids, branch_grad, attended_own).reshape(group * width, -1)
    proj_grad = lax.psum_scatter(
        after(proj_parts, *att_grads), "ctx", scatter_dimension=0, tiled=True
    )
    branch2_mids = []
    branch2_terms = scatter(branches, *att_grads, mids=branch2_mids)
    qkv_grad, qkv_sums = attend_back(qkv, key_bias, attended, after(lse, proj_parts), att_grads)
    *norm1_parts, norm1_sums = qkv_back(qkv_grad, weight_qkv, tokens_pieces, mean1, inverse1)
    if direct:
        other = after(other_mlp, norm1_sums)
        summed = (keep_mlp.astype(F32) + other.astype(F32)).astype(BF)
        lines = [[side + 2 * z for z in range(replicas // 2)] for side in range(2)]
        owned_mlp = lax.psum_scatter(
            summed, "dp", scatter_dimension=0, tiled=True, axis_index_groups=lines
        )
    else:
        ordered = jnp.stack(
            [part.reshape(-1, 128, 2 * hidden_part) for part in (keep_mlp, send_mlp)], axis=1
        )
        owned_mlp = lax.psum_scatter(
            ordered.reshape(width, 2 * hidden_part), "dp", scatter_dimension=0, tiled=True
        )
    before = branch2_mids + ([summed] if direct else [])
    parts = attn_weights(
        ids, after(normed1, *before), qkv_grad,
        [norm1_sums, qkv_sums, turn_sums, own_sums, grad_scale2, sums_near, sums_far],
        [proj_grad], replicas if direct else 0, rows,
    )
    norm1_terms = scatter(norm1_parts)
    if direct:
        def add(left, right):
            return (left.astype(F32) + right.astype(F32)).astype(BF)

        keep0, keep1, keep2, keep3, send32, send10 = parts
        size = keep0.shape[0]
        other32 = swap(send32, 1, "dp")
        other10 = swap(after(send10, other32, branch2_terms[-1]), 1, "dp")
        across = swap(add(keep3, other32[:size]), 2, "dp")
        near2 = add(add(keep2, other32[size:]), across)
        far = swap(after(near2, norm1_terms[-1]), 4, "dp")
        across0 = swap(add(keep1, other10[:size]), 2, "dp")
        terms = [add(keep0, other10[size:]), across0, far]
        settled = [across]
        cuts_mlp = total(after(ids, *settled), [owned_mlp], group)
    else:
        owned_attn = lax.psum_scatter(parts[0], "dp", scatter_dimension=0, tiled=True)

        def relative(owned):
            blocks = owned.reshape(group, rows, -1)
            return [lax.dynamic_index_in_dim(blocks, place ^ k, 0, False) for k in range(group)]

        cuts_mlp = relative(owned_mlp)
        settled = []
    out_fc1, out_fc2 = place_mlp(ids, exchange(cuts_mlp), hidden)
    input_grad = begin(
        vector_rows, after(tokens[0], *settled), mean1, inverse1, middle_grad, norm1_terms
    )
    output = finish(after(vector_rows, *settled), middle, branch2_terms)
    if direct:
        cuts_attn = total(after(ids, input_grad, output, out_fc1), terms, group)
    else:
        cuts_attn = relative(owned_attn)

    out_qkv, out_proj, out_vectors, out_bias = place_attn(
        ids, exchange(cuts_attn), width, vector_count, bias_cols
    )
    return (
        output[None],
        input_grad[None],
        out_qkv,
        out_proj.T,
        out_fc1,
        out_bias.reshape(-1),
        out_fc2.T,
        out_vectors,
    )


def solution(mesh):
    both = ("dp", "ctx")
    in_specs = (
        P("dp", "ctx", None),
        P("dp", "ctx"),
        P(both, None),
        P(None, both),
        P(both, None),
        P(both),
        P(None, both),
        P(None, both),
        P("dp", "ctx", None),
    )
    out_specs = (
        P("dp", "ctx", None),
        P("dp", "ctx", None),
        P(both, None),
        P(None, both),
        P(both, None),
        P(both),
        P(None, both),
        P(None, both),
    )
    return jax.shard_map(local, mesh=mesh, in_specs=in_specs, out_specs=out_specs, check_vma=False)
```

```python
import jax
import jax.numpy as jnp
from jax import lax
from jax.experimental import pallas as pl
from jax.experimental.pallas import tpu as pltpu
from jax.sharding import PartitionSpec as P

HD = 64
PAIR = 2 * HD
EXTRA = 128
EPSILON = 1e-06
MASKED_SCORE = -1e30
SQRT_HALF = 0.7071067811865476
INV_ROOT_TWO_PI = 0.3989422804014327
BF = jnp.bfloat16
F32 = jnp.float32
PARAMS = pltpu.CompilerParams(vmem_limit_bytes=60 * 1024 * 1024)
SMALL = pl.CostEstimate(flops=1_000_000_000, bytes_accessed=1_000_000, transcendentals=0)
TINY = pl.CostEstimate(flops=1_000, bytes_accessed=1_000, transcendentals=0)
VMEM = pl.BlockSpec(memory_space=pltpu.VMEM)
SMEM = pl.BlockSpec(memory_space=pltpu.SMEM)


def shaped(shape, dtype):
    return jax.ShapeDtypeStruct(shape, dtype)


def dot(left, right, left_dim, right_dim):
    return lax.dot_general(
        left, right, (((left_dim,), (right_dim,)), ((), ())), preferred_element_type=F32
    )


def lanes(start, size):
    return pl.ds(pl.multiple_of(start, 128), size)


def unit_rows(inputs):
    centered = inputs - jnp.mean(inputs, axis=-1, keepdims=True)
    spread = jnp.mean(centered * centered, axis=-1, keepdims=True)
    inverse = lax.rsqrt(spread + EPSILON)
    return (centered * inverse, inverse)


def norm_back(grad_in, unit, inverse, gain):
    scaled = grad_in * gain
    inner = (
        scaled
        - jnp.mean(scaled, axis=-1, keepdims=True)
        - unit * jnp.mean(scaled * unit, axis=-1, keepdims=True)
    )
    return inner * inverse


def cut_kernel(ids_ref, count_ref, qkv_ref, proj_ref, fc1_ref, fc2_ref, vec_ref, bias_ref, *rest):
    outs, (extra_ref, turn_ref) = rest[:-2], rest[-2:]
    group = len(outs) // 2
    place = ids_ref[0]
    width = proj_ref.shape[1]
    part = width // group
    hidden_part = fc1_ref.shape[1] // group
    vector_count, bias_cols = vec_ref.shape[0], bias_ref.shape[1] // vec_ref.shape[1]
    column = vector_count + bias_cols
    lane = lax.broadcasted_iota(jnp.int32, extra_ref.shape, 1)
    count = count_ref[0, 0]
    high = (count >> 7).astype(F32)
    low = (count & 127).astype(F32)
    extra_ref[...] = jnp.where(lane == column, high, jnp.where(lane == column + 1, low, 0.0))
    extra_ref[:, :vector_count] = vec_ref[...].astype(F32).T
    rows = qkv_ref.shape[0]
    for line in range(bias_cols):
        turn_ref[line : line + 1, :] = bias_ref[0:1, line * rows : (line + 1) * rows].astype(F32)
    extra_ref[:, vector_count:column] = turn_ref[0:bias_cols, :].T
    extra = extra_ref[...].astype(BF)
    for k in range(group):
        target = place ^ k
        first, second = outs[k], outs[group + k]
        for third in range(3):
            for pair in range(part // PAIR):
                spot = (pair * 3 + third) * PAIR
                first[:, spot : spot + PAIR] = qkv_ref[
                    :, lanes(third * width + target * part + pair * PAIR, PAIR)
                ]
        first[:, 3 * part : 4 * part] = proj_ref[:, lanes(target * part, part)]
        first[:, 4 * part :] = extra
        second[:, :hidden_part] = fc1_ref[:, lanes(target * hidden_part, hidden_part)]
        second[:, hidden_part:] = fc2_ref[:, lanes(target * hidden_part, hidden_part)]


def cut(ids, counts, w_qkv, w_proj_t, w_fc1, w_fc2_t, vectors, bias, group):
    rows, width = w_proj_t.shape
    part, hidden_part = width // group, w_fc1.shape[1] // group
    return pl.pallas_call(
        cut_kernel,
        in_specs=[SMEM, SMEM] + [VMEM] * 6,
        out_specs=[VMEM] * (2 * group),
        out_shape=[shaped((rows, 4 * part + EXTRA), BF)] * group
        + [shaped((rows, 2 * hidden_part), BF)] * group,
        scratch_shapes=[pltpu.VMEM((rows, EXTRA), F32), pltpu.VMEM((8, rows), F32)],
        compiler_params=PARAMS,
        name="cut",
    )(ids, counts, w_qkv, w_proj_t, w_fc1, w_fc2_t, vectors, bias)


def project_kernel(ordered, group, count_column, ids_ref, *rest):
    tokens, blocks, rest = rest[:group], rest[group : 2 * group], rest[2 * group :]
    pieces, outs, lives, scratch = (
        rest[: -12 - group], rest[-12 - group : -3 - group], rest[-3 - group : -3], rest[-3:]
    )
    qkv_w, proj_w, rows_ref, normed_ref, out_ref, mean_ref, inv_ref, fc1_ref, key_ref = outs
    extra_ref, bias_ref, small_ref = scratch
    place, row = ids_ref[0], ids_ref[1]
    capacity, width = tokens[0].shape
    part = proj_w.shape[1]
    size = pieces[0].shape[0]

    def lay(block, start, count):
        where = pl.ds(start, count)
        qkv_w[where, :] = block[:, : 3 * part]
        proj_w[where, :] = block[:, 3 * part : 4 * part]
        extra_ref[where, :] = block[:, 4 * part :].astype(F32)

    if ordered:
        lay(pieces[0], 0, size)
        shard = ordered
    else:
        sub = shard = size // group
        for m, piece in enumerate(pieces):
            for j in range(group):
                start = (row ^ m) * size + (place ^ j) * sub
                lay(piece.at[j * sub : (j + 1) * sub], pl.multiple_of(start, sub), sub)
    slot = lax.broadcasted_iota(jnp.int32, (capacity, 1), 0).astype(F32)
    for j, (block, live_ref) in enumerate(zip(blocks, lives)):
        extra = block[:, 4 * part :].astype(F32)[0:1, :]
        bound = extra[:, count_column : count_column + 1] * 128.0
        bound = bound + extra[:, count_column + 1 : count_column + 2]
        live = jnp.where(slot < bound, 1.0, 0.0)
        live_ref[...] = live
        key_ref[j * capacity : (j + 1) * capacity, :] = (1.0 - live) * MASKED_SCORE
    turned = extra_ref[...].T
    rows_ref[...] = turned[: rows_ref.shape[0]]
    bias_ref[...] = jnp.zeros(bias_ref.shape, F32)
    for pair in range(part // PAIR):
        for third, line in ((0, 2), (2, 3)):
            spot = (pair * 3 + third) * PAIR
            bias_ref[0:1, spot : spot + PAIR] = rows_ref[
                line : line + 1, lanes(place * part + pair * PAIR, PAIR)
            ]
    cols = fc1_ref.shape[1] // part
    small_ref[0:cols, :] = rows_ref[10 : 10 + cols, lanes(place * part, part)]
    for owner in range(part // shard):
        for line in range(cols):
            spot = (owner * cols + line) * shard
            fc1_ref[0:1, spot : spot + shard] = small_ref[
                line : line + 1, owner * shard : (owner + 1) * shard
            ]
    gain, shift, bias = rows_ref[0:1, :], rows_ref[1:2, :], bias_ref[0:1, :]
    for first in range(0, group, 2):
        span = slice(first * capacity, (first + 2) * capacity)
        inputs = jnp.concatenate([tokens[first][...].astype(F32), tokens[first + 1][...].astype(F32)])
        mean = jnp.mean(inputs, axis=-1, keepdims=True)
        centered = inputs - mean
        inverse = lax.rsqrt(jnp.mean(centered * centered, axis=-1, keepdims=True) + EPSILON)
        normed = (centered * inverse * gain + shift).astype(BF)
        normed_ref[span, :] = normed
        mean_ref[span, :] = mean
        inv_ref[span, :] = inverse
        out_ref[span, :] = (dot(normed, qkv_w[...], 1, 0) + bias).astype(BF)


def project(ids, tokens, blocks, pieces, hidden_part, count_column, ordered):
    capacity, width = tokens[0].shape
    group = len(tokens)
    length = group * capacity
    part = width // group
    return pl.pallas_call(
        lambda *refs: project_kernel(ordered, group, count_column, *refs),
        in_specs=[SMEM] + [VMEM] * (2 * group + len(pieces)),
        out_specs=[VMEM] * (9 + group),
        out_shape=[
            shaped((width, 3 * part), BF),
            shaped((width, part), BF),
            shaped((16, width), F32),
            shaped((length, width), BF),
            shaped((length, 3 * part), BF),
            shaped((length, 1), F32),
            shaped((length, 1), F32),
            shaped((1, hidden_part), F32),
            shaped((length, 1), F32),
        ]
        + [shaped((capacity, 1), F32)] * group,
        scratch_shapes=[
            pltpu.VMEM((width, EXTRA), F32),
            pltpu.VMEM((8, 3 * part), F32),
            pltpu.VMEM((8, part), F32),
        ],
        compiler_params=PARAMS,
        cost_estimate=SMALL,
        name="project",
    )(ids, *tokens, *blocks, *pieces)


def query_chunks(length):
    step = 512
    return [(start, min(step, length - start)) for start in range(0, length, step)]


def attend_kernel(qkv_ref, bias_ref, out_ref, lse_ref, *lows):
    length = qkv_ref.shape[0]
    key_bias = bias_ref[...]
    for head in range(2):
        keys = qkv_ref[:, PAIR + head * HD : PAIR + (head + 1) * HD]
        values = qkv_ref[:, 2 * PAIR + head * HD : 2 * PAIR + (head + 1) * HD]
        for start, size in query_chunks(length):
            queries = qkv_ref[start : start + size, head * HD : (head + 1) * HD]
            queries = queries * jnp.asarray(HD**-0.5, BF)
            scores = dot(keys, queries, 1, 1) + key_bias
            top = jnp.max(scores, axis=0, keepdims=True)
            expo = jnp.exp(scores - top)
            total = jnp.sum(expo, axis=0, keepdims=True)
            mixed = (dot(values, expo.astype(BF), 0, 0) / total).T
            out_ref[start : start + size, head * HD : (head + 1) * HD] = mixed
            lse_ref[0, head : head + 1, start : start + size] = top + jnp.log(total)
    for j, low in enumerate(lows):
        size = low.shape[0]
        low[...] = out_ref[j * size : (j + 1) * size, :].astype(BF)


def attend(qkv, key_bias, group):
    length, columns = qkv.shape
    pairs = columns // (3 * PAIR)
    return pl.pallas_call(
        attend_kernel,
        grid=(pairs,),
        in_specs=[
            pl.BlockSpec((length, 3 * PAIR), lambda p: (0, p)),
            pl.BlockSpec((length, 1), lambda p: (0, 0)),
        ],
        out_specs=[
            pl.BlockSpec((length, PAIR), lambda p: (0, p)),
            pl.BlockSpec((1, 2, length), lambda p: (p, 0, 0)),
        ]
        + [pl.BlockSpec((length // group, PAIR), lambda p: (0, p))] * group,
        out_shape=[
            shaped((length, pairs * PAIR), F32),
            shaped((pairs, 2, length), F32),
        ]
        + [shaped((length // group, pairs * PAIR), BF)] * group,
        compiler_params=PARAMS,
        cost_estimate=SMALL,
        name="attend",
    )(qkv, key_bias)


def attend_back_kernel(qkv_ref, bias_ref, att_ref, lse_ref, *rest):
    pieces, (out_ref, sums_ref, grad_ref) = rest[:-3], rest[-3:]
    length = qkv_ref.shape[0]
    size = pieces[0].shape[0]
    factor = HD**-0.5
    key_bias = bias_ref[...]
    for j, piece in enumerate(pieces):
        grad_ref[j * size : (j + 1) * size, :] = piece[...].astype(F32)
    for head in range(2):
        low, high = head * HD, (head + 1) * HD
        keys = qkv_ref[:, PAIR + low : PAIR + high]
        values = qkv_ref[:, 2 * PAIR + low : 2 * PAIR + high]
        key_grad = jnp.zeros((length, HD), F32)
        value_grad = jnp.zeros((length, HD), F32)
        for start, size in query_chunks(length):
            rows = slice(start, start + size)
            queries = qkv_ref[rows, low:high] * jnp.asarray(factor, BF)
            product = grad_ref[rows, low:high] * att_ref[rows, low:high]
            grads = grad_ref[rows, low:high].astype(BF)
            delta = jnp.sum(product.T, axis=0, keepdims=True)
            scores = dot(keys, queries, 1, 1) + key_bias
            probs = jnp.exp(scores - lse_ref[0, head : head + 1, rows])
            value_grad += dot(probs.astype(BF), grads, 1, 0)
            raw = (probs * (dot(values, grads, 1, 1) - delta)).astype(BF)
            key_grad += dot(raw, queries, 1, 0)
            query_grad = dot(keys, raw, 0, 0).T * factor
            out_ref[rows, low:high] = query_grad.astype(BF)
        out_ref[:, PAIR + low : PAIR + high] = key_grad.astype(BF)
        out_ref[:, 2 * PAIR + low : 2 * PAIR + high] = value_grad.astype(BF)
    sums_ref[0] = jnp.sum(out_ref[...].astype(F32), axis=0, keepdims=True)


def attend_back(qkv, key_bias, attended, lse, pieces):
    length, columns = qkv.shape
    pairs = columns // (3 * PAIR)
    size = pieces[0].shape[0]
    return pl.pallas_call(
        attend_back_kernel,
        grid=(pairs,),
        in_specs=[
            pl.BlockSpec((length, 3 * PAIR), lambda p: (0, p)),
            pl.BlockSpec((length, 1), lambda p: (0, 0)),
            pl.BlockSpec((length, PAIR), lambda p: (0, p)),
            pl.BlockSpec((1, 2, length), lambda p: (p, 0, 0)),
        ]
        + [pl.BlockSpec((size, PAIR), lambda p: (0, p))] * len(pieces),
        out_specs=[
            pl.BlockSpec((length, 3 * PAIR), lambda p: (0, p)),
            pl.BlockSpec((1, 1, 3 * PAIR), lambda p: (p, 0, 0)),
        ],
        out_shape=[shaped((length, columns), BF), shaped((pairs, 1, 3 * PAIR), F32)],
        scratch_shapes=[pltpu.VMEM((length, PAIR), F32)],
        compiler_params=PARAMS,
        cost_estimate=TINY,
        name="attend_back",
    )(qkv, key_bias, attended, lse, *pieces)


def middle_kernel(group, rows_ref, tokens_ref, *rest):
    parts, weights, (branch_ref, middle_ref, normed_ref, unit_ref, inv_ref) = (
        rest[:group], rest[group : 2 * group], rest[2 * group :]
    )
    branch = dot(parts[0][...], weights[0][...], 1, 1)
    for part, weight in zip(parts[1:], weights[1:]):
        branch = branch + dot(part[...], weight[...], 1, 1)
    branch = branch + rows_ref[4:5, :]
    branch_ref[...] = branch
    middle = tokens_ref[...].astype(F32) + rows_ref[5:6, :] * branch
    middle_ref[...] = middle
    unit, inverse = unit_rows(middle)
    unit_ref[...] = unit
    inv_ref[...] = inverse
    normed_ref[...] = (unit * rows_ref[6:7, :] + rows_ref[7:8, :]).astype(BF)


def middle_step(rows, tokens, parts, weights):
    length, width = tokens.shape
    group = len(parts)
    full = shaped((length, width), F32)
    return pl.pallas_call(
        lambda *refs: middle_kernel(group, *refs),
        in_specs=[VMEM] * (2 + 2 * group),
        out_specs=[VMEM] * 5,
        out_shape=[full, full, shaped((length, width), BF), full, shaped((length, 1), F32)],
        compiler_params=PARAMS,
        cost_estimate=SMALL,
        name="middle",
    )(rows, tokens, *parts, *weights)


def turn_kernel(group, terms, rows_ref, live_ref, cot_ref, unit_ref, inv_ref, branch_ref, *rest):
    backs, weights, outs = rest[:terms], rest[terms : terms + group], rest[terms + group :]
    middle_ref, grad_ref, sums_ref = outs[:3]
    norm_grad = backs[0][...].astype(F32)
    for ref in backs[1:]:
        norm_grad = norm_grad + ref[...].astype(F32)
    unit = unit_ref[...]
    out_grad = cot_ref[...].astype(F32) * live_ref[...]
    middle = out_grad + norm_back(norm_grad, unit, inv_ref[...], rows_ref[6:7, :])
    middle_ref[...] = middle
    low = (middle * rows_ref[5:6, :]).astype(BF)
    grad_ref[...] = low
    sums_ref[...] = jnp.zeros(sums_ref.shape, F32)
    sums_ref[0:1, :] = jnp.sum(low.astype(F32), axis=0, keepdims=True)
    sums_ref[1:2, :] = jnp.sum(middle * branch_ref[...], axis=0, keepdims=True)
    sums_ref[2:3, :] = jnp.sum(norm_grad * unit, axis=0, keepdims=True)
    sums_ref[3:4, :] = jnp.sum(norm_grad, axis=0, keepdims=True)
    for out, weight in zip(outs[3:], weights):
        out[...] = dot(low, weight[...], 1, 0).astype(BF)


def turn(rows, live, cotangent, unit, inverse, branch, backs, weights):
    length, width = cotangent.shape
    part = weights[0].shape[1]
    group = len(weights)
    return pl.pallas_call(
        lambda *refs: turn_kernel(group, len(backs), *refs),
        in_specs=[VMEM] * (6 + len(backs) + group),
        out_specs=[VMEM] * (3 + group),
        out_shape=[shaped((length, width), F32), shaped((length, width), BF), shaped((8, width), F32)]
        + [shaped((length, part), BF)] * group,
        compiler_params=PARAMS,
        cost_estimate=TINY,
        name="turn",
    )(rows, live, cotangent, unit, inverse, branch, *backs, *weights)


def proj_weights_kernel(ids_ref, grad_ref, *rest):
    parts, out_ref = rest[:-1], rest[-1]
    for j, part in enumerate(parts):
        out_ref[ids_ref[0] ^ j] = dot(grad_ref[...], part[...], 0, 0).astype(BF)


def proj_weights(ids, grads, parts):
    width = grads.shape[1]
    part = parts[0].shape[1]
    return pl.pallas_call(
        proj_weights_kernel,
        in_specs=[SMEM] + [VMEM] * (1 + len(parts)),
        out_specs=VMEM,
        out_shape=shaped((len(parts), width, part), BF),
        compiler_params=PARAMS,
        cost_estimate=TINY,
        name="proj_weights",
    )(ids, grads, *parts)


def mlp_kernel(count, shards, group, rows_ref, *rest):
    normed_in, cots, lives = rest[:count], rest[count : 2 * count], rest[2 * count : 3 * count]
    ids_ref, bias_ref = rest[3 * count : 3 * count + 2]
    rest = rest[3 * count + 2 :]
    pieces, backs, rest = rest[:shards], rest[shards : shards + count], rest[shards + count :]
    normed_ref, out_ref, act_ref, pre_ref, sums_ref, own_ref = rest[:6]
    if shards > 1:
        weight_ref, grad_ref, back_acc = rest[6:]
    else:
        weight_ref = pieces[0]
        grad_ref, back_acc = rest[6:]
    step = pl.program_id(0)
    size = cots[0].shape[0]

    @pl.when(step == 0)
    def _():
        if shards > 1:
            whole_size = pieces[0].shape[0]
            sub = whole_size // group
            for m, piece in enumerate(pieces):
                for j in range(group):
                    start = (ids_ref[1] ^ m) * whole_size + (ids_ref[0] ^ j) * sub
                    weight_ref[pl.ds(pl.multiple_of(start, sub), sub), :] = piece[
                        j * sub : (j + 1) * sub, :
                    ]
        normed_ref[...] = jnp.concatenate([ref[...].astype(F32) for ref in normed_in]).astype(BF)
        scale = rows_ref[9:10, :]
        grads = [cot[...].astype(F32) * live[...] for cot, live in zip(cots, lives)]
        whole_grad = jnp.concatenate(grads)
        out_ref[...] = whole_grad.astype(BF)
        scaled = (whole_grad * scale).astype(BF)
        grad_ref[...] = scaled
        own_ref[0:1, :] = jnp.sum(scaled.astype(F32)[:size], axis=0, keepdims=True)
        own_ref[1:2, :] = jnp.sum(grads[0], axis=0, keepdims=True)

    hidden = weight_ref.shape[1] // 2
    span = act_ref.shape[1]
    chunk = span // 2
    for cols in (slice(0, chunk), slice(chunk, 2 * chunk)):
        here = lanes(step * span + cols.start, chunk)
        there = lanes(hidden + step * span + cols.start, chunk)
        pre = dot(normed_ref[...], weight_ref[:, here], 1, 0) + bias_ref[:, cols]
        act_grad = dot(grad_ref[...], weight_ref[:, there], 1, 0)
        cdf = 0.5 * (1.0 + lax.erf(pre * SQRT_HALF))
        act_ref[:, cols] = (pre * cdf).astype(BF)
        slope = cdf + pre * (jnp.exp(-0.5 * pre * pre) * INV_ROOT_TWO_PI)
        pre_grad = (act_grad * slope).astype(BF)
        pre_ref[:, cols] = pre_grad
        sums_ref[:, cols] = jnp.sum(pre_grad.astype(F32), axis=0, keepdims=True)
    back = dot(pre_ref[...], weight_ref[:, lanes(step * span, span)], 1, 1)

    @pl.when(step == 0)
    def _():
        back_acc[...] = back

    @pl.when(step == pl.num_programs(0) - 1)
    def _():
        whole = back_acc[...] + back
        for j, ref in enumerate(backs):
            ref[...] = whole[j * size : (j + 1) * size].astype(BF)


def mlp(rows, normed, cots, lives, ids, bias, weights, group):
    size, width = normed[0].shape
    count, shards = len(normed), len(weights)
    length = count * size
    hidden = weights[0].shape[1] // 2
    laid = shards > 1
    step = hidden // 2

    def whole(*shape):
        return pl.BlockSpec(shape, lambda i: (0, 0))

    cols = pl.BlockSpec((length, step), lambda i: (0, i))
    return pl.pallas_call(
        lambda *refs: mlp_kernel(count, shards, group, *refs),
        grid=(2,),
        in_specs=[whole(*rows.shape)]
        + [whole(size, width)] * (2 * count)
        + [whole(size, 1)] * count
        + [SMEM, pl.BlockSpec((1, step), lambda i: (0, i))]
        + [whole(*piece.shape) for piece in weights],
        out_specs=[whole(size, width)] * count
        + [whole(length, width)] * 2
        + [cols, cols, pl.BlockSpec((1, step), lambda i: (0, i)), whole(8, width)]
        + [whole(width, 2 * hidden)] * laid,
        out_shape=[shaped((size, width), BF)] * count
        + [shaped((length, width), BF)] * 2
        + [shaped((length, hidden), BF)] * 2
        + [shaped((1, hidden), F32), shaped((8, width), F32)]
        + [shaped((width, 2 * hidden), BF)] * laid,
        scratch_shapes=[pltpu.VMEM((length, width), BF), pltpu.VMEM((length, width), F32)],
        compiler_params=PARAMS,
        cost_estimate=SMALL,
        name="mlp",
    )(rows, *normed, *cots, *lives, ids, bias, *weights)


def mlp_weights_kernel(
    direct, ids_ref, norm_a, norm_b, grad_a, grad_b, rows_ref, fc2_ref, pre_a, pre_b, act_a, act_b,
    own_ref, *rest
):
    keep_ref, send_ref, scale2_ref, *branches, out_ref = rest
    hidden = pre_a.shape[1]
    first = dot(norm_a[...], pre_a[...], 0, 0) + dot(norm_b[...], pre_b[...], 0, 0)
    size = keep_ref.shape[0]
    out_ref[0, :, :hidden] = first[:size].astype(BF)
    out_ref[1, :, :hidden] = first[size:].astype(BF)
    outs = [grad_a[...].astype(F32), grad_b[...].astype(F32)]
    scaled = [(out * rows_ref[9:10, :]).astype(BF) for out in outs]
    second = dot(scaled[0], act_a[...], 0, 0) + dot(scaled[1], act_b[...], 0, 0)
    out_ref[0, :, hidden:] = second[:size].astype(BF)
    out_ref[1, :, hidden:] = second[size:].astype(BF)
    side = (ids_ref[1] & 1) if direct else 0
    keep_ref[...] = out_ref[side]
    send_ref[...] = out_ref[1 - side]
    scale2 = own_ref[1:2, :] * rows_ref[8:9, :]
    count = len(branches) // 2
    size = branches[0].shape[0]
    for half, act in enumerate((act_a, act_b)):
        branch = dot(act[...], fc2_ref[...], 1, 1)
        scale2 = scale2 + jnp.sum(outs[half] * branch, axis=0, keepdims=True)
        for j in range(count):
            branches[half * count + j][...] = branch[j * size : (j + 1) * size].astype(BF)
    scale2_ref[...] = scale2


def mlp_weights(rows, own, normed, grads, pres, acts, weights, group, ids, direct):
    length, width = normed[0].shape
    hidden = pres[0].shape[1]
    size = 2 * length // group
    step = 256

    cols = pl.BlockSpec((length, step), lambda i, ids_ref: (0, i))
    whole = pl.BlockSpec((length, hidden), lambda i, ids_ref: (0, 0))

    def line(count):
        return pl.BlockSpec((count, step), lambda i, ids_ref: (0, i))

    part = pl.BlockSpec((step // 2, 2 * hidden), lambda i, ids_ref: (i, 0))
    return pl.pallas_call(
        lambda *refs: mlp_weights_kernel(direct, *refs),
        grid_spec=pltpu.PrefetchScalarGridSpec(
            num_scalar_prefetch=1,
            grid=(width // step,),
            in_specs=[cols] * 4
            + [line(rows.shape[0])]
            + [pl.BlockSpec((step, hidden), lambda i, ids_ref: (i, 1))]
            + [whole] * 4
            + [line(own.shape[0])],
            out_specs=[part, part, line(1)] + [line(size)] * group,
            scratch_shapes=[pltpu.VMEM((2, step // 2, 2 * hidden), BF)],
        ),
        out_shape=[shaped((width // 2, 2 * hidden), BF)] * 2
        + [shaped((1, width), F32)]
        + [shaped((size, width), BF)] * group,
        compiler_params=PARAMS,
        cost_estimate=SMALL,
        name="mlp_weights",
    )(ids, *normed, *grads, rows, weights, *pres, *acts, own)


def finish_kernel(rows_ref, middle_ref, *rest):
    terms, out_ref = rest[:-1], rest[-1]
    branch = terms[0][...].astype(F32)
    for ref in terms[1:]:
        branch = branch + ref[...].astype(F32)
    branch = branch + rows_ref[8:9, :]
    out_ref[...] = (middle_ref[...] + rows_ref[9:10, :] * branch).astype(BF)


def finish(rows, middle, terms):
    return pl.pallas_call(
        finish_kernel,
        in_specs=[VMEM] * (2 + len(terms)),
        out_specs=VMEM,
        out_shape=shaped(middle.shape, BF),
        compiler_params=PARAMS,
        name="finish",
    )(rows, middle, *terms)


def begin_kernel(rows_ref, tokens_ref, mean_ref, inv_ref, middle_ref, *rest):
    terms, out_ref = rest[:-1], rest[-1]
    grads = terms[0][...].astype(F32)
    for ref in terms[1:]:
        grads = grads + ref[...].astype(F32)
    inverse = inv_ref[...]
    unit = (tokens_ref[...].astype(F32) - mean_ref[...]) * inverse
    out_ref[...] = (middle_ref[...] + norm_back(grads, unit, inverse, rows_ref[0:1, :])).astype(BF)


def begin(rows, tokens, mean, inverse, middle_grad, terms):
    length, width = tokens.shape
    column = pl.BlockSpec((length, 1), lambda i: (0, 0))
    whole = pl.BlockSpec((length, width), lambda i: (0, 0))
    return pl.pallas_call(
        begin_kernel,
        grid=(1,),
        in_specs=[pl.BlockSpec(rows.shape, lambda i: (0, 0)), whole, column, column, whole]
        + [whole] * len(terms),
        out_specs=whole,
        out_shape=shaped((length, width), BF),
        compiler_params=PARAMS,
        name="begin",
    )(rows, tokens, mean, inverse, middle_grad, *terms)


def qkv_back_kernel(group, grad_ref, weight_ref, mean_ref, inv_ref, *rest):
    tokens, outs, sums_ref = rest[:group], rest[group:-1], rest[-1]
    size = tokens[0].shape[0]
    gain = shift = 0.0
    for first in range(0, group, 2):
        span = slice(first * size, (first + 2) * size)
        part = dot(grad_ref[span, :], weight_ref[...], 1, 1)
        inputs = jnp.concatenate([tokens[first][...].astype(F32), tokens[first + 1][...].astype(F32)])
        unit = (inputs - mean_ref[span, :]) * inv_ref[span, :]
        outs[first][...] = part[:size].astype(BF)
        outs[first + 1][...] = part[size:].astype(BF)
        gain = gain + jnp.sum(part * unit, axis=0, keepdims=True)
        shift = shift + jnp.sum(part, axis=0, keepdims=True)
    sums_ref[...] = jnp.zeros(sums_ref.shape, F32)
    sums_ref[0:1, :] = gain
    sums_ref[1:2, :] = shift


def qkv_back(qkv_grad, weight, tokens, mean, inverse):
    size, width = tokens[0].shape
    group = len(tokens)
    return pl.pallas_call(
        lambda *refs: qkv_back_kernel(group, *refs),
        in_specs=[VMEM] * (4 + group),
        out_specs=[VMEM] * (group + 1),
        out_shape=[shaped((size, width), BF)] * group + [shaped((8, width), F32)],
        compiler_params=PARAMS,
        cost_estimate=TINY,
        name="qkv_back",
    )(qkv_grad, weight, mean, inverse, *tokens)


def attn_weights_kernel(
    direct, shard, terms, ids_ref, normed_ref, grad_ref, norm1_ref, sums_ref, turn_ref, fbias_ref,
    scale2_ref, bias_a_ref, bias_b_ref, *rest,
):
    projs, outs = rest[:terms], rest[terms:-5]
    rows_ref, turned_ref, block_ref, small_ref, stage_ref = rest[-5:]
    place, row = ids_ref[0], ids_ref[1]
    width = normed_ref.shape[1]
    part = projs[0].shape[1]
    rows_ref[...] = jnp.zeros(rows_ref.shape, F32)
    rows_ref[0:2, :] = norm1_ref[0:2, :]
    for pair in range(part // PAIR):
        where = lanes(place * part + pair * PAIR, PAIR)
        rows_ref[2:3, where] = sums_ref[pair, :, :PAIR]
        rows_ref[3:4, where] = sums_ref[pair, :, 2 * PAIR :]
    rows_ref[4:8, :] = turn_ref[0:4, :]
    rows_ref[8:9, :] = fbias_ref[0:1, :]
    rows_ref[9:10, :] = scale2_ref[...]
    cols = bias_a_ref.shape[1] // part
    for owner in range(part // shard):
        for line in range(cols):
            spot = (owner * cols + line) * shard
            small_ref[line : line + 1, owner * shard : (owner + 1) * shard] = (
                bias_a_ref[0:1, spot : spot + shard] + bias_b_ref[0:1, spot : spot + shard]
            )
    rows_ref[10 : 10 + cols, lanes(place * part, part)] = small_ref[0:cols, :]
    turned_ref[...] = rows_ref[...].T
    step = block_ref.shape[0]
    for k in range(width // step):
        start = pl.multiple_of(((row >> 1) ^ k) * step, step) if direct else k * step
        cols = pl.ds(start, step)
        block_ref[:, : 3 * part] = dot(normed_ref[:, cols], grad_ref[...], 0, 0)
        proj = projs[0][cols, :].astype(F32)
        for ref in projs[1:]:
            proj = proj + ref[cols, :].astype(F32)
        block_ref[:, 3 * part : 4 * part] = proj
        block_ref[:, 4 * part :] = turned_ref[cols, :]
        if direct:
            size = step // 2
            stage_ref[0] = block_ref[:size, :].astype(BF)
            stage_ref[1] = block_ref[size:, :].astype(BF)
            side = row & 1
            blocks = width // step
            outs[k][...] = stage_ref[side]
            spot = (k + 1) % 2 * size
            outs[blocks + (blocks - 1 - k) // 2][spot : spot + size, :] = stage_ref[1 - side]
        else:
            outs[0][k * step : (k + 1) * step, :] = block_ref[...].astype(BF)


def attn_weights(ids, normed1, qkv_grad, sums, projs, blocks, shard):
    length, width = normed1.shape
    part = projs[0].shape[1]
    columns = 4 * part + EXTRA
    direct = blocks > 0
    step = 2 * (width // blocks) if direct else 256
    out_shape = [shaped((width, columns), BF)]
    if direct:
        size = width // blocks
        out_shape = [shaped((size, columns), BF)] * (blocks // 2)
        out_shape += [shaped((2 * size, columns), BF)] * (blocks // 4)
    return pl.pallas_call(
        lambda *refs: attn_weights_kernel(direct, shard, len(projs), *refs),
        in_specs=[SMEM] + [VMEM] * (2 + len(sums) + len(projs)),
        out_specs=[VMEM] * len(out_shape),
        out_shape=out_shape,
        scratch_shapes=[
            pltpu.VMEM((EXTRA, width), F32),
            pltpu.VMEM((width, EXTRA), F32),
            pltpu.VMEM((step, columns), F32),
            pltpu.VMEM((8, part), F32),
            pltpu.VMEM((2, step // 2, columns), BF),
        ],
        compiler_params=PARAMS,
        cost_estimate=SMALL,
        name="attn_weights",
    )(ids, normed1, qkv_grad, *sums, *projs)


def total(ids, terms, group):
    size, columns = terms[0].shape
    rows = size // group

    def kernel(ids_ref, *refs):
        ins, outs, sum_ref = refs[: len(terms)], refs[len(terms) : -1], refs[-1]
        value = ins[0][...].astype(F32)
        for ref in ins[1:]:
            value = value + ref[...].astype(F32)
        sum_ref[...] = value
        for k, out in enumerate(outs):
            start = pl.multiple_of((ids_ref[0] ^ k) * rows, rows)
            out[...] = sum_ref[pl.ds(start, rows), :].astype(BF)

    return pl.pallas_call(
        kernel,
        in_specs=[SMEM] + [VMEM] * len(terms),
        out_specs=[VMEM] * group,
        out_shape=[shaped((rows, columns), BF)] * group,
        scratch_shapes=[pltpu.VMEM((size, columns), F32)],
        compiler_params=PARAMS,
        name="total",
    )(ids, *terms)


def place_attn_kernel(ids_ref, *refs):
    group = len(refs) - 4
    blocks, (qkv_ref, proj_ref, vec_ref, bias_ref) = refs[:group], refs[group:]
    width = proj_ref.shape[1]
    part = width // group
    extra = jnp.zeros((qkv_ref.shape[0], EXTRA), F32)
    for k, block in enumerate(blocks):
        source = ids_ref[0] ^ k
        for third in range(3):
            for pair in range(part // PAIR):
                spot = (pair * 3 + third) * PAIR
                where = lanes(third * width + source * part + pair * PAIR, PAIR)
                qkv_ref[:, where] = block[:, spot : spot + PAIR].astype(F32)
        proj_ref[:, lanes(source * part, part)] = block[:, 3 * part : 4 * part].astype(F32)
        extra = extra + block[:, 4 * part :].astype(F32)
    turned = extra.T
    count = vec_ref.shape[0]
    vec_ref[...] = turned[:count]
    rows = qkv_ref.shape[0]
    for line in range(bias_ref.shape[1] // rows):
        bias_ref[0:1, line * rows : (line + 1) * rows] = turned[count + line : count + line + 1]


def place_attn(ids, blocks, width, vector_count, bias_cols):
    rows = blocks[0].shape[0]
    return pl.pallas_call(
        place_attn_kernel,
        in_specs=[SMEM] + [VMEM] * len(blocks),
        out_specs=[VMEM] * 4,
        out_shape=[
            shaped((rows, 3 * width), F32),
            shaped((rows, width), F32),
            shaped((vector_count, rows), F32),
            shaped((1, bias_cols * rows), F32),
        ],
        compiler_params=PARAMS,
        name="place_attn",
    )(ids, *blocks)


def place_mlp_kernel(ids_ref, *refs):
    group = len(refs) - 2
    blocks, (fc1_ref, fc2_ref) = refs[:group], refs[group:]
    part = fc1_ref.shape[1] // group
    for k, block in enumerate(blocks):
        where = lanes((ids_ref[0] ^ k) * part, part)
        fc1_ref[:, where] = block[:, :part].astype(F32)
        fc2_ref[:, where] = block[:, part:].astype(F32)


def place_mlp(ids, blocks, hidden):
    rows = blocks[0].shape[0]
    return pl.pallas_call(
        place_mlp_kernel,
        in_specs=[SMEM] + [VMEM] * len(blocks),
        out_specs=[VMEM] * 2,
        out_shape=[shaped((rows, hidden), F32)] * 2,
        compiler_params=PARAMS,
        name="place_mlp",
    )(ids, *blocks)


def local(tokens, counts, w_qkv, w_proj, w_fc1, fc1_bias, w_fc2, vectors, cotangent):
    _, capacity, width = tokens.shape
    hidden = w_fc1.shape[1]
    rows = w_qkv.shape[0]
    group, replicas = lax.axis_size("ctx"), lax.axis_size("dp")
    place, replica = lax.axis_index("ctx"), lax.axis_index("dp")
    ids = jnp.stack([place, replica]).astype(jnp.int32)
    head_width = width // group
    hidden_part = hidden // group
    bias_cols = hidden // width
    vector_count = vectors.shape[0]
    direct = replicas == 8

    def swap(value, bit, axis="ctx"):
        size = group if axis == "ctx" else replicas
        return lax.ppermute(value, axis, [(i, i ^ bit) for i in range(size)])

    def after(value, *before):
        return lax.optimization_barrier((value,) + before)[0]

    def gather(own, *before):
        pieces = [own]
        for j in range(1, group):
            bit = j & -j
            source = pieces[j ^ bit]
            pieces.append(swap(after(source, *before) if j ^ bit else source, bit))
        return pieces

    def scatter(parts, *before, mids=None, axis="ctx", scale=1, gates=None):
        pieces = {j: [part] for j, part in enumerate(parts)}

        def added(terms):
            if len(terms) == 1:
                return terms[0]
            return sum(term.astype(F32) for term in terms).astype(BF)

        bit = 1
        sent = []
        while bit < len(parts):
            for j in sorted((j for j in pieces if j & bit), reverse=True):
                value = added(pieces.pop(j))
                if bit > 1:
                    if mids is not None:
                        mids.append(value)
                    value = after(value, *before)
                elif axis == "dp":
                    value = after(value, *sent[-2:-1])
                if gates and bit in gates:
                    value = after(value, *gates[bit])
                sent.append(swap(value, bit * scale, axis))
                pieces[j ^ bit].append(sent[-1])
            bit *= 2
        return pieces[0]

    def exchange(relative):
        return [relative[0]] + [swap(relative[k], k) for k in range(1, group)]

    def in_order(relative):
        stacked = jnp.stack(relative)
        return jnp.concatenate(
            [lax.dynamic_index_in_dim(stacked, place ^ s, 0, False) for s in range(group)], axis=0
        )

    cuts = cut(
        ids, counts, w_qkv, w_proj.T, w_fc1, w_fc2.T, vectors, fc1_bias.reshape(1, -1), group
    )
    first = exchange(cuts[:group])
    tokens_far = swap(after(tokens[0], *first), group // 2)

    def widen(shards, *before):
        for m in range(2, replicas):
            low = m & -m
            if m ^ low:
                shards[m] = swap(after(shards[m ^ low], *before), low, "dp")

    second = exchange([after(block, *first) for block in cuts[group:]])
    if direct:
        shards = {0: jnp.concatenate(first, axis=0)}
        for bit in (4, 2, 1):
            shards[bit] = swap(shards[0], bit, "dp")
        arrived = [shards[bit] for bit in (4, 2, 1)] + second[1:]
        widen(shards, *arrived)
        first_pieces = [shards[m] for m in range(replicas)]
        nearly = [shards[3], shards[5], shards[7]]
    else:
        first_pieces = [lax.all_gather(in_order(first), "dp", axis=0, tiled=True)]
        arrived = nearly = [tokens_far]
    second_shard = after(in_order(second), *arrived)
    second_all = lax.all_gather(second_shard, "dp", axis=0, tiled=True)
    cotangent_far = swap(after(cotangent[0], *arrived), group // 2)
    nearly = nearly + [cotangent_far]
    tokens_pieces = [tokens[0]]
    for j in range(1, group):
        source = tokens_pieces[j ^ (j & -j)]
        if j == group // 2:
            tokens_pieces.append(tokens_far)
        else:
            tokens_pieces.append(swap(after(source, *nearly), j & -j))
    tokens_own = after(tokens[0], second_shard)
    count_column = vector_count + bias_cols
    (
        weight_qkv, weight_proj, vector_rows, normed1, qkv, mean1, inverse1, bias_fc1, key_bias,
        *live,
    ) = project(
        ids, [tokens_own] + tokens_pieces[1:], first, first_pieces, hidden_part, count_column,
        0 if direct else rows,
    )

    cotangent_pieces = [cotangent[0]]
    for j in range(1, group):
        source = cotangent_pieces[j ^ (j & -j)]
        if j == group // 2:
            cotangent_pieces.append(cotangent_far)
        else:
            cotangent_pieces.append(swap(after(source, qkv), j & -j))
    attended, lse, *attended_low = attend(qkv, key_bias, group)
    projs = gather(weight_proj, lse)
    attended_own = exchange(attended_low)
    branch1, middle, normed2_own, unit2, inverse2 = middle_step(
        vector_rows, tokens[0], attended_own, projs
    )
    half = group // 2
    normed2 = [normed2_own]
    while len(normed2) < half:
        normed2 += [swap(piece, len(normed2)) for piece in normed2]

    def feed(where, pieces, weights):
        return mlp(
            vector_rows, pieces, cotangent_pieces[where], live[where], ids, bias_fc1, weights, group
        )

    *backs_near, norm_near, grad_near, act_near, pre_near, sums_near, own_sums = feed(
        slice(0, half), normed2, [second_all]
    )
    normed2_far = [swap(normed2_own, half)]
    while len(normed2_far) < half:
        normed2_far += [
            swap(after(piece, sums_near), len(normed2_far)) for piece in normed2_far
        ]
    *backs_far, norm_far, grad_far, act_far, pre_far, sums_far, _ = feed(
        slice(half, group), normed2_far, [second_all]
    )
    mids = []
    norm2_terms = scatter(backs_near + backs_far, mids=mids)
    keep_mlp, send_mlp, grad_scale2, *branches = mlp_weights(
        vector_rows, own_sums, [norm_near, norm_far], [grad_near, grad_far], [after(pre_near, *mids), pre_far],
        [act_near, act_far], second_all, group, ids, direct,
    )
    other_mlp = None
    if direct:
        other_mlp = swap(after(send_mlp, *norm2_terms), 1, "dp")
    middle_grad, branch_grad, turn_sums, *att_grads = turn(
        after(vector_rows, grad_scale2), live[0], cotangent[0], unit2, inverse2, branch1, norm2_terms, projs
    )
    att_grads = exchange(att_grads)
    proj_parts = proj_weights(ids, branch_grad, attended_own).reshape(group * width, -1)
    proj_grad = lax.psum_scatter(
        after(proj_parts, *att_grads), "ctx", scatter_dimension=0, tiled=True
    )
    branch2_mids = []
    branch2_terms = scatter(branches, *att_grads, mids=branch2_mids)
    qkv_grad, qkv_sums = attend_back(qkv, key_bias, attended, after(lse, proj_parts), att_grads)
    *norm1_parts, norm1_sums = qkv_back(qkv_grad, weight_qkv, tokens_pieces, mean1, inverse1)
    before = branch2_mids
    parts = attn_weights(
        ids, after(normed1, *before), qkv_grad,
        [norm1_sums, qkv_sums, turn_sums, own_sums, grad_scale2, sums_near, sums_far],
        [proj_grad], replicas if direct else 0, rows,
    )
    if direct:
        other = after(other_mlp, parts[0])
        summed = (keep_mlp.astype(F32) + other.astype(F32)).astype(BF)
        lines = [[side + 2 * z for z in range(replicas // 2)] for side in range(2)]
        owned_mlp = lax.psum_scatter(
            summed, "dp", scatter_dimension=0, tiled=True, axis_index_groups=lines
        )
    else:
        ordered = jnp.stack(
            [part.reshape(-1, 128, 2 * hidden_part) for part in (keep_mlp, send_mlp)], axis=1
        )
        owned_mlp = lax.psum_scatter(
            ordered.reshape(width, 2 * hidden_part), "dp", scatter_dimension=0, tiled=True
        )
    norm1_terms = scatter(norm1_parts)
    if direct:
        def add(left, right):
            return (left.astype(F32) + right.astype(F32)).astype(BF)

        keep0, keep1, keep2, keep3, send32, send10 = parts
        size = keep0.shape[0]
        other32 = swap(send32, 1, "dp")
        other10 = swap(after(send10, other32, branch2_terms[-1]), 1, "dp")
        across = swap(add(keep3, other32[:size]), 2, "dp")
        near2 = add(add(keep2, other32[size:]), across)
        far = swap(after(near2, norm1_terms[-1]), 4, "dp")
        across0 = swap(add(keep1, other10[:size]), 2, "dp")
        terms = [add(keep0, other10[size:]), across0, far]
        settled = [across]
    else:
        owned_attn = lax.psum_scatter(parts[0], "dp", scatter_dimension=0, tiled=True)

        def relative(owned):
            blocks = owned.reshape(group, rows, -1)
            return [lax.dynamic_index_in_dim(blocks, place ^ k, 0, False) for k in range(group)]

        cuts_mlp = relative(owned_mlp)
        settled = []
    input_grad = begin(
        vector_rows, after(tokens[0], *settled), mean1, inverse1, middle_grad, norm1_terms
    )
    output = finish(after(vector_rows, *settled), middle, branch2_terms)
    if direct:
        cuts_attn = total(after(ids, input_grad, output), terms, group)
        cuts_mlp = total(after(ids, *cuts_attn), [owned_mlp], group)
    else:
        cuts_attn = relative(owned_attn)

    out_fc1, out_fc2 = place_mlp(ids, exchange(cuts_mlp), hidden)
    out_qkv, out_proj, out_vectors, out_bias = place_attn(
        ids, exchange(cuts_attn), width, vector_count, bias_cols
    )
    return (
        output[None],
        input_grad[None],
        out_qkv,
        out_proj.T,
        out_fc1,
        out_bias.reshape(-1),
        out_fc2.T,
        out_vectors,
    )


def solution(mesh):
    both = ("dp", "ctx")
    in_specs = (
        P("dp", "ctx", None),
        P("dp", "ctx"),
        P(both, None),
        P(None, both),
        P(both, None),
        P(both),
        P(None, both),
        P(None, both),
        P("dp", "ctx", None),
    )
    out_specs = (
        P("dp", "ctx", None),
        P("dp", "ctx", None),
        P(both, None),
        P(None, both),
        P(both, None),
        P(both),
        P(None, both),
        P(None, both),
    )
    return jax.shard_map(local, mesh=mesh, in_specs=in_specs, out_specs=out_specs, check_vma=False)
```
